32 devices in a mesh: groups: 2 (over x), seq: 4 (over y, core), tp: 4 (over z).
Axes of the slice: x: 2, y: 2, z: 4, core: 2. Of those that a mesh axis runs over, the one named last changes fastest.
Arguments:
- prefill_states: bfloat16 [8192, 8192], P(('groups', 'seq'), 'tp'), parts along dimension 0, may hold values from -6 to 6
- kv_weight: bfloat16 [8192, 2048], P('tp'), may hold values from -0.0625 to 0.0625
- page_counts: int32 [16], P('groups'), parts along dimension 0, may hold values from 1 to 16, 32 in all
- tail_tokens: int32 [16], P('groups'), parts along dimension 0, may hold values from 1 to 128
- new_query: bfloat16 [16, 2, 8192], P(('groups', 'seq'), None, 'tp'), parts along dimension 0, may hold values from -60 to 60
- new_keyval: bfloat16 [16, 2, 2048], P(('groups', 'seq'), None, 'tp'), parts along dimension 0, may hold values from -6 to 6
- residual: bfloat16 [16, 2, 8192], P('groups', None, 'seq'), parts along dimension 0, may hold values from -6 to 6
- out_weight: bfloat16 [8192, 8192], P('tp', 'seq'), may hold values from -0.0625 to 0.0625
Outputs:
- mixed: float32 [16, 2, 8192], P('groups', None, 'seq'), parts along dimension 0
The draws below stay inside these ranges and needn't reach their ends.
There are 2 independent parts, one for each index of `groups`. The reference program is written for one: setup_inputs(seed, part) draws one part's arguments, and reference() takes and returns one part's arrays. A program takes and returns all parts, laid end to end along the dimension named above; an argument that names none is the same for every part. Nothing has to cross between parts.
Inputs may be any that keep to these rules, and one draw needn't show every extreme that they name: `page_counts`: prompts are laid end to end over the 32 pages of a part in request order; the page counts sum to 32; the longest prompt has exactly 16 pages. Request r is decoded by index r // 2 of seq.
All inputs are finite; a program needn't handle non-finite values.
Results may differ from the reference program's by a relative error of at most 0.025.
Values may be sent and summed in bfloat16 or wider, within the bound.
No kernel may reach another device: no remote copies, remote signals or barrier semaphores. Data moves between devices by JAX's collectives and lax.ppermute only.
A program may use at most 128 MiB of HBM per device.

```python
import math
import jax
import jax.numpy as jnp
import numpy as np
from jax import lax

D = 8192
QH = 64
KVH = 8
HD = 128
PAGE = 128
NEW = 2
MOSTP = 16
TOKENS = 4096
PAGES = 32
REQUESTS = 8
N_TP = 4


def draw_new_query(key, part):
    key = jax.random.fold_in(key, 11)
    noise_key, scale_key = jax.random.split(key)
    shape = (REQUESTS, NEW, QH * HD)
    base = jax.random.normal(noise_key, shape, jnp.float32)
    scales = jnp.exp(jax.random.uniform(scale_key, (REQUESTS, NEW, QH, 1), jnp.float32, 0.0, math.log(4.0)))
    scaled = (base.reshape(REQUESTS, NEW, QH, HD) * scales).reshape(shape)
    return jnp.clip(scaled, -60.0, 60.0).astype(jnp.bfloat16)


def touch_ends(drawn, rng, low, top_value):
    longest = drawn.shape.index(max(drawn.shape))
    spots = []
    for shift in (0, 1):
        where = [jax.random.randint(jax.random.fold_in(rng, axis), (), 0, length) for axis, length in enumerate(drawn.shape)]
        where[longest] = (where[longest] + shift) % drawn.shape[longest]
        spots.append(tuple(where))
    return drawn.at[spots[0]].set(low).at[spots[1]].set(top_value)


def level_of(rng, shape, pieces, low, largest):
    def one(dim, shards_of):
        draws = jax.random.uniform(jax.random.fold_in(jax.random.fold_in(rng, 6), dim), (shards_of,), jnp.float32, low / len(pieces), largest / len(pieces))
        return jnp.repeat(jnp.exp(draws), shape[dim] // shards_of).reshape((-1,) + (1,) * (len(shape) - dim - 1))

    loudness = one(*pieces[0])
    for cut in pieces[1:]:
        loudness = loudness * one(*cut)
    return loudness


def profile(number_of, total, most, skew):
    portions = [(1 << 20) // math.isqrt(standing ** skew) + 1 for standing in range(2, number_of + 1)]
    surplus, given = total - most - (number_of - 1), [1] * (number_of - 1)
    while surplus > 0:
        free = [i for i in range(number_of - 1) if given[i] < most]
        mass, budget = sum([portions[i] for i in free]), surplus
        for i in free:
            more = min(most - given[i], max(1, budget * portions[i] // mass), surplus)
            given[i] = given[i] + more
            surplus = surplus - more
    return np.array([most] + given)


def uneven_parts(stream_key, count, total, most, lean):
    if count == 2:
        one = jax.random.randint(stream_key, (), max(1, total - most), min(most, total - 1) + 1)
        return jnp.stack([one, total - one])
    sizes = jnp.asarray(profile(count, total, most, lean), jnp.int32)
    pairs = (count - 1) // 2
    giver, sink = sizes[1:1 + 2 * pairs:2], sizes[2:2 + 2 * pairs:2]
    room = jnp.minimum(giver - 1, most - sink)
    shifted = jax.random.randint(jax.random.fold_in(stream_key, 1), (pairs,), 0, 1 << 20) % (room + 1)
    sizes = sizes.at[1:1 + 2 * pairs:2].set(giver - shifted).at[2:2 + 2 * pairs:2].set(sink + shifted)
    return sizes[jax.random.permutation(jax.random.fold_in(stream_key, 2), count)]


def centred(key, dims, width, bound, shards=(), held_as=jnp.bfloat16):
    result = width * jax.random.normal(key, dims, jnp.float32)
    if shards:
        result = result * level_of(key, dims, shards, -0.22, 0.18)
    return jnp.clip(result, -bound, bound).astype(held_as)


def setup_inputs(seed: int = 0, part: int = 0) -> dict:
    keys = jax.random.split(jax.random.key(seed), 9)
    part_keys = jax.random.split(jax.random.fold_in(keys[8], part), 9)
    prefill_states = centred(part_keys[0], (TOKENS, D), 1.0, 6.0, ((0, 4), (1, 4)))
    kv_weight = centred(keys[1], (D, KVH * 2 * HD), D ** -0.5, 0.0625, ((0, 4),))
    page_counts = uneven_parts(part_keys[2], REQUESTS, PAGES, MOSTP, 2).astype(jnp.int32)
    tail_tokens = touch_ends(jax.random.randint(part_keys[3], (REQUESTS,), 1, PAGE + 1), jax.random.fold_in(part_keys[3], 1), 1, PAGE).astype(jnp.int32)
    new_query = draw_new_query(jax.random.fold_in(jax.random.fold_in(keys[8], part), 71), part)
    new_keyval = centred(part_keys[5], (REQUESTS, NEW, KVH * 2 * HD), 1.0, 6.0, ((0, 4), (2, 4)))
    residual = centred(part_keys[6], (REQUESTS, NEW, D), 1.0, 6.0, ((2, 4),))
    out_weight = centred(keys[7], (QH * HD, D), (QH * HD) ** -0.5, 0.0625, ((0, 4), (1, 4)))
    return {"prefill_states": prefill_states, "kv_weight": kv_weight, "page_counts": page_counts, "tail_tokens": tail_tokens, "new_query": new_query, "new_keyval": new_keyval, "residual": residual, "out_weight": out_weight}


def rotary(values_in, where_at):
    half_dim = values_in.shape[-1] // 2
    steps = jnp.arange(half_dim, dtype=jnp.float32)
    freqs = jnp.exp(-(steps * (2.0 / values_in.shape[-1])) * math.log(500000.0))
    angles = where_at[..., None] * freqs
    cosine = jnp.cos(angles)
    sine = jnp.sin(angles)
    first = values_in[..., :half_dim]
    second = values_in[..., half_dim:]
    return jnp.concatenate([first * cosine - second * sine, second * cosine + first * sine], axis=-1)

def layout(page_counts, tail_tokens):
    page_ends = jnp.cumsum(page_counts).astype(jnp.int32)
    starts = (page_ends - page_counts).astype(jnp.int32)
    lengths = ((page_counts - 1) * PAGE + tail_tokens).astype(jnp.int32)
    return (starts, lengths)

def owners(token_index, starts, lengths):
    prompts = starts.shape[0]
    page_index = token_index // PAGE
    covered = (page_index[:, None] >= starts[None, :]).astype(jnp.int32)
    prompt = lax.optimization_barrier(jnp.sum(covered, axis=1)).astype(jnp.int32) - 1
    onehot = prompt[:, None] == jnp.arange(prompts, dtype=jnp.int32)[None, :]
    begin_token = lax.optimization_barrier(jnp.sum(jnp.where(onehot, starts[None, :], 0), axis=1)).astype(jnp.int32) * PAGE
    limit_len = lax.optimization_barrier(jnp.sum(jnp.where(onehot, lengths[None, :], 0), axis=1)).astype(jnp.int32)
    position = token_index - begin_token
    return (prompt, position, position < limit_len)

def reference(prefill_states, kv_weight, page_counts, tail_tokens, new_query, new_keyval, residual, out_weight):
    shard_width = D // N_TP
    projected = jnp.zeros((TOKENS, KVH * 2 * HD), jnp.float32)
    for slice_index in range(N_TP):
        lower = slice_index * shard_width
        product = jnp.dot(prefill_states[:, lower:lower + shard_width], kv_weight[lower:lower + shard_width], preferred_element_type=jnp.float32)
        rounded = lax.optimization_barrier(product.astype(jnp.bfloat16))
        projected = projected + rounded.astype(jnp.float32)
    projected = projected.reshape(TOKENS, KVH, 2, HD)
    starts, lengths = layout(page_counts, tail_tokens)
    token_index = jnp.arange(TOKENS, dtype=jnp.int32)
    prompt, position, is_live = owners(token_index, starts, lengths)
    cache_keys = rotary(projected[:, :, 0], position.astype(jnp.float32)[:, None]).astype(jnp.bfloat16)
    cache_values = projected[:, :, 1].astype(jnp.bfloat16)
    group_size = QH // KVH
    new_pos = (lengths[:, None] + jnp.arange(NEW, dtype=jnp.int32)[None, :]).astype(jnp.float32)
    queries = new_query.astype(jnp.float32).reshape(REQUESTS, NEW, KVH, group_size, HD)
    queries = rotary(queries, new_pos[:, :, None, None]).astype(jnp.bfloat16)
    fresh = new_keyval.astype(jnp.float32).reshape(REQUESTS, NEW, KVH, 2, HD)
    fresh_keys = rotary(fresh[:, :, :, 0], new_pos[:, :, None]).astype(jnp.bfloat16)
    fresh_values = fresh[:, :, :, 1].astype(jnp.bfloat16)
    key_mask = (prompt[None, :] == jnp.arange(REQUESTS, dtype=jnp.int32)[:, None]) & is_live[None, :]
    causal = jnp.arange(NEW)[None, :] <= jnp.arange(NEW)[:, None]
    scale = 1.0 / math.sqrt(HD)

    def one_head(head_index):
        head_query = queries[:, :, head_index].astype(jnp.float32)
        head_keys = cache_keys[:, head_index].astype(jnp.float32)
        head_values = cache_values[:, head_index].astype(jnp.float32)
        own_keys = fresh_keys[:, :, head_index].astype(jnp.float32)
        own_values = fresh_values[:, :, head_index].astype(jnp.float32)
        old_scores = jnp.einsum('rnjd,td->rnjt', head_query, head_keys) * scale
        old_scores = jnp.where(key_mask[:, None, None, :], old_scores, -1e+30)
        new_scores = jnp.einsum('rnjd,rmd->rnjm', head_query, own_keys) * scale
        new_scores = jnp.where(causal[None, :, None, :], new_scores, -1e+30)
        maxima = jnp.maximum(lax.optimization_barrier(jnp.max(old_scores, axis=-1)), lax.optimization_barrier(jnp.max(new_scores, axis=-1)))
        old_weights = jnp.where(key_mask[:, None, None, :], jnp.exp(old_scores - maxima[..., None]), 0.0)
        new_weights = jnp.where(causal[None, :, None, :], jnp.exp(new_scores - maxima[..., None]), 0.0)
        totals = lax.optimization_barrier(jnp.sum(old_weights, axis=-1)) + lax.optimization_barrier(jnp.sum(new_weights, axis=-1))
        summed = jnp.einsum('rnjt,td->rnjd', old_weights.astype(jnp.bfloat16).astype(jnp.float32), head_values)
        summed = summed + jnp.einsum('rnjm,rmd->rnjd', new_weights.astype(jnp.bfloat16).astype(jnp.float32), own_values)
        return summed / totals[..., None]
    per_head = lax.map(one_head, jnp.arange(KVH, dtype=jnp.int32))
    attended = per_head.transpose(1, 2, 0, 3, 4).reshape(REQUESTS * NEW, QH * HD).astype(jnp.bfloat16)
    projected_out = jnp.dot(attended, out_weight, preferred_element_type=jnp.float32).reshape(REQUESTS, NEW, D)
    return residual.astype(jnp.float32) + projected_out
```

```python
import functools
import math

import jax
import jax.numpy as jnp
from jax import lax
from jax.experimental import pallas as pl
from jax.experimental.pallas import tpu as pltpu
from jax.sharding import PartitionSpec as P

QH = 64
KVH = 8
HD = 128
PAGE = 128
GROUP = QH // KVH
NEG = -1e30
F32 = jnp.float32
BF16 = jnp.bfloat16
MIB = 1 << 20

VMEM = pl.BlockSpec(memory_space=pltpu.VMEM)
SMEM = pl.BlockSpec(memory_space=pltpu.SMEM)


def shifts(value, axis):
    size = lax.axis_size(axis)
    return [value] + [
        lax.ppermute(value, axis, [(i, (i + d) % size) for i in range(size)])
        for d in range(1, size)
    ]


def exchange(chunks, axis):
    size = lax.axis_size(axis)
    return [chunks[0]] + [
        lax.ppermute(chunks[d], axis, [(i, (i + d) % size) for i in range(size)])
        for d in range(1, size)
    ]


def lane_freqs(rows):
    lane = lax.broadcasted_iota(jnp.int32, (rows, HD), 1) % (HD // 2)
    return jnp.exp(-(lane.astype(F32) * (2.0 / HD)) * math.log(500000.0))


def sine_sign(rows):
    lane = lax.broadcasted_iota(jnp.int32, (rows, HD), 1)
    return jnp.where(lane < HD // 2, -1.0, 1.0)


def ring(axis, back):
    size = lax.axis_size(axis)
    return lax.rem(lax.axis_index(axis) + size - back, size)


def ahead(axis, forward):
    return lax.rem(lax.axis_index(axis) + forward, lax.axis_size(axis))


def keys_kernel(pages, prompts, x_ref, wa_ref, wb_ref, counts, tails, out_ref, meta, cos_s, sin_s):
    step = pl.program_id(0)
    tokens = x_ref.shape[0]
    local_pages = tokens // PAGE

    @pl.when(step == 0)
    def _():
        def one_prompt(r, start):
            length = (counts[r] - 1) * PAGE + tails[r]
            meta[3 * pages + r] = length

            def one_page(i, carry):
                meta[start + i] = r
                meta[pages + start + i] = i * PAGE
                meta[2 * pages + start + i] = jnp.minimum(length - i * PAGE, PAGE)
                return carry

            lax.fori_loop(0, counts[r], one_page, 0)
            return start + counts[r]

        lax.fori_loop(0, prompts, one_prompt, 0)
        freqs = lane_freqs(PAGE)
        offset = lax.broadcasted_iota(jnp.int32, (PAGE, HD), 0).astype(F32) * freqs
        cos_off, sin_off = jnp.cos(offset), jnp.sin(offset)
        row_freqs = lane_freqs(8)
        sign = sine_sign(PAGE)
        first = lax.axis_index("seq") * local_pages
        for p in range(local_pages):
            base = meta[pages + first + p].astype(F32) * row_freqs
            cos_base, sin_base = jnp.cos(base)[:1], jnp.sin(base)[:1]
            cos_s[p * PAGE : (p + 1) * PAGE] = cos_off * cos_base - sin_off * sin_base
            sin_s[p * PAGE : (p + 1) * PAGE] = sign * (sin_off * cos_base + cos_off * sin_base)

    weight = jnp.concatenate([wa_ref[...], wb_ref[...]], axis=1)

    def rows(i, carry):
        at = pl.ds(pl.multiple_of(i * 256, 256), 256)
        product = jnp.dot(x_ref[at], weight, preferred_element_type=F32)
        cosine, sine = cos_s[at], sin_s[at]
        for half in range(2):
            k = product[:, half * HD : (half + 1) * HD]
            k = k * cosine + pltpu.roll(k, HD // 2, 1) * sine
            out_ref[at, half * HD : (half + 1) * HD] = k.astype(BF16)
        return carry

    lax.fori_loop(0, tokens // 256, rows, 0)


def values_kernel(x_ref, wa_ref, wb_ref, out_ref):
    weight = jnp.concatenate([wa_ref[...], wb_ref[...]], axis=1)

    def rows(i, carry):
        at = pl.ds(pl.multiple_of(i * 256, 256), 256)
        out_ref[at] = jnp.dot(x_ref[at], weight, preferred_element_type=F32).astype(BF16)
        return carry

    lax.fori_loop(0, x_ref.shape[0] // 256, rows, 0)


def project_keys(x, kv_weight, counts, tails, pages):
    tokens, depth = x.shape
    prompts = counts.shape[0]
    return pl.pallas_call(
        functools.partial(keys_kernel, pages, prompts),
        grid=(KVH // 2,),
        in_specs=[
            pl.BlockSpec((tokens, depth), lambda i: (0, 0)),
            pl.BlockSpec((depth, HD), lambda i: (0, 4 * i)),
            pl.BlockSpec((depth, HD), lambda i: (0, 4 * i + 2)),
            SMEM,
            SMEM,
        ],
        out_specs=[pl.BlockSpec((tokens, 2 * HD), lambda i: (0, i)), SMEM],
        out_shape=[
            jax.ShapeDtypeStruct((tokens, KVH * HD), BF16),
            jax.ShapeDtypeStruct((3 * pages + prompts,), jnp.int32),
        ],
        scratch_shapes=[pltpu.VMEM((tokens, HD), F32), pltpu.VMEM((tokens, HD), F32)],
        compiler_params=pltpu.CompilerParams(vmem_limit_bytes=40 * MIB),
        cost_estimate=pl.CostEstimate(
            flops=2 * tokens * depth * KVH * HD, bytes_accessed=12 * MIB, transcendentals=0
        ),
        name="keys",
    )(x, kv_weight, kv_weight, counts, tails)


def project_values(x, kv_weight):
    tokens, depth = x.shape
    return pl.pallas_call(
        values_kernel,
        grid=(KVH // 2,),
        in_specs=[
            pl.BlockSpec((tokens, depth), lambda i: (0, 0)),
            pl.BlockSpec((depth, HD), lambda i: (0, 4 * i + 1)),
            pl.BlockSpec((depth, HD), lambda i: (0, 4 * i + 3)),
        ],
        out_specs=pl.BlockSpec((tokens, 2 * HD), lambda i: (0, i)),
        out_shape=jax.ShapeDtypeStruct((tokens, KVH * HD), BF16),
        compiler_params=pltpu.CompilerParams(vmem_limit_bytes=40 * MIB),
        cost_estimate=pl.CostEstimate(
            flops=2 * tokens * depth * KVH * HD, bytes_accessed=12 * MIB, transcendentals=0
        ),
        name="values",
    )(x, kv_weight, kv_weight)


def scores_kernel(pages, own_rows, n_seq, n_tp, *refs):
    pieces = refs[:n_seq]
    k_ref, meta = refs[n_seq : n_seq + 2]
    outs = refs[n_seq + 2 : n_seq + 2 + n_tp]
    own_ref, all_q = refs[n_seq + 2 + n_tp :]
    kv_local = KVH // n_tp
    local_pages = k_ref.shape[0] // PAGE
    new_count = pieces[0].shape[2]
    rows = new_count * GROUP
    freqs = lane_freqs(8)
    sign = sine_sign(8)
    for ds in range(n_seq):
        for rr in range(own_rows):
            request = ring("seq", ds) * own_rows + rr
            length = meta[3 * pages + request]
            cosines, sines = [], []
            for n in range(new_count):
                angle = (length + n).astype(F32) * freqs
                cosines.append(jnp.cos(angle))
                sines.append(jnp.sin(angle) * sign)
            for dt in range(n_tp):
                heads = [pieces[ds][dt, rr, n].astype(F32) for n in range(new_count)]
                for g in range(kv_local):
                    parts = []
                    for n in range(new_count):
                        q = heads[n][g * GROUP : (g + 1) * GROUP]
                        parts.append(q * cosines[n] + pltpu.roll(q, HD // 2, 1) * sines[n])
                    block = jnp.concatenate(parts, axis=0).astype(BF16)
                    at = (ring("tp", dt) * kv_local + g) * rows
                    all_q[request, pl.ds(pl.multiple_of(at, rows), rows)] = block
                    if dt == 0:
                        own_ref[request, g * rows : (g + 1) * rows] = block
    first = lax.axis_index("seq") * local_pages

    def one_page(p, carry):
        request = meta[first + p]
        tokens = pl.ds(pl.multiple_of(p * PAGE, PAGE), PAGE)
        for dt in range(n_tp):
            for g in range(kv_local):
                head = ahead("tp", dt) * kv_local + g
                k = k_ref[tokens, pl.ds(pl.multiple_of(head * HD, HD), HD)]
                q = all_q[request, pl.ds(pl.multiple_of(head * rows, rows), rows)]
                s = lax.dot_general(q, k, (((1,), (1,)), ((), ())), preferred_element_type=F32)
                outs[dt][g * rows : (g + 1) * rows, tokens] = (s * (1.0 / math.sqrt(HD))).astype(
                    BF16
                )
        return carry

    lax.fori_loop(0, local_pages, one_page, 0)


def partial_scores(pieces, k, meta, pages, prompts):
    n_seq, n_tp = lax.axis_size("seq"), lax.axis_size("tp")
    own_rows, new_count = pieces[0].shape[1], pieces[0].shape[2]
    tokens = k.shape[0]
    rows = KVH // n_tp * new_count * GROUP
    return pl.pallas_call(
        functools.partial(scores_kernel, pages, own_rows, n_seq, n_tp),
        in_specs=[VMEM] * (n_seq + 1) + [SMEM],
        out_specs=[VMEM] * (n_tp + 1),
        out_shape=[jax.ShapeDtypeStruct((rows, tokens), BF16)] * n_tp
        + [jax.ShapeDtypeStruct((prompts, rows, HD), BF16)],
        scratch_shapes=[pltpu.VMEM((prompts, rows * n_tp, HD), BF16)],
        compiler_params=pltpu.CompilerParams(vmem_limit_bytes=32 * MIB),
        cost_estimate=pl.CostEstimate(
            flops=2 * tokens * rows * n_tp * HD, bytes_accessed=3 * MIB, transcendentals=0
        ),
        name="scores",
    )(*pieces, k, meta)


def weights_kernel(pages, n_tp, *refs):
    chunks = refs[:n_tp]
    meta, w_ref, stats_ref = refs[n_tp:]
    rows, tokens = w_ref.shape
    local_pages = tokens // PAGE
    first = lax.axis_index("seq") * local_pages
    scores, maxima = [], []
    lane = lax.broadcasted_iota(jnp.int32, (rows, PAGE), 1)
    masks = []
    for p in range(local_pages):
        at = slice(p * PAGE, (p + 1) * PAGE)
        total = chunks[0][:, at].astype(F32)
        for d in range(1, n_tp):
            total = total + chunks[d][:, at].astype(F32)
        mask = lane < meta[2 * pages + first + p]
        total = jnp.where(mask, total, NEG)
        masks.append(mask)
        scores.append(total)
        maxima.append(jnp.max(total, axis=1, keepdims=True))
    stats = jnp.zeros((rows, PAGE), F32)
    for p in range(local_pages):
        top = maxima[p]
        for other in range(local_pages):
            if other != p:
                same = meta[first + p] == meta[first + other]
                top = jnp.where(same, jnp.maximum(top, maxima[other]), top)
        w = jnp.where(masks[p], jnp.exp(scores[p] - top), 0.0)
        w_ref[:, p * PAGE : (p + 1) * PAGE] = w.astype(BF16)
        stats = jnp.where(lane == p, top, stats)
        stats = jnp.where(lane == local_pages + p, jnp.sum(w, axis=1, keepdims=True), stats)
    stats_ref[...] = stats


def softmax_weights(chunks, meta, pages):
    n_tp = len(chunks)
    rows, tokens = chunks[0].shape
    return pl.pallas_call(
        functools.partial(weights_kernel, pages, n_tp),
        in_specs=[VMEM] * n_tp + [SMEM],
        out_specs=[VMEM, VMEM],
        out_shape=[
            jax.ShapeDtypeStruct((rows, tokens), BF16),
            jax.ShapeDtypeStruct((rows, PAGE), F32),
        ],
        name="weights",
    )(*chunks, meta)


def weighted_kernel(pages, n_tp, *refs):
    pieces = refs[:n_tp]
    v_ref, meta = refs[n_tp : n_tp + 2]
    outs = refs[n_tp + 2 : n_tp + 2 + n_tp]
    total = refs[-1]
    kv_local = KVH // n_tp
    rows_local = pieces[0].shape[0]
    rows = rows_local // kv_local
    local_pages = v_ref.shape[0] // PAGE
    first = lax.axis_index("seq") * local_pages
    total[...] = jnp.zeros_like(total)

    def one_page(p, carry):
        request = meta[first + p]
        tokens = pl.ds(pl.multiple_of(p * PAGE, PAGE), PAGE)
        for dt in range(n_tp):
            for g in range(kv_local):
                head = ring("tp", dt) * kv_local + g
                v = v_ref[tokens, pl.ds(pl.multiple_of(head * HD, HD), HD)]
                w = pieces[dt][g * rows : (g + 1) * rows, tokens]
                at = pl.ds(pl.multiple_of(head * rows, rows), rows)
                total[request, at] += jnp.dot(w, v, preferred_element_type=F32)
        return carry

    lax.fori_loop(0, local_pages, one_page, 0)
    for dt in range(n_tp):
        at = pl.ds(pl.multiple_of(ahead("tp", dt) * rows_local, rows_local), rows_local)
        outs[dt][...] = total[:, at].astype(BF16)


def weighted_values(pieces, v, meta, pages, prompts):
    n_tp = len(pieces)
    rows, tokens = pieces[0].shape
    return pl.pallas_call(
        functools.partial(weighted_kernel, pages, n_tp),
        in_specs=[VMEM] * (n_tp + 1) + [SMEM],
        out_specs=[VMEM] * n_tp,
        out_shape=[jax.ShapeDtypeStruct((prompts, rows, HD), BF16)] * n_tp,
        scratch_shapes=[pltpu.VMEM((prompts, rows * n_tp, HD), F32)],
        compiler_params=pltpu.CompilerParams(vmem_limit_bytes=32 * MIB),
        name="weighted",
    )(*pieces, v, meta)


def merge_kernel(pages, own_rows, n_seq, *refs):
    stats = refs[:n_seq]
    fresh = refs[n_seq : 2 * n_seq]
    q_ref, meta, factor_ref, add_ref, all_stats, tops, sums = refs[2 * n_seq :]
    prompts, rows_local, _ = q_ref.shape
    new_count = fresh[0].shape[1]
    rows = new_count * GROUP
    kv_local = rows_local // rows
    local_pages = pages // n_seq
    scale = 1.0 / math.sqrt(HD)
    freqs = lane_freqs(8)
    sign = sine_sign(8)
    step = lax.broadcasted_iota(jnp.int32, (rows, HD), 0) // GROUP
    for ds in range(n_seq):
        all_stats[ring("seq", ds)] = stats[ds][...]
    kept = []
    for ds in range(n_seq):
        for rr in range(own_rows):
            request = ring("seq", ds) * own_rows + rr
            length = meta[3 * pages + request]
            for g in range(kv_local):
                q = q_ref[request, g * rows : (g + 1) * rows].astype(F32)
                points = []
                for n in range(new_count):
                    angle = (length + n).astype(F32) * freqs
                    cosine, sine = jnp.cos(angle)[:1], (jnp.sin(angle) * sign)[:1]
                    both = fresh[ds][rr, n].astype(F32)
                    k = both[2 * g : 2 * g + 1]
                    k = k * cosine + pltpu.roll(k, HD // 2, 1) * sine
                    k = k.astype(BF16).astype(F32)
                    s = jnp.sum(q * k, axis=1, keepdims=True) * scale
                    s = jnp.broadcast_to(s, (rows, HD))
                    points.append((jnp.where(step >= n, s, NEG), both[2 * g + 1 : 2 * g + 2]))
                top = points[0][0]
                for s, _ in points[1:]:
                    top = jnp.maximum(top, s)
                at = slice(g * rows, (g + 1) * rows)
                tops[request, at] = top
                kept.append((request, at, points))

    def grow(page, carry):
        request = meta[page]
        block = all_stats[page // local_pages]
        lane = lax.broadcasted_iota(jnp.int32, block.shape, 1)
        here = lane == page % local_pages
        top = jnp.max(jnp.where(here, block, 2 * NEG), axis=1, keepdims=True)
        tops[request] = jnp.maximum(tops[request], top)
        return carry

    lax.fori_loop(0, pages, grow, 0)
    for request, at, points in kept:
        part = jnp.zeros((rows, HD), F32)
        weighted = jnp.zeros((rows, HD), F32)
        for n, (s, value) in enumerate(points):
            w = jnp.where(step >= n, jnp.exp(s - tops[request, at]), 0.0)
            part = part + w
            weighted = weighted + w * value
        sums[request, at] = part
        add_ref[request, at] = weighted

    def collect(page, carry):
        request = meta[page]
        block = all_stats[page // local_pages]
        lane = lax.broadcasted_iota(jnp.int32, block.shape, 1)
        place = page % local_pages
        top = jnp.sum(jnp.where(lane == place, block, 0.0), axis=1, keepdims=True)
        part = jnp.sum(jnp.where(lane == local_pages + place, block, 0.0), axis=1, keepdims=True)
        sums[request] += part * jnp.exp(top - tops[request])
        return carry

    lax.fori_loop(0, pages, collect, 0)
    factor_ref[...] = jnp.zeros_like(factor_ref)
    first = lax.axis_index("seq") * local_pages
    mine = stats[0][...]

    for p in range(local_pages):
        request = meta[first + p]
        factor_ref[request] = jnp.exp(mine[:, p : p + 1] - tops[request]) / sums[request]
    add_ref[...] = add_ref[...] / sums[...]


def merge(stats, fresh, own_q, meta, pages):
    n_seq = len(stats)
    prompts, rows, _ = own_q.shape
    own_rows = fresh[0].shape[0]
    return pl.pallas_call(
        functools.partial(merge_kernel, pages, own_rows, n_seq),
        in_specs=[VMEM] * (2 * n_seq + 1) + [SMEM],
        out_specs=[VMEM, VMEM],
        out_shape=[jax.ShapeDtypeStruct((prompts, rows, HD), F32)] * 2,
        scratch_shapes=[
            pltpu.VMEM((n_seq,) + stats[0].shape, F32),
            pltpu.VMEM((prompts, rows, HD), F32),
            pltpu.VMEM((prompts, rows, HD), F32),
        ],
        name="merge",
    )(*stats, *fresh, own_q, meta)


def scaled_kernel(n_tp, *refs):
    chunks = refs[:n_tp]
    factor_ref, out_ref = refs[n_tp:]
    total = chunks[0][...].astype(F32)
    for d in range(1, n_tp):
        total = total + chunks[d][...].astype(F32)
    out_ref[...] = (total * factor_ref[...]).astype(BF16)


def scaled_sum(chunks, factor):
    n_tp = len(chunks)
    return pl.pallas_call(
        functools.partial(scaled_kernel, n_tp),
        in_specs=[VMEM] * (n_tp + 1),
        out_specs=VMEM,
        out_shape=jax.ShapeDtypeStruct(chunks[0].shape, BF16),
        name="scaled",
    )(*chunks, factor)


def output_kernel(n_seq, new_count, *refs):
    pieces = refs[:n_seq]
    add_ref, w_ref, out_ref, held = refs[n_seq:]
    prompts, rows_local, _ = add_ref.shape
    rows = new_count * GROUP
    kv_local = rows_local // rows

    @pl.when(pl.program_id(0) == 0)
    def _():
        for r in range(prompts):
            total = add_ref[r]
            for d in range(n_seq):
                total = total + pieces[d][r].astype(F32)
            for g in range(kv_local):
                for n in range(new_count):
                    at = g * rows + n * GROUP
                    held[g * GROUP : (g + 1) * GROUP, r * new_count + n] = total[at : at + GROUP]

    heads = kv_local * GROUP
    left = jnp.concatenate([held[h].astype(BF16) for h in range(heads)], axis=1)
    out_ref[...] = jnp.dot(left, w_ref[...], preferred_element_type=F32).astype(BF16)


def output_partial(pieces, add, out_weight, new_count):
    n_seq = len(pieces)
    prompts, rows, _ = add.shape
    depth, columns = out_weight.shape
    width = min(columns, 512)
    whole = pl.BlockSpec((prompts, rows, HD), lambda i: (0, 0, 0))
    return pl.pallas_call(
        functools.partial(output_kernel, n_seq, new_count),
        grid=(columns // width,),
        in_specs=[whole] * (n_seq + 1) + [pl.BlockSpec((depth, width), lambda i: (0, i))],
        out_specs=pl.BlockSpec((prompts * new_count, width), lambda i: (0, i)),
        out_shape=jax.ShapeDtypeStruct((prompts * new_count, columns), BF16),
        scratch_shapes=[pltpu.VMEM((depth // HD, prompts * new_count, HD), F32)],
        compiler_params=pltpu.CompilerParams(vmem_limit_bytes=32 * MIB),
        name="output",
    )(*pieces, add, out_weight)


def final_kernel(n_tp, *refs):
    pieces = refs[:n_tp]
    res_ref, out_ref = refs[n_tp:]
    prompts, new_count, _ = out_ref.shape
    total = pieces[0][...].astype(F32)
    for d in range(1, n_tp):
        total = total + pieces[d][...].astype(F32)
    for r in range(prompts):
        out_ref[r] = res_ref[r].astype(F32) + total[r * new_count : (r + 1) * new_count]


def final_sum(pieces, residual):
    n_tp = len(pieces)
    return pl.pallas_call(
        functools.partial(final_kernel, n_tp),
        in_specs=[VMEM] * (n_tp + 1),
        out_specs=VMEM,
        out_shape=jax.ShapeDtypeStruct(residual.shape, F32),
        name="final",
    )(*pieces, residual)


def on_device(
    prefill_states, kv_weight, page_counts, tail_tokens, new_query, new_keyval, residual, out_weight
):
    n_seq, n_tp = lax.axis_size("seq"), lax.axis_size("tp")
    own_rows, new_count, _ = new_query.shape
    prompts = page_counts.shape[0]
    pages = prefill_states.shape[0] // PAGE * n_seq
    heads = QH // n_tp
    query = new_query.reshape(own_rows, new_count, heads, HD)
    query = jnp.stack(shifts(query, "tp"))
    fresh = new_keyval.reshape(own_rows, new_count, 2 * KVH // n_tp, HD)
    fresh = shifts(fresh, "seq")
    k, meta = project_keys(prefill_states, kv_weight, page_counts, tail_tokens, pages)
    queries = shifts(query, "seq")
    v = project_values(prefill_states, kv_weight)
    *chunks, own_q = partial_scores(queries, k, meta, pages, prompts)
    weights, stats = softmax_weights(exchange(chunks, "tp"), meta, pages)
    stats = shifts(stats, "seq")
    chunks = weighted_values(shifts(weights, "tp"), v, meta, pages, prompts)
    factor, add = merge(stats, fresh, own_q, meta, pages)
    part = scaled_sum(exchange(chunks, "tp"), factor)
    partial = output_partial(shifts(part, "seq"), add, out_weight, new_count)
    return final_sum(shifts(partial, "tp"), residual)


def solution(mesh):
    placed = (
        P(("groups", "seq"), "tp"),
        P("tp", None),
        P("groups"),
        P("groups"),
        P(("groups", "seq"), None, "tp"),
        P(("groups", "seq"), None, "tp"),
        P("groups", None, "seq"),
        P("tp", "seq"),
    )
    return jax.shard_map(
        on_device, mesh=mesh, in_specs=placed, out_specs=P("groups", None, "seq"), check_vma=False
    )
```

```python
import functools
import math

import jax
import jax.numpy as jnp
from jax import lax
from jax.experimental import pallas as pl
from jax.experimental.pallas import tpu as pltpu
from jax.sharding import PartitionSpec as P

QH = 64
KVH = 8
HD = 128
PAGE = 128
GROUP = QH // KVH
NEG = -1e30
F32 = jnp.float32
BF16 = jnp.bfloat16
MIB = 1 << 20

VMEM = pl.BlockSpec(memory_space=pltpu.VMEM)
SMEM = pl.BlockSpec(memory_space=pltpu.SMEM)


def exchange(chunks, axis):
    return lax.all_to_all(chunks, axis, 0, 0)


def lane_freqs(rows):
    lane = lax.broadcasted_iota(jnp.int32, (rows, HD), 1) % (HD // 2)
    return jnp.exp(-(lane.astype(F32) * (2.0 / HD)) * math.log(500000.0))


def sine_sign(rows):
    lane = lax.broadcasted_iota(jnp.int32, (rows, HD), 1)
    return jnp.where(lane < HD // 2, -1.0, 1.0)


def keys_kernel(pages, prompts, x_ref, wa_ref, wb_ref, counts, tails, out_ref, meta, cos_s, sin_s):
    step = pl.program_id(0)
    tokens = x_ref.shape[0]
    local_pages = tokens // PAGE

    @pl.when(step == 0)
    def _():
        def one_prompt(r, start):
            length = (counts[r] - 1) * PAGE + tails[r]
            meta[3 * pages + r] = length

            def one_page(i, carry):
                meta[start + i] = r
                meta[pages + start + i] = i * PAGE
                meta[2 * pages + start + i] = jnp.minimum(length - i * PAGE, PAGE)
                return carry

            lax.fori_loop(0, counts[r], one_page, 0)
            return start + counts[r]

        lax.fori_loop(0, prompts, one_prompt, 0)
        freqs = lane_freqs(PAGE)
        offset = lax.broadcasted_iota(jnp.int32, (PAGE, HD), 0).astype(F32) * freqs
        cos_off, sin_off = jnp.cos(offset), jnp.sin(offset)
        row_freqs = lane_freqs(8)
        sign = sine_sign(PAGE)
        first = lax.axis_index("seq") * local_pages
        for p in range(local_pages):
            base = meta[pages + first + p].astype(F32) * row_freqs
            cos_base, sin_base = jnp.cos(base)[:1], jnp.sin(base)[:1]
            cos_s[p * PAGE : (p + 1) * PAGE] = cos_off * cos_base - sin_off * sin_base
            sin_s[p * PAGE : (p + 1) * PAGE] = sign * (sin_off * cos_base + cos_off * sin_base)

    weight = jnp.concatenate([wa_ref[...], wb_ref[...]], axis=1)
    for start in range(0, tokens, 512):
        at = slice(start, start + 512)
        product = jnp.dot(x_ref[at], weight, preferred_element_type=F32)
        cosine, sine = cos_s[at], sin_s[at]
        for half in range(2):
            k = product[:, half * HD : (half + 1) * HD]
            k = k * cosine + pltpu.roll(k, HD // 2, 1) * sine
            out_ref[at, half * HD : (half + 1) * HD] = k.astype(BF16)


def values_kernel(x_ref, wa_ref, wb_ref, out_ref):
    weight = jnp.concatenate([wa_ref[...], wb_ref[...]], axis=1)
    out_ref[...] = jnp.dot(x_ref[...], weight, preferred_element_type=F32).astype(BF16)


def project_keys(x, kv_weight, counts, tails, pages):
    tokens, depth = x.shape
    prompts = counts.shape[0]
    return pl.pallas_call(
        functools.partial(keys_kernel, pages, prompts),
        grid=(KVH // 2,),
        in_specs=[
            pl.BlockSpec((tokens, depth), lambda i: (0, 0)),
            pl.BlockSpec((depth, HD), lambda i: (0, 4 * i)),
            pl.BlockSpec((depth, HD), lambda i: (0, 4 * i + 2)),
            SMEM,
            SMEM,
        ],
        out_specs=[pl.BlockSpec((tokens, 2 * HD), lambda i: (0, i)), SMEM],
        out_shape=[
            jax.ShapeDtypeStruct((tokens, KVH * HD), BF16),
            jax.ShapeDtypeStruct((3 * pages + prompts,), jnp.int32),
        ],
        scratch_shapes=[pltpu.VMEM((tokens, HD), F32), pltpu.VMEM((tokens, HD), F32)],
        compiler_params=pltpu.CompilerParams(vmem_limit_bytes=24 * MIB),
        cost_estimate=pl.CostEstimate(
            flops=2 * tokens * depth * KVH * HD, bytes_accessed=12 * MIB, transcendentals=0
        ),
        name="keys",
    )(x, kv_weight, kv_weight, counts, tails)


def project_values(x, kv_weight):
    tokens, depth = x.shape
    return pl.pallas_call(
        values_kernel,
        grid=(KVH // 2,),
        in_specs=[
            pl.BlockSpec((tokens, depth), lambda i: (0, 0)),
            pl.BlockSpec((depth, HD), lambda i: (0, 4 * i + 1)),
            pl.BlockSpec((depth, HD), lambda i: (0, 4 * i + 3)),
        ],
        out_specs=pl.BlockSpec((tokens, 2 * HD), lambda i: (0, i)),
        out_shape=jax.ShapeDtypeStruct((tokens, KVH * HD), BF16),
        compiler_params=pltpu.CompilerParams(vmem_limit_bytes=24 * MIB),
        cost_estimate=pl.CostEstimate(
            flops=2 * tokens * depth * KVH * HD, bytes_accessed=12 * MIB, transcendentals=0
        ),
        name="values",
    )(x, kv_weight, kv_weight)


def scores_kernel(pages, n_seq, n_tp, new_ref, k_ref, meta, out_ref, fresh_ref, all_q):
    kv_local = KVH // n_tp
    local_pages = k_ref.shape[0] // PAGE
    _, own_rows, new_count, _, _ = new_ref.shape
    rows = new_count * GROUP
    heads = kv_local * GROUP
    scale = 1.0 / math.sqrt(HD)
    freqs = lane_freqs(8)
    sign = sine_sign(8)
    me = lax.axis_index("tp")
    first = lax.axis_index("seq") * local_pages
    step = lax.broadcasted_iota(jnp.int32, (kv_local * rows, HD), 0) % rows // GROUP
    lane = lax.broadcasted_iota(jnp.int32, (kv_local * rows, HD), 1)
    found = [jnp.full((kv_local * rows, HD), NEG, F32) for _ in range(new_count)]
    for ds in range(n_seq):
        for rr in range(own_rows):
            request = ds * own_rows + rr
            length = meta[3 * pages + request]
            cosines, sines = [], []
            for n in range(new_count):
                angle = (length + n).astype(F32) * freqs
                cosines.append(jnp.cos(angle))
                sines.append(jnp.sin(angle) * sign)
            for dt in range(n_tp):
                held = [new_ref[ds * n_tp + dt, rr, n].astype(F32) for n in range(new_count)]
                for g in range(kv_local):
                    parts = []
                    for n in range(new_count):
                        q = held[n][g * GROUP : (g + 1) * GROUP]
                        parts.append(q * cosines[n] + pltpu.roll(q, HD // 2, 1) * sines[n])
                    at = (dt * kv_local + g) * rows
                    all_q[request, at : at + rows] = jnp.concatenate(parts, axis=0).astype(BF16)
            own = pl.ds(pl.multiple_of(me * kv_local * rows, kv_local * rows), kv_local * rows)
            own_q = all_q[request, own].astype(F32)
            for n in range(new_count):
                both = new_ref[ds * n_tp + me, rr, n].astype(F32)
                spread = []
                for g in range(kv_local):
                    k = both[heads + 2 * g : heads + 2 * g + 1]
                    k = k * cosines[n][:1] + pltpu.roll(k, HD // 2, 1) * sines[n][:1]
                    k = k.astype(BF16).astype(F32)
                    spread.append(jnp.broadcast_to(k, (rows, HD)))
                k = jnp.concatenate(spread, axis=0)
                s = jnp.sum(own_q * k, axis=1, keepdims=True) * scale
                found[n] = jnp.where((lane == request) & (step >= n), s, found[n])
    for n in range(new_count):
        fresh_ref[n] = found[n]

    def one_page(p, carry):
        request = meta[first + p]
        tokens = pl.ds(pl.multiple_of(p * PAGE, PAGE), PAGE)
        for head in range(KVH):
            k = k_ref[tokens, head * HD : (head + 1) * HD]
            q = all_q[request, head * rows : (head + 1) * rows]
            s = lax.dot_general(q, k, (((1,), (1,)), ((), ())), preferred_element_type=F32)
            at = head % kv_local * rows
            out_ref[head // kv_local, at : at + rows, tokens] = (s * scale).astype(BF16)
        return carry

    lax.fori_loop(0, local_pages, one_page, 0)


def partial_scores(new, k, meta, pages, prompts, n_seq, n_tp):
    new_count = new.shape[2]
    tokens = k.shape[0]
    rows = KVH // n_tp * new_count * GROUP
    return pl.pallas_call(
        functools.partial(scores_kernel, pages, n_seq, n_tp),
        in_specs=[VMEM, VMEM, SMEM],
        out_specs=[VMEM, VMEM],
        out_shape=[
            jax.ShapeDtypeStruct((n_tp, rows, tokens), BF16),
            jax.ShapeDtypeStruct((new_count, rows, HD), F32),
        ],
        scratch_shapes=[pltpu.VMEM((prompts, rows * n_tp, HD), BF16)],
        compiler_params=pltpu.CompilerParams(vmem_limit_bytes=16 * MIB),
        cost_estimate=pl.CostEstimate(
            flops=2 * tokens * rows * n_tp * HD, bytes_accessed=3 * MIB, transcendentals=0
        ),
        name="scores",
    )(new, k, meta)


def weights_kernel(pages, prompts, in_ref, meta, w_ref, stats_ref):
    n_tp, rows, tokens = in_ref.shape
    local_pages = tokens // PAGE
    first = lax.axis_index("seq") * local_pages
    lane = lax.broadcasted_iota(jnp.int32, (rows, PAGE), 1)
    scores, maxima, masks, owners = [], [], [], []
    for p in range(local_pages):
        at = slice(p * PAGE, (p + 1) * PAGE)
        total = in_ref[0, :, at].astype(F32)
        for d in range(1, n_tp):
            total = total + in_ref[d, :, at].astype(F32)
        mask = lane < meta[2 * pages + first + p]
        total = jnp.where(mask, total, NEG)
        masks.append(mask)
        scores.append(total)
        maxima.append(jnp.max(total, axis=1, keepdims=True))
        owners.append(meta[first + p])
    quarter = lane // prompts
    spot = lane % prompts
    stats = jnp.where(quarter == 0, NEG, 0.0)
    sums = []
    for p in range(local_pages):
        top = maxima[p]
        for other in range(local_pages):
            if other != p:
                top = jnp.where(owners[p] == owners[other], jnp.maximum(top, maxima[other]), top)
        high = top.astype(BF16).astype(F32)
        low = (top - high).astype(BF16).astype(F32)
        w = jnp.where(masks[p], jnp.exp(scores[p] - (high + low)), 0.0)
        for d in range(n_tp):
            w_ref[d, :, p * PAGE : (p + 1) * PAGE] = w.astype(BF16)
        here = spot == owners[p]
        stats = jnp.where(here & (quarter == 0), high, stats)
        stats = jnp.where(here & (quarter == 1), low, stats)
        part = jnp.sum(w, axis=1, keepdims=True)
        stats = stats + jnp.where(here & (quarter == 2), part, 0.0)
    high = stats.astype(BF16).astype(F32)
    low = pltpu.roll(stats - high, prompts, 1)
    stats_ref[...] = jnp.where(quarter == 3, low, stats).astype(BF16)


def softmax_weights(chunks, meta, pages, prompts):
    n_tp, rows, tokens = chunks.shape
    return pl.pallas_call(
        functools.partial(weights_kernel, pages, prompts),
        in_specs=[VMEM, SMEM],
        out_specs=[VMEM, VMEM],
        out_shape=[
            jax.ShapeDtypeStruct((n_tp, rows, tokens), BF16),
            jax.ShapeDtypeStruct((rows, PAGE), BF16),
        ],
        compiler_params=pltpu.CompilerParams(vmem_limit_bytes=8 * MIB),
        name="weights",
    )(chunks, meta)


def weighted_kernel(w_ref, v_ref, meta, out_ref, total):
    n_tp, rows_local, tokens_here = w_ref.shape
    kv_local = KVH // n_tp
    rows = rows_local // kv_local
    local_pages = tokens_here // PAGE
    first = lax.axis_index("seq") * local_pages
    total[...] = jnp.zeros_like(total)

    def one_page(p, carry):
        request = meta[first + p]
        tokens = pl.ds(pl.multiple_of(p * PAGE, PAGE), PAGE)
        for head in range(KVH):
            v = v_ref[tokens, head * HD : (head + 1) * HD]
            at = head % kv_local * rows
            w = w_ref[head // kv_local, at : at + rows, tokens]
            total[request, head * rows : (head + 1) * rows] += jnp.dot(
                w, v, preferred_element_type=F32
            )
        return carry

    lax.fori_loop(0, local_pages, one_page, 0)
    for d in range(n_tp):
        out_ref[d] = total[:, d * rows_local : (d + 1) * rows_local].astype(BF16)


def weighted_values(weights, v, meta, prompts):
    n_tp, rows, _ = weights.shape
    return pl.pallas_call(
        weighted_kernel,
        in_specs=[VMEM, VMEM, SMEM],
        out_specs=VMEM,
        out_shape=jax.ShapeDtypeStruct((n_tp, prompts, rows, HD), BF16),
        scratch_shapes=[pltpu.VMEM((prompts, rows * n_tp, HD), F32)],
        compiler_params=pltpu.CompilerParams(vmem_limit_bytes=24 * MIB),
        name="weighted",
    )(weights, v, meta)


def summed_kernel(in_ref, stats_ref, out_ref):
    n_tp, prompts, _, _ = in_ref.shape
    total = in_ref[0].astype(F32)
    for d in range(1, n_tp):
        total = total + in_ref[d].astype(F32)
    for s in range(out_ref.shape[0]):
        out_ref[s, :prompts] = total.astype(BF16)
        out_ref[s, prompts] = stats_ref[...]


def summed(chunks, stats, n_seq):
    _, prompts, rows, _ = chunks.shape
    return pl.pallas_call(
        summed_kernel,
        in_specs=[VMEM, VMEM],
        out_specs=VMEM,
        out_shape=jax.ShapeDtypeStruct((n_seq, prompts + 1, rows, HD), BF16),
        compiler_params=pltpu.CompilerParams(vmem_limit_bytes=8 * MIB),
        name="summed",
    )(chunks, stats)


def output_kernel(n_tp, in_ref, fresh_ref, new_ref, w_ref, out_ref, held):
    n_seq, more, rows_local, _ = in_ref.shape
    prompts = more - 1
    new_count = fresh_ref.shape[0]
    rows = new_count * GROUP
    kv_local = rows_local // rows
    heads = kv_local * GROUP
    own_rows = prompts // n_seq
    me = lax.axis_index("tp")

    @pl.when(pl.program_id(0) == 0)
    def _():
        tops, parts = [], []
        for s in range(n_seq):
            stats = in_ref[s, prompts].astype(F32)
            folded = stats + pltpu.roll(stats, HD - prompts, 1)
            tops.append(folded)
            parts.append(pltpu.roll(folded, HD - 2 * prompts, 1))
        fresh = [fresh_ref[n] for n in range(new_count)]
        top = fresh[0]
        for other in fresh[1:] + tops:
            top = jnp.maximum(top, other)
        weights = [jnp.exp(f - top) for f in fresh]
        factors = [jnp.exp(t - top) for t in tops]
        total = weights[0]
        for w in weights[1:]:
            total = total + w
        for f, part in zip(factors, parts):
            total = total + f * part
        weights = [w / total for w in weights]
        factors = [f / total for f in factors]
        for r in range(prompts):
            sums = jnp.zeros((rows_local, HD), F32)
            for s in range(n_seq):
                sums = sums + factors[s][:, r : r + 1] * in_ref[s, r].astype(F32)
            for n in range(new_count):
                both = new_ref[r // own_rows * n_tp + me, r % own_rows, n].astype(F32)
                value = jnp.concatenate(
                    [
                        jnp.broadcast_to(both[heads + 2 * g + 1 : heads + 2 * g + 2], (rows, HD))
                        for g in range(kv_local)
                    ],
                    axis=0,
                )
                sums = sums + weights[n][:, r : r + 1] * value
            for g in range(kv_local):
                for n in range(new_count):
                    at = g * rows + n * GROUP
                    held[g * GROUP : (g + 1) * GROUP, r * new_count + n] = sums[at : at + GROUP]

    left = jnp.concatenate([held[h].astype(BF16) for h in range(heads)], axis=1)
    product = jnp.dot(left, w_ref[...], preferred_element_type=F32).astype(BF16)
    for d in range(n_tp):
        out_ref[d] = product


def output_partial(gathered, fresh, new, out_weight, n_tp):
    new_count = fresh.shape[0]
    prompts = gathered.shape[1] - 1
    depth, columns = out_weight.shape
    width = min(columns, 512)
    whole = lambda a: pl.BlockSpec(a.shape, lambda i: (0,) * a.ndim)
    return pl.pallas_call(
        functools.partial(output_kernel, n_tp),
        grid=(columns // width,),
        in_specs=[
            whole(gathered),
            whole(fresh),
            whole(new),
            pl.BlockSpec((depth, width), lambda i: (0, i)),
        ],
        out_specs=pl.BlockSpec((n_tp, prompts * new_count, width), lambda i: (0, 0, i)),
        out_shape=jax.ShapeDtypeStruct((n_tp, prompts * new_count, columns), BF16),
        scratch_shapes=[pltpu.VMEM((depth // HD, prompts * new_count, HD), F32)],
        compiler_params=pltpu.CompilerParams(vmem_limit_bytes=24 * MIB),
        name="output",
    )(gathered, fresh, new, out_weight)


def final_kernel(in_ref, res_ref, out_ref):
    prompts, new_count, _ = out_ref.shape
    total = in_ref[0].astype(F32)
    for d in range(1, in_ref.shape[0]):
        total = total + in_ref[d].astype(F32)
    for r in range(prompts):
        out_ref[r] = res_ref[r].astype(F32) + total[r * new_count : (r + 1) * new_count]


def final_sum(pieces, residual):
    return pl.pallas_call(
        final_kernel,
        in_specs=[VMEM, VMEM],
        out_specs=VMEM,
        out_shape=jax.ShapeDtypeStruct(residual.shape, F32),
        compiler_params=pltpu.CompilerParams(vmem_limit_bytes=8 * MIB),
        name="final",
    )(pieces, residual)


def on_device(
    prefill_states, kv_weight, page_counts, tail_tokens, new_query, new_keyval, residual, out_weight
):
    n_seq, n_tp = lax.axis_size("seq"), lax.axis_size("tp")
    own_rows, new_count, _ = new_query.shape
    prompts = page_counts.shape[0]
    pages = prefill_states.shape[0] // PAGE * n_seq
    new = jnp.concatenate(
        [
            new_query.reshape(own_rows, new_count, QH // n_tp, HD),
            new_keyval.reshape(own_rows, new_count, 2 * KVH // n_tp, HD),
        ],
        axis=2,
    )
    new = exchange(jnp.broadcast_to(new, (n_seq * n_tp,) + new.shape), ("seq", "tp"))
    k, meta = project_keys(prefill_states, kv_weight, page_counts, tail_tokens, pages)
    v = project_values(prefill_states, kv_weight)
    scores, fresh = partial_scores(new, k, meta, pages, prompts, n_seq, n_tp)
    weights, stats = softmax_weights(exchange(scores, "tp"), meta, pages, prompts)
    chunks = weighted_values(exchange(weights, "tp"), v, meta, prompts)
    gathered = exchange(summed(exchange(chunks, "tp"), stats, n_seq), "seq")
    partial = output_partial(gathered, fresh, new, out_weight, n_tp)
    return final_sum(exchange(partial, "tp"), residual)


def solution(mesh):
    placed = (
        P(("groups", "seq"), "tp"),
        P("tp", None),
        P("groups"),
        P("groups"),
        P(("groups", "seq"), None, "tp"),
        P(("groups", "seq"), None, "tp"),
        P("groups", None, "seq"),
        P("tp", "seq"),
    )
    return jax.shard_map(
        on_device, mesh=mesh, in_specs=placed, out_specs=P("groups", None, "seq"), check_vma=False
    )
```

```python
import functools
import math

import jax
import jax.numpy as jnp
from jax import lax
from jax.experimental import pallas as pl
from jax.experimental.pallas import tpu as pltpu
from jax.sharding import PartitionSpec as P

QH = 64
KVH = 8
HD = 128
PAGE = 128
GROUP = QH // KVH
NEG = -1e30
F32 = jnp.float32
BF16 = jnp.bfloat16
MIB = 1 << 20

VMEM = pl.BlockSpec(memory_space=pltpu.VMEM)
SMEM = pl.BlockSpec(memory_space=pltpu.SMEM)


def pairs(value, axis, d):
    return lax.ppermute(value, axis, [(i, i ^ d) for i in range(lax.axis_size(axis))])


def exchange(chunks, axis):
    return [chunks[0]] + [pairs(chunks[d], axis, d) for d in range(1, len(chunks))]


def gather(value, axis):
    return exchange([value] * lax.axis_size(axis), axis)


def lane_freqs(rows):
    lane = lax.broadcasted_iota(jnp.int32, (rows, HD), 1) % (HD // 2)
    return jnp.exp(-(lane.astype(F32) * (2.0 / HD)) * math.log(500000.0))


def sine_sign(rows):
    lane = lax.broadcasted_iota(jnp.int32, (rows, HD), 1)
    return jnp.where(lane < HD // 2, -1.0, 1.0)


def by_row(rows, numbers):
    row = lax.broadcasted_iota(jnp.int32, (rows, HD), 0)
    out = jnp.zeros((rows, HD), F32)
    for i, number in enumerate(numbers):
        out = jnp.where(row == i, number.astype(F32), out)
    return out


def page_table(pages, prompts, counts, tails, meta):
    def one_prompt(r, start):
        length = (counts[r] - 1) * PAGE + tails[r]
        meta[3 * pages + r] = length

        def one_page(i, carry):
            meta[start + i] = r
            meta[pages + start + i] = i * PAGE
            meta[2 * pages + start + i] = jnp.minimum(length - i * PAGE, PAGE)
            return carry

        lax.fori_loop(0, counts[r], one_page, 0)
        return start + counts[r]

    lax.fori_loop(0, prompts, one_prompt, 0)


def rotation_tables(pages, local_pages, meta, cos_s, sin_s):
    freqs = lane_freqs(8)
    low = lax.broadcasted_iota(jnp.int32, (8, HD), 0).astype(F32) * freqs
    low_cos, low_sin = jnp.cos(low), jnp.sin(low)
    high = lax.broadcasted_iota(jnp.int32, (PAGE // 8, HD), 0).astype(F32) * 8.0
    high = high * lane_freqs(PAGE // 8)
    high_cos, high_sin = jnp.cos(high), jnp.sin(high)
    first = lax.axis_index("seq") * local_pages
    base = by_row(local_pages, [meta[pages + first + p] for p in range(local_pages)])
    base = base * lane_freqs(local_pages)
    base_cos, base_sin = jnp.cos(base), jnp.sin(base)
    sign = sine_sign(8)
    for i in range(PAGE // 8):
        c, s = high_cos[i : i + 1], high_sin[i : i + 1]
        cosine, sine = low_cos * c - low_sin * s, low_sin * c + low_cos * s
        for p in range(local_pages):
            at = slice(p * PAGE + i * 8, p * PAGE + i * 8 + 8)
            c, s = base_cos[p : p + 1], base_sin[p : p + 1]
            cos_s[at] = cosine * c - sine * s
            sin_s[at] = sign * (sine * c + cosine * s)


def accumulate(x_ref, weights, acc, finish):
    step, last = pl.program_id(0), pl.num_programs(0) - 1
    weight = jnp.concatenate([w[...] for w in weights], axis=1)
    tall = 512

    def product(start):
        return jnp.dot(x_ref[start : start + tall], weight, preferred_element_type=F32)

    starts = range(0, x_ref.shape[0], tall)

    @pl.when(step == 0)
    def _():
        for start in starts:
            acc[start : start + tall] = product(start)

    @pl.when((step > 0) & (step < last))
    def _():
        for start in starts:
            acc[start : start + tall] += product(start)

    @pl.when(step == last)
    def _():
        for start in starts:
            finish(slice(start, start + tall), acc[start : start + tall] + product(start))


def keys_kernel(pages, prompts, heads, table, *refs):
    x_ref, *weights = refs[: heads + 1]
    if table:
        counts, tails, out_ref, meta, cos_s, sin_s, acc = refs[heads + 1 :]
    else:
        meta, _, out_ref, cos_s, sin_s, acc = refs[heads + 1 :]

    @pl.when(pl.program_id(0) == 0)
    def _():
        if table:
            page_table(pages, prompts, counts, tails, meta)
        rotation_tables(pages, x_ref.shape[0] // PAGE, meta, cos_s, sin_s)

    def finish(at, product):
        cosine, sine = cos_s[at], sin_s[at]
        for h in range(heads):
            k = product[:, h * HD : (h + 1) * HD]
            k = k * cosine + pltpu.roll(k, HD // 2, 1) * sine
            out_ref[at, h * HD : (h + 1) * HD] = k.astype(BF16)

    accumulate(x_ref, weights, acc, finish)


def values_kernel(heads, *refs):
    x_ref, *weights = refs[: heads + 1]
    _, out_ref, acc = refs[heads + 1 :]

    def finish(at, product):
        out_ref[at] = product.astype(BF16)

    accumulate(x_ref, weights, acc, finish)


BIG = 57 * MIB


def projection_specs(x, heads, columns):
    tokens, depth = x.shape
    block = min(depth // 2, 512)
    at = lambda c: pl.BlockSpec((block, HD), lambda i: (i, c))
    specs = [pl.BlockSpec((tokens, block), lambda i: (0, i))] + [at(c) for c in columns]
    return dict(
        grid=(depth // block,),
        compiler_params=pltpu.CompilerParams(vmem_limit_bytes=BIG),
        cost_estimate=pl.CostEstimate(
            flops=2 * tokens * depth * heads * HD,
            bytes_accessed=2 * depth * (tokens + heads * HD) + 2 * tokens * heads * HD,
            transcendentals=0,
        ),
    ), specs


def project_keys(x, kv_weight, first, heads, pages, prompts, scalars, after=None):
    tokens, _ = x.shape
    table = after is None
    call, specs = projection_specs(x, heads, [2 * (first + h) for h in range(heads)])
    out_specs = [pl.BlockSpec((tokens, heads * HD), lambda i: (0, 0)), SMEM]
    out_shape = [
        jax.ShapeDtypeStruct((tokens, heads * HD), BF16),
        jax.ShapeDtypeStruct((3 * pages + prompts,), jnp.int32),
    ]
    extra = [SMEM, SMEM] if table else [SMEM, pl.BlockSpec(memory_space=pl.ANY)]
    operands = list(scalars) + ([] if table else [after])
    return pl.pallas_call(
        functools.partial(keys_kernel, pages, prompts, heads, table),
        in_specs=specs + extra,
        out_specs=out_specs if table else out_specs[0],
        out_shape=out_shape if table else out_shape[0],
        scratch_shapes=[
            pltpu.VMEM((tokens, HD), F32),
            pltpu.VMEM((tokens, HD), F32),
            pltpu.VMEM((tokens, heads * HD), F32),
        ],
        name="keys",
        **call,
    )(x, *[kv_weight] * heads, *operands)


def project_values(x, kv_weight, first, heads, after):
    tokens, _ = x.shape
    call, specs = projection_specs(x, heads, [2 * (first + h) + 1 for h in range(heads)])
    return pl.pallas_call(
        functools.partial(values_kernel, heads),
        in_specs=specs + [pl.BlockSpec(memory_space=pl.ANY)],
        out_specs=pl.BlockSpec((tokens, heads * HD), lambda i: (0, 0)),
        out_shape=jax.ShapeDtypeStruct((tokens, heads * HD), BF16),
        scratch_shapes=[pltpu.VMEM((tokens, heads * HD), F32)],
        name="values",
        **call,
    )(x, *[kv_weight] * heads, after)


def stacked_kernel(n_tp, *refs):
    for d in range(n_tp):
        refs[-1][d] = refs[d][...]


def stacked(pieces, after):
    n_tp = len(pieces)
    return pl.pallas_call(
        functools.partial(stacked_kernel, n_tp),
        in_specs=[VMEM] * n_tp + [pl.BlockSpec(memory_space=pl.ANY)],
        out_specs=VMEM,
        out_shape=jax.ShapeDtypeStruct((n_tp,) + pieces[0].shape, BF16),
        compiler_params=pltpu.CompilerParams(vmem_limit_bytes=8 * MIB),
        name="stacked",
    )(*pieces, after)


def scores_kernel(pages, n_seq, n_tp, *refs):
    new = refs[:n_seq]
    ka_ref, kb_ref, meta = refs[n_seq : n_seq + 3]
    outs = refs[n_seq + 3 : n_seq + 3 + n_tp]
    fresh_ref, all_q, held, ready, cosines, sines = refs[n_seq + 3 + n_tp :]
    kv_local = KVH // n_tp
    local_pages = ka_ref.shape[0] // PAGE
    _, own_rows, new_count, _, _ = new[0].shape
    prompts = own_rows * n_seq
    rows = new_count * GROUP
    heads = kv_local * GROUP
    scale = 1.0 / math.sqrt(HD)
    me = lax.axis_index("tp")
    seq = lax.axis_index("seq")
    first = seq * local_pages
    step = lax.broadcasted_iota(jnp.int32, (kv_local * rows, HD), 0) % rows // GROUP
    lane = lax.broadcasted_iota(jnp.int32, (kv_local * rows, HD), 1)
    found = [jnp.full((kv_local * rows, HD), NEG, F32) for _ in range(new_count)]
    spots = [meta[3 * pages + r] + n for r in range(prompts) for n in range(new_count)]
    angles = by_row(len(spots), spots) * lane_freqs(len(spots))
    cosines[...] = jnp.cos(angles)
    sines[...] = jnp.sin(angles) * sine_sign(len(spots))
    for ds in range(n_seq):
        for rr in range(own_rows):
            request = (seq ^ ds) * own_rows + rr
            turn = [
                (
                    cosines[pl.ds(request * new_count + n, 1)],
                    sines[pl.ds(request * new_count + n, 1)],
                )
                for n in range(new_count)
            ]
            for dt in range(n_tp):
                block = [new[ds][dt, rr, n].astype(F32) for n in range(new_count)]
                for g in range(kv_local):
                    parts = []
                    for n in range(new_count):
                        q = block[n][g * GROUP : (g + 1) * GROUP]
                        parts.append(q * turn[n][0] + pltpu.roll(q, HD // 2, 1) * turn[n][1])
                    part = jnp.concatenate(parts, axis=0).astype(BF16)
                    at = ((me ^ dt) * kv_local + g) * rows
                    all_q[request, pl.ds(pl.multiple_of(at, rows), rows)] = part
                    if dt == 0:
                        held[g * rows : (g + 1) * rows] = part.astype(F32)
                if dt == 0:
                    for n in range(new_count):
                        spread = []
                        for g in range(kv_local):
                            k = block[n][heads + 2 * g : heads + 2 * g + 1]
                            k = k * turn[n][0] + pltpu.roll(k, HD // 2, 1) * turn[n][1]
                            k = k.astype(BF16).astype(F32)
                            spread.append(jnp.broadcast_to(k, (rows, HD)))
                        k = jnp.concatenate(spread, axis=0)
                        s = jnp.sum(held[...] * k, axis=1, keepdims=True) * scale
                        found[n] = jnp.where((lane == request) & (step >= n), s, found[n])
    for n in range(new_count):
        fresh_ref[n] = found[n]
    half = ka_ref.shape[1] // HD
    for p in range(local_pages):
        request = meta[first + p]
        tokens = slice(p * PAGE, (p + 1) * PAGE)
        for head in range(KVH):
            k_ref = ka_ref if head < half else kb_ref
            k = k_ref[tokens, head % half * HD : (head % half + 1) * HD]
            q = all_q[request, head * rows : (head + 1) * rows]
            s = lax.dot_general(q, k, (((1,), (1,)), ((), ())), preferred_element_type=F32)
            ready[head * rows : (head + 1) * rows, tokens] = (s * scale).astype(BF16)
    count = kv_local * rows
    for d in range(n_tp):
        outs[d][...] = ready[pl.ds(pl.multiple_of((me ^ d) * count, count), count)]


def partial_scores(new, ka, kb, meta, pages, prompts, n_tp):
    n_seq = len(new)
    new_count = new[0].shape[2]
    tokens = ka.shape[0]
    rows = KVH // n_tp * new_count * GROUP
    return pl.pallas_call(
        functools.partial(scores_kernel, pages, n_seq, n_tp),
        in_specs=[VMEM] * (n_seq + 2) + [SMEM],
        out_specs=[VMEM] * (n_tp + 1),
        out_shape=[jax.ShapeDtypeStruct((rows, tokens), BF16)] * n_tp
        + [jax.ShapeDtypeStruct((new_count, rows, HD), F32)],
        scratch_shapes=[
            pltpu.VMEM((prompts, rows * n_tp, HD), BF16),
            pltpu.VMEM((rows, HD), F32),
            pltpu.VMEM((rows * n_tp, tokens), BF16),
            pltpu.VMEM((prompts * new_count, HD), F32),
            pltpu.VMEM((prompts * new_count, HD), F32),
        ],
        compiler_params=pltpu.CompilerParams(vmem_limit_bytes=24 * MIB),
        cost_estimate=pl.CostEstimate(
            flops=2 * tokens * rows * n_tp * HD, bytes_accessed=6 * MIB, transcendentals=0
        ),
        name="scores",
    )(*new, ka, kb, meta)


def weights_kernel(pages, prompts, n_tp, *refs):
    chunks = refs[:n_tp]
    meta, w_ref, stats_ref = refs[n_tp:]
    rows, tokens = w_ref.shape
    local_pages = tokens // PAGE
    first = lax.axis_index("seq") * local_pages
    lane = lax.broadcasted_iota(jnp.int32, (rows, PAGE), 1)
    scores, maxima, masks, owners = [], [], [], []
    for p in range(local_pages):
        at = slice(p * PAGE, (p + 1) * PAGE)
        total = chunks[0][:, at].astype(F32)
        for d in range(1, n_tp):
            total = total + chunks[d][:, at].astype(F32)
        mask = lane < meta[2 * pages + first + p]
        total = jnp.where(mask, total, NEG)
        masks.append(mask)
        scores.append(total)
        maxima.append(jnp.max(total, axis=1, keepdims=True))
        owners.append(meta[first + p])
    quarter = lane // prompts
    spot = lane % prompts
    stats = jnp.where(quarter == 0, NEG, 0.0)
    sums = []
    for p in range(local_pages):
        top = maxima[p]
        for other in range(local_pages):
            if other != p:
                top = jnp.where(owners[p] == owners[other], jnp.maximum(top, maxima[other]), top)
        high = top.astype(BF16).astype(F32)
        low = (top - high).astype(BF16).astype(F32)
        w = jnp.where(masks[p], jnp.exp(scores[p] - (high + low)), 0.0)
        w_ref[:, p * PAGE : (p + 1) * PAGE] = w.astype(BF16)
        here = spot == owners[p]
        stats = jnp.where(here & (quarter == 0), high, stats)
        stats = jnp.where(here & (quarter == 1), low, stats)
        part = jnp.sum(w, axis=1, keepdims=True)
        stats = stats + jnp.where(here & (quarter == 2), part, 0.0)
    high = stats.astype(BF16).astype(F32)
    low = pltpu.roll(stats - high, prompts, 1)
    stats_ref[...] = jnp.where(quarter == 3, low, stats).astype(BF16)


def softmax_weights(chunks, meta, pages, prompts):
    n_tp = len(chunks)
    rows, tokens = chunks[0].shape
    return pl.pallas_call(
        functools.partial(weights_kernel, pages, prompts, n_tp),
        in_specs=[VMEM] * n_tp + [SMEM],
        out_specs=[VMEM, VMEM],
        out_shape=[
            jax.ShapeDtypeStruct((rows, tokens), BF16),
            jax.ShapeDtypeStruct((rows, PAGE), BF16),
        ],
        compiler_params=pltpu.CompilerParams(vmem_limit_bytes=8 * MIB),
        name="weights",
    )(*chunks, meta)


def weighted_kernel(n_tp, *refs):
    pieces = refs[:n_tp]
    va_ref, vb_ref, meta = refs[n_tp : n_tp + 3]
    outs = refs[n_tp + 3 : n_tp + 3 + n_tp]
    ready, total = refs[n_tp + 3 + n_tp :]
    rows_local, tokens_here = pieces[0].shape
    kv_local = KVH // n_tp
    rows = rows_local // kv_local
    local_pages = tokens_here // PAGE
    first = lax.axis_index("seq") * local_pages
    me = lax.axis_index("tp")
    own = [pl.ds(pl.multiple_of((me ^ d) * rows_local, rows_local), rows_local) for d in range(n_tp)]
    for d in range(n_tp):
        ready[own[d]] = pieces[d][...]
    total[...] = jnp.zeros_like(total)
    half = va_ref.shape[1] // HD
    for p in range(local_pages):
        request = meta[first + p]
        tokens = slice(p * PAGE, (p + 1) * PAGE)
        for head in range(KVH):
            v_ref = va_ref if head < half else vb_ref
            v = v_ref[tokens, head % half * HD : (head % half + 1) * HD]
            at = slice(head * rows, (head + 1) * rows)
            total[request, at] += jnp.dot(ready[at, tokens], v, preferred_element_type=F32)
    for d in range(n_tp):
        outs[d][...] = total[:, own[d]].astype(BF16)


def weighted_values(pieces, va, vb, meta, prompts):
    n_tp = len(pieces)
    rows, tokens = pieces[0].shape
    return pl.pallas_call(
        functools.partial(weighted_kernel, n_tp),
        in_specs=[VMEM] * (n_tp + 2) + [SMEM],
        out_specs=[VMEM] * n_tp,
        out_shape=[jax.ShapeDtypeStruct((prompts, rows, HD), BF16)] * n_tp,
        scratch_shapes=[
            pltpu.VMEM((rows * n_tp, tokens), BF16),
            pltpu.VMEM((prompts, rows * n_tp, HD), F32),
        ],
        compiler_params=pltpu.CompilerParams(vmem_limit_bytes=24 * MIB),
        cost_estimate=pl.CostEstimate(
            flops=2 * tokens * rows * n_tp * HD, bytes_accessed=8 * MIB, transcendentals=0
        ),
        name="weighted",
    )(*pieces, va, vb, meta)


def summed_kernel(n_tp, *refs):
    chunks = refs[:n_tp]
    stats_ref, out_ref = refs[n_tp:]
    prompts = chunks[0].shape[0]
    total = chunks[0][...].astype(F32)
    for d in range(1, n_tp):
        total = total + chunks[d][...].astype(F32)
    out_ref[:prompts] = total.astype(BF16)
    out_ref[prompts] = stats_ref[...]


def summed(chunks, stats):
    n_tp = len(chunks)
    prompts, rows, _ = chunks[0].shape
    return pl.pallas_call(
        functools.partial(summed_kernel, n_tp),
        in_specs=[VMEM] * (n_tp + 1),
        out_specs=VMEM,
        out_shape=jax.ShapeDtypeStruct((prompts + 1, rows, HD), BF16),
        compiler_params=pltpu.CompilerParams(vmem_limit_bytes=8 * MIB),
        cost_estimate=pl.CostEstimate(flops=0, bytes_accessed=4 * MIB, transcendentals=0),
        name="summed",
    )(*chunks, stats)


def output_kernel(n_seq, *refs):
    pieces = refs[:n_seq]
    fresh_ref = refs[n_seq]
    new = refs[n_seq + 1 : 2 * n_seq + 1]
    w_ref, out_ref, held = refs[2 * n_seq + 1 :]
    more, rows_local, _ = pieces[0].shape
    prompts = more - 1
    new_count = fresh_ref.shape[0]
    rows = new_count * GROUP
    kv_local = rows_local // rows
    heads = kv_local * GROUP
    own_rows = prompts // n_seq
    seq = lax.axis_index("seq")
    tops, parts = [], []
    for s in range(n_seq):
        stats = pieces[s][prompts].astype(F32)
        folded = stats + pltpu.roll(stats, HD - prompts, 1)
        tops.append(folded)
        parts.append(pltpu.roll(folded, HD - 2 * prompts, 1))
    fresh = [fresh_ref[n] for n in range(new_count)]
    top = fresh[0]
    for other in fresh[1:] + tops:
        top = jnp.maximum(top, other)
    weights = [jnp.exp(f - top) for f in fresh]
    factors = [jnp.exp(t - top) for t in tops]
    total = weights[0]
    for w in weights[1:]:
        total = total + w
    for f, part in zip(factors, parts):
        total = total + f * part
    weights = [w / total for w in weights]
    factors = [f / total for f in factors]
    lane = lax.broadcasted_iota(jnp.int32, (rows_local, HD), 1)
    for r in range(prompts):
        sums = jnp.zeros((rows_local, HD), F32)
        for s in range(n_seq):
            sums = sums + factors[s][:, r : r + 1] * pieces[s][r].astype(F32)
        for g in range(kv_local):
            for n in range(new_count):
                at = g * rows + n * GROUP
                held[g * GROUP : (g + 1) * GROUP, r * new_count + n] = sums[at : at + GROUP]
    for ds in range(n_seq):
        for rr in range(own_rows):
            request = (seq ^ ds) * own_rows + rr
            share = [
                jnp.sum(jnp.where(lane == request, w, 0.0), axis=1, keepdims=True) for w in weights
            ]
            sums = jnp.zeros((rows_local, HD), F32)
            for n in range(new_count):
                both = new[ds][0, rr, n].astype(F32)
                value = [both[heads + 2 * g + 1 : heads + 2 * g + 2] for g in range(kv_local)]
                value = [jnp.broadcast_to(v, (rows, HD)) for v in value]
                sums = sums + share[n] * jnp.concatenate(value, axis=0)
            for g in range(kv_local):
                for n in range(new_count):
                    at = g * rows + n * GROUP
                    held[g * GROUP : (g + 1) * GROUP, request * new_count + n] += sums[
                        at : at + GROUP
                    ]
    left = jnp.concatenate([held[h].astype(BF16) for h in range(heads)], axis=1)
    out_ref[...] = jnp.dot(left, w_ref[...], preferred_element_type=F32).astype(BF16)


def output_partial(pieces, fresh, new, out_weight):
    n_seq = len(pieces)
    new_count = fresh.shape[0]
    prompts = pieces[0].shape[0] - 1
    depth, columns = out_weight.shape
    return pl.pallas_call(
        functools.partial(output_kernel, n_seq),
        in_specs=[VMEM] * (2 * n_seq + 2),
        out_specs=VMEM,
        out_shape=jax.ShapeDtypeStruct((prompts * new_count, columns), BF16),
        scratch_shapes=[pltpu.VMEM((depth // HD, prompts * new_count, HD), F32)],
        compiler_params=pltpu.CompilerParams(vmem_limit_bytes=24 * MIB),
        name="output",
    )(*pieces, fresh, *new, out_weight)


def final_kernel(n_tp, *refs):
    pieces = refs[:n_tp]
    res_ref, out_ref = refs[n_tp:]
    prompts, new_count, _ = out_ref.shape
    total = pieces[0][...].astype(F32)
    for d in range(1, n_tp):
        total = total + pieces[d][...].astype(F32)
    for r in range(prompts):
        out_ref[r] = res_ref[r].astype(F32) + total[r * new_count : (r + 1) * new_count]


def final_sum(pieces, residual):
    n_tp = len(pieces)
    return pl.pallas_call(
        functools.partial(final_kernel, n_tp),
        in_specs=[VMEM] * (n_tp + 1),
        out_specs=VMEM,
        out_shape=jax.ShapeDtypeStruct(residual.shape, F32),
        compiler_params=pltpu.CompilerParams(vmem_limit_bytes=8 * MIB),
        name="final",
    )(*pieces, residual)


def on_device(
    prefill_states, kv_weight, page_counts, tail_tokens, new_query, new_keyval, residual, out_weight
):
    n_seq, n_tp = lax.axis_size("seq"), lax.axis_size("tp")
    own_rows, new_count, _ = new_query.shape
    prompts = page_counts.shape[0]
    pages = prefill_states.shape[0] // PAGE * n_seq
    new = jnp.concatenate(
        [
            new_query.reshape(own_rows, new_count, QH // n_tp, HD),
            new_keyval.reshape(own_rows, new_count, 2 * KVH // n_tp, HD),
        ],
        axis=2,
    )
    half = KVH // 2
    new = gather(new, "tp")
    scalars = (page_counts, tail_tokens)
    ka, meta = project_keys(prefill_states, kv_weight, 0, half, pages, prompts, scalars)
    new = stacked(new, meta)
    kb = project_keys(prefill_states, kv_weight, half, half, pages, prompts, (meta,), new)
    new = gather(new, "seq")
    *scores, fresh = partial_scores(new, ka, kb, meta, pages, prompts, n_tp)
    va = project_values(prefill_states, kv_weight, 0, half, fresh)
    weights, stats = softmax_weights(exchange(scores, "tp"), meta, pages, prompts)
    vb = project_values(prefill_states, kv_weight, half, half, stats)
    chunks = weighted_values(gather(weights, "tp"), va, vb, meta, prompts)
    pieces = gather(summed(exchange(chunks, "tp"), stats), "seq")
    partial = output_partial(pieces, fresh, new, out_weight)
    return final_sum(gather(partial, "tp"), residual)


def solution(mesh):
    placed = (
        P(("groups", "seq"), "tp"),
        P("tp", None),
        P("groups"),
        P("groups"),
        P(("groups", "seq"), None, "tp"),
        P(("groups", "seq"), None, "tp"),
        P("groups", None, "seq"),
        P("tp", "seq"),
    )
    return jax.shard_map(
        on_device, mesh=mesh, in_specs=placed, out_specs=P("groups", None, "seq"), check_vma=False
    )
```

```python
import functools
import math

import jax
import jax.numpy as jnp
from jax import lax
from jax.experimental import pallas as pl
from jax.experimental.pallas import tpu as pltpu
from jax.sharding import PartitionSpec as P

QH = 64
KVH = 8
HD = 128
PAGE = 128
GROUP = QH // KVH
NEG = -1e30
F32 = jnp.float32
BF16 = jnp.bfloat16
MIB = 1 << 20

VMEM = pl.BlockSpec(memory_space=pltpu.VMEM)
SMEM = pl.BlockSpec(memory_space=pltpu.SMEM)


def pairs(value, axis, d):
    return lax.ppermute(value, axis, [(i, i ^ d) for i in range(lax.axis_size(axis))])


def exchange(chunks, axis):
    return [chunks[0]] + [pairs(chunks[d], axis, d) for d in range(1, len(chunks))]


def gather(value, axis):
    return exchange([value] * lax.axis_size(axis), axis)


def lane_freqs(rows):
    lane = lax.broadcasted_iota(jnp.int32, (rows, HD), 1) % (HD // 2)
    return jnp.exp(-(lane.astype(F32) * (2.0 / HD)) * math.log(500000.0))


def sine_sign(rows):
    lane = lax.broadcasted_iota(jnp.int32, (rows, HD), 1)
    return jnp.where(lane < HD // 2, -1.0, 1.0)


def in_hbm(value):
    return pltpu.with_memory_space_constraint(value, pltpu.HBM)


def by_row(rows, numbers):
    row = lax.broadcasted_iota(jnp.int32, (rows, HD), 0)
    out = jnp.zeros((rows, HD), F32)
    for i, number in enumerate(numbers):
        out = jnp.where(row == i, number.astype(F32), out)
    return out


def page_table(pages, prompts, counts, tails, meta):
    def one_prompt(r, start):
        length = (counts[r] - 1) * PAGE + tails[r]
        meta[3 * pages + r] = length

        def one_page(i, carry):
            meta[start + i] = r
            meta[pages + start + i] = i * PAGE
            meta[2 * pages + start + i] = jnp.minimum(length - i * PAGE, PAGE)
            return carry

        lax.fori_loop(0, counts[r], one_page, 0)
        return start + counts[r]

    lax.fori_loop(0, prompts, one_prompt, 0)


def rotation_tables(pages, local_pages, meta, cos_s, sin_s):
    freqs = lane_freqs(8)
    low = lax.broadcasted_iota(jnp.int32, (8, HD), 0).astype(F32) * freqs
    low_cos, low_sin = jnp.cos(low), jnp.sin(low)
    high = lax.broadcasted_iota(jnp.int32, (PAGE // 8, HD), 0).astype(F32) * 8.0
    high = high * lane_freqs(PAGE // 8)
    high_cos, high_sin = jnp.cos(high), jnp.sin(high)
    first = lax.axis_index("seq") * local_pages
    base = by_row(local_pages, [meta[pages + first + p] for p in range(local_pages)])
    base = base * lane_freqs(local_pages)
    base_cos, base_sin = jnp.cos(base), jnp.sin(base)
    sign = sine_sign(8)
    for i in range(PAGE // 8):
        c, s = high_cos[i : i + 1], high_sin[i : i + 1]
        cosine, sine = low_cos * c - low_sin * s, low_sin * c + low_cos * s
        for p in range(local_pages):
            at = slice(p * PAGE + i * 8, p * PAGE + i * 8 + 8)
            c, s = base_cos[p : p + 1], base_sin[p : p + 1]
            cos_s[at] = cosine * c - sine * s
            sin_s[at] = sign * (sine * c + cosine * s)


def keys_kernel(pages, prompts, x_hbm, w_hbm, counts, tails, k_ref, x_ref, v_ref, meta, *scratch):
    w_ref, cos_s, sin_s, x_sems, k_sems, v_sems = scratch
    tokens = x_ref.shape[0]
    tall = tokens // 2

    def x_copy(i):
        at = pl.ds(i * tall, tall)
        return pltpu.make_async_copy(x_hbm.at[at], x_ref.at[at], x_sems.at[i])

    def w_copy(head, part):
        to, sems = (w_ref, k_sems) if part == 0 else (v_ref, v_sems)
        return pltpu.make_async_copy(
            w_hbm.at[:, pl.ds((2 * head + part) * HD, HD)],
            to.at[:, pl.ds(head * HD, HD)],
            sems.at[head],
        )

    x_copy(0).start()
    w_copy(0, 0).start()
    w_copy(1, 0).start()
    x_copy(1).start()
    for head in range(2, KVH):
        w_copy(head, 0).start()
    for head in range(KVH):
        w_copy(head, 1).start()
    page_table(pages, prompts, counts, tails, meta)
    rotation_tables(pages, tokens // PAGE, meta, cos_s, sin_s)
    for pair in range(KVH // 2):
        w_copy(2 * pair, 0).wait()
        w_copy(2 * pair + 1, 0).wait()
        columns = slice(2 * pair * HD, 2 * (pair + 1) * HD)
        for i in range(2):
            if pair == 0:
                x_copy(i).wait()
            at = slice(i * tall, (i + 1) * tall)
            product = jnp.dot(x_ref[at], w_ref[:, columns], preferred_element_type=F32)
            cosine, sine = cos_s[at], sin_s[at]
            for h in range(2):
                k = product[:, h * HD : (h + 1) * HD]
                k = k * cosine + pltpu.roll(k, HD // 2, 1) * sine
                k_ref[at, (2 * pair + h) * HD : (2 * pair + h + 1) * HD] = k.astype(BF16)
    for head in range(KVH):
        w_copy(head, 1).wait()


def project_keys(x, kv_weight, counts, tails, pages):
    tokens, depth = x.shape
    prompts = counts.shape[0]
    hbm = pl.BlockSpec(memory_space=pltpu.HBM)
    return pl.pallas_call(
        functools.partial(keys_kernel, pages, prompts),
        in_specs=[hbm, hbm, SMEM, SMEM],
        out_specs=[VMEM, VMEM, VMEM, SMEM],
        out_shape=[
            pltpu.VMEM((tokens, KVH * HD), BF16),
            pltpu.VMEM((tokens, depth), BF16),
            pltpu.VMEM((depth, KVH * HD), BF16),
            jax.ShapeDtypeStruct((3 * pages + prompts,), jnp.int32),
        ],
        scratch_shapes=[
            pltpu.VMEM((depth, KVH * HD), BF16),
            pltpu.VMEM((tokens, HD), F32),
            pltpu.VMEM((tokens, HD), F32),
            pltpu.SemaphoreType.DMA((2,)),
            pltpu.SemaphoreType.DMA((KVH,)),
            pltpu.SemaphoreType.DMA((KVH,)),
        ],
        compiler_params=pltpu.CompilerParams(vmem_limit_bytes=28 * MIB),
        cost_estimate=pl.CostEstimate(
            flops=2 * tokens * depth * KVH * HD,
            bytes_accessed=2 * depth * (tokens + 2 * KVH * HD) + 2 * tokens * KVH * HD,
            transcendentals=0,
        ),
        name="keys",
    )(*[in_hbm(a) for a in (x, kv_weight, counts, tails)])


def values_kernel(first, x_ref, w_ref, o_hbm, after, v_ref, o_ref, sem):
    depth = o_ref.shape[0]
    copy = pltpu.make_async_copy(o_hbm.at[pl.ds(first * depth, depth)], o_ref, sem)
    copy.start()
    tokens, columns = v_ref.shape
    tall = tokens // 2
    for c in range(0, columns, 2 * HD):
        for i in range(2):
            at = slice(i * tall, (i + 1) * tall)
            weight = w_ref[:, first * columns + c : first * columns + c + 2 * HD]
            v_ref[at, c : c + 2 * HD] = jnp.dot(
                x_ref[at], weight, preferred_element_type=F32
            ).astype(BF16)
    copy.wait()


def project_values(x, weight, out_weight, first, after):
    tokens, depth = x.shape
    columns = weight.shape[1] // 2
    rows = out_weight.shape[0] // 2
    return pl.pallas_call(
        functools.partial(values_kernel, first),
        in_specs=[
            VMEM,
            VMEM,
            pl.BlockSpec(memory_space=pltpu.HBM),
            pl.BlockSpec(memory_space=pl.ANY),
        ],
        out_specs=[VMEM, VMEM],
        out_shape=[
            pltpu.VMEM((tokens, columns), BF16),
            pltpu.VMEM((rows, out_weight.shape[1]), BF16),
        ],
        scratch_shapes=[pltpu.SemaphoreType.DMA],
        compiler_params=pltpu.CompilerParams(vmem_limit_bytes=24 * MIB),
        cost_estimate=pl.CostEstimate(
            flops=2 * tokens * depth * columns,
            bytes_accessed=2 * (depth * (tokens + columns) + tokens * columns),
            transcendentals=0,
        ),
        name="values",
    )(x, weight, in_hbm(out_weight), after)


def prepare_kernel(q_ref, kv_ref, out_ref):
    own_rows, new_count, _, _ = out_ref.shape
    for r in range(own_rows):
        q, kv = q_ref[r].astype(F32), kv_ref[r].astype(F32)
        for n in range(new_count):
            parts = [a[n : n + 1, c : c + HD] for a in (q, kv) for c in range(0, a.shape[1], HD)]
            out_ref[r, n] = jnp.concatenate(parts, axis=0).astype(BF16)


def prepare(new_query, new_keyval):
    own_rows, new_count, columns = new_query.shape
    heads = (columns + new_keyval.shape[2]) // HD
    return pl.pallas_call(
        prepare_kernel,
        in_specs=[VMEM, VMEM],
        out_specs=VMEM,
        out_shape=jax.ShapeDtypeStruct((own_rows, new_count, heads, HD), BF16),
        compiler_params=pltpu.CompilerParams(vmem_limit_bytes=8 * MIB),
        cost_estimate=pl.CostEstimate(flops=0, bytes_accessed=MIB, transcendentals=0),
        name="prepare",
    )(in_hbm(new_query), in_hbm(new_keyval))


def stacked_kernel(n_tp, *refs):
    for d in range(n_tp):
        refs[-1][d] = refs[d][...]


def stacked(pieces, after):
    n_tp = len(pieces)
    return pl.pallas_call(
        functools.partial(stacked_kernel, n_tp),
        in_specs=[VMEM] * n_tp + [pl.BlockSpec(memory_space=pl.ANY)],
        out_specs=VMEM,
        out_shape=jax.ShapeDtypeStruct((n_tp,) + pieces[0].shape, BF16),
        compiler_params=pltpu.CompilerParams(vmem_limit_bytes=8 * MIB),
        name="stacked",
    )(*pieces, after)


def scores_kernel(pages, n_seq, n_tp, *refs):
    new = refs[:n_seq]
    k_ref, meta = refs[n_seq : n_seq + 2]
    outs = refs[n_seq + 2 : n_seq + 2 + n_tp]
    fresh_ref, all_q, held, ready, cosines, sines = refs[n_seq + 2 + n_tp :]
    kv_local = KVH // n_tp
    local_pages = k_ref.shape[0] // PAGE
    _, own_rows, new_count, _, _ = new[0].shape
    prompts = own_rows * n_seq
    rows = new_count * GROUP
    heads = kv_local * GROUP
    scale = 1.0 / math.sqrt(HD)
    me = lax.axis_index("tp")
    seq = lax.axis_index("seq")
    first = seq * local_pages
    step = lax.broadcasted_iota(jnp.int32, (kv_local * rows, HD), 0) % rows // GROUP
    lane = lax.broadcasted_iota(jnp.int32, (kv_local * rows, HD), 1)
    found = [jnp.full((kv_local * rows, HD), NEG, F32) for _ in range(new_count)]
    spots = [meta[3 * pages + r] + n for r in range(prompts) for n in range(new_count)]
    angles = by_row(len(spots), spots) * lane_freqs(len(spots))
    cosines[...] = jnp.cos(angles)
    sines[...] = jnp.sin(angles) * sine_sign(len(spots))
    for ds in range(n_seq):
        for rr in range(own_rows):
            request = (seq ^ ds) * own_rows + rr
            turn = [
                (
                    cosines[pl.ds(request * new_count + n, 1)],
                    sines[pl.ds(request * new_count + n, 1)],
                )
                for n in range(new_count)
            ]
            for dt in range(n_tp):
                block = [new[ds][dt, rr, n].astype(F32) for n in range(new_count)]
                for g in range(kv_local):
                    parts = []
                    for n in range(new_count):
                        q = block[n][g * GROUP : (g + 1) * GROUP]
                        parts.append(q * turn[n][0] + pltpu.roll(q, HD // 2, 1) * turn[n][1])
                    part = jnp.concatenate(parts, axis=0).astype(BF16)
                    at = ((me ^ dt) * kv_local + g) * rows
                    all_q[request, pl.ds(pl.multiple_of(at, rows), rows)] = part
                    if dt == 0:
                        held[g * rows : (g + 1) * rows] = part.astype(F32)
                if dt == 0:
                    for n in range(new_count):
                        spread = []
                        for g in range(kv_local):
                            k = block[n][heads + 2 * g : heads + 2 * g + 1]
                            k = k * turn[n][0] + pltpu.roll(k, HD // 2, 1) * turn[n][1]
                            k = k.astype(BF16).astype(F32)
                            spread.append(jnp.broadcast_to(k, (rows, HD)))
                        k = jnp.concatenate(spread, axis=0)
                        s = jnp.sum(held[...] * k, axis=1, keepdims=True) * scale
                        found[n] = jnp.where((lane == request) & (step >= n), s, found[n])
    for n in range(new_count):
        fresh_ref[n] = found[n]
    for p in range(local_pages):
        request = meta[first + p]
        tokens = slice(p * PAGE, (p + 1) * PAGE)
        for head in range(KVH):
            k = k_ref[tokens, head * HD : (head + 1) * HD]
            q = all_q[request, head * rows : (head + 1) * rows]
            s = lax.dot_general(q, k, (((1,), (1,)), ((), ())), preferred_element_type=F32)
            ready[head * rows : (head + 1) * rows, tokens] = (s * scale).astype(BF16)
    count = kv_local * rows
    for d in range(n_tp):
        outs[d][...] = ready[pl.ds(pl.multiple_of((me ^ d) * count, count), count)]


def partial_scores(new, k, meta, pages, prompts, n_tp):
    n_seq = len(new)
    new_count = new[0].shape[2]
    tokens = k.shape[0]
    rows = KVH // n_tp * new_count * GROUP
    return pl.pallas_call(
        functools.partial(scores_kernel, pages, n_seq, n_tp),
        in_specs=[VMEM] * (n_seq + 1) + [SMEM],
        out_specs=[VMEM] * (n_tp + 1),
        out_shape=[jax.ShapeDtypeStruct((rows, tokens), BF16)] * n_tp
        + [jax.ShapeDtypeStruct((new_count, rows, HD), F32)],
        scratch_shapes=[
            pltpu.VMEM((prompts, rows * n_tp, HD), BF16),
            pltpu.VMEM((rows, HD), F32),
            pltpu.VMEM((rows * n_tp, tokens), BF16),
            pltpu.VMEM((prompts * new_count, HD), F32),
            pltpu.VMEM((prompts * new_count, HD), F32),
        ],
        compiler_params=pltpu.CompilerParams(vmem_limit_bytes=24 * MIB),
        cost_estimate=pl.CostEstimate(
            flops=2 * tokens * rows * n_tp * HD, bytes_accessed=6 * MIB, transcendentals=0
        ),
        name="scores",
    )(*new, k, meta)


def weights_kernel(pages, prompts, n_tp, *refs):
    chunks = refs[:n_tp]
    meta, w_ref, stats_ref = refs[n_tp:]
    rows, tokens = w_ref.shape
    local_pages = tokens // PAGE
    first = lax.axis_index("seq") * local_pages
    lane = lax.broadcasted_iota(jnp.int32, (rows, PAGE), 1)
    scores, maxima, masks, owners = [], [], [], []
    for p in range(local_pages):
        at = slice(p * PAGE, (p + 1) * PAGE)
        total = chunks[0][:, at].astype(F32)
        for d in range(1, n_tp):
            total = total + chunks[d][:, at].astype(F32)
        mask = lane < meta[2 * pages + first + p]
        total = jnp.where(mask, total, NEG)
        masks.append(mask)
        scores.append(total)
        maxima.append(jnp.max(total, axis=1, keepdims=True))
        owners.append(meta[first + p])
    quarter = lane // prompts
    spot = lane % prompts
    stats = jnp.where(quarter == 0, NEG, 0.0)
    sums = []
    for p in range(local_pages):
        top = maxima[p]
        for other in range(local_pages):
            if other != p:
                top = jnp.where(owners[p] == owners[other], jnp.maximum(top, maxima[other]), top)
        high = top.astype(BF16).astype(F32)
        low = (top - high).astype(BF16).astype(F32)
        w = jnp.where(masks[p], jnp.exp(scores[p] - (high + low)), 0.0)
        w_ref[:, p * PAGE : (p + 1) * PAGE] = w.astype(BF16)
        here = spot == owners[p]
        stats = jnp.where(here & (quarter == 0), high, stats)
        stats = jnp.where(here & (quarter == 1), low, stats)
        part = jnp.sum(w, axis=1, keepdims=True)
        stats = stats + jnp.where(here & (quarter == 2), part, 0.0)
    high = stats.astype(BF16).astype(F32)
    low = pltpu.roll(stats - high, prompts, 1)
    stats_ref[...] = jnp.where(quarter == 3, low, stats).astype(BF16)


def softmax_weights(chunks, meta, pages, prompts):
    n_tp = len(chunks)
    rows, tokens = chunks[0].shape
    return pl.pallas_call(
        functools.partial(weights_kernel, pages, prompts, n_tp),
        in_specs=[VMEM] * n_tp + [SMEM],
        out_specs=[VMEM, VMEM],
        out_shape=[
            jax.ShapeDtypeStruct((rows, tokens), BF16),
            jax.ShapeDtypeStruct((rows, PAGE), BF16),
        ],
        compiler_params=pltpu.CompilerParams(vmem_limit_bytes=8 * MIB),
        name="weights",
    )(*chunks, meta)


def weighted_kernel(n_tp, *refs):
    pieces = refs[:n_tp]
    va_ref, vb_ref, meta = refs[n_tp : n_tp + 3]
    outs = refs[n_tp + 3 : n_tp + 3 + n_tp]
    ready, total = refs[n_tp + 3 + n_tp :]
    rows_local, tokens_here = pieces[0].shape
    kv_local = KVH // n_tp
    rows = rows_local // kv_local
    local_pages = tokens_here // PAGE
    first = lax.axis_index("seq") * local_pages
    me = lax.axis_index("tp")
    own = [pl.ds(pl.multiple_of((me ^ d) * rows_local, rows_local), rows_local) for d in range(n_tp)]
    for d in range(n_tp):
        ready[own[d]] = pieces[d][...]
    total[...] = jnp.zeros_like(total)
    half = va_ref.shape[1] // HD
    for p in range(local_pages):
        request = meta[first + p]
        tokens = slice(p * PAGE, (p + 1) * PAGE)
        for head in range(KVH):
            v_ref = va_ref if head < half else vb_ref
            v = v_ref[tokens, head % half * HD : (head % half + 1) * HD]
            at = slice(head * rows, (head + 1) * rows)
            total[request, at] += jnp.dot(ready[at, tokens], v, preferred_element_type=F32)
    for d in range(n_tp):
        outs[d][...] = total[:, own[d]].astype(BF16)


def weighted_values(pieces, va, vb, meta, prompts):
    n_tp = len(pieces)
    rows, tokens = pieces[0].shape
    return pl.pallas_call(
        functools.partial(weighted_kernel, n_tp),
        in_specs=[VMEM] * (n_tp + 2) + [SMEM],
        out_specs=[VMEM] * n_tp,
        out_shape=[jax.ShapeDtypeStruct((prompts, rows, HD), BF16)] * n_tp,
        scratch_shapes=[
            pltpu.VMEM((rows * n_tp, tokens), BF16),
            pltpu.VMEM((prompts, rows * n_tp, HD), F32),
        ],
        compiler_params=pltpu.CompilerParams(vmem_limit_bytes=24 * MIB),
        cost_estimate=pl.CostEstimate(
            flops=2 * tokens * rows * n_tp * HD, bytes_accessed=8 * MIB, transcendentals=0
        ),
        name="weighted",
    )(*pieces, va, vb, meta)


def summed_kernel(n_tp, *refs):
    chunks = refs[:n_tp]
    stats_ref, out_ref = refs[n_tp:]
    prompts = chunks[0].shape[0]
    total = chunks[0][...].astype(F32)
    for d in range(1, n_tp):
        total = total + chunks[d][...].astype(F32)
    out_ref[:prompts] = total.astype(BF16)
    out_ref[prompts] = stats_ref[...]


def summed(chunks, stats):
    n_tp = len(chunks)
    prompts, rows, _ = chunks[0].shape
    return pl.pallas_call(
        functools.partial(summed_kernel, n_tp),
        in_specs=[VMEM] * (n_tp + 1),
        out_specs=VMEM,
        out_shape=jax.ShapeDtypeStruct((prompts + 1, rows, HD), BF16),
        compiler_params=pltpu.CompilerParams(vmem_limit_bytes=8 * MIB),
        cost_estimate=pl.CostEstimate(flops=0, bytes_accessed=4 * MIB, transcendentals=0),
        name="summed",
    )(*chunks, stats)


def output_kernel(n_seq, *refs):
    pieces = refs[:n_seq]
    fresh_ref = refs[n_seq]
    new = refs[n_seq + 1 : 2 * n_seq + 1]
    wa_ref, wb_ref, out_ref, held = refs[2 * n_seq + 1 :]
    more, rows_local, _ = pieces[0].shape
    prompts = more - 1
    new_count = fresh_ref.shape[0]
    rows = new_count * GROUP
    kv_local = rows_local // rows
    heads = kv_local * GROUP
    own_rows = prompts // n_seq
    seq = lax.axis_index("seq")
    tops, parts = [], []
    for s in range(n_seq):
        stats = pieces[s][prompts].astype(F32)
        folded = stats + pltpu.roll(stats, HD - prompts, 1)
        tops.append(folded)
        parts.append(pltpu.roll(folded, HD - 2 * prompts, 1))
    fresh = [fresh_ref[n] for n in range(new_count)]
    top = fresh[0]
    for other in fresh[1:] + tops:
        top = jnp.maximum(top, other)
    weights = [jnp.exp(f - top) for f in fresh]
    factors = [jnp.exp(t - top) for t in tops]
    total = weights[0]
    for w in weights[1:]:
        total = total + w
    for f, part in zip(factors, parts):
        total = total + f * part
    weights = [w / total for w in weights]
    factors = [f / total for f in factors]
    lane = lax.broadcasted_iota(jnp.int32, (rows_local, HD), 1)
    for r in range(prompts):
        sums = jnp.zeros((rows_local, HD), F32)
        for s in range(n_seq):
            sums = sums + factors[s][:, r : r + 1] * pieces[s][r].astype(F32)
        for g in range(kv_local):
            for n in range(new_count):
                at = g * rows + n * GROUP
                held[g * GROUP : (g + 1) * GROUP, r * new_count + n] = sums[at : at + GROUP]
    for ds in range(n_seq):
        for rr in range(own_rows):
            request = (seq ^ ds) * own_rows + rr
            share = [
                jnp.sum(jnp.where(lane == request, w, 0.0), axis=1, keepdims=True) for w in weights
            ]
            sums = jnp.zeros((rows_local, HD), F32)
            for n in range(new_count):
                both = new[ds][0, rr, n].astype(F32)
                value = [both[heads + 2 * g + 1 : heads + 2 * g + 2] for g in range(kv_local)]
                value = [jnp.broadcast_to(v, (rows, HD)) for v in value]
                sums = sums + share[n] * jnp.concatenate(value, axis=0)
            for g in range(kv_local):
                for n in range(new_count):
                    at = g * rows + n * GROUP
                    held[g * GROUP : (g + 1) * GROUP, request * new_count + n] += sums[
                        at : at + GROUP
                    ]
    half = heads // 2
    product = jnp.zeros(out_ref.shape, F32)
    for w_ref, at in ((wa_ref, 0), (wb_ref, half)):
        left = [held[h].astype(BF16) for h in range(at, at + half)]
        left = jnp.concatenate(left, axis=1)
        product = product + jnp.dot(left, w_ref[...], preferred_element_type=F32)
    out_ref[...] = product.astype(BF16)


def output_partial(pieces, fresh, new, weights):
    n_seq = len(pieces)
    new_count = fresh.shape[0]
    prompts = pieces[0].shape[0] - 1
    depth, columns = weights[0].shape
    return pl.pallas_call(
        functools.partial(output_kernel, n_seq),
        in_specs=[VMEM] * (2 * n_seq + 3),
        out_specs=VMEM,
        out_shape=jax.ShapeDtypeStruct((prompts * new_count, columns), BF16),
        scratch_shapes=[pltpu.VMEM((2 * depth // HD, prompts * new_count, HD), F32)],
        compiler_params=pltpu.CompilerParams(vmem_limit_bytes=24 * MIB),
        name="output",
    )(*pieces, fresh, *new, *weights)


def final_kernel(n_tp, *refs):
    pieces = refs[:n_tp]
    res_ref, out_ref = refs[n_tp:]
    prompts, new_count, _ = out_ref.shape
    total = pieces[0][...].astype(F32)
    for d in range(1, n_tp):
        total = total + pieces[d][...].astype(F32)
    for r in range(prompts):
        out_ref[r] = res_ref[r].astype(F32) + total[r * new_count : (r + 1) * new_count]


def final_sum(pieces, residual):
    n_tp = len(pieces)
    return pl.pallas_call(
        functools.partial(final_kernel, n_tp),
        in_specs=[VMEM] * (n_tp + 1),
        out_specs=VMEM,
        out_shape=jax.ShapeDtypeStruct(residual.shape, F32),
        compiler_params=pltpu.CompilerParams(vmem_limit_bytes=8 * MIB),
        name="final",
    )(*pieces, residual)


def on_device(
    prefill_states, kv_weight, page_counts, tail_tokens, new_query, new_keyval, residual, out_weight
):
    n_seq, n_tp = lax.axis_size("seq"), lax.axis_size("tp")
    own_rows, new_count, _ = new_query.shape
    prompts = page_counts.shape[0]
    pages = prefill_states.shape[0] // PAGE * n_seq
    new = gather(prepare(new_query, new_keyval), "tp")
    k, x, w, meta = project_keys(prefill_states, kv_weight, page_counts, tail_tokens, pages)
    new = stacked(new, meta)
    va, oa = project_values(x, w, out_weight, 0, new)
    new = gather(new, "seq")
    *scores, fresh = partial_scores(new, k, meta, pages, prompts, n_tp)
    vb, ob = project_values(x, w, out_weight, 1, fresh)
    weights, stats = softmax_weights(exchange(scores, "tp"), meta, pages, prompts)
    chunks = weighted_values(gather(weights, "tp"), va, vb, meta, prompts)
    pieces = gather(summed(exchange(chunks, "tp"), stats), "seq")
    partial = output_partial(pieces, fresh, new, (oa, ob))
    return final_sum(gather(partial, "tp"), residual)


def solution(mesh):
    placed = (
        P(("groups", "seq"), "tp"),
        P("tp", None),
        P("groups"),
        P("groups"),
        P(("groups", "seq"), None, "tp"),
        P(("groups", "seq"), None, "tp"),
        P("groups", None, "seq"),
        P("tp", "seq"),
    )
    return jax.shard_map(
        on_device, mesh=mesh, in_specs=placed, out_specs=P("groups", None, "seq"), check_vma=False
    )
```

```python
import functools
import math

import jax
import jax.numpy as jnp
from jax import lax
from jax.experimental import pallas as pl
from jax.experimental.pallas import tpu as pltpu
from jax.sharding import PartitionSpec as P

QH = 64
KVH = 8
HD = 128
PAGE = 128
GROUP = QH // KVH
NEG = -1e30
F32 = jnp.float32
BF16 = jnp.bfloat16
MIB = 1 << 20

VMEM = pl.BlockSpec(memory_space=pltpu.VMEM)
SMEM = pl.BlockSpec(memory_space=pltpu.SMEM)


def pairs(value, axis, d):
    return lax.ppermute(value, axis, [(i, i ^ d) for i in range(lax.axis_size(axis))])


def exchange(chunks, axis):
    got = {d: pairs(chunks[d], axis, d) for d in reversed(range(1, len(chunks)))}
    return [chunks[0]] + [got[d] for d in range(1, len(chunks))]


def gather(value, axis):
    size = lax.axis_size(axis)
    return [value] + [pairs(value, axis, d) for d in range(1, size)]


def lane_freqs(rows):
    lane = lax.broadcasted_iota(jnp.int32, (rows, HD), 1) % (HD // 2)
    return jnp.exp(-(lane.astype(F32) * (2.0 / HD)) * math.log(500000.0))


def sine_sign(rows):
    lane = lax.broadcasted_iota(jnp.int32, (rows, HD), 1)
    return jnp.where(lane < HD // 2, -1.0, 1.0)


def in_hbm(value):
    return pltpu.with_memory_space_constraint(value, pltpu.HBM)


def by_row(rows, numbers):
    row = lax.broadcasted_iota(jnp.int32, (rows, HD), 0)
    out = jnp.zeros((rows, HD), F32)
    for i, number in enumerate(numbers):
        out = jnp.where(row == i, number.astype(F32), out)
    return out


def page_table(pages, prompts, counts, tails, meta):
    def one_prompt(r, start):
        length = (counts[r] - 1) * PAGE + tails[r]
        meta[3 * pages + r] = length

        def one_page(i, carry):
            meta[start + i] = r
            meta[pages + start + i] = i * PAGE
            meta[2 * pages + start + i] = jnp.minimum(length - i * PAGE, PAGE)
            return carry

        lax.fori_loop(0, counts[r], one_page, 0)
        return start + counts[r]

    lax.fori_loop(0, prompts, one_prompt, 0)


def rotation_tables(pages, local_pages, meta, cos_s, sin_s):
    freqs = lane_freqs(8)
    low = lax.broadcasted_iota(jnp.int32, (8, HD), 0).astype(F32) * freqs
    low_cos, low_sin = jnp.cos(low), jnp.sin(low)
    high = lax.broadcasted_iota(jnp.int32, (PAGE // 8, HD), 0).astype(F32) * 8.0
    high = high * lane_freqs(PAGE // 8)
    high_cos, high_sin = jnp.cos(high), jnp.sin(high)
    first = lax.axis_index("seq") * local_pages
    base = by_row(local_pages, [meta[pages + first + p] for p in range(local_pages)])
    base = base * lane_freqs(local_pages)
    base_cos, base_sin = jnp.cos(base), jnp.sin(base)
    sign = sine_sign(8)
    for i in range(PAGE // 8):
        c, s = high_cos[i : i + 1], high_sin[i : i + 1]
        cosine, sine = low_cos * c - low_sin * s, low_sin * c + low_cos * s
        for p in range(local_pages):
            at = slice(p * PAGE + i * 8, p * PAGE + i * 8 + 8)
            c, s = base_cos[p : p + 1], base_sin[p : p + 1]
            cos_s[at] = cosine * c - sine * s
            sin_s[at] = sign * (sine * c + cosine * s)


def pair_columns(w_ref, rows, pair, part):
    at = [(2 * head + part) * HD for head in (2 * pair, 2 * pair + 1)]
    return jnp.concatenate([w_ref[rows, c : c + HD] for c in at], axis=1)


def load_kernel(pages, prompts, new_count, x_hbm, w_hbm, counts, tails, *refs):
    acc, x_ref, w_ref, cos_ref, sin_ref, cos_q, sin_q, meta, x_sems, w_sems = refs
    tokens, depth = x_ref.shape
    half, tall = depth // 2, tokens // 2
    copies = []
    for i in range(2):
        at = pl.ds(i * half, half)
        x_copy = pltpu.make_async_copy(x_hbm.at[:, at], x_ref.at[:, at], x_sems.at[i])
        w_copy = pltpu.make_async_copy(w_hbm.at[at], w_ref.at[at], w_sems.at[i])
        x_copy.start()
        w_copy.start()
        copies.append((x_copy, w_copy))
    page_table(pages, prompts, counts, tails, meta)
    rotation_tables(pages, tokens // PAGE, meta, cos_ref, sin_ref)
    spots = [meta[3 * pages + r] + n for r in range(prompts) for n in range(new_count)]
    angles = by_row(len(spots), spots) * lane_freqs(len(spots))
    cos_q[...] = jnp.cos(angles)
    sin_q[...] = jnp.sin(angles) * sine_sign(len(spots))
    for copy in copies[0]:
        copy.wait()
    rows = slice(0, half)
    for pair in range(KVH // 2):
        weight = pair_columns(w_ref, rows, pair, 0)
        for start in range(0, tokens, tall):
            at = slice(start, start + tall)
            acc[at, 2 * pair * HD : 2 * (pair + 1) * HD] = jnp.dot(
                x_ref[at, rows], weight, preferred_element_type=F32
            )
    for copy in copies[1]:
        copy.wait()


def load(x, kv_weight, counts, tails, pages, new_count):
    tokens, depth = x.shape
    columns = kv_weight.shape[1]
    prompts = counts.shape[0]
    hbm = pl.BlockSpec(memory_space=pltpu.HBM)
    return pl.pallas_call(
        functools.partial(load_kernel, pages, prompts, new_count),
        in_specs=[hbm, hbm, SMEM, SMEM],
        out_specs=[VMEM] * 7 + [SMEM],
        out_shape=[
            pltpu.VMEM((tokens, KVH * HD), F32),
            pltpu.VMEM((tokens, depth), BF16),
            pltpu.VMEM((depth, columns), BF16),
            pltpu.VMEM((tokens, HD), F32),
            pltpu.VMEM((tokens, HD), F32),
            pltpu.VMEM((prompts * new_count, HD), F32),
            pltpu.VMEM((prompts * new_count, HD), F32),
            jax.ShapeDtypeStruct((3 * pages + prompts,), jnp.int32),
        ],
        scratch_shapes=[pltpu.SemaphoreType.DMA((2,)), pltpu.SemaphoreType.DMA((2,))],
        compiler_params=pltpu.CompilerParams(vmem_limit_bytes=28 * MIB),
        cost_estimate=pl.CostEstimate(
            flops=tokens * depth * KVH * HD,
            bytes_accessed=2 * depth * (tokens + columns),
            transcendentals=0,
        ),
        name="load",
    )(*[in_hbm(a) for a in (x, kv_weight, counts, tails)])


def keys_kernel(acc, x_ref, w_ref, cos_ref, sin_ref, after, k_ref):
    tokens, depth = x_ref.shape
    tall = tokens // 2
    rows = slice(depth // 2, depth)
    for pair in range(KVH // 2):
        weight = pair_columns(w_ref, rows, pair, 0)
        columns = slice(2 * pair * HD, 2 * (pair + 1) * HD)
        for start in range(0, tokens, tall):
            at = slice(start, start + tall)
            product = acc[at, columns] + jnp.dot(
                x_ref[at, rows], weight, preferred_element_type=F32
            )
            cosine, sine = cos_ref[at], sin_ref[at]
            for h in range(2):
                k = product[:, h * HD : (h + 1) * HD]
                k = k * cosine + pltpu.roll(k, HD // 2, 1) * sine
                k_ref[at, (2 * pair + h) * HD : (2 * pair + h + 1) * HD] = k.astype(BF16)


def rotated_keys(acc, x, weight, cosine, sine, after):
    tokens, depth = x.shape
    return pl.pallas_call(
        keys_kernel,
        in_specs=[VMEM] * 5 + [pl.BlockSpec(memory_space=pl.ANY)],
        out_specs=VMEM,
        out_shape=pltpu.VMEM((tokens, KVH * HD), BF16),
        compiler_params=pltpu.CompilerParams(vmem_limit_bytes=24 * MIB),
        cost_estimate=pl.CostEstimate(
            flops=tokens * depth * KVH * HD, bytes_accessed=8 * MIB, transcendentals=0
        ),
        name="keys",
    )(acc, x, weight, cosine, sine, after)


def values_kernel(first, x_ref, w_ref, o_hbm, after, v_ref, o_ref, sem):
    depth = o_ref.shape[0]
    copy = pltpu.make_async_copy(o_hbm.at[pl.ds(first * depth, depth)], o_ref, sem)
    copy.start()
    tokens, columns = v_ref.shape
    tall = tokens // 2
    pairs_here = columns // (2 * HD)
    for pair in range(pairs_here):
        weight = pair_columns(w_ref, slice(None), first * pairs_here + pair, 1)
        for i in range(2):
            at = slice(i * tall, (i + 1) * tall)
            v_ref[at, 2 * pair * HD : 2 * (pair + 1) * HD] = jnp.dot(
                x_ref[at], weight, preferred_element_type=F32
            ).astype(BF16)
    copy.wait()


def project_values(x, weight, out_weight, first, after):
    tokens, depth = x.shape
    columns = KVH // 2 * HD
    rows = out_weight.shape[0] // 2
    return pl.pallas_call(
        functools.partial(values_kernel, first),
        in_specs=[
            VMEM,
            VMEM,
            pl.BlockSpec(memory_space=pltpu.HBM),
            pl.BlockSpec(memory_space=pl.ANY),
        ],
        out_specs=[VMEM, VMEM],
        out_shape=[
            pltpu.VMEM((tokens, columns), BF16),
            pltpu.VMEM((rows, out_weight.shape[1]), BF16),
        ],
        scratch_shapes=[pltpu.SemaphoreType.DMA],
        compiler_params=pltpu.CompilerParams(vmem_limit_bytes=24 * MIB),
        cost_estimate=pl.CostEstimate(
            flops=2 * tokens * depth * columns, bytes_accessed=8 * MIB, transcendentals=0
        ),
        name="values",
    )(x, weight, in_hbm(out_weight), after)


def prepare_kernel(q_ref, kv_ref, out_ref):
    own_rows, new_count, _, _ = out_ref.shape
    for r in range(own_rows):
        q, kv = q_ref[r].astype(F32), kv_ref[r].astype(F32)
        for n in range(new_count):
            parts = [a[n : n + 1, c : c + HD] for a in (q, kv) for c in range(0, a.shape[1], HD)]
            out_ref[r, n] = jnp.concatenate(parts, axis=0).astype(BF16)


def prepare(new_query, new_keyval):
    own_rows, new_count, columns = new_query.shape
    heads = (columns + new_keyval.shape[2]) // HD
    return pl.pallas_call(
        prepare_kernel,
        in_specs=[VMEM, VMEM],
        out_specs=VMEM,
        out_shape=jax.ShapeDtypeStruct((own_rows, new_count, heads, HD), BF16),
        compiler_params=pltpu.CompilerParams(vmem_limit_bytes=8 * MIB),
        cost_estimate=pl.CostEstimate(flops=0, bytes_accessed=MIB, transcendentals=0),
        name="prepare",
    )(in_hbm(new_query), in_hbm(new_keyval))


def stacked_kernel(n_tp, *refs):
    for d in range(n_tp):
        refs[-1][d] = refs[d][...]


def stacked(pieces, after):
    n_tp = len(pieces)
    return pl.pallas_call(
        functools.partial(stacked_kernel, n_tp),
        in_specs=[VMEM] * n_tp + [pl.BlockSpec(memory_space=pl.ANY)],
        out_specs=VMEM,
        out_shape=jax.ShapeDtypeStruct((n_tp,) + pieces[0].shape, BF16),
        compiler_params=pltpu.CompilerParams(vmem_limit_bytes=8 * MIB),
        name="stacked",
    )(*pieces, after)


def scores_kernel(n_seq, n_tp, *refs):
    new = refs[:n_seq]
    k_ref, cos_q, sin_q, meta = refs[n_seq : n_seq + 4]
    outs = refs[n_seq + 4 : n_seq + 4 + n_tp]
    own_q, all_q, ready = refs[n_seq + 4 + n_tp :]
    kv_local = KVH // n_tp
    local_pages = k_ref.shape[0] // PAGE
    _, own_rows, new_count, _, _ = new[0].shape
    rows = new_count * GROUP
    count = kv_local * rows
    scale = 1.0 / math.sqrt(HD)
    me = lax.axis_index("tp")
    seq = lax.axis_index("seq")
    first = seq * local_pages
    for ds in range(n_seq):
        for rr in range(own_rows):
            request = (seq ^ ds) * own_rows + rr
            spots = [pl.ds(request * new_count + n, 1) for n in range(new_count)]
            turn = [(cos_q[spot], sin_q[spot]) for spot in spots]
            for dt in range(n_tp):
                block = [new[ds][dt, rr, n].astype(F32) for n in range(new_count)]
                for g in range(kv_local):
                    parts = []
                    for n in range(new_count):
                        q = block[n][g * GROUP : (g + 1) * GROUP]
                        parts.append(q * turn[n][0] + pltpu.roll(q, HD // 2, 1) * turn[n][1])
                    part = jnp.concatenate(parts, axis=0).astype(BF16)
                    at = ((me ^ dt) * kv_local + g) * rows
                    all_q[request, pl.ds(pl.multiple_of(at, rows), rows)] = part
                    if dt == 0:
                        own_q[request, g * rows : (g + 1) * rows] = part
    for p in range(local_pages):
        request = meta[first + p]
        tokens = slice(p * PAGE, (p + 1) * PAGE)
        for head in range(KVH):
            k = k_ref[tokens, head * HD : (head + 1) * HD]
            q = all_q[request, head * rows : (head + 1) * rows]
            s = lax.dot_general(q, k, (((1,), (1,)), ((), ())), preferred_element_type=F32)
            ready[head * rows : (head + 1) * rows, tokens] = (s * scale).astype(BF16)
    for d in range(n_tp):
        outs[d][...] = ready[pl.ds(pl.multiple_of((me ^ d) * count, count), count)]


def partial_scores(new, k, cos_q, sin_q, meta, prompts, n_tp):
    n_seq = len(new)
    new_count = new[0].shape[2]
    tokens = k.shape[0]
    rows = KVH // n_tp * new_count * GROUP
    return pl.pallas_call(
        functools.partial(scores_kernel, n_seq, n_tp),
        in_specs=[VMEM] * (n_seq + 3) + [SMEM],
        out_specs=[VMEM] * (n_tp + 1),
        out_shape=[jax.ShapeDtypeStruct((rows, tokens), BF16)] * n_tp
        + [jax.ShapeDtypeStruct((prompts, rows, HD), BF16)],
        scratch_shapes=[
            pltpu.VMEM((prompts, rows * n_tp, HD), BF16),
            pltpu.VMEM((rows * n_tp, tokens), BF16),
        ],
        compiler_params=pltpu.CompilerParams(vmem_limit_bytes=24 * MIB),
        cost_estimate=pl.CostEstimate(
            flops=2 * tokens * rows * n_tp * HD, bytes_accessed=6 * MIB, transcendentals=0
        ),
        name="scores",
    )(*new, k, cos_q, sin_q, meta)


def fresh_kernel(n_seq, *refs):
    new = refs[:n_seq]
    q_ref, cos_q, sin_q, score_ref, value_ref = refs[n_seq:]
    prompts, rows_local, _ = q_ref.shape
    _, own_rows, new_count, _, _ = new[0].shape
    rows = new_count * GROUP
    kv_local = rows_local // rows
    heads = kv_local * GROUP
    scale = 1.0 / math.sqrt(HD)
    seq = lax.axis_index("seq")
    step = lax.broadcasted_iota(jnp.int32, (rows_local, HD), 0) % rows // GROUP
    lane = lax.broadcasted_iota(jnp.int32, (rows_local, HD), 1)
    found = [jnp.full((rows_local, HD), NEG, F32) for _ in range(new_count)]
    for ds in range(n_seq):
        for rr in range(own_rows):
            request = (seq ^ ds) * own_rows + rr
            q = q_ref[request].astype(F32)
            for n in range(new_count):
                spot = pl.ds(request * new_count + n, 1)
                cosine, sine = cos_q[spot], sin_q[spot]
                both = new[ds][0, rr, n].astype(F32)
                keys, values = [], []
                for g in range(kv_local):
                    k = both[heads + 2 * g : heads + 2 * g + 1]
                    k = k * cosine + pltpu.roll(k, HD // 2, 1) * sine
                    k = k.astype(BF16).astype(F32)
                    keys.append(jnp.broadcast_to(k, (rows, HD)))
                    v = both[heads + 2 * g + 1 : heads + 2 * g + 2]
                    values.append(jnp.broadcast_to(v, (rows, HD)))
                s = jnp.sum(q * jnp.concatenate(keys, axis=0), axis=1, keepdims=True) * scale
                found[n] = jnp.where((lane == request) & (step >= n), s, found[n])
                value_ref[request * new_count + n] = jnp.concatenate(values, axis=0)
    for n in range(new_count):
        score_ref[n] = found[n]


def fresh_scores(new, own_q, cos_q, sin_q):
    n_seq = len(new)
    new_count = new[0].shape[2]
    prompts, rows, _ = own_q.shape
    return pl.pallas_call(
        functools.partial(fresh_kernel, n_seq),
        in_specs=[VMEM] * (n_seq + 3),
        out_specs=[VMEM, VMEM],
        out_shape=[
            jax.ShapeDtypeStruct((new_count, rows, HD), F32),
            jax.ShapeDtypeStruct((prompts * new_count, rows, HD), F32),
        ],
        compiler_params=pltpu.CompilerParams(vmem_limit_bytes=16 * MIB),
        cost_estimate=pl.CostEstimate(flops=0, bytes_accessed=2 * MIB, transcendentals=0),
        name="fresh",
    )(*new, own_q, cos_q, sin_q)


def weights_kernel(pages, prompts, n_tp, *refs):
    chunks = refs[:n_tp]
    meta, w_ref, stats_ref = refs[n_tp:]
    rows, tokens = w_ref.shape
    local_pages = tokens // PAGE
    first = lax.axis_index("seq") * local_pages
    lane = lax.broadcasted_iota(jnp.int32, (rows, PAGE), 1)
    scores, maxima, masks, owners = [], [], [], []
    for p in range(local_pages):
        at = slice(p * PAGE, (p + 1) * PAGE)
        total = chunks[0][:, at].astype(F32)
        for d in range(1, n_tp):
            total = total + chunks[d][:, at].astype(F32)
        mask = lane < meta[2 * pages + first + p]
        total = jnp.where(mask, total, NEG)
        masks.append(mask)
        scores.append(total)
        maxima.append(jnp.max(total, axis=1, keepdims=True))
        owners.append(meta[first + p])
    quarter = lane // prompts
    spot = lane % prompts
    stats = jnp.where(quarter == 0, NEG, 0.0)
    sums = []
    for p in range(local_pages):
        top = maxima[p]
        for other in range(local_pages):
            if other != p:
                top = jnp.where(owners[p] == owners[other], jnp.maximum(top, maxima[other]), top)
        high = top.astype(BF16).astype(F32)
        low = (top - high).astype(BF16).astype(F32)
        w = jnp.where(masks[p], jnp.exp(scores[p] - (high + low)), 0.0)
        w_ref[:, p * PAGE : (p + 1) * PAGE] = w.astype(BF16)
        here = spot == owners[p]
        stats = jnp.where(here & (quarter == 0), high, stats)
        stats = jnp.where(here & (quarter == 1), low, stats)
        part = jnp.sum(w, axis=1, keepdims=True)
        stats = stats + jnp.where(here & (quarter == 2), part, 0.0)
    high = stats.astype(BF16).astype(F32)
    low = pltpu.roll(stats - high, prompts, 1)
    stats_ref[...] = jnp.where(quarter == 3, low, stats).astype(BF16)


def softmax_weights(chunks, meta, pages, prompts):
    n_tp = len(chunks)
    rows, tokens = chunks[0].shape
    return pl.pallas_call(
        functools.partial(weights_kernel, pages, prompts, n_tp),
        in_specs=[VMEM] * n_tp + [SMEM],
        out_specs=[VMEM, VMEM],
        out_shape=[
            jax.ShapeDtypeStruct((rows, tokens), BF16),
            jax.ShapeDtypeStruct((rows, PAGE), BF16),
        ],
        compiler_params=pltpu.CompilerParams(vmem_limit_bytes=8 * MIB),
        name="weights",
    )(*chunks, meta)


def weighted_kernel(n_tp, *refs):
    pieces = refs[:n_tp]
    va_ref, vb_ref, meta = refs[n_tp : n_tp + 3]
    outs = refs[n_tp + 3 : n_tp + 3 + n_tp]
    ready, total = refs[n_tp + 3 + n_tp :]
    rows_local, tokens_here = pieces[0].shape
    kv_local = KVH // n_tp
    rows = rows_local // kv_local
    local_pages = tokens_here // PAGE
    first = lax.axis_index("seq") * local_pages
    me = lax.axis_index("tp")
    own = [pl.ds(pl.multiple_of((me ^ d) * rows_local, rows_local), rows_local) for d in range(n_tp)]
    for d in range(n_tp):
        ready[own[d]] = pieces[d][...]
    total[...] = jnp.zeros_like(total)
    half = va_ref.shape[1] // HD
    for p in range(local_pages):
        request = meta[first + p]
        tokens = slice(p * PAGE, (p + 1) * PAGE)
        for head in range(KVH):
            v_ref = va_ref if head < half else vb_ref
            v = v_ref[tokens, head % half * HD : (head % half + 1) * HD]
            at = slice(head * rows, (head + 1) * rows)
            total[request, at] += jnp.dot(ready[at, tokens], v, preferred_element_type=F32)
    for d in range(n_tp):
        outs[d][...] = total[:, own[d]].astype(BF16)


def weighted_values(pieces, va, vb, meta, prompts):
    n_tp = len(pieces)
    rows, tokens = pieces[0].shape
    return pl.pallas_call(
        functools.partial(weighted_kernel, n_tp),
        in_specs=[VMEM] * (n_tp + 2) + [SMEM],
        out_specs=[VMEM] * n_tp,
        out_shape=[jax.ShapeDtypeStruct((prompts, rows, HD), BF16)] * n_tp,
        scratch_shapes=[
            pltpu.VMEM((rows * n_tp, tokens), BF16),
            pltpu.VMEM((prompts, rows * n_tp, HD), F32),
        ],
        compiler_params=pltpu.CompilerParams(vmem_limit_bytes=24 * MIB),
        cost_estimate=pl.CostEstimate(
            flops=2 * tokens * rows * n_tp * HD, bytes_accessed=8 * MIB, transcendentals=0
        ),
        name="weighted",
    )(*pieces, va, vb, meta)


def summed_kernel(n_tp, *refs):
    chunks = refs[:n_tp]
    stats_ref, out_ref = refs[n_tp:]
    prompts = chunks[0].shape[0]
    total = chunks[0][...].astype(F32)
    for d in range(1, n_tp):
        total = total + chunks[d][...].astype(F32)
    out_ref[:prompts] = total.astype(BF16)
    out_ref[prompts] = stats_ref[...]


def summed(chunks, stats):
    n_tp = len(chunks)
    prompts, rows, _ = chunks[0].shape
    return pl.pallas_call(
        functools.partial(summed_kernel, n_tp),
        in_specs=[VMEM] * (n_tp + 1),
        out_specs=VMEM,
        out_shape=jax.ShapeDtypeStruct((prompts + 1, rows, HD), BF16),
        compiler_params=pltpu.CompilerParams(vmem_limit_bytes=8 * MIB),
        cost_estimate=pl.CostEstimate(flops=0, bytes_accessed=4 * MIB, transcendentals=0),
        name="summed",
    )(*chunks, stats)


def output_kernel(n_seq, *refs):
    pieces = refs[:n_seq]
    fresh_ref, value_ref, wa_ref, wb_ref, out_ref, held = refs[n_seq:]
    more, rows_local, _ = pieces[0].shape
    prompts = more - 1
    new_count = fresh_ref.shape[0]
    rows = new_count * GROUP
    kv_local = rows_local // rows
    heads = kv_local * GROUP
    tops, parts = [], []
    for s in range(n_seq):
        stats = pieces[s][prompts].astype(F32)
        folded = stats + pltpu.roll(stats, HD - prompts, 1)
        tops.append(folded)
        parts.append(pltpu.roll(folded, HD - 2 * prompts, 1))
    fresh = [fresh_ref[n] for n in range(new_count)]
    top = fresh[0]
    for other in fresh[1:] + tops:
        top = jnp.maximum(top, other)
    weights = [jnp.exp(f - top) for f in fresh]
    factors = [jnp.exp(t - top) for t in tops]
    total = weights[0]
    for w in weights[1:]:
        total = total + w
    for f, part in zip(factors, parts):
        total = total + f * part
    weights = [w / total for w in weights]
    factors = [f / total for f in factors]
    for r in range(prompts):
        sums = jnp.zeros((rows_local, HD), F32)
        for s in range(n_seq):
            sums = sums + factors[s][:, r : r + 1] * pieces[s][r].astype(F32)
        for n in range(new_count):
            sums = sums + weights[n][:, r : r + 1] * value_ref[r * new_count + n]
        for g in range(kv_local):
            for n in range(new_count):
                at = g * rows + n * GROUP
                held[g * GROUP : (g + 1) * GROUP, r * new_count + n] = sums[at : at + GROUP]
    half = heads // 2
    product = jnp.zeros(out_ref.shape, F32)
    for w_ref, at in ((wa_ref, 0), (wb_ref, half)):
        left = [held[h].astype(BF16) for h in range(at, at + half)]
        left = jnp.concatenate(left, axis=1)
        product = product + jnp.dot(left, w_ref[...], preferred_element_type=F32)
    out_ref[...] = product.astype(BF16)


def output_partial(pieces, fresh, values, weights):
    n_seq = len(pieces)
    new_count = fresh.shape[0]
    prompts = pieces[0].shape[0] - 1
    depth, columns = weights[0].shape
    return pl.pallas_call(
        functools.partial(output_kernel, n_seq),
        in_specs=[VMEM] * (n_seq + 4),
        out_specs=VMEM,
        out_shape=jax.ShapeDtypeStruct((prompts * new_count, columns), BF16),
        scratch_shapes=[pltpu.VMEM((2 * depth // HD, prompts * new_count, HD), F32)],
        compiler_params=pltpu.CompilerParams(vmem_limit_bytes=24 * MIB),
        name="output",
    )(*pieces, fresh, values, *weights)


def final_kernel(n_tp, *refs):
    pieces = refs[:n_tp]
    res_ref, out_ref = refs[n_tp:]
    prompts, new_count, _ = out_ref.shape
    total = pieces[0][...].astype(F32)
    for d in range(1, n_tp):
        total = total + pieces[d][...].astype(F32)
    for r in range(prompts):
        out_ref[r] = res_ref[r].astype(F32) + total[r * new_count : (r + 1) * new_count]


def final_sum(pieces, residual):
    n_tp = len(pieces)
    return pl.pallas_call(
        functools.partial(final_kernel, n_tp),
        in_specs=[VMEM] * (n_tp + 1),
        out_specs=VMEM,
        out_shape=jax.ShapeDtypeStruct(residual.shape, F32),
        compiler_params=pltpu.CompilerParams(vmem_limit_bytes=8 * MIB),
        name="final",
    )(*pieces, residual)


def on_device(
    prefill_states, kv_weight, page_counts, tail_tokens, new_query, new_keyval, residual, out_weight
):
    n_seq, n_tp = lax.axis_size("seq"), lax.axis_size("tp")
    own_rows, new_count, _ = new_query.shape
    prompts = page_counts.shape[0]
    pages = prefill_states.shape[0] // PAGE * n_seq
    new = gather(prepare(new_query, new_keyval), "tp")
    acc, x, w, cosine, sine, cos_q, sin_q, meta = load(
        prefill_states, kv_weight, page_counts, tail_tokens, pages, new_count
    )
    new = stacked(new, meta)
    k = rotated_keys(acc, x, w, cosine, sine, new)
    new = gather(new, "seq")
    *scores, own_q = partial_scores(new, k, cos_q, sin_q, meta, prompts, n_tp)
    va, oa = project_values(x, w, out_weight, 0, own_q)
    fresh, values = fresh_scores(new, own_q, cos_q, sin_q)
    weights, stats = softmax_weights(exchange(scores, "tp"), meta, pages, prompts)
    vb, ob = project_values(x, w, out_weight, 1, stats)
    chunks = weighted_values(gather(weights, "tp"), va, vb, meta, prompts)
    pieces = gather(summed(exchange(chunks, "tp"), stats), "seq")
    partial = output_partial(pieces, fresh, values, (oa, ob))
    return final_sum(gather(partial, "tp"), residual)


def solution(mesh):
    placed = (
        P(("groups", "seq"), "tp"),
        P("tp", None),
        P("groups"),
        P("groups"),
        P(("groups", "seq"), None, "tp"),
        P(("groups", "seq"), None, "tp"),
        P("groups", None, "seq"),
        P("tp", "seq"),
    )
    return jax.shard_map(
        on_device, mesh=mesh, in_specs=placed, out_specs=P("groups", None, "seq"), check_vma=False
    )
```

```python
import functools
import math

import jax
import jax.numpy as jnp
from jax import lax
from jax.experimental import pallas as pl
from jax.experimental.pallas import tpu as pltpu
from jax.sharding import PartitionSpec as P

QH = 64
KVH = 8
HD = 128
PAGE = 128
GROUP = QH // KVH
NEG = -1e30
F32 = jnp.float32
BF16 = jnp.bfloat16
MIB = 1 << 20

VMEM = pl.BlockSpec(memory_space=pltpu.VMEM)
SMEM = pl.BlockSpec(memory_space=pltpu.SMEM)


def pairs(value, axis, d):
    return lax.ppermute(value, axis, [(i, i ^ d) for i in range(lax.axis_size(axis))])


def repeat_kernel(in_ref, out_ref):
    out_ref[...] = in_ref[...]


def repeated(value):
    return pl.pallas_call(
        repeat_kernel,
        in_specs=[VMEM],
        out_specs=VMEM,
        out_shape=jax.ShapeDtypeStruct(value.shape, value.dtype),
        compiler_params=pltpu.CompilerParams(vmem_limit_bytes=8 * MIB),
        name="repeat",
    )(value)


def far_first(size):
    return list(range(size // 2, size)) + list(range(1, size // 2))


def gather(value, axis):
    size = lax.axis_size(axis)
    got = {0: value}
    near = repeated(value)
    for d in far_first(size):
        got[d] = pairs(value if d >= size // 2 else near, axis, d)
    return [got[d] for d in range(size)]


def own_copy(value, axis):
    return pairs(value, axis, 0)


def lane_freqs(rows):
    lane = lax.broadcasted_iota(jnp.int32, (rows, HD), 1) % (HD // 2)
    return jnp.exp(-(lane.astype(F32) * (2.0 / HD)) * math.log(500000.0))


def sine_sign(rows):
    lane = lax.broadcasted_iota(jnp.int32, (rows, HD), 1)
    return jnp.where(lane < HD // 2, -1.0, 1.0)


def in_hbm(value):
    return pltpu.with_memory_space_constraint(value, pltpu.HBM)


def in_vmem(value):
    return pltpu.with_memory_space_constraint(value, pltpu.VMEM)


def by_row(rows, numbers):
    row = lax.broadcasted_iota(jnp.int32, (rows, HD), 0)
    out = jnp.zeros((rows, HD), F32)
    for i, number in enumerate(numbers):
        out = jnp.where(row == i, number.astype(F32), out)
    return out


def page_table(pages, prompts, counts, tails, meta):
    def one_prompt(r, start):
        length = (counts[r] - 1) * PAGE + tails[r]
        meta[3 * pages + r] = length

        def one_page(i, carry):
            meta[start + i] = r
            meta[pages + start + i] = i * PAGE
            meta[2 * pages + start + i] = jnp.minimum(length - i * PAGE, PAGE)
            return carry

        lax.fori_loop(0, counts[r], one_page, 0)
        return start + counts[r]

    lax.fori_loop(0, prompts, one_prompt, 0)


def rotation_tables(pages, local_pages, meta, cos_s, sin_s):
    freqs = lane_freqs(8)
    low = lax.broadcasted_iota(jnp.int32, (8, HD), 0).astype(F32) * freqs
    low_cos, low_sin = jnp.cos(low), jnp.sin(low)
    high = lax.broadcasted_iota(jnp.int32, (PAGE // 8, HD), 0).astype(F32) * 8.0
    high = high * lane_freqs(PAGE // 8)
    high_cos, high_sin = jnp.cos(high), jnp.sin(high)
    first = lax.axis_index("seq") * local_pages
    base = by_row(local_pages, [meta[pages + first + p] for p in range(local_pages)])
    base = base * lane_freqs(local_pages)
    base_cos, base_sin = jnp.cos(base), jnp.sin(base)
    sign = sine_sign(8)
    for i in range(PAGE // 8):
        c, s = high_cos[i : i + 1], high_sin[i : i + 1]
        cosine, sine = low_cos * c - low_sin * s, low_sin * c + low_cos * s
        for p in range(local_pages):
            at = slice(p * PAGE + i * 8, p * PAGE + i * 8 + 8)
            c, s = base_cos[p : p + 1], base_sin[p : p + 1]
            cos_s[at] = cosine * c - sine * s
            sin_s[at] = sign * (sine * c + cosine * s)


def pair_columns(w_ref, rows, pair, part):
    at = [(2 * head + part) * HD for head in (2 * pair, 2 * pair + 1)]
    return jnp.concatenate([w_ref[rows, c : c + HD] for c in at], axis=1)


def keys_kernel(pages, prompts, x_ref, w_ref, counts, tails, k_ref, cos_q, sin_q, meta, cos_s, sin_s):
    tokens = x_ref.shape[0]
    tall = tokens // 2
    page_table(pages, prompts, counts, tails, meta)
    rotation_tables(pages, tokens // PAGE, meta, cos_s, sin_s)
    new_count = cos_q.shape[0] // prompts
    spots = [meta[3 * pages + r] + n for r in range(prompts) for n in range(new_count)]
    angles = by_row(len(spots), spots) * lane_freqs(len(spots))
    cos_q[...] = jnp.cos(angles)
    sin_q[...] = jnp.sin(angles) * sine_sign(len(spots))
    for pair in range(KVH // 2):
        weight = pair_columns(w_ref, slice(None), pair, 0)
        for start in range(0, tokens, tall):
            at = slice(start, start + tall)
            product = jnp.dot(x_ref[at], weight, preferred_element_type=F32)
            cosine, sine = cos_s[at], sin_s[at]
            for h in range(2):
                k = product[:, h * HD : (h + 1) * HD]
                k = k * cosine + pltpu.roll(k, HD // 2, 1) * sine
                k_ref[at, (2 * pair + h) * HD : (2 * pair + h + 1) * HD] = k.astype(BF16)


def project_keys(x, kv_weight, counts, tails, pages, new_count):
    tokens, depth = x.shape
    prompts = counts.shape[0]
    return pl.pallas_call(
        functools.partial(keys_kernel, pages, prompts),
        in_specs=[VMEM, VMEM, SMEM, SMEM],
        out_specs=[VMEM, VMEM, VMEM, SMEM],
        out_shape=[
            pltpu.VMEM((tokens, KVH * HD), BF16),
            pltpu.VMEM((prompts * new_count, HD), F32),
            pltpu.VMEM((prompts * new_count, HD), F32),
            jax.ShapeDtypeStruct((3 * pages + prompts,), jnp.int32),
        ],
        scratch_shapes=[pltpu.VMEM((tokens, HD), F32), pltpu.VMEM((tokens, HD), F32)],
        compiler_params=pltpu.CompilerParams(vmem_limit_bytes=24 * MIB),
        cost_estimate=pl.CostEstimate(
            flops=2 * tokens * depth * KVH * HD, bytes_accessed=12 * MIB, transcendentals=0
        ),
        name="keys",
    )(in_vmem(x), in_vmem(kv_weight), in_hbm(counts), in_hbm(tails))


def values_kernel(first, x_ref, w_ref, o_hbm, after, v_ref, o_ref, sem):
    depth = o_ref.shape[0]
    copy = pltpu.make_async_copy(o_hbm.at[pl.ds(first * depth, depth)], o_ref, sem)
    copy.start()
    tokens, columns = v_ref.shape
    tall = tokens // 2
    pairs_here = columns // (2 * HD)
    for pair in range(pairs_here):
        weight = pair_columns(w_ref, slice(None), first * pairs_here + pair, 1)
        for i in range(2):
            at = slice(i * tall, (i + 1) * tall)
            v_ref[at, 2 * pair * HD : 2 * (pair + 1) * HD] = jnp.dot(
                x_ref[at], weight, preferred_element_type=F32
            ).astype(BF16)
    copy.wait()


def project_values(x, weight, out_weight, first, after):
    tokens, depth = x.shape
    columns = KVH // 2 * HD
    rows = out_weight.shape[0] // 2
    return pl.pallas_call(
        functools.partial(values_kernel, first),
        in_specs=[
            VMEM,
            VMEM,
            pl.BlockSpec(memory_space=pltpu.HBM),
            pl.BlockSpec(memory_space=pl.ANY),
        ],
        out_specs=[VMEM, VMEM],
        out_shape=[
            pltpu.VMEM((tokens, columns), BF16),
            pltpu.VMEM((rows, out_weight.shape[1]), BF16),
        ],
        scratch_shapes=[pltpu.SemaphoreType.DMA],
        compiler_params=pltpu.CompilerParams(vmem_limit_bytes=24 * MIB),
        cost_estimate=pl.CostEstimate(
            flops=2 * tokens * depth * columns, bytes_accessed=8 * MIB, transcendentals=0
        ),
        name="values",
    )(in_vmem(x), in_vmem(weight), in_hbm(out_weight), after)


def prepare_kernel(q_ref, kv_ref, out_ref):
    copies, own_rows, new_count, _, _ = out_ref.shape
    for r in range(own_rows):
        q, kv = q_ref[r].astype(F32), kv_ref[r].astype(F32)
        for n in range(new_count):
            parts = [a[n : n + 1, c : c + HD] for a in (q, kv) for c in range(0, a.shape[1], HD)]
            block = jnp.concatenate(parts, axis=0).astype(BF16)
            for i in range(copies):
                out_ref[i, r, n] = block


def prepare(new_query, new_keyval, copies):
    own_rows, new_count, columns = new_query.shape
    heads = (columns + new_keyval.shape[2]) // HD
    return pl.pallas_call(
        prepare_kernel,
        in_specs=[VMEM, VMEM],
        out_specs=VMEM,
        out_shape=jax.ShapeDtypeStruct((copies, own_rows, new_count, heads, HD), BF16),
        compiler_params=pltpu.CompilerParams(vmem_limit_bytes=8 * MIB),
        cost_estimate=pl.CostEstimate(flops=0, bytes_accessed=MIB, transcendentals=0),
        name="prepare",
    )(in_hbm(new_query), in_hbm(new_keyval))


def turned_queries(new_ref, cos_q, sin_q, all_q, n_seq, n_tp):
    _, own_rows, new_count, _, _ = new_ref.shape
    kv_local = KVH // n_tp
    rows = new_count * GROUP
    for ds in range(n_seq):
        for rr in range(own_rows):
            request = ds * own_rows + rr
            spots = [slice(request * new_count + n, request * new_count + n + 1) for n in range(new_count)]
            turn = [(cos_q[spot], sin_q[spot]) for spot in spots]
            for dt in range(n_tp):
                block = [new_ref[ds * n_tp + dt, rr, n].astype(F32) for n in range(new_count)]
                for g in range(kv_local):
                    parts = []
                    for n in range(new_count):
                        q = block[n][g * GROUP : (g + 1) * GROUP]
                        parts.append(q * turn[n][0] + pltpu.roll(q, HD // 2, 1) * turn[n][1])
                    at = (dt * kv_local + g) * rows
                    all_q[request, at : at + rows] = jnp.concatenate(parts, axis=0).astype(BF16)


def page_scores(all_q, k_ref, meta, outs, entries, rows):
    local_pages = k_ref.shape[0] // PAGE
    kv_local = outs[0].shape[0] // rows
    scale = 1.0 / math.sqrt(HD)
    me = lax.axis_index("tp")
    first = lax.axis_index("seq") * local_pages
    for p in range(local_pages):
        request = meta[first + p]
        tokens = slice(p * PAGE, (p + 1) * PAGE)
        for out, d in zip(outs, entries):
            for g in range(kv_local):
                head = (me ^ d) * kv_local + g
                k = k_ref[tokens, pl.ds(pl.multiple_of(head * HD, HD), HD)]
                q = all_q[request, pl.ds(pl.multiple_of(head * rows, rows), rows)]
                s = lax.dot_general(q, k, (((1,), (1,)), ((), ())), preferred_element_type=F32)
                out[g * rows : (g + 1) * rows, tokens] = (s * scale).astype(BF16)


def far_kernel(n_seq, n_tp, entries, new_ref, k_ref, cos_q, sin_q, meta, all_q, *outs):
    turned_queries(new_ref, cos_q, sin_q, all_q, n_seq, n_tp)
    page_scores(all_q, k_ref, meta, outs, entries, new_ref.shape[2] * GROUP)


def near_kernel(rows, entries, all_q, k_ref, meta, *outs):
    page_scores(all_q, k_ref, meta, outs, entries, rows)


def partial_scores(new, k, cos_q, sin_q, meta, prompts, n_seq, n_tp):
    new_count = new.shape[2]
    tokens = k.shape[0]
    rows = new_count * GROUP
    count = KVH // n_tp * rows
    chunk = jax.ShapeDtypeStruct((count, tokens), BF16)
    params = dict(
        compiler_params=pltpu.CompilerParams(vmem_limit_bytes=24 * MIB),
        cost_estimate=pl.CostEstimate(
            flops=tokens * count * n_tp * HD, bytes_accessed=3 * MIB, transcendentals=0
        ),
    )
    far, near = list(range(n_tp // 2, n_tp)), list(range(n_tp // 2))
    all_q, *outs = pl.pallas_call(
        functools.partial(far_kernel, n_seq, n_tp, far),
        in_specs=[VMEM] * 4 + [SMEM],
        out_specs=[VMEM] * (1 + len(far)),
        out_shape=[pltpu.VMEM((prompts, count * n_tp, HD), BF16)] + [chunk] * len(far),
        name="far_scores",
        **params,
    )(new, k, cos_q, sin_q, meta)
    got = {d: pairs(out, "tp", d) for d, out in zip(far, outs)}
    outs = pl.pallas_call(
        functools.partial(near_kernel, rows, near),
        in_specs=[VMEM] * 2 + [SMEM],
        out_specs=[VMEM] * len(near),
        out_shape=[chunk] * len(near),
        name="near_scores",
        **params,
    )(all_q, k, meta)
    for d, out in zip(near, outs):
        got[d] = pairs(out, "tp", d) if d else out
    return all_q, [got[d] for d in range(n_tp)]


def fresh_kernel(n_seq, n_tp, new_ref, all_q, cos_q, sin_q, score_ref, value_ref):
    rows_local = score_ref.shape[1]
    _, own_rows, new_count, _, _ = new_ref.shape
    rows = new_count * GROUP
    kv_local = rows_local // rows
    heads = kv_local * GROUP
    scale = 1.0 / math.sqrt(HD)
    me = lax.axis_index("tp")
    own = pl.ds(pl.multiple_of(me * rows_local, rows_local), rows_local)
    step = lax.broadcasted_iota(jnp.int32, (rows_local, HD), 0) % rows // GROUP
    lane = lax.broadcasted_iota(jnp.int32, (rows_local, HD), 1)
    found = [jnp.full((rows_local, HD), NEG, F32) for _ in range(new_count)]
    for ds in range(n_seq):
        for rr in range(own_rows):
            request = ds * own_rows + rr
            q = all_q[request, own].astype(F32)
            for n in range(new_count):
                spot = slice(request * new_count + n, request * new_count + n + 1)
                cosine, sine = cos_q[spot], sin_q[spot]
                both = new_ref[ds * n_tp + me, rr, n].astype(F32)
                keys, values = [], []
                for g in range(kv_local):
                    k = both[heads + 2 * g : heads + 2 * g + 1]
                    k = k * cosine + pltpu.roll(k, HD // 2, 1) * sine
                    k = k.astype(BF16).astype(F32)
                    keys.append(jnp.broadcast_to(k, (rows, HD)))
                    v = both[heads + 2 * g + 1 : heads + 2 * g + 2]
                    values.append(jnp.broadcast_to(v, (rows, HD)))
                s = jnp.sum(q * jnp.concatenate(keys, axis=0), axis=1, keepdims=True) * scale
                found[n] = jnp.where((lane == request) & (step >= n), s, found[n])
                value_ref[request * new_count + n] = jnp.concatenate(values, axis=0)
    for n in range(new_count):
        score_ref[n] = found[n]


def fresh_scores(new, all_q, cos_q, sin_q, n_seq, n_tp):
    new_count = new.shape[2]
    prompts, rows, _ = all_q.shape
    rows = rows // n_tp
    return pl.pallas_call(
        functools.partial(fresh_kernel, n_seq, n_tp),
        in_specs=[VMEM] * 4,
        out_specs=[VMEM, VMEM],
        out_shape=[
            jax.ShapeDtypeStruct((new_count, rows, HD), F32),
            jax.ShapeDtypeStruct((prompts * new_count, rows, HD), F32),
        ],
        compiler_params=pltpu.CompilerParams(vmem_limit_bytes=16 * MIB),
        cost_estimate=pl.CostEstimate(flops=0, bytes_accessed=2 * MIB, transcendentals=0),
        name="fresh",
    )(new, all_q, cos_q, sin_q)


def weights_kernel(pages, prompts, n_tp, *refs):
    chunks = refs[:n_tp]
    meta, w_ref, stats_ref = refs[n_tp:]
    rows, tokens = w_ref.shape
    local_pages = tokens // PAGE
    first = lax.axis_index("seq") * local_pages
    lane = lax.broadcasted_iota(jnp.int32, (rows, PAGE), 1)
    scores, maxima, masks, owners = [], [], [], []
    for p in range(local_pages):
        at = slice(p * PAGE, (p + 1) * PAGE)
        total = chunks[0][:, at].astype(F32)
        for d in range(1, n_tp):
            total = total + chunks[d][:, at].astype(F32)
        mask = lane < meta[2 * pages + first + p]
        total = jnp.where(mask, total, NEG)
        masks.append(mask)
        scores.append(total)
        maxima.append(jnp.max(total, axis=1, keepdims=True))
        owners.append(meta[first + p])
    quarter = lane // prompts
    spot = lane % prompts
    stats = jnp.where(quarter == 0, NEG, 0.0)
    sums = []
    for p in range(local_pages):
        top = maxima[p]
        for other in range(local_pages):
            if other != p:
                top = jnp.where(owners[p] == owners[other], jnp.maximum(top, maxima[other]), top)
        high = top.astype(BF16).astype(F32)
        low = (top - high).astype(BF16).astype(F32)
        w = jnp.where(masks[p], jnp.exp(scores[p] - (high + low)), 0.0)
        w_ref[:, p * PAGE : (p + 1) * PAGE] = w.astype(BF16)
        here = spot == owners[p]
        stats = jnp.where(here & (quarter == 0), high, stats)
        stats = jnp.where(here & (quarter == 1), low, stats)
        part = jnp.sum(w, axis=1, keepdims=True)
        stats = stats + jnp.where(here & (quarter == 2), part, 0.0)
    high = stats.astype(BF16).astype(F32)
    low = pltpu.roll(stats - high, prompts, 1)
    stats_ref[...] = jnp.where(quarter == 3, low, stats).astype(BF16)


def softmax_weights(chunks, meta, pages, prompts):
    n_tp = len(chunks)
    rows, tokens = chunks[0].shape
    return pl.pallas_call(
        functools.partial(weights_kernel, pages, prompts, n_tp),
        in_specs=[VMEM] * n_tp + [SMEM],
        out_specs=[VMEM, VMEM],
        out_shape=[
            jax.ShapeDtypeStruct((rows, tokens), BF16),
            jax.ShapeDtypeStruct((rows, PAGE), BF16),
        ],
        compiler_params=pltpu.CompilerParams(vmem_limit_bytes=8 * MIB),
        name="weights",
    )(*chunks, meta)


def weighted_kernel(n_tp, entries, *refs):
    pieces = refs[: len(entries)]
    va_ref, vb_ref, meta = refs[len(entries) : len(entries) + 3]
    outs, total = refs[len(entries) + 3 : -1], refs[-1]
    rows_local, tokens_here = pieces[0].shape
    kv_local = KVH // n_tp
    rows = rows_local // kv_local
    local_pages = tokens_here // PAGE
    first = lax.axis_index("seq") * local_pages
    half = va_ref.shape[1] // HD
    me = lax.axis_index("tp")
    total[...] = jnp.zeros_like(total)
    for p in range(local_pages):
        request = meta[first + p]
        tokens = slice(p * PAGE, (p + 1) * PAGE)
        for i, (piece, d) in enumerate(zip(pieces, entries)):
            for g in range(kv_local):
                head = (me ^ d) * kv_local + g
                at = pl.ds(pl.multiple_of(head % half * HD, HD), HD)
                v = jnp.where(head < half, va_ref[tokens, at], vb_ref[tokens, at])
                to = slice((i * kv_local + g) * rows, (i * kv_local + g + 1) * rows)
                total[request, to] += jnp.dot(
                    piece[g * rows : (g + 1) * rows, tokens], v, preferred_element_type=F32
                )
    for i, out in enumerate(outs):
        out[...] = total[:, i * rows_local : (i + 1) * rows_local].astype(BF16)


def weighted_values(pieces, va, vb, meta, prompts):
    n_tp = len(pieces)
    rows, tokens = pieces[0].shape

    def call(entries):
        return pl.pallas_call(
            functools.partial(weighted_kernel, n_tp, entries),
            in_specs=[VMEM] * (len(entries) + 2) + [SMEM],
            out_specs=[VMEM] * len(entries),
            out_shape=[jax.ShapeDtypeStruct((prompts, rows, HD), BF16)] * len(entries),
            scratch_shapes=[pltpu.VMEM((prompts, rows * len(entries), HD), F32)],
            compiler_params=pltpu.CompilerParams(vmem_limit_bytes=24 * MIB),
            cost_estimate=pl.CostEstimate(
                flops=tokens * rows * n_tp * HD, bytes_accessed=4 * MIB, transcendentals=0
            ),
            name="weighted",
        )(*[pieces[d] for d in entries], va, vb, meta)

    got = {}
    far, near = list(range(n_tp // 2, n_tp)), list(range(n_tp // 2))
    for d, out in zip(far, call(far)):
        got[d] = pairs(out, "tp", d)
    for d, out in zip(near, call(near)):
        got[d] = pairs(out, "tp", d) if d else out
    return [got[d] for d in range(n_tp)]


def summed_kernel(n_tp, *refs):
    chunks = refs[:n_tp]
    stats_ref, out_ref = refs[n_tp:]
    prompts = chunks[0].shape[0]
    total = chunks[0][...].astype(F32)
    for d in range(1, n_tp):
        total = total + chunks[d][...].astype(F32)
    out_ref[:prompts] = total.astype(BF16)
    out_ref[prompts] = stats_ref[...]


def summed(chunks, stats):
    n_tp = len(chunks)
    prompts, rows, _ = chunks[0].shape
    return pl.pallas_call(
        functools.partial(summed_kernel, n_tp),
        in_specs=[VMEM] * (n_tp + 1),
        out_specs=VMEM,
        out_shape=jax.ShapeDtypeStruct((prompts + 1, rows, HD), BF16),
        compiler_params=pltpu.CompilerParams(vmem_limit_bytes=8 * MIB),
        cost_estimate=pl.CostEstimate(flops=0, bytes_accessed=4 * MIB, transcendentals=0),
        name="summed",
    )(*chunks, stats)


def output_kernel(n_seq, *refs):
    pieces = refs[:n_seq]
    fresh_ref, value_ref, wa_ref, wb_ref, out_ref, held = refs[n_seq:]
    more, rows_local, _ = pieces[0].shape
    prompts = more - 1
    new_count = fresh_ref.shape[0]
    rows = new_count * GROUP
    kv_local = rows_local // rows
    heads = kv_local * GROUP
    tops, parts = [], []
    for s in range(n_seq):
        stats = pieces[s][prompts].astype(F32)
        folded = stats + pltpu.roll(stats, HD - prompts, 1)
        tops.append(folded)
        parts.append(pltpu.roll(folded, HD - 2 * prompts, 1))
    fresh = [fresh_ref[n] for n in range(new_count)]
    top = fresh[0]
    for other in fresh[1:] + tops:
        top = jnp.maximum(top, other)
    weights = [jnp.exp(f - top) for f in fresh]
    factors = [jnp.exp(t - top) for t in tops]
    total = weights[0]
    for w in weights[1:]:
        total = total + w
    for f, part in zip(factors, parts):
        total = total + f * part
    weights = [w / total for w in weights]
    factors = [f / total for f in factors]
    for r in range(prompts):
        sums = jnp.zeros((rows_local, HD), F32)
        for s in range(n_seq):
            sums = sums + factors[s][:, r : r + 1] * pieces[s][r].astype(F32)
        for n in range(new_count):
            sums = sums + weights[n][:, r : r + 1] * value_ref[r * new_count + n]
        for g in range(kv_local):
            for n in range(new_count):
                at = g * rows + n * GROUP
                held[g * GROUP : (g + 1) * GROUP, r * new_count + n] = sums[at : at + GROUP]
    half = heads // 2
    product = jnp.zeros(out_ref.shape, F32)
    for w_ref, at in ((wa_ref, 0), (wb_ref, half)):
        left = [held[h].astype(BF16) for h in range(at, at + half)]
        left = jnp.concatenate(left, axis=1)
        product = product + jnp.dot(left, w_ref[...], preferred_element_type=F32)
    out_ref[...] = product.astype(BF16)


def output_partial(pieces, fresh, values, weights):
    n_seq = len(pieces)
    new_count = fresh.shape[0]
    prompts = pieces[0].shape[0] - 1
    depth, columns = weights[0].shape
    return pl.pallas_call(
        functools.partial(output_kernel, n_seq),
        in_specs=[VMEM] * (n_seq + 4),
        out_specs=VMEM,
        out_shape=jax.ShapeDtypeStruct((prompts * new_count, columns), BF16),
        scratch_shapes=[pltpu.VMEM((2 * depth // HD, prompts * new_count, HD), F32)],
        compiler_params=pltpu.CompilerParams(vmem_limit_bytes=24 * MIB),
        name="output",
    )(*pieces, fresh, values, *weights)


def final_kernel(n_tp, *refs):
    pieces = refs[:n_tp]
    res_ref, out_ref = refs[n_tp:]
    prompts, new_count, _ = out_ref.shape
    total = pieces[0][...].astype(F32)
    for d in range(1, n_tp):
        total = total + pieces[d][...].astype(F32)
    for r in range(prompts):
        out_ref[r] = res_ref[r].astype(F32) + total[r * new_count : (r + 1) * new_count]


def final_sum(pieces, residual):
    n_tp = len(pieces)
    return pl.pallas_call(
        functools.partial(final_kernel, n_tp),
        in_specs=[VMEM] * (n_tp + 1),
        out_specs=VMEM,
        out_shape=jax.ShapeDtypeStruct(residual.shape, F32),
        compiler_params=pltpu.CompilerParams(vmem_limit_bytes=8 * MIB),
        name="final",
    )(*pieces, residual)


def on_device(
    prefill_states, kv_weight, page_counts, tail_tokens, new_query, new_keyval, residual, out_weight
):
    n_seq, n_tp = lax.axis_size("seq"), lax.axis_size("tp")
    own_rows, new_count, _ = new_query.shape
    prompts = page_counts.shape[0]
    pages = prefill_states.shape[0] // PAGE * n_seq
    x, w = own_copy(prefill_states, "tp"), own_copy(kv_weight, "tp")
    new = prepare(new_query, new_keyval, n_seq * n_tp)
    new = lax.all_to_all(new, ("seq", "tp"), 0, 0)
    k, cos_q, sin_q, meta = project_keys(x, w, page_counts, tail_tokens, pages, new_count)
    all_q, scores = partial_scores(new, k, cos_q, sin_q, meta, prompts, n_seq, n_tp)
    va, oa = project_values(x, w, out_weight, 0, all_q)
    fresh, values = fresh_scores(new, all_q, cos_q, sin_q, n_seq, n_tp)
    weights, stats = softmax_weights(scores, meta, pages, prompts)
    vb, ob = project_values(x, w, out_weight, 1, stats)
    chunks = weighted_values(gather(weights, "tp"), va, vb, meta, prompts)
    pieces = gather(summed(chunks, stats), "seq")
    partial = output_partial(pieces, fresh, values, (oa, ob))
    return final_sum(gather(partial, "tp"), residual)


def solution(mesh):
    placed = (
        P(("groups", "seq"), "tp"),
        P("tp", None),
        P("groups"),
        P("groups"),
        P(("groups", "seq"), None, "tp"),
        P(("groups", "seq"), None, "tp"),
        P("groups", None, "seq"),
        P("tp", "seq"),
    )
    return jax.shard_map(
        on_device, mesh=mesh, in_specs=placed, out_specs=P("groups", None, "seq"), check_vma=False
    )
```

```python
import functools
import math

import jax
import jax.numpy as jnp
from jax import lax
from jax.experimental import pallas as pl
from jax.experimental.pallas import tpu as pltpu
from jax.sharding import PartitionSpec as P

QH = 64
KVH = 8
HD = 128
PAGE = 128
GROUP = QH // KVH
NEG = -1e30
F32 = jnp.float32
BF16 = jnp.bfloat16
MIB = 1 << 20

VMEM = pl.BlockSpec(memory_space=pltpu.VMEM)
SMEM = pl.BlockSpec(memory_space=pltpu.SMEM)
ANY = pl.BlockSpec(memory_space=pl.ANY)


def partner(me, entry, size):
    return me ^ ((size - entry) % size)


def pairs(value, axis, entry):
    size = lax.axis_size(axis)
    return lax.ppermute(value, axis, [(i, partner(i, entry, size)) for i in range(size)])


def exchange(chunks, axis):
    return [chunks[0]] + [pairs(chunks[i], axis, i) for i in range(1, len(chunks))]


def gather(value, axis):
    return exchange([value] * lax.axis_size(axis), axis)


def lane_freqs(rows):
    lane = lax.broadcasted_iota(jnp.int32, (rows, HD), 1) % (HD // 2)
    return jnp.exp(-(lane.astype(F32) * (2.0 / HD)) * math.log(500000.0))


def sine_sign(rows):
    lane = lax.broadcasted_iota(jnp.int32, (rows, HD), 1)
    return jnp.where(lane < HD // 2, -1.0, 1.0)


def in_hbm(value):
    return pltpu.with_memory_space_constraint(value, pltpu.HBM)


def by_row(rows, numbers):
    row = lax.broadcasted_iota(jnp.int32, (rows, HD), 0)
    out = jnp.zeros((rows, HD), F32)
    for i, number in enumerate(numbers):
        out = jnp.where(row == i, number.astype(F32), out)
    return out


def page_table(pages, prompts, counts, tails, meta):
    def one_prompt(r, start):
        length = (counts[r] - 1) * PAGE + tails[r]
        meta[3 * pages + r] = length

        def one_page(i, carry):
            meta[start + i] = r
            meta[pages + start + i] = i * PAGE
            meta[2 * pages + start + i] = jnp.minimum(length - i * PAGE, PAGE)
            return carry

        lax.fori_loop(0, counts[r], one_page, 0)
        return start + counts[r]

    lax.fori_loop(0, prompts, one_prompt, 0)


def rotation_tables(pages, local_pages, meta, cos_s, sin_s):
    freqs = lane_freqs(8)
    low = lax.broadcasted_iota(jnp.int32, (8, HD), 0).astype(F32) * freqs
    low_cos, low_sin = jnp.cos(low), jnp.sin(low)
    high = lax.broadcasted_iota(jnp.int32, (PAGE // 8, HD), 0).astype(F32) * 8.0
    high = high * lane_freqs(PAGE // 8)
    high_cos, high_sin = jnp.cos(high), jnp.sin(high)
    first = lax.axis_index("seq") * local_pages
    base = by_row(local_pages, [meta[pages + first + p] for p in range(local_pages)])
    base = base * lane_freqs(local_pages)
    base_cos, base_sin = jnp.cos(base), jnp.sin(base)
    sign = sine_sign(8)
    for i in range(PAGE // 8):
        c, s = high_cos[i : i + 1], high_sin[i : i + 1]
        cosine, sine = low_cos * c - low_sin * s, low_sin * c + low_cos * s
        for p in range(local_pages):
            at = slice(p * PAGE + i * 8, p * PAGE + i * 8 + 8)
            c, s = base_cos[p : p + 1], base_sin[p : p + 1]
            cos_s[at] = cosine * c - sine * s
            sin_s[at] = sign * (sine * c + cosine * s)


def pair_columns(w_ref, rows, pair, part):
    at = [(2 * head + part) * HD for head in (2 * pair, 2 * pair + 1)]
    return jnp.concatenate([w_ref[rows, c : c + HD] for c in at], axis=1)


PARTS = 4


def load_kernel(pages, prompts, new_count, x_hbm, w_hbm, counts, tails, *refs):
    acc, x_ref, w_ref, cos_ref, sin_ref, cos_q, sin_q, meta, x_sems, w_sems = refs
    tokens, depth = x_ref.shape
    size, tall = depth // PARTS, tokens // 2
    copies = []
    for i in range(PARTS):
        at = pl.ds(i * size, size)
        x_copy = pltpu.make_async_copy(x_hbm.at[:, at], x_ref.at[:, at], x_sems.at[i])
        w_copy = pltpu.make_async_copy(w_hbm.at[at], w_ref.at[at], w_sems.at[i])
        x_copy.start()
        w_copy.start()
        copies.append((x_copy, w_copy))
    page_table(pages, prompts, counts, tails, meta)
    rotation_tables(pages, tokens // PAGE, meta, cos_ref, sin_ref)
    spots = [meta[3 * pages + r] + n for r in range(prompts) for n in range(new_count)]
    angles = by_row(len(spots), spots) * lane_freqs(len(spots))
    cos_q[...] = jnp.cos(angles)
    sin_q[...] = jnp.sin(angles) * sine_sign(len(spots))
    for i in range(PARTS - 1):
        for copy in copies[i]:
            copy.wait()
        rows = slice(i * size, (i + 1) * size)
        for pair in range(KVH // 2):
            weight = pair_columns(w_ref, rows, pair, 0)
            columns = slice(2 * pair * HD, 2 * (pair + 1) * HD)
            for start in range(0, tokens, tall):
                at = slice(start, start + tall)
                product = jnp.dot(x_ref[at, rows], weight, preferred_element_type=F32)
                acc[at, columns] = product if i == 0 else acc[at, columns] + product
    for copy in copies[-1]:
        copy.wait()


def load(x, kv_weight, counts, tails, pages, new_count):
    tokens, depth = x.shape
    columns = kv_weight.shape[1]
    prompts = counts.shape[0]
    hbm = pl.BlockSpec(memory_space=pltpu.HBM)
    return pl.pallas_call(
        functools.partial(load_kernel, pages, prompts, new_count),
        in_specs=[hbm, hbm, SMEM, SMEM],
        out_specs=[VMEM] * 7 + [SMEM],
        out_shape=[
            pltpu.VMEM((tokens, KVH * HD), F32),
            pltpu.VMEM((tokens, depth), BF16),
            pltpu.VMEM((depth, columns), BF16),
            pltpu.VMEM((tokens, HD), F32),
            pltpu.VMEM((tokens, HD), F32),
            pltpu.VMEM((prompts * new_count, HD), F32),
            pltpu.VMEM((prompts * new_count, HD), F32),
            jax.ShapeDtypeStruct((3 * pages + prompts,), jnp.int32),
        ],
        scratch_shapes=[pltpu.SemaphoreType.DMA((PARTS,)), pltpu.SemaphoreType.DMA((PARTS,))],
        compiler_params=pltpu.CompilerParams(vmem_limit_bytes=28 * MIB),
        cost_estimate=pl.CostEstimate(
            flops=3 * tokens * depth // 2 * KVH * HD,
            bytes_accessed=2 * depth * (tokens + columns),
            transcendentals=0,
        ),
        name="load",
    )(*[in_hbm(a) for a in (x, kv_weight, counts, tails)])


def keys_kernel(acc, x_ref, w_ref, cos_ref, sin_ref, after, k_ref):
    tokens, depth = x_ref.shape
    tall = tokens // 2
    rows = slice(depth - depth // PARTS, depth)
    for pair in range(KVH // 2):
        weight = pair_columns(w_ref, rows, pair, 0)
        columns = slice(2 * pair * HD, 2 * (pair + 1) * HD)
        for start in range(0, tokens, tall):
            at = slice(start, start + tall)
            product = acc[at, columns] + jnp.dot(
                x_ref[at, rows], weight, preferred_element_type=F32
            )
            cosine, sine = cos_ref[at], sin_ref[at]
            for h in range(2):
                k = product[:, h * HD : (h + 1) * HD]
                k = k * cosine + pltpu.roll(k, HD // 2, 1) * sine
                k_ref[at, (2 * pair + h) * HD : (2 * pair + h + 1) * HD] = k.astype(BF16)


def rotated_keys(acc, x, weight, cosine, sine, after):
    tokens, depth = x.shape
    return pl.pallas_call(
        keys_kernel,
        in_specs=[VMEM] * 5 + [ANY],
        out_specs=VMEM,
        out_shape=pltpu.VMEM((tokens, KVH * HD), BF16),
        compiler_params=pltpu.CompilerParams(vmem_limit_bytes=24 * MIB),
        cost_estimate=pl.CostEstimate(
            flops=tokens * depth // 2 * KVH * HD, bytes_accessed=8 * MIB, transcendentals=0
        ),
        name="keys",
    )(acc, x, weight, cosine, sine, after)


def values_kernel(first, x_ref, w_ref, o_hbm, after, v_ref, o_ref, sem):
    depth = o_ref.shape[0]
    copy = pltpu.make_async_copy(o_hbm.at[pl.ds(first * depth, depth)], o_ref, sem)
    copy.start()
    tokens, columns = v_ref.shape
    tall = tokens // 2
    pairs_here = columns // (2 * HD)
    for pair in range(pairs_here):
        weight = pair_columns(w_ref, slice(None), first * pairs_here + pair, 1)
        for i in range(2):
            at = slice(i * tall, (i + 1) * tall)
            v_ref[at, 2 * pair * HD : 2 * (pair + 1) * HD] = jnp.dot(
                x_ref[at], weight, preferred_element_type=F32
            ).astype(BF16)
    copy.wait()


def project_values(x, weight, out_weight, first, after):
    tokens, depth = x.shape
    columns = KVH // 2 * HD
    rows = out_weight.shape[0] // 2
    return pl.pallas_call(
        functools.partial(values_kernel, first),
        in_specs=[
            VMEM,
            VMEM,
            pl.BlockSpec(memory_space=pltpu.HBM),
            ANY,
        ],
        out_specs=[VMEM, VMEM],
        out_shape=[
            pltpu.VMEM((tokens, columns), BF16),
            pltpu.VMEM((rows, out_weight.shape[1]), BF16),
        ],
        scratch_shapes=[pltpu.SemaphoreType.DMA],
        compiler_params=pltpu.CompilerParams(vmem_limit_bytes=24 * MIB),
        cost_estimate=pl.CostEstimate(
            flops=2 * tokens * depth * columns, bytes_accessed=8 * MIB, transcendentals=0
        ),
        name="values",
    )(x, weight, in_hbm(out_weight), after)


def prepare_kernel(q_ref, kv_ref, out_ref):
    own_rows, new_count, _, _ = out_ref.shape
    for r in range(own_rows):
        q, kv = q_ref[r].astype(F32), kv_ref[r].astype(F32)
        for n in range(new_count):
            parts = [a[n : n + 1, c : c + HD] for a in (q, kv) for c in range(0, a.shape[1], HD)]
            out_ref[r, n] = jnp.concatenate(parts, axis=0).astype(BF16)


def prepare(new_query, new_keyval):
    own_rows, new_count, columns = new_query.shape
    heads = (columns + new_keyval.shape[2]) // HD
    return pl.pallas_call(
        prepare_kernel,
        in_specs=[VMEM, VMEM],
        out_specs=VMEM,
        out_shape=jax.ShapeDtypeStruct((own_rows, new_count, heads, HD), BF16),
        compiler_params=pltpu.CompilerParams(vmem_limit_bytes=8 * MIB),
        cost_estimate=pl.CostEstimate(flops=0, bytes_accessed=MIB, transcendentals=0),
        name="prepare",
    )(in_hbm(new_query), in_hbm(new_keyval))


def stacked_kernel(n_tp, *refs):
    for d in range(n_tp):
        refs[-1][d] = refs[d][...]


def stacked(pieces, after):
    n_tp = len(pieces)
    return pl.pallas_call(
        functools.partial(stacked_kernel, n_tp),
        in_specs=[VMEM] * n_tp + [ANY],
        out_specs=VMEM,
        out_shape=jax.ShapeDtypeStruct((n_tp,) + pieces[0].shape, BF16),
        compiler_params=pltpu.CompilerParams(vmem_limit_bytes=8 * MIB),
        name="stacked",
    )(*pieces, after)


def scores_kernel(n_seq, n_tp, *refs):
    new = refs[:n_seq]
    k_ref, cos_q, sin_q, meta = refs[n_seq : n_seq + 4]
    outs = refs[n_seq + 5 : n_seq + 5 + n_tp]
    own_q, all_q, ready = refs[n_seq + 5 + n_tp :]
    kv_local = KVH // n_tp
    local_pages = k_ref.shape[0] // PAGE
    _, own_rows, new_count, _, _ = new[0].shape
    rows = new_count * GROUP
    count = kv_local * rows
    scale = 1.0 / math.sqrt(HD)
    me = lax.axis_index("tp")
    seq = lax.axis_index("seq")
    first = seq * local_pages
    for ds in range(n_seq):
        for rr in range(own_rows):
            request = partner(seq, ds, n_seq) * own_rows + rr
            spots = [pl.ds(request * new_count + n, 1) for n in range(new_count)]
            turn = [(cos_q[spot], sin_q[spot]) for spot in spots]
            for dt in range(n_tp):
                block = [new[ds][dt, rr, n].astype(F32) for n in range(new_count)]
                for g in range(kv_local):
                    parts = []
                    for n in range(new_count):
                        q = block[n][g * GROUP : (g + 1) * GROUP]
                        parts.append(q * turn[n][0] + pltpu.roll(q, HD // 2, 1) * turn[n][1])
                    part = jnp.concatenate(parts, axis=0).astype(BF16)
                    at = (partner(me, dt, n_tp) * kv_local + g) * rows
                    all_q[request, pl.ds(pl.multiple_of(at, rows), rows)] = part
                    if dt == 0:
                        own_q[request, g * rows : (g + 1) * rows] = part
    for p in range(local_pages):
        request = meta[first + p]
        tokens = slice(p * PAGE, (p + 1) * PAGE)
        for head in range(KVH):
            k = k_ref[tokens, head * HD : (head + 1) * HD]
            q = all_q[request, head * rows : (head + 1) * rows]
            s = lax.dot_general(q, k, (((1,), (1,)), ((), ())), preferred_element_type=F32)
            ready[head * rows : (head + 1) * rows, tokens] = (s * scale).astype(BF16)
    for d in range(n_tp):
        outs[d][...] = ready[pl.ds(pl.multiple_of(partner(me, d, n_tp) * count, count), count)]


def partial_scores(new, k, cos_q, sin_q, meta, after, prompts, n_tp):
    n_seq = len(new)
    new_count = new[0].shape[2]
    tokens = k.shape[0]
    rows = KVH // n_tp * new_count * GROUP
    return pl.pallas_call(
        functools.partial(scores_kernel, n_seq, n_tp),
        in_specs=[VMEM] * (n_seq + 3) + [SMEM, ANY],
        out_specs=[VMEM] * (n_tp + 1),
        out_shape=[jax.ShapeDtypeStruct((rows, tokens), BF16)] * n_tp
        + [jax.ShapeDtypeStruct((prompts, rows, HD), BF16)],
        scratch_shapes=[
            pltpu.VMEM((prompts, rows * n_tp, HD), BF16),
            pltpu.VMEM((rows * n_tp, tokens), BF16),
        ],
        compiler_params=pltpu.CompilerParams(vmem_limit_bytes=24 * MIB),
        cost_estimate=pl.CostEstimate(
            flops=2 * tokens * rows * n_tp * HD, bytes_accessed=6 * MIB, transcendentals=0
        ),
        name="scores",
    )(*new, k, cos_q, sin_q, meta, after)


def fresh_kernel(n_seq, *refs):
    new = refs[:n_seq]
    q_ref, cos_q, sin_q, score_ref, value_ref = refs[n_seq:]
    prompts, rows_local, _ = q_ref.shape
    _, own_rows, new_count, _, _ = new[0].shape
    rows = new_count * GROUP
    kv_local = rows_local // rows
    heads = kv_local * GROUP
    scale = 1.0 / math.sqrt(HD)
    seq = lax.axis_index("seq")
    step = lax.broadcasted_iota(jnp.int32, (rows_local, HD), 0) % rows // GROUP
    lane = lax.broadcasted_iota(jnp.int32, (rows_local, HD), 1)
    found = [jnp.full((rows_local, HD), NEG, F32) for _ in range(new_count)]
    for ds in range(n_seq):
        for rr in range(own_rows):
            request = partner(seq, ds, n_seq) * own_rows + rr
            q = q_ref[request].astype(F32)
            for n in range(new_count):
                spot = pl.ds(request * new_count + n, 1)
                cosine, sine = cos_q[spot], sin_q[spot]
                both = new[ds][0, rr, n].astype(F32)
                keys, values = [], []
                for g in range(kv_local):
                    k = both[heads + 2 * g : heads + 2 * g + 1]
                    k = k * cosine + pltpu.roll(k, HD // 2, 1) * sine
                    k = k.astype(BF16).astype(F32)
                    keys.append(jnp.broadcast_to(k, (rows, HD)))
                    v = both[heads + 2 * g + 1 : heads + 2 * g + 2]
                    values.append(jnp.broadcast_to(v, (rows, HD)))
                s = jnp.sum(q * jnp.concatenate(keys, axis=0), axis=1, keepdims=True) * scale
                found[n] = jnp.where((lane == request) & (step >= n), s, found[n])
                value_ref[request * new_count + n] = jnp.concatenate(values, axis=0)
    for n in range(new_count):
        score_ref[n] = found[n]


def fresh_scores(new, own_q, cos_q, sin_q):
    n_seq = len(new)
    new_count = new[0].shape[2]
    prompts, rows, _ = own_q.shape
    return pl.pallas_call(
        functools.partial(fresh_kernel, n_seq),
        in_specs=[VMEM] * (n_seq + 3),
        out_specs=[VMEM, VMEM],
        out_shape=[
            jax.ShapeDtypeStruct((new_count, rows, HD), F32),
            jax.ShapeDtypeStruct((prompts * new_count, rows, HD), F32),
        ],
        compiler_params=pltpu.CompilerParams(vmem_limit_bytes=16 * MIB),
        cost_estimate=pl.CostEstimate(flops=0, bytes_accessed=2 * MIB, transcendentals=0),
        name="fresh",
    )(*new, own_q, cos_q, sin_q)


def weights_kernel(pages, prompts, n_tp, *refs):
    chunks = refs[:n_tp]
    meta, _, w_ref, stats_ref = refs[n_tp:]
    rows, tokens = w_ref.shape
    local_pages = tokens // PAGE
    first = lax.axis_index("seq") * local_pages
    lane = lax.broadcasted_iota(jnp.int32, (rows, PAGE), 1)
    scores, maxima, masks, owners = [], [], [], []
    for p in range(local_pages):
        at = slice(p * PAGE, (p + 1) * PAGE)
        total = chunks[0][:, at].astype(F32)
        for d in range(1, n_tp):
            total = total + chunks[d][:, at].astype(F32)
        mask = lane < meta[2 * pages + first + p]
        total = jnp.where(mask, total, NEG)
        masks.append(mask)
        scores.append(total)
        maxima.append(jnp.max(total, axis=1, keepdims=True))
        owners.append(meta[first + p])
    quarter = lane // prompts
    spot = lane % prompts
    stats = jnp.where(quarter == 0, NEG, 0.0)
    sums = []
    for p in range(local_pages):
        top = maxima[p]
        for other in range(local_pages):
            if other != p:
                top = jnp.where(owners[p] == owners[other], jnp.maximum(top, maxima[other]), top)
        high = top.astype(BF16).astype(F32)
        low = (top - high).astype(BF16).astype(F32)
        w = jnp.where(masks[p], jnp.exp(scores[p] - (high + low)), 0.0)
        w_ref[:, p * PAGE : (p + 1) * PAGE] = w.astype(BF16)
        here = spot == owners[p]
        stats = jnp.where(here & (quarter == 0), high, stats)
        stats = jnp.where(here & (quarter == 1), low, stats)
        part = jnp.sum(w, axis=1, keepdims=True)
        stats = stats + jnp.where(here & (quarter == 2), part, 0.0)
    high = stats.astype(BF16).astype(F32)
    low = pltpu.roll(stats - high, prompts, 1)
    stats_ref[...] = jnp.where(quarter == 3, low, stats).astype(BF16)


def softmax_weights(chunks, meta, after, pages, prompts):
    n_tp = len(chunks)
    rows, tokens = chunks[0].shape
    return pl.pallas_call(
        functools.partial(weights_kernel, pages, prompts, n_tp),
        in_specs=[VMEM] * n_tp + [SMEM, ANY],
        out_specs=[VMEM, VMEM],
        out_shape=[
            jax.ShapeDtypeStruct((rows, tokens), BF16),
            jax.ShapeDtypeStruct((rows, PAGE), BF16),
        ],
        compiler_params=pltpu.CompilerParams(vmem_limit_bytes=8 * MIB),
        name="weights",
    )(*chunks, meta, after)


def weighted_kernel(n_tp, *refs):
    pieces = refs[:n_tp]
    va_ref, vb_ref, meta = refs[n_tp : n_tp + 3]
    outs = refs[n_tp + 3 : n_tp + 3 + n_tp]
    ready, total = refs[n_tp + 3 + n_tp :]
    rows_local, tokens_here = pieces[0].shape
    kv_local = KVH // n_tp
    rows = rows_local // kv_local
    local_pages = tokens_here // PAGE
    first = lax.axis_index("seq") * local_pages
    me = lax.axis_index("tp")
    own = [pl.ds(pl.multiple_of(partner(me, d, n_tp) * rows_local, rows_local), rows_local) for d in range(n_tp)]
    for d in range(n_tp):
        ready[own[d]] = pieces[d][...]
    total[...] = jnp.zeros_like(total)
    half = va_ref.shape[1] // HD
    for p in range(local_pages):
        request = meta[first + p]
        tokens = slice(p * PAGE, (p + 1) * PAGE)
        for head in range(KVH):
            v_ref = va_ref if head < half else vb_ref
            v = v_ref[tokens, head % half * HD : (head % half + 1) * HD]
            at = slice(head * rows, (head + 1) * rows)
            total[request, at] += jnp.dot(ready[at, tokens], v, preferred_element_type=F32)
    for d in range(n_tp):
        outs[d][...] = total[:, own[d]].astype(BF16)


def weighted_values(pieces, va, vb, meta, prompts):
    n_tp = len(pieces)
    rows, tokens = pieces[0].shape
    return pl.pallas_call(
        functools.partial(weighted_kernel, n_tp),
        in_specs=[VMEM] * (n_tp + 2) + [SMEM],
        out_specs=[VMEM] * n_tp,
        out_shape=[jax.ShapeDtypeStruct((prompts, rows, HD), BF16)] * n_tp,
        scratch_shapes=[
            pltpu.VMEM((rows * n_tp, tokens), BF16),
            pltpu.VMEM((prompts, rows * n_tp, HD), F32),
        ],
        compiler_params=pltpu.CompilerParams(vmem_limit_bytes=24 * MIB),
        cost_estimate=pl.CostEstimate(
            flops=2 * tokens * rows * n_tp * HD, bytes_accessed=8 * MIB, transcendentals=0
        ),
        name="weighted",
    )(*pieces, va, vb, meta)


def summed_kernel(n_tp, *refs):
    chunks = refs[:n_tp]
    stats_ref, out_ref = refs[n_tp:]
    prompts = chunks[0].shape[0]
    total = chunks[0][...].astype(F32)
    for d in range(1, n_tp):
        total = total + chunks[d][...].astype(F32)
    out_ref[:prompts] = total.astype(BF16)
    out_ref[prompts] = stats_ref[...]


def summed(chunks, stats):
    n_tp = len(chunks)
    prompts, rows, _ = chunks[0].shape
    return pl.pallas_call(
        functools.partial(summed_kernel, n_tp),
        in_specs=[VMEM] * (n_tp + 1),
        out_specs=VMEM,
        out_shape=jax.ShapeDtypeStruct((prompts + 1, rows, HD), BF16),
        compiler_params=pltpu.CompilerParams(vmem_limit_bytes=8 * MIB),
        cost_estimate=pl.CostEstimate(flops=0, bytes_accessed=4 * MIB, transcendentals=0),
        name="summed",
    )(*chunks, stats)


def output_kernel(n_seq, *refs):
    pieces = refs[:n_seq]
    fresh_ref, value_ref, wa_ref, wb_ref, out_ref, held = refs[n_seq:]
    more, rows_local, _ = pieces[0].shape
    prompts = more - 1
    new_count = fresh_ref.shape[0]
    rows = new_count * GROUP
    kv_local = rows_local // rows
    heads = kv_local * GROUP
    tops, parts = [], []
    for s in range(n_seq):
        stats = pieces[s][prompts].astype(F32)
        folded = stats + pltpu.roll(stats, HD - prompts, 1)
        tops.append(folded)
        parts.append(pltpu.roll(folded, HD - 2 * prompts, 1))
    fresh = [fresh_ref[n] for n in range(new_count)]
    top = fresh[0]
    for other in fresh[1:] + tops:
        top = jnp.maximum(top, other)
    weights = [jnp.exp(f - top) for f in fresh]
    factors = [jnp.exp(t - top) for t in tops]
    total = weights[0]
    for w in weights[1:]:
        total = total + w
    for f, part in zip(factors, parts):
        total = total + f * part
    weights = [w / total for w in weights]
    factors = [f / total for f in factors]
    for r in range(prompts):
        sums = jnp.zeros((rows_local, HD), F32)
        for s in range(n_seq):
            sums = sums + factors[s][:, r : r + 1] * pieces[s][r].astype(F32)
        for n in range(new_count):
            sums = sums + weights[n][:, r : r + 1] * value_ref[r * new_count + n]
        for g in range(kv_local):
            for n in range(new_count):
                at = g * rows + n * GROUP
                held[g * GROUP : (g + 1) * GROUP, r * new_count + n] = sums[at : at + GROUP]
    half = heads // 2
    product = jnp.zeros(out_ref.shape, F32)
    for w_ref, at in ((wa_ref, 0), (wb_ref, half)):
        left = [held[h].astype(BF16) for h in range(at, at + half)]
        left = jnp.concatenate(left, axis=1)
        product = product + jnp.dot(left, w_ref[...], preferred_element_type=F32)
    out_ref[...] = product.astype(BF16)


def output_partial(pieces, fresh, values, weights):
    n_seq = len(pieces)
    new_count = fresh.shape[0]
    prompts = pieces[0].shape[0] - 1
    depth, columns = weights[0].shape
    return pl.pallas_call(
        functools.partial(output_kernel, n_seq),
        in_specs=[VMEM] * (n_seq + 4),
        out_specs=VMEM,
        out_shape=jax.ShapeDtypeStruct((prompts * new_count, columns), BF16),
        scratch_shapes=[pltpu.VMEM((2 * depth // HD, prompts * new_count, HD), F32)],
        compiler_params=pltpu.CompilerParams(vmem_limit_bytes=24 * MIB),
        name="output",
    )(*pieces, fresh, values, *weights)


def final_kernel(n_tp, *refs):
    pieces = refs[:n_tp]
    res_ref, out_ref = refs[n_tp:]
    prompts, new_count, _ = out_ref.shape
    total = pieces[0][...].astype(F32)
    for d in range(1, n_tp):
        total = total + pieces[d][...].astype(F32)
    for r in range(prompts):
        out_ref[r] = res_ref[r].astype(F32) + total[r * new_count : (r + 1) * new_count]


def final_sum(pieces, residual):
    n_tp = len(pieces)
    return pl.pallas_call(
        functools.partial(final_kernel, n_tp),
        in_specs=[VMEM] * (n_tp + 1),
        out_specs=VMEM,
        out_shape=jax.ShapeDtypeStruct(residual.shape, F32),
        compiler_params=pltpu.CompilerParams(vmem_limit_bytes=8 * MIB),
        name="final",
    )(*pieces, residual)


def on_device(
    prefill_states, kv_weight, page_counts, tail_tokens, new_query, new_keyval, residual, out_weight
):
    n_seq, n_tp = lax.axis_size("seq"), lax.axis_size("tp")
    own_rows, new_count, _ = new_query.shape
    prompts = page_counts.shape[0]
    pages = prefill_states.shape[0] // PAGE * n_seq
    new = gather(prepare(new_query, new_keyval), "tp")
    acc, x, w, cosine, sine, cos_q, sin_q, meta = load(
        prefill_states, kv_weight, page_counts, tail_tokens, pages, new_count
    )
    new = stacked(new, meta)
    k = rotated_keys(acc, x, w, cosine, sine, new)
    va, oa = project_values(x, w, out_weight, 0, new)
    new = gather(new, "seq")
    *scores, own_q = partial_scores(new, k, cos_q, sin_q, meta, va, prompts, n_tp)
    vb, ob = project_values(x, w, out_weight, 1, own_q)
    fresh, values = fresh_scores(new, own_q, cos_q, sin_q)
    weights, stats = softmax_weights(exchange(scores, "tp"), meta, vb, pages, prompts)
    chunks = weighted_values(gather(weights, "tp"), va, vb, meta, prompts)
    pieces = gather(summed(exchange(chunks, "tp"), stats), "seq")
    partial = output_partial(pieces, fresh, values, (oa, ob))
    return final_sum(gather(partial, "tp"), residual)


def solution(mesh):
    placed = (
        P(("groups", "seq"), "tp"),
        P("tp", None),
        P("groups"),
        P("groups"),
        P(("groups", "seq"), None, "tp"),
        P(("groups", "seq"), None, "tp"),
        P("groups", None, "seq"),
        P("tp", "seq"),
    )
    return jax.shard_map(
        on_device, mesh=mesh, in_specs=placed, out_specs=P("groups", None, "seq"), check_vma=False
    )
```

```python
import functools
import math

import jax
import jax.numpy as jnp
from jax import lax
from jax.experimental import pallas as pl
from jax.experimental.pallas import tpu as pltpu
from jax.sharding import PartitionSpec as P

QH = 64
KVH = 8
HD = 128
PAGE = 128
GROUP = QH // KVH
NEG = -1e30
F32 = jnp.float32
BF16 = jnp.bfloat16
MIB = 1 << 20

VMEM = pl.BlockSpec(memory_space=pltpu.VMEM)
SMEM = pl.BlockSpec(memory_space=pltpu.SMEM)
ANY = pl.BlockSpec(memory_space=pl.ANY)


def partner(me, entry, size):
    return me ^ ((size - entry) % size)


def pairs(value, axis, entry):
    size = lax.axis_size(axis)
    return lax.ppermute(value, axis, [(i, partner(i, entry, size)) for i in range(size)])


def exchange(chunks, axis):
    return [chunks[0]] + [pairs(chunks[i], axis, i) for i in range(1, len(chunks))]


def gather(value, axis):
    return exchange([value] * lax.axis_size(axis), axis)


def gather_by_index(value, axis):
    size = lax.axis_size(axis)
    return [value] + [pairs(value, axis, size - d) for d in range(1, size)]


def lane_freqs(rows):
    lane = lax.broadcasted_iota(jnp.int32, (rows, HD), 1) % (HD // 2)
    return jnp.exp(-(lane.astype(F32) * (2.0 / HD)) * math.log(500000.0))


def sine_sign(rows):
    lane = lax.broadcasted_iota(jnp.int32, (rows, HD), 1)
    return jnp.where(lane < HD // 2, -1.0, 1.0)


def in_hbm(value):
    return pltpu.with_memory_space_constraint(value, pltpu.HBM)


def by_row(rows, numbers):
    row = lax.broadcasted_iota(jnp.int32, (rows, HD), 0)
    out = jnp.zeros((rows, HD), F32)
    for i, number in enumerate(numbers):
        out = jnp.where(row == i, number.astype(F32), out)
    return out


def page_table(pages, prompts, counts, tails, meta):
    def one_prompt(r, start):
        length = (counts[r] - 1) * PAGE + tails[r]
        meta[3 * pages + r] = length

        def one_page(i, carry):
            meta[start + i] = r
            meta[pages + start + i] = i * PAGE
            meta[2 * pages + start + i] = jnp.minimum(length - i * PAGE, PAGE)
            return carry

        lax.fori_loop(0, counts[r], one_page, 0)
        return start + counts[r]

    lax.fori_loop(0, prompts, one_prompt, 0)


def rotation_tables(pages, local_pages, meta, cos_s, sin_s):
    freqs = lane_freqs(8)
    low = lax.broadcasted_iota(jnp.int32, (8, HD), 0).astype(F32) * freqs
    low_cos, low_sin = jnp.cos(low), jnp.sin(low)
    high = lax.broadcasted_iota(jnp.int32, (PAGE // 8, HD), 0).astype(F32) * 8.0
    high = high * lane_freqs(PAGE // 8)
    high_cos, high_sin = jnp.cos(high), jnp.sin(high)
    first = lax.axis_index("seq") * local_pages
    base = by_row(local_pages, [meta[pages + first + p] for p in range(local_pages)])
    base = base * lane_freqs(local_pages)
    base_cos, base_sin = jnp.cos(base), jnp.sin(base)
    sign = sine_sign(8)
    for i in range(PAGE // 8):
        c, s = high_cos[i : i + 1], high_sin[i : i + 1]
        cosine, sine = low_cos * c - low_sin * s, low_sin * c + low_cos * s
        for p in range(local_pages):
            at = slice(p * PAGE + i * 8, p * PAGE + i * 8 + 8)
            c, s = base_cos[p : p + 1], base_sin[p : p + 1]
            cos_s[at] = cosine * c - sine * s
            sin_s[at] = sign * (sine * c + cosine * s)


def pair_columns(w_ref, rows, pair, part):
    at = [(2 * head + part) * HD for head in (2 * pair, 2 * pair + 1)]
    return jnp.concatenate([w_ref[rows, c : c + HD] for c in at], axis=1)


PARTS = 4


def load_kernel(pages, prompts, new_count, x_hbm, w_hbm, counts, tails, *refs):
    acc, x_ref, w_ref, cos_ref, sin_ref, cos_q, sin_q, meta, x_sems, w_sems = refs
    tokens, depth = x_ref.shape
    size, tall = depth // PARTS, tokens // 2
    copies = []
    for i in range(PARTS):
        at = pl.ds(i * size, size)
        x_copy = pltpu.make_async_copy(x_hbm.at[:, at], x_ref.at[:, at], x_sems.at[i])
        w_copy = pltpu.make_async_copy(w_hbm.at[at], w_ref.at[at], w_sems.at[i])
        x_copy.start()
        w_copy.start()
        copies.append((x_copy, w_copy))
    page_table(pages, prompts, counts, tails, meta)
    rotation_tables(pages, tokens // PAGE, meta, cos_ref, sin_ref)
    spots = [meta[3 * pages + r] + n for r in range(prompts) for n in range(new_count)]
    angles = by_row(len(spots), spots) * lane_freqs(len(spots))
    cos_q[...] = jnp.cos(angles)
    sin_q[...] = jnp.sin(angles) * sine_sign(len(spots))
    for i in range(PARTS // 2):
        for copy in copies[i]:
            copy.wait()
        rows = slice(i * size, (i + 1) * size)
        for pair in range(KVH // 2):
            weight = pair_columns(w_ref, rows, pair, 0)
            columns = slice(2 * pair * HD, 2 * (pair + 1) * HD)
            for start in range(0, tokens, tall):
                at = slice(start, start + tall)
                product = jnp.dot(x_ref[at, rows], weight, preferred_element_type=F32)
                acc[at, columns] = product if i == 0 else acc[at, columns] + product
    for pair_of_copies in copies[PARTS // 2 :]:
        for copy in pair_of_copies:
            copy.wait()


def load(x, kv_weight, counts, tails, pages, new_count):
    tokens, depth = x.shape
    columns = kv_weight.shape[1]
    prompts = counts.shape[0]
    hbm = pl.BlockSpec(memory_space=pltpu.HBM)
    return pl.pallas_call(
        functools.partial(load_kernel, pages, prompts, new_count),
        in_specs=[hbm, hbm, SMEM, SMEM],
        out_specs=[VMEM] * 7 + [SMEM],
        out_shape=[
            pltpu.VMEM((tokens, KVH * HD), F32),
            pltpu.VMEM((tokens, depth), BF16),
            pltpu.VMEM((depth, columns), BF16),
            pltpu.VMEM((tokens, HD), F32),
            pltpu.VMEM((tokens, HD), F32),
            pltpu.VMEM((prompts * new_count, HD), F32),
            pltpu.VMEM((prompts * new_count, HD), F32),
            jax.ShapeDtypeStruct((3 * pages + prompts,), jnp.int32),
        ],
        scratch_shapes=[pltpu.SemaphoreType.DMA((PARTS,)), pltpu.SemaphoreType.DMA((PARTS,))],
        compiler_params=pltpu.CompilerParams(vmem_limit_bytes=28 * MIB),
        cost_estimate=pl.CostEstimate(
            flops=3 * tokens * depth // 2 * KVH * HD,
            bytes_accessed=2 * depth * (tokens + columns),
            transcendentals=0,
        ),
        name="load",
    )(*[in_hbm(a) for a in (x, kv_weight, counts, tails)])


def keys_kernel(acc, x_ref, w_ref, cos_ref, sin_ref, after, k_ref):
    tokens, depth = x_ref.shape
    tall = tokens // 2
    rows = slice(depth // 2, depth)
    for pair in range(KVH // 2):
        weight = pair_columns(w_ref, rows, pair, 0)
        columns = slice(2 * pair * HD, 2 * (pair + 1) * HD)
        for start in range(0, tokens, tall):
            at = slice(start, start + tall)
            product = acc[at, columns] + jnp.dot(
                x_ref[at, rows], weight, preferred_element_type=F32
            )
            cosine, sine = cos_ref[at], sin_ref[at]
            for h in range(2):
                k = product[:, h * HD : (h + 1) * HD]
                k = k * cosine + pltpu.roll(k, HD // 2, 1) * sine
                k_ref[at, (2 * pair + h) * HD : (2 * pair + h + 1) * HD] = k.astype(BF16)


def rotated_keys(acc, x, weight, cosine, sine, after):
    tokens, depth = x.shape
    return pl.pallas_call(
        keys_kernel,
        in_specs=[VMEM] * 5 + [ANY],
        out_specs=VMEM,
        out_shape=pltpu.VMEM((tokens, KVH * HD), BF16),
        compiler_params=pltpu.CompilerParams(vmem_limit_bytes=24 * MIB),
        cost_estimate=pl.CostEstimate(
            flops=tokens * depth // 2 * KVH * HD, bytes_accessed=8 * MIB, transcendentals=0
        ),
        name="keys",
    )(acc, x, weight, cosine, sine, after)


def values_kernel(first, x_ref, w_ref, o_hbm, after, v_ref, o_ref, sem):
    depth = o_ref.shape[0]
    copy = pltpu.make_async_copy(o_hbm.at[pl.ds(first * depth, depth)], o_ref, sem)
    copy.start()
    tokens, columns = v_ref.shape
    tall = tokens // 2
    pairs_here = columns // (2 * HD)
    for pair in range(pairs_here):
        weight = pair_columns(w_ref, slice(None), first * pairs_here + pair, 1)
        for i in range(2):
            at = slice(i * tall, (i + 1) * tall)
            v_ref[at, 2 * pair * HD : 2 * (pair + 1) * HD] = jnp.dot(
                x_ref[at], weight, preferred_element_type=F32
            ).astype(BF16)
    copy.wait()


def project_values(x, weight, out_weight, first, after):
    tokens, depth = x.shape
    columns = KVH // 2 * HD
    rows = out_weight.shape[0] // 2
    return pl.pallas_call(
        functools.partial(values_kernel, first),
        in_specs=[
            VMEM,
            VMEM,
            pl.BlockSpec(memory_space=pltpu.HBM),
            ANY,
        ],
        out_specs=[VMEM, VMEM],
        out_shape=[
            pltpu.VMEM((tokens, columns), BF16),
            pltpu.VMEM((rows, out_weight.shape[1]), BF16),
        ],
        scratch_shapes=[pltpu.SemaphoreType.DMA],
        compiler_params=pltpu.CompilerParams(vmem_limit_bytes=24 * MIB),
        cost_estimate=pl.CostEstimate(
            flops=2 * tokens * depth * columns, bytes_accessed=8 * MIB, transcendentals=0
        ),
        name="values",
    )(x, weight, in_hbm(out_weight), after)


def by_heads(row):
    return jnp.concatenate([row[:, c : c + HD] for c in range(0, row.shape[1], HD)], axis=0)


def prepare_kernel(q_ref, kv_ref, q_out, kv_out):
    for r in range(q_ref.shape[0]):
        q, kv = q_ref[r].astype(F32), kv_ref[r].astype(F32)
        for n in range(q_ref.shape[1]):
            q_out[r, n] = by_heads(q[n : n + 1]).astype(BF16)
            kv_out[r, n] = by_heads(kv[n : n + 1])


def prepare(new_query, new_keyval):
    own_rows, new_count, columns = new_query.shape
    shape = lambda a: (own_rows, new_count, a.shape[2] // HD, HD)
    return pl.pallas_call(
        prepare_kernel,
        in_specs=[VMEM, VMEM],
        out_specs=[VMEM, VMEM],
        out_shape=[
            jax.ShapeDtypeStruct(shape(new_query), BF16),
            jax.ShapeDtypeStruct(shape(new_keyval), F32),
        ],
        compiler_params=pltpu.CompilerParams(vmem_limit_bytes=8 * MIB),
        cost_estimate=pl.CostEstimate(flops=0, bytes_accessed=MIB, transcendentals=0),
        name="prepare",
    )(in_hbm(new_query), in_hbm(new_keyval))


def stacked_kernel(n_tp, *refs):
    kv_ref, _, out_ref = refs[n_tp:]
    own_rows, new_count, heads, _ = refs[0].shape
    for r in range(own_rows):
        for n in range(new_count):
            rows = [refs[d][r, n].astype(F32) for d in range(n_tp)] + [kv_ref[r, n]]
            rows.append(jnp.zeros((out_ref.shape[2] - n_tp * heads - kv_ref.shape[2], HD), F32))
            out_ref[r, n] = jnp.concatenate(rows, axis=0).astype(BF16)


def stacked(pieces, fresh, after):
    n_tp = len(pieces)
    own_rows, new_count, heads, _ = pieces[0].shape
    rows = n_tp * heads + 16
    return pl.pallas_call(
        functools.partial(stacked_kernel, n_tp),
        in_specs=[VMEM] * (n_tp + 1) + [ANY],
        out_specs=VMEM,
        out_shape=jax.ShapeDtypeStruct((own_rows, new_count, rows, HD), BF16),
        compiler_params=pltpu.CompilerParams(vmem_limit_bytes=8 * MIB),
        name="stacked",
    )(*pieces, fresh, after)


def scores_kernel(n_seq, n_tp, *refs):
    new = refs[:n_seq]
    k_ref, cos_q, sin_q, meta = refs[n_seq : n_seq + 4]
    outs = refs[n_seq + 5 : n_seq + 5 + n_tp]
    own_q, all_q, ready = refs[n_seq + 5 + n_tp :]
    kv_local = KVH // n_tp
    local_pages = k_ref.shape[0] // PAGE
    own_rows, new_count, _, _ = new[0].shape
    rows = new_count * GROUP
    count = kv_local * rows
    scale = 1.0 / math.sqrt(HD)
    me = lax.axis_index("tp")
    seq = lax.axis_index("seq")
    first = seq * local_pages
    for ds in range(n_seq):
        for rr in range(own_rows):
            request = partner(seq, ds, n_seq) * own_rows + rr
            spots = [pl.ds(request * new_count + n, 1) for n in range(new_count)]
            turn = [(cos_q[spot], sin_q[spot]) for spot in spots]
            held = [new[ds][rr, n].astype(F32) for n in range(new_count)]
            for dt in range(n_tp):
                for g in range(kv_local):
                    parts = []
                    for n in range(new_count):
                        row = (dt * kv_local + g) * GROUP
                        q = held[n][row : row + GROUP]
                        parts.append(q * turn[n][0] + pltpu.roll(q, HD // 2, 1) * turn[n][1])
                    part = jnp.concatenate(parts, axis=0).astype(BF16)
                    at = (partner(me, dt, n_tp) * kv_local + g) * rows
                    all_q[request, pl.ds(pl.multiple_of(at, rows), rows)] = part
                    if dt == 0:
                        own_q[request, g * rows : (g + 1) * rows] = part
    for p in range(local_pages):
        request = meta[first + p]
        tokens = slice(p * PAGE, (p + 1) * PAGE)
        for head in range(KVH):
            k = k_ref[tokens, head * HD : (head + 1) * HD]
            q = all_q[request, head * rows : (head + 1) * rows]
            s = lax.dot_general(q, k, (((1,), (1,)), ((), ())), preferred_element_type=F32)
            ready[head * rows : (head + 1) * rows, tokens] = (s * scale).astype(BF16)
    for d in range(n_tp):
        outs[d][...] = ready[pl.ds(pl.multiple_of(partner(me, d, n_tp) * count, count), count)]


def partial_scores(new, k, cos_q, sin_q, meta, after, prompts, n_tp):
    n_seq = len(new)
    new_count = new[0].shape[1]
    tokens = k.shape[0]
    rows = KVH // n_tp * new_count * GROUP
    return pl.pallas_call(
        functools.partial(scores_kernel, n_seq, n_tp),
        in_specs=[VMEM] * (n_seq + 3) + [SMEM, ANY],
        out_specs=[VMEM] * (n_tp + 1),
        out_shape=[jax.ShapeDtypeStruct((rows, tokens), BF16)] * n_tp
        + [jax.ShapeDtypeStruct((prompts, rows, HD), BF16)],
        scratch_shapes=[
            pltpu.VMEM((prompts, rows * n_tp, HD), BF16),
            pltpu.VMEM((rows * n_tp, tokens), BF16),
        ],
        compiler_params=pltpu.CompilerParams(vmem_limit_bytes=24 * MIB),
        cost_estimate=pl.CostEstimate(
            flops=2 * tokens * rows * n_tp * HD, bytes_accessed=6 * MIB, transcendentals=0
        ),
        name="scores",
    )(*new, k, cos_q, sin_q, meta, after)


def fresh_kernel(n_seq, *refs):
    new = refs[:n_seq]
    q_ref, cos_q, sin_q, score_ref, value_ref = refs[n_seq:]
    prompts, rows_local, _ = q_ref.shape
    own_rows, new_count, _, _ = new[0].shape
    rows = new_count * GROUP
    kv_local = rows_local // rows
    heads = QH
    scale = 1.0 / math.sqrt(HD)
    seq = lax.axis_index("seq")
    step = lax.broadcasted_iota(jnp.int32, (rows_local, HD), 0) % rows // GROUP
    lane = lax.broadcasted_iota(jnp.int32, (rows_local, HD), 1)
    found = [jnp.full((rows_local, HD), NEG, F32) for _ in range(new_count)]
    for ds in range(n_seq):
        for rr in range(own_rows):
            request = partner(seq, ds, n_seq) * own_rows + rr
            q = q_ref[request].astype(F32)
            for n in range(new_count):
                spot = pl.ds(request * new_count + n, 1)
                cosine, sine = cos_q[spot], sin_q[spot]
                both = new[ds][rr, n].astype(F32)
                keys, values = [], []
                for g in range(kv_local):
                    k = both[heads + 2 * g : heads + 2 * g + 1]
                    k = k * cosine + pltpu.roll(k, HD // 2, 1) * sine
                    k = k.astype(BF16).astype(F32)
                    keys.append(jnp.broadcast_to(k, (rows, HD)))
                    v = both[heads + 2 * g + 1 : heads + 2 * g + 2]
                    values.append(jnp.broadcast_to(v, (rows, HD)))
                s = jnp.sum(q * jnp.concatenate(keys, axis=0), axis=1, keepdims=True) * scale
                found[n] = jnp.where((lane == request) & (step >= n), s, found[n])
                value_ref[request * new_count + n] = jnp.concatenate(values, axis=0)
    for n in range(new_count):
        score_ref[n] = found[n]


def fresh_scores(new, own_q, cos_q, sin_q):
    n_seq = len(new)
    new_count = new[0].shape[1]
    prompts, rows, _ = own_q.shape
    return pl.pallas_call(
        functools.partial(fresh_kernel, n_seq),
        in_specs=[VMEM] * (n_seq + 3),
        out_specs=[VMEM, VMEM],
        out_shape=[
            jax.ShapeDtypeStruct((new_count, rows, HD), F32),
            jax.ShapeDtypeStruct((prompts * new_count, rows, HD), F32),
        ],
        compiler_params=pltpu.CompilerParams(vmem_limit_bytes=16 * MIB),
        cost_estimate=pl.CostEstimate(flops=0, bytes_accessed=2 * MIB, transcendentals=0),
        name="fresh",
    )(*new, own_q, cos_q, sin_q)


def weights_kernel(pages, prompts, n_tp, *refs):
    chunks = refs[:n_tp]
    meta, _, w_ref, stats_ref = refs[n_tp:]
    rows, tokens = w_ref.shape
    local_pages = tokens // PAGE
    first = lax.axis_index("seq") * local_pages
    lane = lax.broadcasted_iota(jnp.int32, (rows, PAGE), 1)
    scores, maxima, masks, owners = [], [], [], []
    for p in range(local_pages):
        at = slice(p * PAGE, (p + 1) * PAGE)
        total = chunks[0][:, at].astype(F32)
        for d in range(1, n_tp):
            total = total + chunks[d][:, at].astype(F32)
        mask = lane < meta[2 * pages + first + p]
        total = jnp.where(mask, total, NEG)
        masks.append(mask)
        scores.append(total)
        maxima.append(jnp.max(total, axis=1, keepdims=True))
        owners.append(meta[first + p])
    quarter = lane // prompts
    spot = lane % prompts
    stats = jnp.where(quarter == 0, NEG, 0.0)
    sums = []
    for p in range(local_pages):
        top = maxima[p]
        for other in range(local_pages):
            if other != p:
                top = jnp.where(owners[p] == owners[other], jnp.maximum(top, maxima[other]), top)
        high = top.astype(BF16).astype(F32)
        low = (top - high).astype(BF16).astype(F32)
        w = jnp.where(masks[p], jnp.exp(scores[p] - (high + low)), 0.0)
        w_ref[:, p * PAGE : (p + 1) * PAGE] = w.astype(BF16)
        here = spot == owners[p]
        stats = jnp.where(here & (quarter == 0), high, stats)
        stats = jnp.where(here & (quarter == 1), low, stats)
        part = jnp.sum(w, axis=1, keepdims=True)
        stats = stats + jnp.where(here & (quarter == 2), part, 0.0)
    high = stats.astype(BF16).astype(F32)
    low = pltpu.roll(stats - high, prompts, 1)
    stats_ref[...] = jnp.where(quarter == 3, low, stats).astype(BF16)


def softmax_weights(chunks, meta, after, pages, prompts):
    n_tp = len(chunks)
    rows, tokens = chunks[0].shape
    return pl.pallas_call(
        functools.partial(weights_kernel, pages, prompts, n_tp),
        in_specs=[VMEM] * n_tp + [SMEM, ANY],
        out_specs=[VMEM, VMEM],
        out_shape=[
            jax.ShapeDtypeStruct((rows, tokens), BF16),
            jax.ShapeDtypeStruct((rows, PAGE), BF16),
        ],
        compiler_params=pltpu.CompilerParams(vmem_limit_bytes=8 * MIB),
        name="weights",
    )(*chunks, meta, after)


def weighted_kernel(n_tp, *refs):
    pieces = refs[:n_tp]
    va_ref, vb_ref, meta = refs[n_tp : n_tp + 3]
    outs = refs[n_tp + 3 : n_tp + 3 + n_tp]
    ready, total = refs[n_tp + 3 + n_tp :]
    rows_local, tokens_here = pieces[0].shape
    kv_local = KVH // n_tp
    rows = rows_local // kv_local
    local_pages = tokens_here // PAGE
    first = lax.axis_index("seq") * local_pages
    me = lax.axis_index("tp")
    own = [pl.ds(pl.multiple_of(partner(me, d, n_tp) * rows_local, rows_local), rows_local) for d in range(n_tp)]
    for d in range(n_tp):
        at = pl.multiple_of((me ^ d) * rows_local, rows_local)
        ready[pl.ds(at, rows_local)] = pieces[d][...]
    total[...] = jnp.zeros_like(total)
    half = va_ref.shape[1] // HD
    for p in range(local_pages):
        request = meta[first + p]
        tokens = slice(p * PAGE, (p + 1) * PAGE)
        for head in range(KVH):
            v_ref = va_ref if head < half else vb_ref
            v = v_ref[tokens, head % half * HD : (head % half + 1) * HD]
            at = slice(head * rows, (head + 1) * rows)
            total[request, at] += jnp.dot(ready[at, tokens], v, preferred_element_type=F32)
    for d in range(n_tp):
        outs[d][...] = total[:, own[d]].astype(BF16)


def weighted_values(pieces, va, vb, meta, prompts):
    n_tp = len(pieces)
    rows, tokens = pieces[0].shape
    return pl.pallas_call(
        functools.partial(weighted_kernel, n_tp),
        in_specs=[VMEM] * (n_tp + 2) + [SMEM],
        out_specs=[VMEM] * n_tp,
        out_shape=[jax.ShapeDtypeStruct((prompts, rows, HD), BF16)] * n_tp,
        scratch_shapes=[
            pltpu.VMEM((rows * n_tp, tokens), BF16),
            pltpu.VMEM((prompts, rows * n_tp, HD), F32),
        ],
        compiler_params=pltpu.CompilerParams(vmem_limit_bytes=24 * MIB),
        cost_estimate=pl.CostEstimate(
            flops=2 * tokens * rows * n_tp * HD, bytes_accessed=8 * MIB, transcendentals=0
        ),
        name="weighted",
    )(*pieces, va, vb, meta)


def summed_kernel(n_tp, *refs):
    chunks = refs[:n_tp]
    stats_ref, out_ref = refs[n_tp:]
    prompts = chunks[0].shape[0]
    total = chunks[0][...].astype(F32)
    for d in range(1, n_tp):
        total = total + chunks[d][...].astype(F32)
    out_ref[:prompts] = total.astype(BF16)
    out_ref[prompts] = stats_ref[...]


def summed(chunks, stats):
    n_tp = len(chunks)
    prompts, rows, _ = chunks[0].shape
    return pl.pallas_call(
        functools.partial(summed_kernel, n_tp),
        in_specs=[VMEM] * (n_tp + 1),
        out_specs=VMEM,
        out_shape=jax.ShapeDtypeStruct((prompts + 1, rows, HD), BF16),
        compiler_params=pltpu.CompilerParams(vmem_limit_bytes=8 * MIB),
        cost_estimate=pl.CostEstimate(flops=0, bytes_accessed=4 * MIB, transcendentals=0),
        name="summed",
    )(*chunks, stats)


def output_kernel(n_seq, *refs):
    pieces = refs[:n_seq]
    fresh_ref, value_ref, wa_ref, wb_ref, out_ref, held = refs[n_seq:]
    more, rows_local, _ = pieces[0].shape
    prompts = more - 1
    new_count = fresh_ref.shape[0]
    rows = new_count * GROUP
    kv_local = rows_local // rows
    heads = kv_local * GROUP
    tops, parts = [], []
    for s in range(n_seq):
        stats = pieces[s][prompts].astype(F32)
        folded = stats + pltpu.roll(stats, HD - prompts, 1)
        tops.append(folded)
        parts.append(pltpu.roll(folded, HD - 2 * prompts, 1))
    fresh = [fresh_ref[n] for n in range(new_count)]
    top = fresh[0]
    for other in fresh[1:] + tops:
        top = jnp.maximum(top, other)
    weights = [jnp.exp(f - top) for f in fresh]
    factors = [jnp.exp(t - top) for t in tops]
    total = weights[0]
    for w in weights[1:]:
        total = total + w
    for f, part in zip(factors, parts):
        total = total + f * part
    weights = [w / total for w in weights]
    factors = [f / total for f in factors]
    for r in range(prompts):
        sums = jnp.zeros((rows_local, HD), F32)
        for s in range(n_seq):
            sums = sums + factors[s][:, r : r + 1] * pieces[s][r].astype(F32)
        for n in range(new_count):
            sums = sums + weights[n][:, r : r + 1] * value_ref[r * new_count + n]
        for g in range(kv_local):
            for n in range(new_count):
                at = g * rows + n * GROUP
                held[g * GROUP : (g + 1) * GROUP, r * new_count + n] = sums[at : at + GROUP]
    half = heads // 2
    product = jnp.zeros(out_ref.shape, F32)
    for w_ref, at in ((wa_ref, 0), (wb_ref, half)):
        left = [held[h].astype(BF16) for h in range(at, at + half)]
        left = jnp.concatenate(left, axis=1)
        product = product + jnp.dot(left, w_ref[...], preferred_element_type=F32)
    out_ref[...] = product.astype(BF16)


def output_partial(pieces, fresh, values, weights):
    n_seq = len(pieces)
    new_count = fresh.shape[0]
    prompts = pieces[0].shape[0] - 1
    depth, columns = weights[0].shape
    return pl.pallas_call(
        functools.partial(output_kernel, n_seq),
        in_specs=[VMEM] * (n_seq + 4),
        out_specs=VMEM,
        out_shape=jax.ShapeDtypeStruct((prompts * new_count, columns), BF16),
        scratch_shapes=[pltpu.VMEM((2 * depth // HD, prompts * new_count, HD), F32)],
        compiler_params=pltpu.CompilerParams(vmem_limit_bytes=24 * MIB),
        name="output",
    )(*pieces, fresh, values, *weights)


def final_kernel(n_tp, *refs):
    pieces = refs[:n_tp]
    res_ref, out_ref = refs[n_tp:]
    prompts, new_count, _ = out_ref.shape
    total = pieces[0][...].astype(F32)
    for d in range(1, n_tp):
        total = total + pieces[d][...].astype(F32)
    for r in range(prompts):
        out_ref[r] = res_ref[r].astype(F32) + total[r * new_count : (r + 1) * new_count]


def final_sum(pieces, residual):
    n_tp = len(pieces)
    return pl.pallas_call(
        functools.partial(final_kernel, n_tp),
        in_specs=[VMEM] * (n_tp + 1),
        out_specs=VMEM,
        out_shape=jax.ShapeDtypeStruct(residual.shape, F32),
        compiler_params=pltpu.CompilerParams(vmem_limit_bytes=8 * MIB),
        name="final",
    )(*pieces, residual)


def on_device(
    prefill_states, kv_weight, page_counts, tail_tokens, new_query, new_keyval, residual, out_weight
):
    n_seq, n_tp = lax.axis_size("seq"), lax.axis_size("tp")
    own_rows, new_count, _ = new_query.shape
    prompts = page_counts.shape[0]
    pages = prefill_states.shape[0] // PAGE * n_seq
    query, new_kv = prepare(new_query, new_keyval)
    query = gather(query, "tp")
    acc, x, w, cosine, sine, cos_q, sin_q, meta = load(
        prefill_states, kv_weight, page_counts, tail_tokens, pages, new_count
    )
    new = stacked(query, new_kv, meta)
    k = rotated_keys(acc, x, w, cosine, sine, new)
    va, oa = project_values(x, w, out_weight, 0, new)
    new = gather(new, "seq")
    *scores, own_q = partial_scores(new, k, cos_q, sin_q, meta, va, prompts, n_tp)
    vb, ob = project_values(x, w, out_weight, 1, own_q)
    fresh, values = fresh_scores(new, own_q, cos_q, sin_q)
    weights, stats = softmax_weights(exchange(scores, "tp"), meta, vb, pages, prompts)
    chunks = weighted_values(gather_by_index(weights, "tp"), va, vb, meta, prompts)
    pieces = gather(summed(exchange(chunks, "tp"), stats), "seq")
    partial = output_partial(pieces, fresh, values, (oa, ob))
    return final_sum(gather(partial, "tp"), residual)


def solution(mesh):
    placed = (
        P(("groups", "seq"), "tp"),
        P("tp", None),
        P("groups"),
        P("groups"),
        P(("groups", "seq"), None, "tp"),
        P(("groups", "seq"), None, "tp"),
        P("groups", None, "seq"),
        P("tp", "seq"),
    )
    return jax.shard_map(
        on_device, mesh=mesh, in_specs=placed, out_specs=P("groups", None, "seq"), check_vma=False
    )
```

```python
import functools
import math

import jax
import jax.numpy as jnp
from jax import lax
from jax.experimental import pallas as pl
from jax.experimental.pallas import tpu as pltpu
from jax.sharding import PartitionSpec as P

QH = 64
KVH = 8
HD = 128
PAGE = 128
GROUP = QH // KVH
NEG = -1e30
F32 = jnp.float32
BF16 = jnp.bfloat16
MIB = 1 << 20

VMEM = pl.BlockSpec(memory_space=pltpu.VMEM)
SMEM = pl.BlockSpec(memory_space=pltpu.SMEM)
ANY = pl.BlockSpec(memory_space=pl.ANY)


def partner(me, entry, size):
    return me ^ ((size - entry) % size)


def pairs(value, axis, entry):
    size = lax.axis_size(axis)
    return lax.ppermute(value, axis, [(i, partner(i, entry, size)) for i in range(size)])


def exchange(chunks, axis):
    return [chunks[0]] + [pairs(chunks[i], axis, i) for i in range(1, len(chunks))]


def gather(value, axis):
    size = lax.axis_size(axis)
    return [value] + [pairs(value, axis, size - d) for d in range(1, size)]


def lane_freqs(rows):
    lane = lax.broadcasted_iota(jnp.int32, (rows, HD), 1) % (HD // 2)
    return jnp.exp(-(lane.astype(F32) * (2.0 / HD)) * math.log(500000.0))


def sine_sign(rows):
    lane = lax.broadcasted_iota(jnp.int32, (rows, HD), 1)
    return jnp.where(lane < HD // 2, -1.0, 1.0)


def in_hbm(value):
    return pltpu.with_memory_space_constraint(value, pltpu.HBM)


def by_row(rows, numbers):
    row = lax.broadcasted_iota(jnp.int32, (rows, HD), 0)
    out = jnp.zeros((rows, HD), F32)
    for i, number in enumerate(numbers):
        out = jnp.where(row == i, number.astype(F32), out)
    return out


def page_table(pages, prompts, counts, tails, meta):
    def one_prompt(r, start):
        length = (counts[r] - 1) * PAGE + tails[r]
        meta[3 * pages + r] = length

        def one_page(i, carry):
            meta[start + i] = r
            meta[pages + start + i] = i * PAGE
            meta[2 * pages + start + i] = jnp.minimum(length - i * PAGE, PAGE)
            return carry

        lax.fori_loop(0, counts[r], one_page, 0)
        return start + counts[r]

    lax.fori_loop(0, prompts, one_prompt, 0)


def rotation_tables(pages, local_pages, meta, cos_s, sin_s):
    freqs = lane_freqs(8)
    low = lax.broadcasted_iota(jnp.int32, (8, HD), 0).astype(F32) * freqs
    low_cos, low_sin = jnp.cos(low), jnp.sin(low)
    high = lax.broadcasted_iota(jnp.int32, (PAGE // 8, HD), 0).astype(F32) * 8.0
    high = high * lane_freqs(PAGE // 8)
    high_cos, high_sin = jnp.cos(high), jnp.sin(high)
    first = lax.axis_index("seq") * local_pages
    base = by_row(local_pages, [meta[pages + first + p] for p in range(local_pages)])
    base = base * lane_freqs(local_pages)
    base_cos, base_sin = jnp.cos(base), jnp.sin(base)
    sign = sine_sign(8)
    for i in range(PAGE // 8):
        c, s = high_cos[i : i + 1], high_sin[i : i + 1]
        cosine, sine = low_cos * c - low_sin * s, low_sin * c + low_cos * s
        for p in range(local_pages):
            at = slice(p * PAGE + i * 8, p * PAGE + i * 8 + 8)
            c, s = base_cos[p : p + 1], base_sin[p : p + 1]
            cos_s[at] = cosine * c - sine * s
            sin_s[at] = sign * (sine * c + cosine * s)


def pair_columns(w_ref, rows, pair, part):
    at = [(2 * head + part) * HD for head in (2 * pair, 2 * pair + 1)]
    return jnp.concatenate([w_ref[rows, c : c + HD] for c in at], axis=1)


PARTS = 4


def load_kernel(pages, prompts, new_count, x_hbm, w_hbm, counts, tails, *refs):
    acc, x_ref, w_ref, cos_ref, sin_ref, cos_q, sin_q, meta, x_sems, w_sems = refs
    tokens, depth = x_ref.shape
    size, tall = depth // PARTS, tokens // 2
    copies = []
    for i in range(PARTS):
        at = pl.ds(i * size, size)
        x_copy = pltpu.make_async_copy(x_hbm.at[:, at], x_ref.at[:, at], x_sems.at[i])
        w_copy = pltpu.make_async_copy(w_hbm.at[at], w_ref.at[at], w_sems.at[i])
        x_copy.start()
        w_copy.start()
        copies.append((x_copy, w_copy))
    page_table(pages, prompts, counts, tails, meta)
    rotation_tables(pages, tokens // PAGE, meta, cos_ref, sin_ref)
    spots = [meta[3 * pages + r] + n for r in range(prompts) for n in range(new_count)]
    angles = by_row(len(spots), spots) * lane_freqs(len(spots))
    cos_q[...] = jnp.cos(angles)
    sin_q[...] = jnp.sin(angles) * sine_sign(len(spots))
    for i in range(PARTS // 2):
        for copy in copies[i]:
            copy.wait()
        rows = slice(i * size, (i + 1) * size)
        for pair in range(KVH // 2):
            weight = pair_columns(w_ref, rows, pair, 0)
            columns = slice(2 * pair * HD, 2 * (pair + 1) * HD)
            for start in range(0, tokens, tall):
                at = slice(start, start + tall)
                product = jnp.dot(x_ref[at, rows], weight, preferred_element_type=F32)
                acc[at, columns] = product if i == 0 else acc[at, columns] + product
    for pair_of_copies in copies[PARTS // 2 :]:
        for copy in pair_of_copies:
            copy.wait()


def load(x, kv_weight, counts, tails, pages, new_count):
    tokens, depth = x.shape
    columns = kv_weight.shape[1]
    prompts = counts.shape[0]
    hbm = pl.BlockSpec(memory_space=pltpu.HBM)
    return pl.pallas_call(
        functools.partial(load_kernel, pages, prompts, new_count),
        in_specs=[hbm, hbm, SMEM, SMEM],
        out_specs=[VMEM] * 7 + [SMEM],
        out_shape=[
            pltpu.VMEM((tokens, KVH * HD), F32),
            pltpu.VMEM((tokens, depth), BF16),
            pltpu.VMEM((depth, columns), BF16),
            pltpu.VMEM((tokens, HD), F32),
            pltpu.VMEM((tokens, HD), F32),
            pltpu.VMEM((prompts * new_count, HD), F32),
            pltpu.VMEM((prompts * new_count, HD), F32),
            jax.ShapeDtypeStruct((3 * pages + prompts,), jnp.int32),
        ],
        scratch_shapes=[pltpu.SemaphoreType.DMA((PARTS,)), pltpu.SemaphoreType.DMA((PARTS,))],
        compiler_params=pltpu.CompilerParams(vmem_limit_bytes=28 * MIB),
        cost_estimate=pl.CostEstimate(
            flops=3 * tokens * depth // 2 * KVH * HD,
            bytes_accessed=2 * depth * (tokens + columns),
            transcendentals=0,
        ),
        name="load",
    )(*[in_hbm(a) for a in (x, kv_weight, counts, tails)])


def keys_kernel(acc, x_ref, w_ref, cos_ref, sin_ref, after, k_ref):
    tokens, depth = x_ref.shape
    tall = tokens // 2
    rows = slice(depth // 2, depth)
    for pair in range(KVH // 2):
        weight = pair_columns(w_ref, rows, pair, 0)
        columns = slice(2 * pair * HD, 2 * (pair + 1) * HD)
        for start in range(0, tokens, tall):
            at = slice(start, start + tall)
            product = acc[at, columns] + jnp.dot(
                x_ref[at, rows], weight, preferred_element_type=F32
            )
            cosine, sine = cos_ref[at], sin_ref[at]
            for h in range(2):
                k = product[:, h * HD : (h + 1) * HD]
                k = k * cosine + pltpu.roll(k, HD // 2, 1) * sine
                k_ref[at, (2 * pair + h) * HD : (2 * pair + h + 1) * HD] = k.astype(BF16)


def rotated_keys(acc, x, weight, cosine, sine, after):
    tokens, depth = x.shape
    return pl.pallas_call(
        keys_kernel,
        in_specs=[VMEM] * 5 + [ANY],
        out_specs=VMEM,
        out_shape=pltpu.VMEM((tokens, KVH * HD), BF16),
        compiler_params=pltpu.CompilerParams(vmem_limit_bytes=24 * MIB),
        cost_estimate=pl.CostEstimate(
            flops=tokens * depth // 2 * KVH * HD, bytes_accessed=8 * MIB, transcendentals=0
        ),
        name="keys",
    )(acc, x, weight, cosine, sine, after)


def values_kernel(first, x_ref, w_ref, o_hbm, after, v_ref, o_ref, sem):
    depth = o_ref.shape[0]
    copy = pltpu.make_async_copy(o_hbm.at[pl.ds(first * depth, depth)], o_ref, sem)
    copy.start()
    tokens, columns = v_ref.shape
    tall = tokens // 2
    pairs_here = columns // (2 * HD)
    for pair in range(pairs_here):
        weight = pair_columns(w_ref, slice(None), first * pairs_here + pair, 1)
        for i in range(2):
            at = slice(i * tall, (i + 1) * tall)
            v_ref[at, 2 * pair * HD : 2 * (pair + 1) * HD] = jnp.dot(
                x_ref[at], weight, preferred_element_type=F32
            ).astype(BF16)
    copy.wait()


def project_values(x, weight, out_weight, first, after):
    tokens, depth = x.shape
    columns = KVH // 2 * HD
    rows = out_weight.shape[0] // 2
    return pl.pallas_call(
        functools.partial(values_kernel, first),
        in_specs=[
            VMEM,
            VMEM,
            pl.BlockSpec(memory_space=pltpu.HBM),
            ANY,
        ],
        out_specs=[VMEM, VMEM],
        out_shape=[
            pltpu.VMEM((tokens, columns), BF16),
            pltpu.VMEM((rows, out_weight.shape[1]), BF16),
        ],
        scratch_shapes=[pltpu.SemaphoreType.DMA],
        compiler_params=pltpu.CompilerParams(vmem_limit_bytes=24 * MIB),
        cost_estimate=pl.CostEstimate(
            flops=2 * tokens * depth * columns, bytes_accessed=8 * MIB, transcendentals=0
        ),
        name="values",
    )(x, weight, in_hbm(out_weight), after)


def by_heads(row):
    return jnp.concatenate([row[:, c : c + HD] for c in range(0, row.shape[1], HD)], axis=0)


def prepare_kernel(q_ref, kv_ref, q_out, kv_out):
    for r in range(q_ref.shape[0]):
        q, kv = q_ref[r].astype(F32), kv_ref[r].astype(F32)
        for n in range(q_ref.shape[1]):
            q_out[r, n] = by_heads(q[n : n + 1]).astype(BF16)
            kv_out[r, n] = by_heads(kv[n : n + 1])


def prepare(new_query, new_keyval):
    own_rows, new_count, columns = new_query.shape
    shape = lambda a: (own_rows, new_count, a.shape[2] // HD, HD)
    return pl.pallas_call(
        prepare_kernel,
        in_specs=[VMEM, VMEM],
        out_specs=[VMEM, VMEM],
        out_shape=[
            jax.ShapeDtypeStruct(shape(new_query), BF16),
            jax.ShapeDtypeStruct(shape(new_keyval), F32),
        ],
        compiler_params=pltpu.CompilerParams(vmem_limit_bytes=8 * MIB),
        cost_estimate=pl.CostEstimate(flops=0, bytes_accessed=MIB, transcendentals=0),
        name="prepare",
    )(in_hbm(new_query), in_hbm(new_keyval))


def stacked_kernel(n_tp, *refs):
    kv_ref, _, out_ref = refs[n_tp:]
    own_rows, new_count, heads, _ = refs[0].shape
    for r in range(own_rows):
        for n in range(new_count):
            rows = [refs[d][r, n].astype(F32) for d in range(n_tp)] + [kv_ref[r, n]]
            rows.append(jnp.zeros((out_ref.shape[2] - n_tp * heads - kv_ref.shape[2], HD), F32))
            out_ref[r, n] = jnp.concatenate(rows, axis=0).astype(BF16)


def stacked(pieces, fresh, after):
    n_tp = len(pieces)
    own_rows, new_count, heads, _ = pieces[0].shape
    rows = n_tp * heads + 16
    return pl.pallas_call(
        functools.partial(stacked_kernel, n_tp),
        in_specs=[VMEM] * (n_tp + 1) + [ANY],
        out_specs=VMEM,
        out_shape=jax.ShapeDtypeStruct((own_rows, new_count, rows, HD), BF16),
        compiler_params=pltpu.CompilerParams(vmem_limit_bytes=8 * MIB),
        name="stacked",
    )(*pieces, fresh, after)


def scores_kernel(n_seq, n_tp, *refs):
    new = refs[:n_seq]
    k_ref, cos_q, sin_q, meta = refs[n_seq : n_seq + 4]
    outs = refs[n_seq + 4 : n_seq + 4 + n_tp]
    own_q, all_q, ready = refs[n_seq + 4 + n_tp :]
    kv_local = KVH // n_tp
    local_pages = k_ref.shape[0] // PAGE
    own_rows, new_count, _, _ = new[0].shape
    rows = new_count * GROUP
    count = kv_local * rows
    scale = 1.0 / math.sqrt(HD)
    me = lax.axis_index("tp")
    seq = lax.axis_index("seq")
    first = seq * local_pages
    for ds in range(n_seq):
        for rr in range(own_rows):
            request = (seq ^ ds) * own_rows + rr
            spots = [pl.ds(request * new_count + n, 1) for n in range(new_count)]
            turn = [(cos_q[spot], sin_q[spot]) for spot in spots]
            held = [new[ds][rr, n].astype(F32) for n in range(new_count)]
            for dt in range(n_tp):
                for g in range(kv_local):
                    parts = []
                    for n in range(new_count):
                        row = (dt * kv_local + g) * GROUP
                        q = held[n][row : row + GROUP]
                        parts.append(q * turn[n][0] + pltpu.roll(q, HD // 2, 1) * turn[n][1])
                    part = jnp.concatenate(parts, axis=0).astype(BF16)
                    at = ((me ^ dt) * kv_local + g) * rows
                    all_q[request, pl.ds(pl.multiple_of(at, rows), rows)] = part
                    if dt == 0:
                        own_q[request, g * rows : (g + 1) * rows] = part
    for p in range(local_pages):
        request = meta[first + p]
        tokens = slice(p * PAGE, (p + 1) * PAGE)
        for head in range(KVH):
            k = k_ref[tokens, head * HD : (head + 1) * HD]
            q = all_q[request, head * rows : (head + 1) * rows]
            s = lax.dot_general(q, k, (((1,), (1,)), ((), ())), preferred_element_type=F32)
            ready[head * rows : (head + 1) * rows, tokens] = (s * scale).astype(BF16)
    for d in range(n_tp):
        outs[d][...] = ready[pl.ds(pl.multiple_of(partner(me, d, n_tp) * count, count), count)]


def partial_scores(new, k, cos_q, sin_q, meta, prompts, n_tp):
    n_seq = len(new)
    new_count = new[0].shape[1]
    tokens = k.shape[0]
    rows = KVH // n_tp * new_count * GROUP
    return pl.pallas_call(
        functools.partial(scores_kernel, n_seq, n_tp),
        in_specs=[VMEM] * (n_seq + 3) + [SMEM],
        out_specs=[VMEM] * (n_tp + 1),
        out_shape=[jax.ShapeDtypeStruct((rows, tokens), BF16)] * n_tp
        + [jax.ShapeDtypeStruct((prompts, rows, HD), BF16)],
        scratch_shapes=[
            pltpu.VMEM((prompts, rows * n_tp, HD), BF16),
            pltpu.VMEM((rows * n_tp, tokens), BF16),
        ],
        compiler_params=pltpu.CompilerParams(vmem_limit_bytes=24 * MIB),
        cost_estimate=pl.CostEstimate(
            flops=2 * tokens * rows * n_tp * HD, bytes_accessed=6 * MIB, transcendentals=0
        ),
        name="scores",
    )(*new, k, cos_q, sin_q, meta)


def fresh_kernel(n_seq, *refs):
    new = refs[:n_seq]
    q_ref, cos_q, sin_q, score_ref, value_ref = refs[n_seq:]
    prompts, rows_local, _ = q_ref.shape
    own_rows, new_count, _, _ = new[0].shape
    rows = new_count * GROUP
    kv_local = rows_local // rows
    heads = QH
    scale = 1.0 / math.sqrt(HD)
    seq = lax.axis_index("seq")
    step = lax.broadcasted_iota(jnp.int32, (rows_local, HD), 0) % rows // GROUP
    lane = lax.broadcasted_iota(jnp.int32, (rows_local, HD), 1)
    found = [jnp.full((rows_local, HD), NEG, F32) for _ in range(new_count)]
    for ds in range(n_seq):
        for rr in range(own_rows):
            request = (seq ^ ds) * own_rows + rr
            q = q_ref[request].astype(F32)
            for n in range(new_count):
                spot = pl.ds(request * new_count + n, 1)
                cosine, sine = cos_q[spot], sin_q[spot]
                both = new[ds][rr, n].astype(F32)
                keys, values = [], []
                for g in range(kv_local):
                    k = both[heads + 2 * g : heads + 2 * g + 1]
                    k = k * cosine + pltpu.roll(k, HD // 2, 1) * sine
                    k = k.astype(BF16).astype(F32)
                    keys.append(jnp.broadcast_to(k, (rows, HD)))
                    v = both[heads + 2 * g + 1 : heads + 2 * g + 2]
                    values.append(jnp.broadcast_to(v, (rows, HD)))
                s = jnp.sum(q * jnp.concatenate(keys, axis=0), axis=1, keepdims=True) * scale
                found[n] = jnp.where((lane == request) & (step >= n), s, found[n])
                value_ref[request * new_count + n] = jnp.concatenate(values, axis=0)
    for n in range(new_count):
        score_ref[n] = found[n]


def fresh_scores(new, own_q, cos_q, sin_q):
    n_seq = len(new)
    new_count = new[0].shape[1]
    prompts, rows, _ = own_q.shape
    return pl.pallas_call(
        functools.partial(fresh_kernel, n_seq),
        in_specs=[VMEM] * (n_seq + 3),
        out_specs=[VMEM, VMEM],
        out_shape=[
            jax.ShapeDtypeStruct((new_count, rows, HD), F32),
            jax.ShapeDtypeStruct((prompts * new_count, rows, HD), F32),
        ],
        compiler_params=pltpu.CompilerParams(vmem_limit_bytes=16 * MIB),
        cost_estimate=pl.CostEstimate(flops=0, bytes_accessed=2 * MIB, transcendentals=0),
        name="fresh",
    )(*new, own_q, cos_q, sin_q)


def weights_kernel(pages, prompts, n_tp, *refs):
    chunks = refs[:n_tp]
    meta, _, w_ref, stats_ref = refs[n_tp:]
    rows, tokens = w_ref.shape
    local_pages = tokens // PAGE
    first = lax.axis_index("seq") * local_pages
    lane = lax.broadcasted_iota(jnp.int32, (rows, PAGE), 1)
    scores, maxima, masks, owners = [], [], [], []
    for p in range(local_pages):
        at = slice(p * PAGE, (p + 1) * PAGE)
        total = chunks[0][:, at].astype(F32)
        for d in range(1, n_tp):
            total = total + chunks[d][:, at].astype(F32)
        mask = lane < meta[2 * pages + first + p]
        total = jnp.where(mask, total, NEG)
        masks.append(mask)
        scores.append(total)
        maxima.append(jnp.max(total, axis=1, keepdims=True))
        owners.append(meta[first + p])
    quarter = lane // prompts
    spot = lane % prompts
    stats = jnp.where(quarter == 0, NEG, 0.0)
    sums = []
    for p in range(local_pages):
        top = maxima[p]
        for other in range(local_pages):
            if other != p:
                top = jnp.where(owners[p] == owners[other], jnp.maximum(top, maxima[other]), top)
        high = top.astype(BF16).astype(F32)
        low = (top - high).astype(BF16).astype(F32)
        w = jnp.where(masks[p], jnp.exp(scores[p] - (high + low)), 0.0)
        w_ref[:, p * PAGE : (p + 1) * PAGE] = w.astype(BF16)
        here = spot == owners[p]
        stats = jnp.where(here & (quarter == 0), high, stats)
        stats = jnp.where(here & (quarter == 1), low, stats)
        part = jnp.sum(w, axis=1, keepdims=True)
        stats = stats + jnp.where(here & (quarter == 2), part, 0.0)
    high = stats.astype(BF16).astype(F32)
    low = pltpu.roll(stats - high, prompts, 1)
    stats_ref[...] = jnp.where(quarter == 3, low, stats).astype(BF16)


def softmax_weights(chunks, meta, after, pages, prompts):
    n_tp = len(chunks)
    rows, tokens = chunks[0].shape
    return pl.pallas_call(
        functools.partial(weights_kernel, pages, prompts, n_tp),
        in_specs=[VMEM] * n_tp + [SMEM, ANY],
        out_specs=[VMEM, VMEM],
        out_shape=[
            jax.ShapeDtypeStruct((rows, tokens), BF16),
            jax.ShapeDtypeStruct((rows, PAGE), BF16),
        ],
        compiler_params=pltpu.CompilerParams(vmem_limit_bytes=8 * MIB),
        name="weights",
    )(*chunks, meta, after)


def weighted_kernel(n_tp, *refs):
    pieces = refs[:n_tp]
    va_ref, vb_ref, meta = refs[n_tp : n_tp + 3]
    outs = refs[n_tp + 3 : n_tp + 3 + n_tp]
    ready, total = refs[n_tp + 3 + n_tp :]
    rows_local, tokens_here = pieces[0].shape
    kv_local = KVH // n_tp
    rows = rows_local // kv_local
    local_pages = tokens_here // PAGE
    first = lax.axis_index("seq") * local_pages
    me = lax.axis_index("tp")
    own = [pl.ds(pl.multiple_of(partner(me, d, n_tp) * rows_local, rows_local), rows_local) for d in range(n_tp)]
    for d in range(n_tp):
        at = pl.multiple_of((me ^ d) * rows_local, rows_local)
        ready[pl.ds(at, rows_local)] = pieces[d][...]
    total[...] = jnp.zeros_like(total)
    half = va_ref.shape[1] // HD
    for p in range(local_pages):
        request = meta[first + p]
        tokens = slice(p * PAGE, (p + 1) * PAGE)
        for head in range(KVH):
            v_ref = va_ref if head < half else vb_ref
            v = v_ref[tokens, head % half * HD : (head % half + 1) * HD]
            at = slice(head * rows, (head + 1) * rows)
            total[request, at] += jnp.dot(ready[at, tokens], v, preferred_element_type=F32)
    for d in range(n_tp):
        outs[d][...] = total[:, own[d]].astype(BF16)


def weighted_values(pieces, va, vb, meta, prompts):
    n_tp = len(pieces)
    rows, tokens = pieces[0].shape
    return pl.pallas_call(
        functools.partial(weighted_kernel, n_tp),
        in_specs=[VMEM] * (n_tp + 2) + [SMEM],
        out_specs=[VMEM] * n_tp,
        out_shape=[jax.ShapeDtypeStruct((prompts, rows, HD), BF16)] * n_tp,
        scratch_shapes=[
            pltpu.VMEM((rows * n_tp, tokens), BF16),
            pltpu.VMEM((prompts, rows * n_tp, HD), F32),
        ],
        compiler_params=pltpu.CompilerParams(vmem_limit_bytes=24 * MIB),
        cost_estimate=pl.CostEstimate(
            flops=2 * tokens * rows * n_tp * HD, bytes_accessed=8 * MIB, transcendentals=0
        ),
        name="weighted",
    )(*pieces, va, vb, meta)


def summed_kernel(n_tp, *refs):
    chunks = refs[:n_tp]
    stats_ref, out_ref = refs[n_tp:]
    prompts = chunks[0].shape[0]
    total = chunks[0][...].astype(F32)
    for d in range(1, n_tp):
        total = total + chunks[d][...].astype(F32)
    out_ref[:prompts] = total.astype(BF16)
    out_ref[prompts] = stats_ref[...]


def summed(chunks, stats):
    n_tp = len(chunks)
    prompts, rows, _ = chunks[0].shape
    return pl.pallas_call(
        functools.partial(summed_kernel, n_tp),
        in_specs=[VMEM] * (n_tp + 1),
        out_specs=VMEM,
        out_shape=jax.ShapeDtypeStruct((prompts + 1, rows, HD), BF16),
        compiler_params=pltpu.CompilerParams(vmem_limit_bytes=8 * MIB),
        cost_estimate=pl.CostEstimate(flops=0, bytes_accessed=4 * MIB, transcendentals=0),
        name="summed",
    )(*chunks, stats)


def output_kernel(n_seq, *refs):
    pieces = refs[:n_seq]
    fresh_ref, value_ref, wa_ref, wb_ref, out_ref, held = refs[n_seq:]
    more, rows_local, _ = pieces[0].shape
    prompts = more - 1
    new_count = fresh_ref.shape[0]
    rows = new_count * GROUP
    kv_local = rows_local // rows
    heads = kv_local * GROUP
    tops, parts = [], []
    for s in range(n_seq):
        stats = pieces[s][prompts].astype(F32)
        folded = stats + pltpu.roll(stats, HD - prompts, 1)
        tops.append(folded)
        parts.append(pltpu.roll(folded, HD - 2 * prompts, 1))
    fresh = [fresh_ref[n] for n in range(new_count)]
    top = fresh[0]
    for other in fresh[1:] + tops:
        top = jnp.maximum(top, other)
    weights = [jnp.exp(f - top) for f in fresh]
    factors = [jnp.exp(t - top) for t in tops]
    total = weights[0]
    for w in weights[1:]:
        total = total + w
    for f, part in zip(factors, parts):
        total = total + f * part
    weights = [w / total for w in weights]
    factors = [f / total for f in factors]
    for r in range(prompts):
        sums = jnp.zeros((rows_local, HD), F32)
        for s in range(n_seq):
            sums = sums + factors[s][:, r : r + 1] * pieces[s][r].astype(F32)
        for n in range(new_count):
            sums = sums + weights[n][:, r : r + 1] * value_ref[r * new_count + n]
        for g in range(kv_local):
            for n in range(new_count):
                at = g * rows + n * GROUP
                held[g * GROUP : (g + 1) * GROUP, r * new_count + n] = sums[at : at + GROUP]
    half = heads // 2
    product = jnp.zeros(out_ref.shape, F32)
    for w_ref, at in ((wa_ref, 0), (wb_ref, half)):
        left = [held[h].astype(BF16) for h in range(at, at + half)]
        left = jnp.concatenate(left, axis=1)
        product = product + jnp.dot(left, w_ref[...], preferred_element_type=F32)
    out_ref[...] = product.astype(BF16)


def output_partial(pieces, fresh, values, weights):
    n_seq = len(pieces)
    new_count = fresh.shape[0]
    prompts = pieces[0].shape[0] - 1
    depth, columns = weights[0].shape
    return pl.pallas_call(
        functools.partial(output_kernel, n_seq),
        in_specs=[VMEM] * (n_seq + 4),
        out_specs=VMEM,
        out_shape=jax.ShapeDtypeStruct((prompts * new_count, columns), BF16),
        scratch_shapes=[pltpu.VMEM((2 * depth // HD, prompts * new_count, HD), F32)],
        compiler_params=pltpu.CompilerParams(vmem_limit_bytes=24 * MIB),
        name="output",
    )(*pieces, fresh, values, *weights)


def final_kernel(n_tp, *refs):
    pieces = refs[:n_tp]
    res_ref, out_ref = refs[n_tp:]
    prompts, new_count, _ = out_ref.shape
    total = pieces[0][...].astype(F32)
    for d in range(1, n_tp):
        total = total + pieces[d][...].astype(F32)
    for r in range(prompts):
        out_ref[r] = res_ref[r].astype(F32) + total[r * new_count : (r + 1) * new_count]


def final_sum(pieces, residual):
    n_tp = len(pieces)
    return pl.pallas_call(
        functools.partial(final_kernel, n_tp),
        in_specs=[VMEM] * (n_tp + 1),
        out_specs=VMEM,
        out_shape=jax.ShapeDtypeStruct(residual.shape, F32),
        compiler_params=pltpu.CompilerParams(vmem_limit_bytes=8 * MIB),
        name="final",
    )(*pieces, residual)


def on_device(
    prefill_states, kv_weight, page_counts, tail_tokens, new_query, new_keyval, residual, out_weight
):
    n_seq, n_tp = lax.axis_size("seq"), lax.axis_size("tp")
    own_rows, new_count, _ = new_query.shape
    prompts = page_counts.shape[0]
    pages = prefill_states.shape[0] // PAGE * n_seq
    query, new_kv = prepare(new_query, new_keyval)
    query = gather(query, "tp")
    acc, x, w, cosine, sine, cos_q, sin_q, meta = load(
        prefill_states, kv_weight, page_counts, tail_tokens, pages, new_count
    )
    new = stacked(query, new_kv, meta)
    k = rotated_keys(acc, x, w, cosine, sine, new)
    new = gather(new, "seq")
    *scores, own_q = partial_scores(new, k, cos_q, sin_q, meta, prompts, n_tp)
    va, oa = project_values(x, w, out_weight, 0, own_q)
    fresh, values = fresh_scores(new, own_q, cos_q, sin_q)
    weights, stats = softmax_weights(exchange(scores, "tp"), meta, va, pages, prompts)
    vb, ob = project_values(x, w, out_weight, 1, stats)
    chunks = weighted_values(gather(weights, "tp"), va, vb, meta, prompts)
    pieces = gather(summed(exchange(chunks, "tp"), stats), "seq")
    partial = output_partial(pieces, fresh, values, (oa, ob))
    return final_sum(gather(partial, "tp"), residual)


def solution(mesh):
    placed = (
        P(("groups", "seq"), "tp"),
        P("tp", None),
        P("groups"),
        P("groups"),
        P(("groups", "seq"), None, "tp"),
        P(("groups", "seq"), None, "tp"),
        P("groups", None, "seq"),
        P("tp", "seq"),
    )
    return jax.shard_map(
        on_device, mesh=mesh, in_specs=placed, out_specs=P("groups", None, "seq"), check_vma=False
    )
```

```python
import functools
import math

import jax
import jax.numpy as jnp
from jax import lax
from jax.experimental import pallas as pl
from jax.experimental.pallas import tpu as pltpu
from jax.sharding import PartitionSpec as P

QH = 64
KVH = 8
HD = 128
PAGE = 128
GROUP = QH // KVH
NEG = -1e30
F32 = jnp.float32
BF16 = jnp.bfloat16
MIB = 1 << 20

VMEM = pl.BlockSpec(memory_space=pltpu.VMEM)
SMEM = pl.BlockSpec(memory_space=pltpu.SMEM)
ANY = pl.BlockSpec(memory_space=pl.ANY)


def partner(me, entry, size):
    return me ^ ((size - entry) % size)


def pairs(value, axis, entry):
    size = lax.axis_size(axis)
    return lax.ppermute(value, axis, [(i, partner(i, entry, size)) for i in range(size)])


def exchange(chunks, axis):
    return [chunks[0]] + [pairs(chunks[i], axis, i) for i in range(1, len(chunks))]


def gather(value, axis):
    size = lax.axis_size(axis)
    return [value] + [pairs(value, axis, size - d) for d in range(1, size)]


def lane_freqs(rows):
    lane = lax.broadcasted_iota(jnp.int32, (rows, HD), 1) % (HD // 2)
    return jnp.exp(-(lane.astype(F32) * (2.0 / HD)) * math.log(500000.0))


def sine_sign(rows):
    lane = lax.broadcasted_iota(jnp.int32, (rows, HD), 1)
    return jnp.where(lane < HD // 2, -1.0, 1.0)


def in_hbm(value):
    return pltpu.with_memory_space_constraint(value, pltpu.HBM)


def by_row(rows, numbers):
    row = lax.broadcasted_iota(jnp.int32, (rows, HD), 0)
    out = jnp.zeros((rows, HD), F32)
    for i, number in enumerate(numbers):
        out = jnp.where(row == i, number.astype(F32), out)
    return out


def page_table(pages, prompts, counts, tails, meta):
    def one_prompt(r, start):
        length = (counts[r] - 1) * PAGE + tails[r]
        meta[3 * pages + r] = length

        def one_page(i, carry):
            meta[start + i] = r
            meta[pages + start + i] = i * PAGE
            meta[2 * pages + start + i] = jnp.minimum(length - i * PAGE, PAGE)
            return carry

        lax.fori_loop(0, counts[r], one_page, 0)
        return start + counts[r]

    lax.fori_loop(0, prompts, one_prompt, 0)


def rotation_tables(pages, local_pages, meta, cos_s, sin_s):
    freqs = lane_freqs(8)
    low = lax.broadcasted_iota(jnp.int32, (8, HD), 0).astype(F32) * freqs
    low_cos, low_sin = jnp.cos(low), jnp.sin(low)
    high = lax.broadcasted_iota(jnp.int32, (PAGE // 8, HD), 0).astype(F32) * 8.0
    high = high * lane_freqs(PAGE // 8)
    high_cos, high_sin = jnp.cos(high), jnp.sin(high)
    first = lax.axis_index("seq") * local_pages
    base = by_row(local_pages, [meta[pages + first + p] for p in range(local_pages)])
    base = base * lane_freqs(local_pages)
    base_cos, base_sin = jnp.cos(base), jnp.sin(base)
    sign = sine_sign(8)
    for i in range(PAGE // 8):
        c, s = high_cos[i : i + 1], high_sin[i : i + 1]
        cosine, sine = low_cos * c - low_sin * s, low_sin * c + low_cos * s
        for p in range(local_pages):
            at = slice(p * PAGE + i * 8, p * PAGE + i * 8 + 8)
            c, s = base_cos[p : p + 1], base_sin[p : p + 1]
            cos_s[at] = cosine * c - sine * s
            sin_s[at] = sign * (sine * c + cosine * s)


def pair_columns(w_ref, rows, pair, part):
    at = [(2 * head + part) * HD for head in (2 * pair, 2 * pair + 1)]
    return jnp.concatenate([w_ref[rows, c : c + HD] for c in at], axis=1)


def copies_of(x_hbm, w_hbm, x_ref, w_ref, sems, first, size, count):
    pairs_of = []
    for i in range(count):
        source, to = pl.ds(first + i * size, size), pl.ds(i * size, size)
        x_copy = pltpu.make_async_copy(x_hbm.at[:, source], x_ref.at[:, to], sems.at[2 * i])
        w_copy = pltpu.make_async_copy(w_hbm.at[source], w_ref.at[to], sems.at[2 * i + 1])
        x_copy.start()
        w_copy.start()
        pairs_of.append((x_copy, w_copy))
    return pairs_of


def add_block(x_ref, w_ref, rows, acc, out, fresh):
    tokens = x_ref.shape[0]
    tall = tokens // 2
    for pair in range(KVH // 2):
        weight = pair_columns(w_ref, rows, pair, 0)
        columns = slice(2 * pair * HD, 2 * (pair + 1) * HD)
        for start in range(0, tokens, tall):
            at = slice(start, start + tall)
            product = jnp.dot(x_ref[at, rows], weight, preferred_element_type=F32)
            out[at, columns] = product if fresh else acc[at, columns] + product


def load_kernel(pages, prompts, new_count, x_hbm, w_hbm, counts, tails, *refs):
    acc, x_ref, w_ref, cos_ref, sin_ref, cos_q, sin_q, meta, sems = refs
    tokens = x_ref.shape[0]
    size = x_ref.shape[1] // 3
    copies = copies_of(x_hbm, w_hbm, x_ref, w_ref, sems, 0, size, 3)
    page_table(pages, prompts, counts, tails, meta)
    rotation_tables(pages, tokens // PAGE, meta, cos_ref, sin_ref)
    spots = [meta[3 * pages + r] + n for r in range(prompts) for n in range(new_count)]
    angles = by_row(len(spots), spots) * lane_freqs(len(spots))
    cos_q[...] = jnp.cos(angles)
    sin_q[...] = jnp.sin(angles) * sine_sign(len(spots))
    for i in range(2):
        for copy in copies[i]:
            copy.wait()
        add_block(x_ref, w_ref, slice(i * size, (i + 1) * size), acc, acc, i == 0)
    for copy in copies[2]:
        copy.wait()


def load(x, kv_weight, counts, tails, pages, new_count):
    tokens, depth = x.shape
    columns = kv_weight.shape[1]
    prompts = counts.shape[0]
    part = depth // 4 * 3
    hbm = pl.BlockSpec(memory_space=pltpu.HBM)
    return pl.pallas_call(
        functools.partial(load_kernel, pages, prompts, new_count),
        in_specs=[hbm, hbm, SMEM, SMEM],
        out_specs=[VMEM] * 7 + [SMEM],
        out_shape=[
            pltpu.VMEM((tokens, KVH * HD), F32),
            pltpu.VMEM((tokens, part), BF16),
            pltpu.VMEM((part, columns), BF16),
            pltpu.VMEM((tokens, HD), F32),
            pltpu.VMEM((tokens, HD), F32),
            pltpu.VMEM((prompts * new_count, HD), F32),
            pltpu.VMEM((prompts * new_count, HD), F32),
            jax.ShapeDtypeStruct((3 * pages + prompts,), jnp.int32),
        ],
        scratch_shapes=[pltpu.SemaphoreType.DMA((6,))],
        compiler_params=pltpu.CompilerParams(vmem_limit_bytes=28 * MIB),
        cost_estimate=pl.CostEstimate(
            flops=tokens * depth * KVH * HD,
            bytes_accessed=2 * part * (tokens + columns),
            transcendentals=0,
        ),
        name="load",
    )(*[in_hbm(a) for a in (x, kv_weight, counts, tails)])


def keys_kernel(acc, xa_ref, wa_ref, x_hbm, w_hbm, cos_ref, sin_ref, after, k_ref, x_ref, w_ref, total, sems):
    tokens, size = x_ref.shape
    tall = tokens // 2
    ((x_copy, w_copy),) = copies_of(x_hbm, w_hbm, x_ref, w_ref, sems, 3 * size, size, 1)
    add_block(xa_ref, wa_ref, slice(2 * size, 3 * size), acc, total, False)
    x_copy.wait()
    w_copy.wait()
    for pair in range(KVH // 2):
        weight = pair_columns(w_ref, slice(None), pair, 0)
        columns = slice(2 * pair * HD, 2 * (pair + 1) * HD)
        for start in range(0, tokens, tall):
            at = slice(start, start + tall)
            product = total[at, columns] + jnp.dot(x_ref[at], weight, preferred_element_type=F32)
            cosine, sine = cos_ref[at], sin_ref[at]
            for h in range(2):
                k = product[:, h * HD : (h + 1) * HD]
                k = k * cosine + pltpu.roll(k, HD // 2, 1) * sine
                k_ref[at, (2 * pair + h) * HD : (2 * pair + h + 1) * HD] = k.astype(BF16)


def rotated_keys(acc, xa, wa, x, kv_weight, cosine, sine, after):
    tokens, depth = x.shape
    columns = kv_weight.shape[1]
    hbm = pl.BlockSpec(memory_space=pltpu.HBM)
    return pl.pallas_call(
        keys_kernel,
        in_specs=[VMEM] * 3 + [hbm] * 2 + [VMEM] * 2 + [ANY],
        out_specs=[VMEM] * 3,
        out_shape=[
            pltpu.VMEM((tokens, KVH * HD), BF16),
            pltpu.VMEM((tokens, depth // 4), BF16),
            pltpu.VMEM((depth // 4, columns), BF16),
        ],
        scratch_shapes=[
            pltpu.VMEM((tokens, KVH * HD), F32),
            pltpu.SemaphoreType.DMA((2,)),
        ],
        compiler_params=pltpu.CompilerParams(vmem_limit_bytes=24 * MIB),
        cost_estimate=pl.CostEstimate(
            flops=tokens * depth * KVH * HD, bytes_accessed=8 * MIB, transcendentals=0
        ),
        name="keys",
    )(acc, xa, wa, in_hbm(x), in_hbm(kv_weight), cosine, sine, after)


def values_kernel(first, xa_ref, wa_ref, xb_ref, wb_ref, o_hbm, after, v_ref, o_ref, sem):
    depth = o_ref.shape[0]
    copy = pltpu.make_async_copy(o_hbm.at[pl.ds(first * depth, depth)], o_ref, sem)
    copy.start()
    tokens, columns = v_ref.shape
    tall = tokens // 2
    pairs_here = columns // (2 * HD)
    for pair in range(pairs_here):
        weights = [pair_columns(w, slice(None), first * pairs_here + pair, 1) for w in (wa_ref, wb_ref)]
        for i in range(2):
            at = slice(i * tall, (i + 1) * tall)
            product = jnp.dot(xa_ref[at], weights[0], preferred_element_type=F32)
            product = product + jnp.dot(xb_ref[at], weights[1], preferred_element_type=F32)
            v_ref[at, 2 * pair * HD : 2 * (pair + 1) * HD] = product.astype(BF16)
    copy.wait()


def project_values(blocks, out_weight, first, after):
    tokens, depth = blocks[0].shape
    columns = KVH // 2 * HD
    rows = out_weight.shape[0] // 2
    return pl.pallas_call(
        functools.partial(values_kernel, first),
        in_specs=[VMEM] * 4 + [pl.BlockSpec(memory_space=pltpu.HBM), ANY],
        out_specs=[VMEM, VMEM],
        out_shape=[
            pltpu.VMEM((tokens, columns), BF16),
            pltpu.VMEM((rows, out_weight.shape[1]), BF16),
        ],
        scratch_shapes=[pltpu.SemaphoreType.DMA],
        compiler_params=pltpu.CompilerParams(vmem_limit_bytes=24 * MIB),
        cost_estimate=pl.CostEstimate(
            flops=2 * tokens * depth * columns, bytes_accessed=8 * MIB, transcendentals=0
        ),
        name="values",
    )(*blocks, in_hbm(out_weight), after)


def by_heads(row):
    return jnp.concatenate([row[:, c : c + HD] for c in range(0, row.shape[1], HD)], axis=0)


def prepare_kernel(q_ref, kv_ref, q_out, kv_out):
    for r in range(q_ref.shape[0]):
        q, kv = q_ref[r].astype(F32), kv_ref[r].astype(F32)
        for n in range(q_ref.shape[1]):
            q_out[r, n] = by_heads(q[n : n + 1]).astype(BF16)
            kv_out[r, n] = by_heads(kv[n : n + 1])


def prepare(new_query, new_keyval):
    own_rows, new_count, columns = new_query.shape
    shape = lambda a: (own_rows, new_count, a.shape[2] // HD, HD)
    return pl.pallas_call(
        prepare_kernel,
        in_specs=[VMEM, VMEM],
        out_specs=[VMEM, VMEM],
        out_shape=[
            jax.ShapeDtypeStruct(shape(new_query), BF16),
            jax.ShapeDtypeStruct(shape(new_keyval), F32),
        ],
        compiler_params=pltpu.CompilerParams(vmem_limit_bytes=8 * MIB),
        cost_estimate=pl.CostEstimate(flops=0, bytes_accessed=MIB, transcendentals=0),
        name="prepare",
    )(in_hbm(new_query), in_hbm(new_keyval))


def turned_kernel(n_tp, *refs):
    kv_ref, cos_q, sin_q, out_ref = refs[n_tp:]
    own_rows, new_count, heads, _ = refs[0].shape
    rows = new_count * GROUP
    kv_local = heads // GROUP
    me, seq = lax.axis_index("tp"), lax.axis_index("seq")
    for r in range(own_rows):
        spots = [pl.ds((seq * own_rows + r) * new_count + n, 1) for n in range(new_count)]
        turns = [(cos_q[spot], sin_q[spot]) for spot in spots]

        def turn(value, n):
            return value * turns[n][0] + pltpu.roll(value, HD // 2, 1) * turns[n][1]

        for d in range(n_tp):
            blocks = [refs[d][r, n].astype(F32) for n in range(new_count)]
            for g in range(kv_local):
                parts = [turn(q[g * GROUP : (g + 1) * GROUP], n) for n, q in enumerate(blocks)]
                at = ((me ^ d) * kv_local + g) * rows
                at = pl.ds(pl.multiple_of(at, rows), rows)
                out_ref[r, at] = jnp.concatenate(parts, axis=0).astype(BF16)
        fresh = []
        for n in range(new_count):
            row = lax.broadcasted_iota(jnp.int32, kv_ref.shape[2:], 0)
            fresh.append(jnp.where(row % 2 == 0, turn(kv_ref[r, n], n), kv_ref[r, n]))
        fresh.append(jnp.zeros((FRESH - new_count * 2 * kv_local, HD), F32))
        out_ref[r, KVH * rows :] = jnp.concatenate(fresh, axis=0).astype(BF16)


FRESH = 16


def turned(pieces, fresh, cos_q, sin_q):
    n_tp = len(pieces)
    own_rows, new_count, _, _ = pieces[0].shape
    rows = KVH * GROUP * new_count + FRESH
    return pl.pallas_call(
        functools.partial(turned_kernel, n_tp),
        in_specs=[VMEM] * (n_tp + 3),
        out_specs=VMEM,
        out_shape=jax.ShapeDtypeStruct((own_rows, rows, HD), BF16),
        compiler_params=pltpu.CompilerParams(vmem_limit_bytes=8 * MIB),
        name="turned",
    )(*pieces, fresh, cos_q, sin_q)


def scores_kernel(n_seq, n_tp, *refs):
    new = refs[:n_seq]
    k_ref, meta = refs[n_seq : n_seq + 2]
    outs = refs[n_seq + 2 : n_seq + 2 + n_tp]
    all_q, ready = refs[n_seq + 2 + n_tp :]
    own_rows = new[0].shape[0]
    local_pages = k_ref.shape[0] // PAGE
    rows = all_q.shape[1] // KVH
    count = all_q.shape[1] // n_tp
    scale = 1.0 / math.sqrt(HD)
    me = lax.axis_index("tp")
    seq = lax.axis_index("seq")
    first = seq * local_pages
    for ds in range(n_seq):
        for rr in range(own_rows):
            all_q[(seq ^ ds) * own_rows + rr] = new[ds][rr, : KVH * rows]
    for p in range(local_pages):
        request = meta[first + p]
        tokens = slice(p * PAGE, (p + 1) * PAGE)
        for head in range(KVH):
            k = k_ref[tokens, head * HD : (head + 1) * HD]
            q = all_q[request, head * rows : (head + 1) * rows]
            s = lax.dot_general(q, k, (((1,), (1,)), ((), ())), preferred_element_type=F32)
            ready[head * rows : (head + 1) * rows, tokens] = (s * scale).astype(BF16)
    for d in range(n_tp):
        outs[d][...] = ready[pl.ds(pl.multiple_of(partner(me, d, n_tp) * count, count), count)]


def partial_scores(new, k, meta, prompts, n_tp):
    n_seq = len(new)
    all_rows = new[0].shape[1] - FRESH
    tokens = k.shape[0]
    rows = all_rows // n_tp
    return pl.pallas_call(
        functools.partial(scores_kernel, n_seq, n_tp),
        in_specs=[VMEM] * (n_seq + 1) + [SMEM],
        out_specs=[VMEM] * n_tp,
        out_shape=[jax.ShapeDtypeStruct((rows, tokens), BF16)] * n_tp,
        scratch_shapes=[
            pltpu.VMEM((prompts, all_rows, HD), BF16),
            pltpu.VMEM((all_rows, tokens), BF16),
        ],
        compiler_params=pltpu.CompilerParams(vmem_limit_bytes=24 * MIB),
        cost_estimate=pl.CostEstimate(
            flops=2 * tokens * all_rows * HD, bytes_accessed=6 * MIB, transcendentals=0
        ),
        name="scores",
    )(*new, k, meta)


def fresh_kernel(n_seq, *refs):
    new = refs[:n_seq]
    _, score_ref, value_ref = refs[n_seq:]
    new_count, rows_local, _ = score_ref.shape
    own_rows = new[0].shape[0]
    rows = new_count * GROUP
    kv_local = rows_local // rows
    scale = 1.0 / math.sqrt(HD)
    seq = lax.axis_index("seq")
    own = pl.ds(pl.multiple_of(lax.axis_index("tp") * rows_local, rows_local), rows_local)
    step = lax.broadcasted_iota(jnp.int32, (rows_local, HD), 0) % rows // GROUP
    lane = lax.broadcasted_iota(jnp.int32, (rows_local, HD), 1)
    found = [jnp.full((rows_local, HD), NEG, F32) for _ in range(new_count)]

    def spread(block, first):
        parts = [block[first + 2 * g : first + 2 * g + 1] for g in range(kv_local)]
        return jnp.concatenate([jnp.broadcast_to(a, (rows, HD)) for a in parts], axis=0)

    for ds in range(n_seq):
        for rr in range(own_rows):
            request = (seq ^ ds) * own_rows + rr
            q = new[ds][rr, own].astype(F32)
            both = new[ds][rr, KVH * rows :].astype(F32)
            for n in range(new_count):
                first = n * 2 * kv_local
                s = jnp.sum(q * spread(both, first), axis=1, keepdims=True) * scale
                found[n] = jnp.where((lane == request) & (step >= n), s, found[n])
                value_ref[request * new_count + n] = spread(both, first + 1)
    for n in range(new_count):
        score_ref[n] = found[n]


def fresh_scores(new, after, prompts, new_count, n_tp):
    n_seq = len(new)
    rows = (new[0].shape[1] - FRESH) // n_tp
    return pl.pallas_call(
        functools.partial(fresh_kernel, n_seq),
        in_specs=[VMEM] * n_seq + [ANY],
        out_specs=[VMEM, VMEM],
        out_shape=[
            jax.ShapeDtypeStruct((new_count, rows, HD), F32),
            jax.ShapeDtypeStruct((prompts * new_count, rows, HD), F32),
        ],
        compiler_params=pltpu.CompilerParams(vmem_limit_bytes=16 * MIB),
        cost_estimate=pl.CostEstimate(flops=0, bytes_accessed=2 * MIB, transcendentals=0),
        name="fresh",
    )(*new, after)


def weights_kernel(pages, prompts, n_tp, *refs):
    chunks = refs[:n_tp]
    meta, _, w_ref, stats_ref = refs[n_tp:]
    rows, tokens = w_ref.shape
    local_pages = tokens // PAGE
    first = lax.axis_index("seq") * local_pages
    lane = lax.broadcasted_iota(jnp.int32, (rows, PAGE), 1)
    scores, maxima, masks, owners = [], [], [], []
    for p in range(local_pages):
        at = slice(p * PAGE, (p + 1) * PAGE)
        total = chunks[0][:, at].astype(F32)
        for d in range(1, n_tp):
            total = total + chunks[d][:, at].astype(F32)
        mask = lane < meta[2 * pages + first + p]
        total = jnp.where(mask, total, NEG)
        masks.append(mask)
        scores.append(total)
        maxima.append(jnp.max(total, axis=1, keepdims=True))
        owners.append(meta[first + p])
    quarter = lane // prompts
    spot = lane % prompts
    stats = jnp.where(quarter == 0, NEG, 0.0)
    sums = []
    for p in range(local_pages):
        top = maxima[p]
        for other in range(local_pages):
            if other != p:
                top = jnp.where(owners[p] == owners[other], jnp.maximum(top, maxima[other]), top)
        high = top.astype(BF16).astype(F32)
        low = (top - high).astype(BF16).astype(F32)
        w = jnp.where(masks[p], jnp.exp(scores[p] - (high + low)), 0.0)
        w_ref[:, p * PAGE : (p + 1) * PAGE] = w.astype(BF16)
        here = spot == owners[p]
        stats = jnp.where(here & (quarter == 0), high, stats)
        stats = jnp.where(here & (quarter == 1), low, stats)
        part = jnp.sum(w, axis=1, keepdims=True)
        stats = stats + jnp.where(here & (quarter == 2), part, 0.0)
    high = stats.astype(BF16).astype(F32)
    low = pltpu.roll(stats - high, prompts, 1)
    stats_ref[...] = jnp.where(quarter == 3, low, stats).astype(BF16)


def softmax_weights(chunks, meta, after, pages, prompts):
    n_tp = len(chunks)
    rows, tokens = chunks[0].shape
    return pl.pallas_call(
        functools.partial(weights_kernel, pages, prompts, n_tp),
        in_specs=[VMEM] * n_tp + [SMEM, ANY],
        out_specs=[VMEM, VMEM],
        out_shape=[
            jax.ShapeDtypeStruct((rows, tokens), BF16),
            jax.ShapeDtypeStruct((rows, PAGE), BF16),
        ],
        compiler_params=pltpu.CompilerParams(vmem_limit_bytes=8 * MIB),
        name="weights",
    )(*chunks, meta, after)


def weighted_kernel(n_tp, *refs):
    pieces = refs[:n_tp]
    va_ref, vb_ref, meta = refs[n_tp : n_tp + 3]
    outs = refs[n_tp + 3 : n_tp + 3 + n_tp]
    ready, total = refs[n_tp + 3 + n_tp :]
    rows_local, tokens_here = pieces[0].shape
    kv_local = KVH // n_tp
    rows = rows_local // kv_local
    local_pages = tokens_here // PAGE
    first = lax.axis_index("seq") * local_pages
    me = lax.axis_index("tp")
    own = [pl.ds(pl.multiple_of(partner(me, d, n_tp) * rows_local, rows_local), rows_local) for d in range(n_tp)]
    for d in range(n_tp):
        at = pl.multiple_of((me ^ d) * rows_local, rows_local)
        ready[pl.ds(at, rows_local)] = pieces[d][...]
    total[...] = jnp.zeros_like(total)
    half = va_ref.shape[1] // HD
    for p in range(local_pages):
        request = meta[first + p]
        tokens = slice(p * PAGE, (p + 1) * PAGE)
        for head in range(KVH):
            v_ref = va_ref if head < half else vb_ref
            v = v_ref[tokens, head % half * HD : (head % half + 1) * HD]
            at = slice(head * rows, (head + 1) * rows)
            total[request, at] += jnp.dot(ready[at, tokens], v, preferred_element_type=F32)
    for d in range(n_tp):
        outs[d][...] = total[:, own[d]].astype(BF16)


def weighted_values(pieces, va, vb, meta, prompts):
    n_tp = len(pieces)
    rows, tokens = pieces[0].shape
    return pl.pallas_call(
        functools.partial(weighted_kernel, n_tp),
        in_specs=[VMEM] * (n_tp + 2) + [SMEM],
        out_specs=[VMEM] * n_tp,
        out_shape=[jax.ShapeDtypeStruct((prompts, rows, HD), BF16)] * n_tp,
        scratch_shapes=[
            pltpu.VMEM((rows * n_tp, tokens), BF16),
            pltpu.VMEM((prompts, rows * n_tp, HD), F32),
        ],
        compiler_params=pltpu.CompilerParams(vmem_limit_bytes=24 * MIB),
        cost_estimate=pl.CostEstimate(
            flops=2 * tokens * rows * n_tp * HD, bytes_accessed=8 * MIB, transcendentals=0
        ),
        name="weighted",
    )(*pieces, va, vb, meta)


def summed_kernel(n_tp, *refs):
    chunks = refs[:n_tp]
    stats_ref, out_ref = refs[n_tp:]
    prompts = chunks[0].shape[0]
    total = chunks[0][...].astype(F32)
    for d in range(1, n_tp):
        total = total + chunks[d][...].astype(F32)
    out_ref[:prompts] = total.astype(BF16)
    out_ref[prompts] = stats_ref[...]


def summed(chunks, stats):
    n_tp = len(chunks)
    prompts, rows, _ = chunks[0].shape
    return pl.pallas_call(
        functools.partial(summed_kernel, n_tp),
        in_specs=[VMEM] * (n_tp + 1),
        out_specs=VMEM,
        out_shape=jax.ShapeDtypeStruct((prompts + 1, rows, HD), BF16),
        compiler_params=pltpu.CompilerParams(vmem_limit_bytes=8 * MIB),
        cost_estimate=pl.CostEstimate(flops=0, bytes_accessed=4 * MIB, transcendentals=0),
        name="summed",
    )(*chunks, stats)


def output_kernel(n_seq, *refs):
    pieces = refs[:n_seq]
    fresh_ref, value_ref, wa_ref, wb_ref, out_ref, held = refs[n_seq:]
    more, rows_local, _ = pieces[0].shape
    prompts = more - 1
    new_count = fresh_ref.shape[0]
    rows = new_count * GROUP
    kv_local = rows_local // rows
    heads = kv_local * GROUP
    tops, parts = [], []
    for s in range(n_seq):
        stats = pieces[s][prompts].astype(F32)
        folded = stats + pltpu.roll(stats, HD - prompts, 1)
        tops.append(folded)
        parts.append(pltpu.roll(folded, HD - 2 * prompts, 1))
    fresh = [fresh_ref[n] for n in range(new_count)]
    top = fresh[0]
    for other in fresh[1:] + tops:
        top = jnp.maximum(top, other)
    weights = [jnp.exp(f - top) for f in fresh]
    factors = [jnp.exp(t - top) for t in tops]
    total = weights[0]
    for w in weights[1:]:
        total = total + w
    for f, part in zip(factors, parts):
        total = total + f * part
    weights = [w / total for w in weights]
    factors = [f / total for f in factors]
    for r in range(prompts):
        sums = jnp.zeros((rows_local, HD), F32)
        for s in range(n_seq):
            sums = sums + factors[s][:, r : r + 1] * pieces[s][r].astype(F32)
        for n in range(new_count):
            sums = sums + weights[n][:, r : r + 1] * value_ref[r * new_count + n]
        for g in range(kv_local):
            for n in range(new_count):
                at = g * rows + n * GROUP
                held[g * GROUP : (g + 1) * GROUP, r * new_count + n] = sums[at : at + GROUP]
    half = heads // 2
    product = jnp.zeros(out_ref.shape, F32)
    for w_ref, at in ((wa_ref, 0), (wb_ref, half)):
        left = [held[h].astype(BF16) for h in range(at, at + half)]
        left = jnp.concatenate(left, axis=1)
        product = product + jnp.dot(left, w_ref[...], preferred_element_type=F32)
    out_ref[...] = product.astype(BF16)


def output_partial(pieces, fresh, values, weights):
    n_seq = len(pieces)
    new_count = fresh.shape[0]
    prompts = pieces[0].shape[0] - 1
    depth, columns = weights[0].shape
    return pl.pallas_call(
        functools.partial(output_kernel, n_seq),
        in_specs=[VMEM] * (n_seq + 4),
        out_specs=VMEM,
        out_shape=jax.ShapeDtypeStruct((prompts * new_count, columns), BF16),
        scratch_shapes=[pltpu.VMEM((2 * depth // HD, prompts * new_count, HD), F32)],
        compiler_params=pltpu.CompilerParams(vmem_limit_bytes=24 * MIB),
        name="output",
    )(*pieces, fresh, values, *weights)


def final_kernel(n_tp, *refs):
    pieces = refs[:n_tp]
    res_ref, out_ref = refs[n_tp:]
    prompts, new_count, _ = out_ref.shape
    total = pieces[0][...].astype(F32)
    for d in range(1, n_tp):
        total = total + pieces[d][...].astype(F32)
    for r in range(prompts):
        out_ref[r] = res_ref[r].astype(F32) + total[r * new_count : (r + 1) * new_count]


def final_sum(pieces, residual):
    n_tp = len(pieces)
    return pl.pallas_call(
        functools.partial(final_kernel, n_tp),
        in_specs=[VMEM] * (n_tp + 1),
        out_specs=VMEM,
        out_shape=jax.ShapeDtypeStruct(residual.shape, F32),
        compiler_params=pltpu.CompilerParams(vmem_limit_bytes=8 * MIB),
        name="final",
    )(*pieces, residual)


def on_device(
    prefill_states, kv_weight, page_counts, tail_tokens, new_query, new_keyval, residual, out_weight
):
    n_seq, n_tp = lax.axis_size("seq"), lax.axis_size("tp")
    own_rows, new_count, _ = new_query.shape
    prompts = page_counts.shape[0]
    pages = prefill_states.shape[0] // PAGE * n_seq
    query, new_kv = prepare(new_query, new_keyval)
    query = gather(query, "tp")
    acc, xa, wa, cosine, sine, cos_q, sin_q, meta = load(
        prefill_states, kv_weight, page_counts, tail_tokens, pages, new_count
    )
    new = turned(query, new_kv, cos_q, sin_q)
    k, xb, wb = rotated_keys(acc, xa, wa, prefill_states, kv_weight, cosine, sine, new)
    new = gather(new, "seq")
    scores = partial_scores(new, k, meta, prompts, n_tp)
    va, oa = project_values((xa, wa, xb, wb), out_weight, 0, scores[0])
    weights, stats = softmax_weights(exchange(scores, "tp"), meta, va, pages, prompts)
    vb, ob = project_values((xa, wa, xb, wb), out_weight, 1, stats)
    fresh, values = fresh_scores(new, stats, prompts, new_count, n_tp)
    chunks = weighted_values(gather(weights, "tp"), va, vb, meta, prompts)
    pieces = gather(summed(exchange(chunks, "tp"), stats), "seq")
    partial = output_partial(pieces, fresh, values, (oa, ob))
    return final_sum(gather(partial, "tp"), residual)


def solution(mesh):
    placed = (
        P(("groups", "seq"), "tp"),
        P("tp", None),
        P("groups"),
        P("groups"),
        P(("groups", "seq"), None, "tp"),
        P(("groups", "seq"), None, "tp"),
        P("groups", None, "seq"),
        P("tp", "seq"),
    )
    return jax.shard_map(
        on_device, mesh=mesh, in_specs=placed, out_specs=P("groups", None, "seq"), check_vma=False
    )
```

```python
import functools
import math

import jax
import jax.numpy as jnp
from jax import lax
from jax.experimental import pallas as pl
from jax.experimental.pallas import tpu as pltpu
from jax.sharding import PartitionSpec as P

QH = 64
KVH = 8
HD = 128
PAGE = 128
GROUP = QH // KVH
NEG = -1e30
F32 = jnp.float32
BF16 = jnp.bfloat16
MIB = 1 << 20

VMEM = pl.BlockSpec(memory_space=pltpu.VMEM)
SMEM = pl.BlockSpec(memory_space=pltpu.SMEM)
ANY = pl.BlockSpec(memory_space=pl.ANY)


def pairs(value, axis, d):
    return lax.ppermute(value, axis, [(i, i ^ d) for i in range(lax.axis_size(axis))])


def partner(me, entry, size):
    return me ^ ((size - entry) % size)


def exchange(chunks, axis):
    size = len(chunks)
    return [chunks[0]] + [pairs(chunks[i], axis, size - i) for i in range(1, size)]


def gather(value, axis):
    return [value] + [pairs(value, axis, d) for d in range(1, lax.axis_size(axis))]


def gather_by_chips(value, axis):
    got = [value]
    for d in range(1, lax.axis_size(axis)):
        got.append(pairs(got[d - 1], axis, 1) if d % 2 else pairs(value, axis, d))
    return got


def lane_freqs(rows):
    lane = lax.broadcasted_iota(jnp.int32, (rows, HD), 1) % (HD // 2)
    return jnp.exp(-(lane.astype(F32) * (2.0 / HD)) * math.log(500000.0))


def sine_sign(rows):
    lane = lax.broadcasted_iota(jnp.int32, (rows, HD), 1)
    return jnp.where(lane < HD // 2, -1.0, 1.0)


def in_hbm(value):
    return pltpu.with_memory_space_constraint(value, pltpu.HBM)


def by_row(rows, numbers):
    row = lax.broadcasted_iota(jnp.int32, (rows, HD), 0)
    out = jnp.zeros((rows, HD), F32)
    for i, number in enumerate(numbers):
        out = jnp.where(row == i, number.astype(F32), out)
    return out


def page_table(pages, prompts, counts, tails, meta):
    def one_prompt(r, start):
        length = (counts[r] - 1) * PAGE + tails[r]
        meta[3 * pages + r] = length

        def one_page(i, carry):
            meta[start + i] = r
            meta[pages + start + i] = i * PAGE
            meta[2 * pages + start + i] = jnp.minimum(length - i * PAGE, PAGE)
            return carry

        lax.fori_loop(0, counts[r], one_page, 0)
        return start + counts[r]

    lax.fori_loop(0, prompts, one_prompt, 0)


def rotation_tables(pages, local_pages, meta, cos_s, sin_s):
    freqs = lane_freqs(8)
    low = lax.broadcasted_iota(jnp.int32, (8, HD), 0).astype(F32) * freqs
    low_cos, low_sin = jnp.cos(low), jnp.sin(low)
    high = lax.broadcasted_iota(jnp.int32, (PAGE // 8, HD), 0).astype(F32) * 8.0
    high = high * lane_freqs(PAGE // 8)
    high_cos, high_sin = jnp.cos(high), jnp.sin(high)
    first = lax.axis_index("seq") * local_pages
    base = by_row(local_pages, [meta[pages + first + p] for p in range(local_pages)])
    base = base * lane_freqs(local_pages)
    base_cos, base_sin = jnp.cos(base), jnp.sin(base)
    sign = sine_sign(8)
    for i in range(PAGE // 8):
        c, s = high_cos[i : i + 1], high_sin[i : i + 1]
        cosine, sine = low_cos * c - low_sin * s, low_sin * c + low_cos * s
        for p in range(local_pages):
            at = slice(p * PAGE + i * 8, p * PAGE + i * 8 + 8)
            c, s = base_cos[p : p + 1], base_sin[p : p + 1]
            cos_s[at] = cosine * c - sine * s
            sin_s[at] = sign * (sine * c + cosine * s)


def pair_columns(w_ref, rows, pair, part):
    at = [(2 * head + part) * HD for head in (2 * pair, 2 * pair + 1)]
    return jnp.concatenate([w_ref[rows, c : c + HD] for c in at], axis=1)


def copies_of(x_hbm, w_hbm, x_ref, w_ref, sems, first, size, count):
    pairs_of = []
    for i in range(count):
        source, to = pl.ds(first + i * size, size), pl.ds(i * size, size)
        x_copy = pltpu.make_async_copy(x_hbm.at[:, source], x_ref.at[:, to], sems.at[2 * i])
        w_copy = pltpu.make_async_copy(w_hbm.at[source], w_ref.at[to], sems.at[2 * i + 1])
        x_copy.start()
        w_copy.start()
        pairs_of.append((x_copy, w_copy))
    return pairs_of


def add_block(x_ref, w_ref, rows, acc, out, fresh):
    tokens = x_ref.shape[0]
    tall = tokens // 2
    for pair in range(KVH // 2):
        weight = pair_columns(w_ref, rows, pair, 0)
        columns = slice(2 * pair * HD, 2 * (pair + 1) * HD)
        for start in range(0, tokens, tall):
            at = slice(start, start + tall)
            product = jnp.dot(x_ref[at, rows], weight, preferred_element_type=F32)
            out[at, columns] = product if fresh else acc[at, columns] + product


def load_kernel(pages, prompts, new_count, x_hbm, w_hbm, counts, tails, *refs):
    acc, x_ref, w_ref, cos_ref, sin_ref, cos_q, sin_q, meta, sems = refs
    tokens = x_ref.shape[0]
    size = x_ref.shape[1] // 3
    copies = copies_of(x_hbm, w_hbm, x_ref, w_ref, sems, 0, size, 3)
    page_table(pages, prompts, counts, tails, meta)
    rotation_tables(pages, tokens // PAGE, meta, cos_ref, sin_ref)
    spots = [meta[3 * pages + r] + n for r in range(prompts) for n in range(new_count)]
    angles = by_row(len(spots), spots) * lane_freqs(len(spots))
    cos_q[...] = jnp.cos(angles)
    sin_q[...] = jnp.sin(angles) * sine_sign(len(spots))
    for copy in copies[0] + copies[1]:
        copy.wait()
    add_block(x_ref, w_ref, slice(0, 2 * size), acc, acc, True)
    for copy in copies[2]:
        copy.wait()


def load(x, kv_weight, counts, tails, pages, new_count):
    tokens, depth = x.shape
    columns = kv_weight.shape[1]
    prompts = counts.shape[0]
    part = depth // 4 * 3
    hbm = pl.BlockSpec(memory_space=pltpu.HBM)
    return pl.pallas_call(
        functools.partial(load_kernel, pages, prompts, new_count),
        in_specs=[hbm, hbm, SMEM, SMEM],
        out_specs=[VMEM] * 7 + [SMEM],
        out_shape=[
            pltpu.VMEM((tokens, KVH * HD), F32),
            pltpu.VMEM((tokens, part), BF16),
            pltpu.VMEM((part, columns), BF16),
            pltpu.VMEM((tokens, HD), F32),
            pltpu.VMEM((tokens, HD), F32),
            pltpu.VMEM((prompts * new_count, HD), F32),
            pltpu.VMEM((prompts * new_count, HD), F32),
            jax.ShapeDtypeStruct((3 * pages + prompts,), jnp.int32),
        ],
        scratch_shapes=[pltpu.SemaphoreType.DMA((6,))],
        compiler_params=pltpu.CompilerParams(vmem_limit_bytes=28 * MIB),
        cost_estimate=pl.CostEstimate(
            flops=tokens * depth * KVH * HD,
            bytes_accessed=2 * part * (tokens + columns),
            transcendentals=0,
        ),
        name="load",
    )(*[in_hbm(a) for a in (x, kv_weight, counts, tails)])


def keys_kernel(acc, xa_ref, wa_ref, x_hbm, w_hbm, cos_ref, sin_ref, after, k_ref, x_ref, w_ref, total, sems):
    tokens, size = x_ref.shape
    tall = tokens // 2
    ((x_copy, w_copy),) = copies_of(x_hbm, w_hbm, x_ref, w_ref, sems, 3 * size, size, 1)
    add_block(xa_ref, wa_ref, slice(2 * size, 3 * size), acc, total, False)
    x_copy.wait()
    w_copy.wait()
    for pair in range(KVH // 2):
        weight = pair_columns(w_ref, slice(None), pair, 0)
        columns = slice(2 * pair * HD, 2 * (pair + 1) * HD)
        for start in range(0, tokens, tall):
            at = slice(start, start + tall)
            product = total[at, columns] + jnp.dot(x_ref[at], weight, preferred_element_type=F32)
            cosine, sine = cos_ref[at], sin_ref[at]
            for h in range(2):
                k = product[:, h * HD : (h + 1) * HD]
                k = k * cosine + pltpu.roll(k, HD // 2, 1) * sine
                k_ref[at, (2 * pair + h) * HD : (2 * pair + h + 1) * HD] = k.astype(BF16)


def rotated_keys(acc, xa, wa, x, kv_weight, cosine, sine, after):
    tokens, depth = x.shape
    columns = kv_weight.shape[1]
    hbm = pl.BlockSpec(memory_space=pltpu.HBM)
    return pl.pallas_call(
        keys_kernel,
        in_specs=[VMEM] * 3 + [hbm] * 2 + [VMEM] * 2 + [ANY],
        out_specs=[VMEM] * 3,
        out_shape=[
            pltpu.VMEM((tokens, KVH * HD), BF16),
            pltpu.VMEM((tokens, depth // 4), BF16),
            pltpu.VMEM((depth // 4, columns), BF16),
        ],
        scratch_shapes=[
            pltpu.VMEM((tokens, KVH * HD), F32),
            pltpu.SemaphoreType.DMA((2,)),
        ],
        compiler_params=pltpu.CompilerParams(vmem_limit_bytes=24 * MIB),
        cost_estimate=pl.CostEstimate(
            flops=tokens * depth * KVH * HD, bytes_accessed=8 * MIB, transcendentals=0
        ),
        name="keys",
    )(acc, xa, wa, in_hbm(x), in_hbm(kv_weight), cosine, sine, after)


def values_kernel(first, xa_ref, wa_ref, xb_ref, wb_ref, o_hbm, after, v_ref, o_ref, sem):
    depth = o_ref.shape[0]
    copy = pltpu.make_async_copy(o_hbm.at[pl.ds(first * depth, depth)], o_ref, sem)
    copy.start()
    tokens, columns = v_ref.shape
    tall = tokens // 2
    pairs_here = columns // (2 * HD)
    for pair in range(pairs_here):
        weights = [pair_columns(w, slice(None), first * pairs_here + pair, 1) for w in (wa_ref, wb_ref)]
        for i in range(2):
            at = slice(i * tall, (i + 1) * tall)
            product = jnp.dot(xa_ref[at], weights[0], preferred_element_type=F32)
            product = product + jnp.dot(xb_ref[at], weights[1], preferred_element_type=F32)
            v_ref[at, 2 * pair * HD : 2 * (pair + 1) * HD] = product.astype(BF16)
    copy.wait()


def project_values(blocks, out_weight, first, after):
    tokens, depth = blocks[0].shape
    columns = KVH // 2 * HD
    rows = out_weight.shape[0] // 2
    return pl.pallas_call(
        functools.partial(values_kernel, first),
        in_specs=[VMEM] * 4 + [pl.BlockSpec(memory_space=pltpu.HBM), ANY],
        out_specs=[VMEM, VMEM],
        out_shape=[
            pltpu.VMEM((tokens, columns), BF16),
            pltpu.VMEM((rows, out_weight.shape[1]), BF16),
        ],
        scratch_shapes=[pltpu.SemaphoreType.DMA],
        compiler_params=pltpu.CompilerParams(vmem_limit_bytes=24 * MIB),
        cost_estimate=pl.CostEstimate(
            flops=2 * tokens * depth * columns, bytes_accessed=8 * MIB, transcendentals=0
        ),
        name="values",
    )(*blocks, in_hbm(out_weight), after)


def by_heads(row):
    return jnp.concatenate([row[:, c : c + HD] for c in range(0, row.shape[1], HD)], axis=0)


def prepare_kernel(q_ref, kv_ref, q_out, kv_out):
    for r in range(q_ref.shape[0]):
        q, kv = q_ref[r].astype(F32), kv_ref[r].astype(F32)
        for n in range(q_ref.shape[1]):
            q_out[r, n] = by_heads(q[n : n + 1]).astype(BF16)
            kv_out[r, n] = by_heads(kv[n : n + 1])


def prepare(new_query, new_keyval):
    own_rows, new_count, columns = new_query.shape
    shape = lambda a: (own_rows, new_count, a.shape[2] // HD, HD)
    return pl.pallas_call(
        prepare_kernel,
        in_specs=[VMEM, VMEM],
        out_specs=[VMEM, VMEM],
        out_shape=[
            jax.ShapeDtypeStruct(shape(new_query), BF16),
            jax.ShapeDtypeStruct(shape(new_keyval), F32),
        ],
        compiler_params=pltpu.CompilerParams(vmem_limit_bytes=8 * MIB),
        cost_estimate=pl.CostEstimate(flops=0, bytes_accessed=MIB, transcendentals=0),
        name="prepare",
    )(in_hbm(new_query), in_hbm(new_keyval))


def turned_kernel(n_tp, *refs):
    kv_ref, cos_q, sin_q, out_ref = refs[n_tp:]
    own_rows, new_count, heads, _ = refs[0].shape
    rows = new_count * GROUP
    kv_local = heads // GROUP
    me, seq = lax.axis_index("tp"), lax.axis_index("seq")
    for r in range(own_rows):
        spots = [pl.ds((seq * own_rows + r) * new_count + n, 1) for n in range(new_count)]
        turns = [(cos_q[spot], sin_q[spot]) for spot in spots]

        def turn(value, n):
            return value * turns[n][0] + pltpu.roll(value, HD // 2, 1) * turns[n][1]

        for d in range(n_tp):
            blocks = [refs[d][r, n].astype(F32) for n in range(new_count)]
            for g in range(kv_local):
                parts = [turn(q[g * GROUP : (g + 1) * GROUP], n) for n, q in enumerate(blocks)]
                at = ((me ^ d) * kv_local + g) * rows
                at = pl.ds(pl.multiple_of(at, rows), rows)
                out_ref[r, at] = jnp.concatenate(parts, axis=0).astype(BF16)
        fresh = []
        for n in range(new_count):
            row = lax.broadcasted_iota(jnp.int32, kv_ref.shape[2:], 0)
            fresh.append(jnp.where(row % 2 == 0, turn(kv_ref[r, n], n), kv_ref[r, n]))
        fresh.append(jnp.zeros((FRESH - new_count * 2 * kv_local, HD), F32))
        out_ref[r, KVH * rows :] = jnp.concatenate(fresh, axis=0).astype(BF16)


FRESH = 16


def turned(pieces, fresh, cos_q, sin_q):
    n_tp = len(pieces)
    own_rows, new_count, _, _ = pieces[0].shape
    rows = KVH * GROUP * new_count + FRESH
    return pl.pallas_call(
        functools.partial(turned_kernel, n_tp),
        in_specs=[VMEM] * (n_tp + 3),
        out_specs=VMEM,
        out_shape=jax.ShapeDtypeStruct((own_rows, rows, HD), BF16),
        compiler_params=pltpu.CompilerParams(vmem_limit_bytes=8 * MIB),
        name="turned",
    )(*pieces, fresh, cos_q, sin_q)


def scores_kernel(n_seq, n_tp, *refs):
    new = refs[:n_seq]
    k_ref, meta = refs[n_seq : n_seq + 2]
    outs = refs[n_seq + 2 : n_seq + 2 + n_tp]
    all_q, ready = refs[n_seq + 2 + n_tp :]
    own_rows = new[0].shape[0]
    local_pages = k_ref.shape[0] // PAGE
    rows = all_q.shape[1] // KVH
    count = all_q.shape[1] // n_tp
    scale = 1.0 / math.sqrt(HD)
    me = lax.axis_index("tp")
    seq = lax.axis_index("seq")
    first = seq * local_pages
    for ds in range(n_seq):
        for rr in range(own_rows):
            all_q[(seq ^ ds) * own_rows + rr] = new[ds][rr, : KVH * rows]
    for p in range(local_pages):
        request = meta[first + p]
        tokens = slice(p * PAGE, (p + 1) * PAGE)
        for head in range(KVH):
            k = k_ref[tokens, head * HD : (head + 1) * HD]
            q = all_q[request, head * rows : (head + 1) * rows]
            s = lax.dot_general(q, k, (((1,), (1,)), ((), ())), preferred_element_type=F32)
            ready[head * rows : (head + 1) * rows, tokens] = (s * scale).astype(BF16)
    for d in range(n_tp):
        outs[d][...] = ready[pl.ds(pl.multiple_of(partner(me, d, n_tp) * count, count), count)]


def partial_scores(new, k, meta, prompts, n_tp):
    n_seq = len(new)
    all_rows = new[0].shape[1] - FRESH
    tokens = k.shape[0]
    rows = all_rows // n_tp
    return pl.pallas_call(
        functools.partial(scores_kernel, n_seq, n_tp),
        in_specs=[VMEM] * (n_seq + 1) + [SMEM],
        out_specs=[VMEM] * n_tp,
        out_shape=[jax.ShapeDtypeStruct((rows, tokens), BF16)] * n_tp,
        scratch_shapes=[
            pltpu.VMEM((prompts, all_rows, HD), BF16),
            pltpu.VMEM((all_rows, tokens), BF16),
        ],
        compiler_params=pltpu.CompilerParams(vmem_limit_bytes=24 * MIB),
        cost_estimate=pl.CostEstimate(
            flops=2 * tokens * all_rows * HD, bytes_accessed=6 * MIB, transcendentals=0
        ),
        name="scores",
    )(*new, k, meta)


def fresh_kernel(n_seq, *refs):
    new = refs[:n_seq]
    _, score_ref, value_ref = refs[n_seq:]
    new_count, rows_local, _ = score_ref.shape
    own_rows = new[0].shape[0]
    rows = new_count * GROUP
    kv_local = rows_local // rows
    scale = 1.0 / math.sqrt(HD)
    seq = lax.axis_index("seq")
    own = pl.ds(pl.multiple_of(lax.axis_index("tp") * rows_local, rows_local), rows_local)
    step = lax.broadcasted_iota(jnp.int32, (rows_local, HD), 0) % rows // GROUP
    lane = lax.broadcasted_iota(jnp.int32, (rows_local, HD), 1)
    found = [jnp.full((rows_local, HD), NEG, F32) for _ in range(new_count)]

    def spread(block, first):
        parts = [block[first + 2 * g : first + 2 * g + 1] for g in range(kv_local)]
        return jnp.concatenate([jnp.broadcast_to(a, (rows, HD)) for a in parts], axis=0)

    for ds in range(n_seq):
        for rr in range(own_rows):
            request = (seq ^ ds) * own_rows + rr
            q = new[ds][rr, own].astype(F32)
            both = new[ds][rr, KVH * rows :].astype(F32)
            for n in range(new_count):
                first = n * 2 * kv_local
                s = jnp.sum(q * spread(both, first), axis=1, keepdims=True) * scale
                found[n] = jnp.where((lane == request) & (step >= n), s, found[n])
                value_ref[request * new_count + n] = spread(both, first + 1)
    for n in range(new_count):
        score_ref[n] = found[n]


def fresh_scores(new, after, prompts, new_count, n_tp):
    n_seq = len(new)
    rows = (new[0].shape[1] - FRESH) // n_tp
    return pl.pallas_call(
        functools.partial(fresh_kernel, n_seq),
        in_specs=[VMEM] * n_seq + [ANY],
        out_specs=[VMEM, VMEM],
        out_shape=[
            jax.ShapeDtypeStruct((new_count, rows, HD), F32),
            jax.ShapeDtypeStruct((prompts * new_count, rows, HD), F32),
        ],
        compiler_params=pltpu.CompilerParams(vmem_limit_bytes=16 * MIB),
        cost_estimate=pl.CostEstimate(flops=0, bytes_accessed=2 * MIB, transcendentals=0),
        name="fresh",
    )(*new, after)


def weights_kernel(pages, prompts, n_tp, *refs):
    chunks = refs[:n_tp]
    meta, _, w_ref, stats_ref = refs[n_tp:]
    rows, tokens = w_ref.shape
    local_pages = tokens // PAGE
    first = lax.axis_index("seq") * local_pages
    lane = lax.broadcasted_iota(jnp.int32, (rows, PAGE), 1)
    scores, maxima, masks, owners = [], [], [], []
    for p in range(local_pages):
        at = slice(p * PAGE, (p + 1) * PAGE)
        total = chunks[0][:, at].astype(F32)
        for d in range(1, n_tp):
            total = total + chunks[d][:, at].astype(F32)
        mask = lane < meta[2 * pages + first + p]
        total = jnp.where(mask, total, NEG)
        masks.append(mask)
        scores.append(total)
        maxima.append(jnp.max(total, axis=1, keepdims=True))
        owners.append(meta[first + p])
    quarter = lane // prompts
    spot = lane % prompts
    stats = jnp.where(quarter == 0, NEG, 0.0)
    sums = []
    for p in range(local_pages):
        top = maxima[p]
        for other in range(local_pages):
            if other != p:
                top = jnp.where(owners[p] == owners[other], jnp.maximum(top, maxima[other]), top)
        high = top.astype(BF16).astype(F32)
        low = (top - high).astype(BF16).astype(F32)
        w = jnp.where(masks[p], jnp.exp(scores[p] - (high + low)), 0.0)
        w_ref[:, p * PAGE : (p + 1) * PAGE] = w.astype(BF16)
        here = spot == owners[p]
        stats = jnp.where(here & (quarter == 0), high, stats)
        stats = jnp.where(here & (quarter == 1), low, stats)
        part = jnp.sum(w, axis=1, keepdims=True)
        stats = stats + jnp.where(here & (quarter == 2), part, 0.0)
    high = stats.astype(BF16).astype(F32)
    low = pltpu.roll(stats - high, prompts, 1)
    stats_ref[...] = jnp.where(quarter == 3, low, stats).astype(BF16)


def softmax_weights(chunks, meta, after, pages, prompts):
    n_tp = len(chunks)
    rows, tokens = chunks[0].shape
    return pl.pallas_call(
        functools.partial(weights_kernel, pages, prompts, n_tp),
        in_specs=[VMEM] * n_tp + [SMEM, ANY],
        out_specs=[VMEM, VMEM],
        out_shape=[
            jax.ShapeDtypeStruct((rows, tokens), BF16),
            jax.ShapeDtypeStruct((rows, PAGE), BF16),
        ],
        compiler_params=pltpu.CompilerParams(vmem_limit_bytes=8 * MIB),
        name="weights",
    )(*chunks, meta, after)


def weighted_kernel(n_tp, *refs):
    pieces = refs[:n_tp]
    va_ref, vb_ref, meta = refs[n_tp : n_tp + 3]
    outs = refs[n_tp + 3 : n_tp + 3 + n_tp]
    ready, total = refs[n_tp + 3 + n_tp :]
    rows_local, tokens_here = pieces[0].shape
    kv_local = KVH // n_tp
    rows = rows_local // kv_local
    local_pages = tokens_here // PAGE
    first = lax.axis_index("seq") * local_pages
    me = lax.axis_index("tp")
    own = [pl.ds(pl.multiple_of(partner(me, d, n_tp) * rows_local, rows_local), rows_local) for d in range(n_tp)]
    for d in range(n_tp):
        at = pl.multiple_of((me ^ d) * rows_local, rows_local)
        ready[pl.ds(at, rows_local)] = pieces[d][...]
    total[...] = jnp.zeros_like(total)
    half = va_ref.shape[1] // HD
    for p in range(local_pages):
        request = meta[first + p]
        tokens = slice(p * PAGE, (p + 1) * PAGE)
        for head in range(KVH):
            v_ref = va_ref if head < half else vb_ref
            v = v_ref[tokens, head % half * HD : (head % half + 1) * HD]
            at = slice(head * rows, (head + 1) * rows)
            total[request, at] += jnp.dot(ready[at, tokens], v, preferred_element_type=F32)
    for d in range(n_tp):
        outs[d][...] = total[:, own[d]].astype(BF16)


def weighted_values(pieces, va, vb, meta, prompts):
    n_tp = len(pieces)
    rows, tokens = pieces[0].shape
    return pl.pallas_call(
        functools.partial(weighted_kernel, n_tp),
        in_specs=[VMEM] * (n_tp + 2) + [SMEM],
        out_specs=[VMEM] * n_tp,
        out_shape=[jax.ShapeDtypeStruct((prompts, rows, HD), BF16)] * n_tp,
        scratch_shapes=[
            pltpu.VMEM((rows * n_tp, tokens), BF16),
            pltpu.VMEM((prompts, rows * n_tp, HD), F32),
        ],
        compiler_params=pltpu.CompilerParams(vmem_limit_bytes=24 * MIB),
        cost_estimate=pl.CostEstimate(
            flops=2 * tokens * rows * n_tp * HD, bytes_accessed=8 * MIB, transcendentals=0
        ),
        name="weighted",
    )(*pieces, va, vb, meta)


def summed_kernel(n_tp, *refs):
    chunks = refs[:n_tp]
    stats_ref, out_ref = refs[n_tp:]
    prompts = chunks[0].shape[0]
    total = chunks[0][...].astype(F32)
    for d in range(1, n_tp):
        total = total + chunks[d][...].astype(F32)
    out_ref[:prompts] = total.astype(BF16)
    out_ref[prompts] = stats_ref[...]


def summed(chunks, stats):
    n_tp = len(chunks)
    prompts, rows, _ = chunks[0].shape
    return pl.pallas_call(
        functools.partial(summed_kernel, n_tp),
        in_specs=[VMEM] * (n_tp + 1),
        out_specs=VMEM,
        out_shape=jax.ShapeDtypeStruct((prompts + 1, rows, HD), BF16),
        compiler_params=pltpu.CompilerParams(vmem_limit_bytes=8 * MIB),
        cost_estimate=pl.CostEstimate(flops=0, bytes_accessed=4 * MIB, transcendentals=0),
        name="summed",
    )(*chunks, stats)


def output_kernel(n_seq, *refs):
    pieces = refs[:n_seq]
    fresh_ref, value_ref, wa_ref, wb_ref, out_ref, held = refs[n_seq:]
    more, rows_local, _ = pieces[0].shape
    prompts = more - 1
    new_count = fresh_ref.shape[0]
    rows = new_count * GROUP
    kv_local = rows_local // rows
    heads = kv_local * GROUP
    tops, parts = [], []
    for s in range(n_seq):
        stats = pieces[s][prompts].astype(F32)
        folded = stats + pltpu.roll(stats, HD - prompts, 1)
        tops.append(folded)
        parts.append(pltpu.roll(folded, HD - 2 * prompts, 1))
    fresh = [fresh_ref[n] for n in range(new_count)]
    top = fresh[0]
    for other in fresh[1:] + tops:
        top = jnp.maximum(top, other)
    weights = [jnp.exp(f - top) for f in fresh]
    factors = [jnp.exp(t - top) for t in tops]
    total = weights[0]
    for w in weights[1:]:
        total = total + w
    for f, part in zip(factors, parts):
        total = total + f * part
    weights = [w / total for w in weights]
    factors = [f / total for f in factors]
    for r in range(prompts):
        sums = jnp.zeros((rows_local, HD), F32)
        for s in range(n_seq):
            sums = sums + factors[s][:, r : r + 1] * pieces[s][r].astype(F32)
        for n in range(new_count):
            sums = sums + weights[n][:, r : r + 1] * value_ref[r * new_count + n]
        for g in range(kv_local):
            for n in range(new_count):
                at = g * rows + n * GROUP
                held[g * GROUP : (g + 1) * GROUP, r * new_count + n] = sums[at : at + GROUP]
    half = heads // 2
    product = jnp.zeros(out_ref.shape, F32)
    for w_ref, at in ((wa_ref, 0), (wb_ref, half)):
        left = [held[h].astype(BF16) for h in range(at, at + half)]
        left = jnp.concatenate(left, axis=1)
        product = product + jnp.dot(left, w_ref[...], preferred_element_type=F32)
    out_ref[...] = product.astype(BF16)


def output_partial(pieces, fresh, values, weights):
    n_seq = len(pieces)
    new_count = fresh.shape[0]
    prompts = pieces[0].shape[0] - 1
    depth, columns = weights[0].shape
    return pl.pallas_call(
        functools.partial(output_kernel, n_seq),
        in_specs=[VMEM] * (n_seq + 4),
        out_specs=VMEM,
        out_shape=jax.ShapeDtypeStruct((prompts * new_count, columns), BF16),
        scratch_shapes=[pltpu.VMEM((2 * depth // HD, prompts * new_count, HD), F32)],
        compiler_params=pltpu.CompilerParams(vmem_limit_bytes=24 * MIB),
        name="output",
    )(*pieces, fresh, values, *weights)


def final_kernel(n_tp, *refs):
    pieces = refs[:n_tp]
    res_ref, out_ref = refs[n_tp:]
    prompts, new_count, _ = out_ref.shape
    total = pieces[0][...].astype(F32)
    for d in range(1, n_tp):
        total = total + pieces[d][...].astype(F32)
    for r in range(prompts):
        out_ref[r] = res_ref[r].astype(F32) + total[r * new_count : (r + 1) * new_count]


def final_sum(pieces, residual):
    n_tp = len(pieces)
    return pl.pallas_call(
        functools.partial(final_kernel, n_tp),
        in_specs=[VMEM] * (n_tp + 1),
        out_specs=VMEM,
        out_shape=jax.ShapeDtypeStruct(residual.shape, F32),
        compiler_params=pltpu.CompilerParams(vmem_limit_bytes=8 * MIB),
        name="final",
    )(*pieces, residual)


def on_device(
    prefill_states, kv_weight, page_counts, tail_tokens, new_query, new_keyval, residual, out_weight
):
    n_seq, n_tp = lax.axis_size("seq"), lax.axis_size("tp")
    own_rows, new_count, _ = new_query.shape
    prompts = page_counts.shape[0]
    pages = prefill_states.shape[0] // PAGE * n_seq
    query, new_kv = prepare(new_query, new_keyval)
    query = gather(query, "tp")
    acc, xa, wa, cosine, sine, cos_q, sin_q, meta = load(
        prefill_states, kv_weight, page_counts, tail_tokens, pages, new_count
    )
    new = turned(query, new_kv, cos_q, sin_q)
    k, xb, wb = rotated_keys(acc, xa, wa, prefill_states, kv_weight, cosine, sine, new)
    new = gather(new, "seq")
    scores = partial_scores(new, k, meta, prompts, n_tp)
    va, oa = project_values((xa, wa, xb, wb), out_weight, 0, scores[0])
    weights, stats = softmax_weights(exchange(scores, "tp"), meta, va, pages, prompts)
    vb, ob = project_values((xa, wa, xb, wb), out_weight, 1, stats)
    fresh, values = fresh_scores(new, stats, prompts, new_count, n_tp)
    chunks = weighted_values(gather(weights, "tp"), va, vb, meta, prompts)
    pieces = gather_by_chips(summed(exchange(chunks, "tp"), stats), "seq")
    partial = output_partial(pieces, fresh, values, (oa, ob))
    return final_sum(gather(partial, "tp"), residual)


def solution(mesh):
    placed = (
        P(("groups", "seq"), "tp"),
        P("tp", None),
        P("groups"),
        P("groups"),
        P(("groups", "seq"), None, "tp"),
        P(("groups", "seq"), None, "tp"),
        P("groups", None, "seq"),
        P("tp", "seq"),
    )
    return jax.shard_map(
        on_device, mesh=mesh, in_specs=placed, out_specs=P("groups", None, "seq"), check_vma=False
    )
```

```python
import functools
import math

import jax
import jax.numpy as jnp
from jax import lax
from jax.experimental import pallas as pl
from jax.experimental.pallas import tpu as pltpu
from jax.sharding import PartitionSpec as P

QH = 64
KVH = 8
HD = 128
PAGE = 128
GROUP = QH // KVH
NEG = -1e30
F32 = jnp.float32
BF16 = jnp.bfloat16
MIB = 1 << 20

VMEM = pl.BlockSpec(memory_space=pltpu.VMEM)
SMEM = pl.BlockSpec(memory_space=pltpu.SMEM)
ANY = pl.BlockSpec(memory_space=pl.ANY)


def pairs(value, axis, d):
    return lax.ppermute(value, axis, [(i, i ^ d) for i in range(lax.axis_size(axis))])


def partner(me, entry, size):
    return me ^ ((size - entry) % size)


def exchange(chunks, axis):
    size = len(chunks)
    return [chunks[0]] + [pairs(chunks[i], axis, size - i) for i in range(1, size)]


def gather(value, axis):
    return [value] + [pairs(value, axis, d) for d in range(1, lax.axis_size(axis))]


def lane_freqs(rows):
    lane = lax.broadcasted_iota(jnp.int32, (rows, HD), 1) % (HD // 2)
    return jnp.exp(-(lane.astype(F32) * (2.0 / HD)) * math.log(500000.0))


def sine_sign(rows):
    lane = lax.broadcasted_iota(jnp.int32, (rows, HD), 1)
    return jnp.where(lane < HD // 2, -1.0, 1.0)


def in_hbm(value):
    return pltpu.with_memory_space_constraint(value, pltpu.HBM)


def by_row(rows, numbers):
    row = lax.broadcasted_iota(jnp.int32, (rows, HD), 0)
    out = jnp.zeros((rows, HD), F32)
    for i, number in enumerate(numbers):
        out = jnp.where(row == i, number.astype(F32), out)
    return out


def page_table(pages, prompts, counts, tails, meta):
    def one_prompt(r, start):
        length = (counts[r] - 1) * PAGE + tails[r]
        meta[3 * pages + r] = length

        def one_page(i, carry):
            meta[start + i] = r
            meta[pages + start + i] = i * PAGE
            meta[2 * pages + start + i] = jnp.minimum(length - i * PAGE, PAGE)
            return carry

        lax.fori_loop(0, counts[r], one_page, 0)
        return start + counts[r]

    lax.fori_loop(0, prompts, one_prompt, 0)


def rotation_tables(pages, local_pages, meta, cos_s, sin_s):
    freqs = lane_freqs(8)
    low = lax.broadcasted_iota(jnp.int32, (8, HD), 0).astype(F32) * freqs
    low_cos, low_sin = jnp.cos(low), jnp.sin(low)
    high = lax.broadcasted_iota(jnp.int32, (PAGE // 8, HD), 0).astype(F32) * 8.0
    high = high * lane_freqs(PAGE // 8)
    high_cos, high_sin = jnp.cos(high), jnp.sin(high)
    first = lax.axis_index("seq") * local_pages
    base = by_row(local_pages, [meta[pages + first + p] for p in range(local_pages)])
    base = base * lane_freqs(local_pages)
    base_cos, base_sin = jnp.cos(base), jnp.sin(base)
    sign = sine_sign(8)
    for i in range(PAGE // 8):
        c, s = high_cos[i : i + 1], high_sin[i : i + 1]
        cosine, sine = low_cos * c - low_sin * s, low_sin * c + low_cos * s
        for p in range(local_pages):
            at = slice(p * PAGE + i * 8, p * PAGE + i * 8 + 8)
            c, s = base_cos[p : p + 1], base_sin[p : p + 1]
            cos_s[at] = cosine * c - sine * s
            sin_s[at] = sign * (sine * c + cosine * s)


def pair_columns(w_ref, rows, pair, part):
    at = [(2 * head + part) * HD for head in (2 * pair, 2 * pair + 1)]
    return jnp.concatenate([w_ref[rows, c : c + HD] for c in at], axis=1)


def copies_of(x_hbm, w_hbm, x_ref, w_ref, sems, first, size, count):
    pairs_of = []
    for i in range(count):
        source, to = pl.ds(first + i * size, size), pl.ds(i * size, size)
        x_copy = pltpu.make_async_copy(x_hbm.at[:, source], x_ref.at[:, to], sems.at[2 * i])
        w_copy = pltpu.make_async_copy(w_hbm.at[source], w_ref.at[to], sems.at[2 * i + 1])
        pairs_of.append((x_copy, w_copy))
    return pairs_of


def start(copies):
    for copy in copies:
        copy.start()


def wait(copies):
    for copy in copies:
        copy.wait()


def add_block(x_ref, w_ref, rows, acc, out, fresh):
    tokens = x_ref.shape[0]
    tall = tokens // 2
    for pair in range(KVH // 2):
        weight = pair_columns(w_ref, rows, pair, 0)
        columns = slice(2 * pair * HD, 2 * (pair + 1) * HD)
        for top in range(0, tokens, tall):
            at = slice(top, top + tall)
            product = jnp.dot(x_ref[at, rows], weight, preferred_element_type=F32)
            out[at, columns] = product if fresh else acc[at, columns] + product


def load_kernel(pages, prompts, new_count, x_hbm, w_hbm, counts, tails, *refs):
    acc, x_ref, w_ref, cos_ref, sin_ref, cos_q, sin_q, meta, sems = refs
    tokens = x_ref.shape[0]
    size = x_ref.shape[1] // 3
    copies = copies_of(x_hbm, w_hbm, x_ref, w_ref, sems, 0, size, 3)
    start(copies[0])
    page_table(pages, prompts, counts, tails, meta)
    rotation_tables(pages, tokens // PAGE, meta, cos_ref, sin_ref)
    spots = [meta[3 * pages + r] + n for r in range(prompts) for n in range(new_count)]
    angles = by_row(len(spots), spots) * lane_freqs(len(spots))
    cos_q[...] = jnp.cos(angles)
    sin_q[...] = jnp.sin(angles) * sine_sign(len(spots))
    start(copies[1])
    for i in range(2):
        wait(copies[i])
        if i == 0:
            start(copies[2])
        add_block(x_ref, w_ref, slice(i * size, (i + 1) * size), acc, acc, i == 0)
    wait(copies[2])


def load(x, kv_weight, counts, tails, pages, new_count):
    tokens, depth = x.shape
    columns = kv_weight.shape[1]
    prompts = counts.shape[0]
    part = depth // 4 * 3
    hbm = pl.BlockSpec(memory_space=pltpu.HBM)
    return pl.pallas_call(
        functools.partial(load_kernel, pages, prompts, new_count),
        in_specs=[hbm, hbm, SMEM, SMEM],
        out_specs=[VMEM] * 7 + [SMEM],
        out_shape=[
            pltpu.VMEM((tokens, KVH * HD), F32),
            pltpu.VMEM((tokens, part), BF16),
            pltpu.VMEM((part, columns), BF16),
            pltpu.VMEM((tokens, HD), F32),
            pltpu.VMEM((tokens, HD), F32),
            pltpu.VMEM((prompts * new_count, HD), F32),
            pltpu.VMEM((prompts * new_count, HD), F32),
            jax.ShapeDtypeStruct((3 * pages + prompts,), jnp.int32),
        ],
        scratch_shapes=[pltpu.SemaphoreType.DMA((6,))],
        compiler_params=pltpu.CompilerParams(vmem_limit_bytes=28 * MIB),
        cost_estimate=pl.CostEstimate(
            flops=tokens * depth * KVH * HD,
            bytes_accessed=2 * part * (tokens + columns),
            transcendentals=0,
        ),
        name="load",
    )(*[in_hbm(a) for a in (x, kv_weight, counts, tails)])


def keys_kernel(acc, xa_ref, wa_ref, x_hbm, w_hbm, cos_ref, sin_ref, after, k_ref, x_ref, w_ref, total, sems):
    tokens, size = x_ref.shape
    tall = tokens // 2
    (copies,) = copies_of(x_hbm, w_hbm, x_ref, w_ref, sems, 3 * size, size, 1)
    start(copies)
    add_block(xa_ref, wa_ref, slice(2 * size, 3 * size), acc, total, False)
    wait(copies)
    for pair in range(KVH // 2):
        weight = pair_columns(w_ref, slice(None), pair, 0)
        columns = slice(2 * pair * HD, 2 * (pair + 1) * HD)
        for top in range(0, tokens, tall):
            at = slice(top, top + tall)
            product = total[at, columns] + jnp.dot(x_ref[at], weight, preferred_element_type=F32)
            cosine, sine = cos_ref[at], sin_ref[at]
            for h in range(2):
                k = product[:, h * HD : (h + 1) * HD]
                k = k * cosine + pltpu.roll(k, HD // 2, 1) * sine
                k_ref[at, (2 * pair + h) * HD : (2 * pair + h + 1) * HD] = k.astype(BF16)


def rotated_keys(acc, xa, wa, x, kv_weight, cosine, sine, after):
    tokens, depth = x.shape
    columns = kv_weight.shape[1]
    hbm = pl.BlockSpec(memory_space=pltpu.HBM)
    return pl.pallas_call(
        keys_kernel,
        in_specs=[VMEM] * 3 + [hbm] * 2 + [VMEM] * 2 + [ANY],
        out_specs=[VMEM] * 3,
        out_shape=[
            pltpu.VMEM((tokens, KVH * HD), BF16),
            pltpu.VMEM((tokens, depth // 4), BF16),
            pltpu.VMEM((depth // 4, columns), BF16),
        ],
        scratch_shapes=[
            pltpu.VMEM((tokens, KVH * HD), F32),
            pltpu.SemaphoreType.DMA((2,)),
        ],
        compiler_params=pltpu.CompilerParams(vmem_limit_bytes=24 * MIB),
        cost_estimate=pl.CostEstimate(
            flops=tokens * depth * KVH * HD, bytes_accessed=8 * MIB, transcendentals=0
        ),
        name="keys",
    )(acc, xa, wa, in_hbm(x), in_hbm(kv_weight), cosine, sine, after)


def values_kernel(first, xa_ref, wa_ref, xb_ref, wb_ref, o_hbm, after, v_ref, o_ref, sem):
    depth = o_ref.shape[0]
    copy = pltpu.make_async_copy(o_hbm.at[pl.ds(first * depth, depth)], o_ref, sem)
    copy.start()
    tokens, columns = v_ref.shape
    tall = tokens // 2
    pairs_here = columns // (2 * HD)
    for pair in range(pairs_here):
        weights = [pair_columns(w, slice(None), first * pairs_here + pair, 1) for w in (wa_ref, wb_ref)]
        for i in range(2):
            at = slice(i * tall, (i + 1) * tall)
            product = jnp.dot(xa_ref[at], weights[0], preferred_element_type=F32)
            product = product + jnp.dot(xb_ref[at], weights[1], preferred_element_type=F32)
            v_ref[at, 2 * pair * HD : 2 * (pair + 1) * HD] = product.astype(BF16)
    copy.wait()


def project_values(blocks, out_weight, first, after):
    tokens, depth = blocks[0].shape
    columns = KVH // 2 * HD
    rows = out_weight.shape[0] // 2
    return pl.pallas_call(
        functools.partial(values_kernel, first),
        in_specs=[VMEM] * 4 + [pl.BlockSpec(memory_space=pltpu.HBM), ANY],
        out_specs=[VMEM, VMEM],
        out_shape=[
            pltpu.VMEM((tokens, columns), BF16),
            pltpu.VMEM((rows, out_weight.shape[1]), BF16),
        ],
        scratch_shapes=[pltpu.SemaphoreType.DMA],
        compiler_params=pltpu.CompilerParams(vmem_limit_bytes=24 * MIB),
        cost_estimate=pl.CostEstimate(
            flops=2 * tokens * depth * columns, bytes_accessed=8 * MIB, transcendentals=0
        ),
        name="values",
    )(*blocks, in_hbm(out_weight), after)


def by_heads(row):
    return jnp.concatenate([row[:, c : c + HD] for c in range(0, row.shape[1], HD)], axis=0)


def prepare_kernel(q_ref, kv_ref, q_out, kv_out):
    for r in range(q_ref.shape[0]):
        q, kv = q_ref[r].astype(F32), kv_ref[r].astype(F32)
        for n in range(q_ref.shape[1]):
            q_out[r, n] = by_heads(q[n : n + 1]).astype(BF16)
            kv_out[r, n] = by_heads(kv[n : n + 1])


def prepare(new_query, new_keyval):
    own_rows, new_count, columns = new_query.shape
    shape = lambda a: (own_rows, new_count, a.shape[2] // HD, HD)
    return pl.pallas_call(
        prepare_kernel,
        in_specs=[VMEM, VMEM],
        out_specs=[VMEM, VMEM],
        out_shape=[
            jax.ShapeDtypeStruct(shape(new_query), BF16),
            jax.ShapeDtypeStruct(shape(new_keyval), F32),
        ],
        compiler_params=pltpu.CompilerParams(vmem_limit_bytes=8 * MIB),
        cost_estimate=pl.CostEstimate(flops=0, bytes_accessed=MIB, transcendentals=0),
        name="prepare",
    )(in_hbm(new_query), in_hbm(new_keyval))


def turned_kernel(n_tp, *refs):
    kv_ref, cos_q, sin_q, out_ref = refs[n_tp:]
    own_rows, new_count, heads, _ = refs[0].shape
    rows = new_count * GROUP
    kv_local = heads // GROUP
    me, seq = lax.axis_index("tp"), lax.axis_index("seq")
    for r in range(own_rows):
        spots = [pl.ds((seq * own_rows + r) * new_count + n, 1) for n in range(new_count)]
        turns = [(cos_q[spot], sin_q[spot]) for spot in spots]

        def turn(value, n):
            return value * turns[n][0] + pltpu.roll(value, HD // 2, 1) * turns[n][1]

        for d in range(n_tp):
            blocks = [refs[d][r, n].astype(F32) for n in range(new_count)]
            for g in range(kv_local):
                parts = [turn(q[g * GROUP : (g + 1) * GROUP], n) for n, q in enumerate(blocks)]
                at = ((me ^ d) * kv_local + g) * rows
                at = pl.ds(pl.multiple_of(at, rows), rows)
                out_ref[r, at] = jnp.concatenate(parts, axis=0).astype(BF16)
        fresh = []
        for n in range(new_count):
            row = lax.broadcasted_iota(jnp.int32, kv_ref.shape[2:], 0)
            fresh.append(jnp.where(row % 2 == 0, turn(kv_ref[r, n], n), kv_ref[r, n]))
        fresh.append(jnp.zeros((FRESH - new_count * 2 * kv_local, HD), F32))
        out_ref[r, KVH * rows :] = jnp.concatenate(fresh, axis=0).astype(BF16)


FRESH = 16


def turned(pieces, fresh, cos_q, sin_q):
    n_tp = len(pieces)
    own_rows, new_count, _, _ = pieces[0].shape
    rows = KVH * GROUP * new_count + FRESH
    return pl.pallas_call(
        functools.partial(turned_kernel, n_tp),
        in_specs=[VMEM] * (n_tp + 3),
        out_specs=VMEM,
        out_shape=jax.ShapeDtypeStruct((own_rows, rows, HD), BF16),
        compiler_params=pltpu.CompilerParams(vmem_limit_bytes=8 * MIB),
        name="turned",
    )(*pieces, fresh, cos_q, sin_q)


def scores_kernel(n_seq, n_tp, *refs):
    new = refs[:n_seq]
    k_ref, meta = refs[n_seq : n_seq + 2]
    outs = refs[n_seq + 2 : n_seq + 2 + n_tp]
    all_q, ready = refs[n_seq + 2 + n_tp :]
    own_rows = new[0].shape[0]
    local_pages = k_ref.shape[0] // PAGE
    rows = all_q.shape[1] // KVH
    count = all_q.shape[1] // n_tp
    scale = 1.0 / math.sqrt(HD)
    me = lax.axis_index("tp")
    seq = lax.axis_index("seq")
    first = seq * local_pages
    for ds in range(n_seq):
        for rr in range(own_rows):
            all_q[(seq ^ ds) * own_rows + rr] = new[ds][rr, : KVH * rows]
    for p in range(local_pages):
        request = meta[first + p]
        tokens = slice(p * PAGE, (p + 1) * PAGE)
        for head in range(KVH):
            k = k_ref[tokens, head * HD : (head + 1) * HD]
            q = all_q[request, head * rows : (head + 1) * rows]
            s = lax.dot_general(q, k, (((1,), (1,)), ((), ())), preferred_element_type=F32)
            ready[head * rows : (head + 1) * rows, tokens] = (s * scale).astype(BF16)
    for d in range(n_tp):
        outs[d][...] = ready[pl.ds(pl.multiple_of(partner(me, d, n_tp) * count, count), count)]


def partial_scores(new, k, meta, prompts, n_tp):
    n_seq = len(new)
    all_rows = new[0].shape[1] - FRESH
    tokens = k.shape[0]
    rows = all_rows // n_tp
    return pl.pallas_call(
        functools.partial(scores_kernel, n_seq, n_tp),
        in_specs=[VMEM] * (n_seq + 1) + [SMEM],
        out_specs=[VMEM] * n_tp,
        out_shape=[jax.ShapeDtypeStruct((rows, tokens), BF16)] * n_tp,
        scratch_shapes=[
            pltpu.VMEM((prompts, all_rows, HD), BF16),
            pltpu.VMEM((all_rows, tokens), BF16),
        ],
        compiler_params=pltpu.CompilerParams(vmem_limit_bytes=24 * MIB),
        cost_estimate=pl.CostEstimate(
            flops=2 * tokens * all_rows * HD, bytes_accessed=6 * MIB, transcendentals=0
        ),
        name="scores",
    )(*new, k, meta)


def fresh_kernel(n_seq, *refs):
    new = refs[:n_seq]
    _, score_ref, value_ref = refs[n_seq:]
    new_count, rows_local, _ = score_ref.shape
    own_rows = new[0].shape[0]
    rows = new_count * GROUP
    kv_local = rows_local // rows
    scale = 1.0 / math.sqrt(HD)
    seq = lax.axis_index("seq")
    own = pl.ds(pl.multiple_of(lax.axis_index("tp") * rows_local, rows_local), rows_local)
    step = lax.broadcasted_iota(jnp.int32, (rows_local, HD), 0) % rows // GROUP
    lane = lax.broadcasted_iota(jnp.int32, (rows_local, HD), 1)
    found = [jnp.full((rows_local, HD), NEG, F32) for _ in range(new_count)]

    def spread(block, first):
        parts = [block[first + 2 * g : first + 2 * g + 1] for g in range(kv_local)]
        return jnp.concatenate([jnp.broadcast_to(a, (rows, HD)) for a in parts], axis=0)

    for ds in range(n_seq):
        for rr in range(own_rows):
            request = (seq ^ ds) * own_rows + rr
            q = new[ds][rr, own].astype(F32)
            both = new[ds][rr, KVH * rows :].astype(F32)
            for n in range(new_count):
                first = n * 2 * kv_local
                s = jnp.sum(q * spread(both, first), axis=1, keepdims=True) * scale
                found[n] = jnp.where((lane == request) & (step >= n), s, found[n])
                value_ref[request * new_count + n] = spread(both, first + 1)
    for n in range(new_count):
        score_ref[n] = found[n]


def fresh_scores(new, after, prompts, new_count, n_tp):
    n_seq = len(new)
    rows = (new[0].shape[1] - FRESH) // n_tp
    return pl.pallas_call(
        functools.partial(fresh_kernel, n_seq),
        in_specs=[VMEM] * n_seq + [ANY],
        out_specs=[VMEM, VMEM],
        out_shape=[
            jax.ShapeDtypeStruct((new_count, rows, HD), F32),
            jax.ShapeDtypeStruct((prompts * new_count, rows, HD), F32),
        ],
        compiler_params=pltpu.CompilerParams(vmem_limit_bytes=16 * MIB),
        cost_estimate=pl.CostEstimate(flops=0, bytes_accessed=2 * MIB, transcendentals=0),
        name="fresh",
    )(*new, after)


def weights_kernel(pages, prompts, n_tp, *refs):
    chunks = refs[:n_tp]
    meta, _, w_ref = refs[n_tp:]
    rows, tokens = chunks[0].shape
    local_pages = tokens // PAGE
    first = lax.axis_index("seq") * local_pages
    lane = lax.broadcasted_iota(jnp.int32, (rows, PAGE), 1)
    scores, maxima, masks, owners = [], [], [], []
    for p in range(local_pages):
        at = slice(p * PAGE, (p + 1) * PAGE)
        total = chunks[0][:, at].astype(F32)
        for d in range(1, n_tp):
            total = total + chunks[d][:, at].astype(F32)
        mask = lane < meta[2 * pages + first + p]
        total = jnp.where(mask, total, NEG)
        masks.append(mask)
        scores.append(total)
        maxima.append(jnp.max(total, axis=1, keepdims=True))
        owners.append(meta[first + p])
    quarter = lane // prompts
    spot = lane % prompts
    stats = jnp.where(quarter == 0, NEG, 0.0)
    sums = []
    for p in range(local_pages):
        top = maxima[p]
        for other in range(local_pages):
            if other != p:
                top = jnp.where(owners[p] == owners[other], jnp.maximum(top, maxima[other]), top)
        high = top.astype(BF16).astype(F32)
        low = (top - high).astype(BF16).astype(F32)
        w = jnp.where(masks[p], jnp.exp(scores[p] - (high + low)), 0.0)
        w_ref[:, p * PAGE : (p + 1) * PAGE] = w.astype(BF16)
        here = spot == owners[p]
        stats = jnp.where(here & (quarter == 0), high, stats)
        stats = jnp.where(here & (quarter == 1), low, stats)
        part = jnp.sum(w, axis=1, keepdims=True)
        stats = stats + jnp.where(here & (quarter == 2), part, 0.0)
    high = stats.astype(BF16).astype(F32)
    low = pltpu.roll(stats - high, prompts, 1)
    w_ref[:, tokens:] = jnp.where(quarter == 3, low, stats).astype(BF16)


def softmax_weights(chunks, meta, after, pages, prompts):
    n_tp = len(chunks)
    rows, tokens = chunks[0].shape
    return pl.pallas_call(
        functools.partial(weights_kernel, pages, prompts, n_tp),
        in_specs=[VMEM] * n_tp + [SMEM, ANY],
        out_specs=VMEM,
        out_shape=jax.ShapeDtypeStruct((rows, tokens + HD), BF16),
        compiler_params=pltpu.CompilerParams(vmem_limit_bytes=8 * MIB),
        name="weights",
    )(*chunks, meta, after)


def unpacked(stats, prompts):
    stats = stats.astype(F32)
    folded = stats + pltpu.roll(stats, HD - prompts, 1)
    return folded, pltpu.roll(folded, HD - 2 * prompts, 1)


def packed(top, total, prompts):
    lane = lax.broadcasted_iota(jnp.int32, top.shape, 1)
    out = jnp.zeros(top.shape, F32)
    for i, value in enumerate((top, total)):
        high = value.astype(BF16).astype(F32)
        for j, piece in enumerate((high, value - high)):
            at = (2 * i + j) * prompts
            piece = pltpu.roll(piece, at, 1) if at else piece
            out = jnp.where((lane >= at) & (lane < at + prompts), piece, out)
    return out.astype(BF16)


def weighted_kernel(n_tp, *refs):
    pieces = refs[:n_tp]
    va_ref, vb_ref, meta, keep_ref, send_ref, ready, total = refs[n_tp:]
    rows_local = pieces[0].shape[0]
    tokens_here = va_ref.shape[0]
    kv_local = KVH // n_tp
    rows = rows_local // kv_local
    local_pages = tokens_here // PAGE
    half = keep_ref.shape[0] - 1
    seq, me = lax.axis_index("seq"), lax.axis_index("tp")
    first = seq * local_pages
    core = seq % 2
    for d in range(n_tp):
        at = pl.ds(pl.multiple_of((me ^ d) * rows_local, rows_local), rows_local)
        ready[at] = pieces[d][:, :tokens_here]
        keep_ref[half, at] = pieces[d][:, tokens_here:]
        send_ref[half, at] = pieces[d][:, tokens_here:]
    total[...] = jnp.zeros_like(total)
    columns = va_ref.shape[1] // HD
    for p in range(local_pages):
        request = meta[first + p]
        tokens = slice(p * PAGE, (p + 1) * PAGE)
        for head in range(KVH):
            v_ref = va_ref if head < columns else vb_ref
            v = v_ref[tokens, head % columns * HD : (head % columns + 1) * HD]
            at = slice(head * rows, (head + 1) * rows)
            total[request, at] += jnp.dot(ready[at, tokens], v, preferred_element_type=F32)
    for i in range(half):
        keep_ref[i] = total[core * half + i].astype(BF16)
        send_ref[i] = total[(1 - core) * half + i].astype(BF16)


def weighted_values(pieces, va, vb, meta, prompts):
    n_tp = len(pieces)
    rows = pieces[0].shape[0] * n_tp
    return pl.pallas_call(
        functools.partial(weighted_kernel, n_tp),
        in_specs=[VMEM] * (n_tp + 2) + [SMEM],
        out_specs=[VMEM] * 2,
        out_shape=[jax.ShapeDtypeStruct((prompts // 2 + 1, rows, HD), BF16)] * 2,
        scratch_shapes=[
            pltpu.VMEM((rows, va.shape[0]), BF16),
            pltpu.VMEM((prompts, rows, HD), F32),
        ],
        compiler_params=pltpu.CompilerParams(vmem_limit_bytes=24 * MIB),
        cost_estimate=pl.CostEstimate(
            flops=2 * va.shape[0] * rows * HD, bytes_accessed=8 * MIB, transcendentals=0
        ),
        name="weighted",
    )(*pieces, va, vb, meta)


def joined_kernel(n_tp, keep_ref, got_ref, *refs):
    outs, stats_ref, ready, facts = refs[:n_tp], refs[n_tp], refs[n_tp + 1], refs[n_tp + 2]
    more, rows, _ = keep_ref.shape
    half = more - 1
    prompts = 2 * half
    count = rows // n_tp
    me = lax.axis_index("tp")
    core = lax.axis_index("seq") % 2
    (top_a, sum_a), (top_b, sum_b) = [unpacked(r[half], prompts) for r in (keep_ref, got_ref)]
    top = jnp.maximum(top_a, top_b)
    factors = [jnp.exp(top_a - top), jnp.exp(top_b - top)]
    facts[...] = packed(top, sum_a * factors[0] + sum_b * factors[1], prompts).astype(F32)
    own = pl.ds(pl.multiple_of(me * count, count), count)
    stats_ref[...] = facts[own].astype(BF16)
    factors = [jnp.where(core == 0, f, pltpu.roll(f, HD - half, 1)) for f in factors]
    for i in range(half):
        total = factors[0][:, i : i + 1] * keep_ref[i].astype(F32)
        total = total + factors[1][:, i : i + 1] * got_ref[i].astype(F32)
        ready[i] = total.astype(BF16)
    for d in range(n_tp):
        at = pl.ds(pl.multiple_of(partner(me, d, n_tp) * count, count), count)
        outs[d][...] = ready[:, at]


def joined(keep, got, n_tp):
    more, rows, _ = keep.shape
    count = rows // n_tp
    return pl.pallas_call(
        functools.partial(joined_kernel, n_tp),
        in_specs=[VMEM, VMEM],
        out_specs=[VMEM] * (n_tp + 1),
        out_shape=[jax.ShapeDtypeStruct((more - 1, count, HD), BF16)] * n_tp
        + [jax.ShapeDtypeStruct((count, HD), BF16)],
        scratch_shapes=[pltpu.VMEM((more - 1, rows, HD), BF16), pltpu.VMEM((rows, HD), F32)],
        compiler_params=pltpu.CompilerParams(vmem_limit_bytes=16 * MIB),
        cost_estimate=pl.CostEstimate(flops=0, bytes_accessed=2 * MIB, transcendentals=0),
        name="joined",
    )(keep, got)


def summed_kernel(n_tp, *refs):
    chunks = refs[:n_tp]
    stats_ref, out_ref = refs[n_tp:]
    half = chunks[0].shape[0]
    total = chunks[0][...].astype(F32)
    for d in range(1, n_tp):
        total = total + chunks[d][...].astype(F32)
    out_ref[:half] = total.astype(BF16)
    out_ref[half] = stats_ref[...]


def summed(chunks, stats):
    n_tp = len(chunks)
    half, rows, _ = chunks[0].shape
    return pl.pallas_call(
        functools.partial(summed_kernel, n_tp),
        in_specs=[VMEM] * (n_tp + 1),
        out_specs=VMEM,
        out_shape=jax.ShapeDtypeStruct((half + 1, rows, HD), BF16),
        compiler_params=pltpu.CompilerParams(vmem_limit_bytes=8 * MIB),
        cost_estimate=pl.CostEstimate(flops=0, bytes_accessed=16 * MIB, transcendentals=0),
        name="summed",
    )(*chunks, stats)


def output_kernel(n_seq, *refs):
    pieces = refs[:n_seq]
    fresh_ref, value_ref, wa_ref, wb_ref, out_ref, held = refs[n_seq:]
    more, rows_local, _ = pieces[0].shape
    own = more - 1
    prompts = 2 * own
    new_count = fresh_ref.shape[0]
    rows = new_count * GROUP
    kv_local = rows_local // rows
    heads = kv_local * GROUP
    core = lax.axis_index("seq") % 2
    tops, parts = zip(*[unpacked(pieces[s][own], prompts) for s in range(0, n_seq, 2)])
    fresh = [fresh_ref[n] for n in range(new_count)]
    top = fresh[0]
    for other in fresh[1:] + list(tops):
        top = jnp.maximum(top, other)
    weights = [jnp.exp(f - top) for f in fresh]
    factors = [jnp.exp(t - top) for t in tops]
    total = weights[0]
    for w in weights[1:]:
        total = total + w
    for f, part in zip(factors, parts):
        total = total + f * part
    lane = lax.broadcasted_iota(jnp.int32, (rows_local, HD), 1)

    def own_first(value):
        other = jnp.where(lane < own, pltpu.roll(value, HD - own, 1), pltpu.roll(value, own, 1))
        return jnp.where(core == 0, value, other)

    weights = [own_first(w / total) for w in weights]
    factors = [own_first(f / total) for f in factors]
    for i in range(prompts):
        side = i // own
        request = (core ^ side) * own + i % own
        sums = jnp.zeros((rows_local, HD), F32)
        for chip in range(n_seq // 2):
            piece = pieces[2 * chip + side][i % own].astype(F32)
            sums = sums + factors[chip][:, i : i + 1] * piece
        for n in range(new_count):
            sums = sums + weights[n][:, i : i + 1] * value_ref[request * new_count + n]
        for g in range(kv_local):
            for n in range(new_count):
                at = g * rows + n * GROUP
                held[g * GROUP : (g + 1) * GROUP, request * new_count + n] = sums[at : at + GROUP]
    half = heads // 2
    product = jnp.zeros(out_ref.shape, F32)
    for w_ref, at in ((wa_ref, 0), (wb_ref, half)):
        left = [held[h].astype(BF16) for h in range(at, at + half)]
        left = jnp.concatenate(left, axis=1)
        product = product + jnp.dot(left, w_ref[...], preferred_element_type=F32)
    out_ref[...] = product.astype(BF16)


def output_partial(pieces, fresh, values, weights):
    n_seq = len(pieces)
    new_count = fresh.shape[0]
    prompts = 2 * (pieces[0].shape[0] - 1)
    depth, columns = weights[0].shape
    return pl.pallas_call(
        functools.partial(output_kernel, n_seq),
        in_specs=[VMEM] * (n_seq + 4),
        out_specs=VMEM,
        out_shape=jax.ShapeDtypeStruct((prompts * new_count, columns), BF16),
        scratch_shapes=[pltpu.VMEM((2 * depth // HD, prompts * new_count, HD), F32)],
        compiler_params=pltpu.CompilerParams(vmem_limit_bytes=24 * MIB),
        name="output",
    )(*pieces, fresh, values, *weights)


def final_kernel(n_tp, *refs):
    pieces = refs[:n_tp]
    res_ref, out_ref = refs[n_tp:]
    prompts, new_count, _ = out_ref.shape
    total = pieces[0][...].astype(F32)
    for d in range(1, n_tp):
        total = total + pieces[d][...].astype(F32)
    for r in range(prompts):
        out_ref[r] = res_ref[r].astype(F32) + total[r * new_count : (r + 1) * new_count]


def final_sum(pieces, residual):
    n_tp = len(pieces)
    return pl.pallas_call(
        functools.partial(final_kernel, n_tp),
        in_specs=[VMEM] * (n_tp + 1),
        out_specs=VMEM,
        out_shape=jax.ShapeDtypeStruct(residual.shape, F32),
        compiler_params=pltpu.CompilerParams(vmem_limit_bytes=8 * MIB),
        name="final",
    )(*pieces, residual)


def on_device(
    prefill_states, kv_weight, page_counts, tail_tokens, new_query, new_keyval, residual, out_weight
):
    n_seq, n_tp = lax.axis_size("seq"), lax.axis_size("tp")
    own_rows, new_count, _ = new_query.shape
    prompts = page_counts.shape[0]
    pages = prefill_states.shape[0] // PAGE * n_seq
    query, new_kv = prepare(new_query, new_keyval)
    query = gather(query, "tp")
    acc, xa, wa, cosine, sine, cos_q, sin_q, meta = load(
        prefill_states, kv_weight, page_counts, tail_tokens, pages, new_count
    )
    new = turned(query, new_kv, cos_q, sin_q)
    k, xb, wb = rotated_keys(acc, xa, wa, prefill_states, kv_weight, cosine, sine, new)
    new = gather(new, "seq")
    scores = partial_scores(new, k, meta, prompts, n_tp)
    va, oa = project_values((xa, wa, xb, wb), out_weight, 0, scores[0])
    weights = softmax_weights(exchange(scores, "tp"), meta, va, pages, prompts)
    vb, ob = project_values((xa, wa, xb, wb), out_weight, 1, weights)
    fresh, values = fresh_scores(new, weights, prompts, new_count, n_tp)
    keep, send = weighted_values(gather(weights, "tp"), va, vb, meta, prompts)
    *chunks, stats = joined(keep, pairs(send, "seq", 1), n_tp)
    pieces = gather(summed(exchange(chunks, "tp"), stats), "seq")
    partial = output_partial(pieces, fresh, values, (oa, ob))
    return final_sum(gather(partial, "tp"), residual)


def solution(mesh):
    placed = (
        P(("groups", "seq"), "tp"),
        P("tp", None),
        P("groups"),
        P("groups"),
        P(("groups", "seq"), None, "tp"),
        P(("groups", "seq"), None, "tp"),
        P("groups", None, "seq"),
        P("tp", "seq"),
    )
    return jax.shard_map(
        on_device, mesh=mesh, in_specs=placed, out_specs=P("groups", None, "seq"), check_vma=False
    )
```

```python
import functools
import math

import jax
import jax.numpy as jnp
from jax import lax
from jax.experimental import pallas as pl
from jax.experimental.pallas import tpu as pltpu
from jax.sharding import PartitionSpec as P

QH = 64
KVH = 8
HD = 128
PAGE = 128
GROUP = QH // KVH
NEG = -1e30
F32 = jnp.float32
BF16 = jnp.bfloat16
MIB = 1 << 20

VMEM = pl.BlockSpec(memory_space=pltpu.VMEM)
SMEM = pl.BlockSpec(memory_space=pltpu.SMEM)
ANY = pl.BlockSpec(memory_space=pl.ANY)


def partner(me, entry, size):
    return me ^ ((size - entry) % size)


def pairs(value, axis, entry):
    size = lax.axis_size(axis)
    return lax.ppermute(value, axis, [(i, partner(i, entry, size)) for i in range(size)])


def exchange(chunks, axis):
    return [chunks[0]] + [pairs(chunks[i], axis, i) for i in range(1, len(chunks))]


def gather(value, axis):
    size = lax.axis_size(axis)
    return [value] + [pairs(value, axis, size - d) for d in range(1, size)]


def lane_freqs(rows):
    lane = lax.broadcasted_iota(jnp.int32, (rows, HD), 1) % (HD // 2)
    return jnp.exp(-(lane.astype(F32) * (2.0 / HD)) * math.log(500000.0))


def sine_sign(rows):
    lane = lax.broadcasted_iota(jnp.int32, (rows, HD), 1)
    return jnp.where(lane < HD // 2, -1.0, 1.0)


def in_hbm(value):
    return pltpu.with_memory_space_constraint(value, pltpu.HBM)


def by_row(rows, numbers):
    row = lax.broadcasted_iota(jnp.int32, (rows, HD), 0)
    out = jnp.zeros((rows, HD), F32)
    for i, number in enumerate(numbers):
        out = jnp.where(row == i, number.astype(F32), out)
    return out


def page_table(pages, prompts, counts, tails, meta):
    def one_prompt(r, start):
        length = (counts[r] - 1) * PAGE + tails[r]
        meta[3 * pages + r] = length

        def one_page(i, carry):
            meta[start + i] = r
            meta[pages + start + i] = i * PAGE
            meta[2 * pages + start + i] = jnp.minimum(length - i * PAGE, PAGE)
            return carry

        lax.fori_loop(0, counts[r], one_page, 0)
        return start + counts[r]

    lax.fori_loop(0, prompts, one_prompt, 0)


def rotation_tables(pages, local_pages, meta, cos_s, sin_s):
    freqs = lane_freqs(8)
    low = lax.broadcasted_iota(jnp.int32, (8, HD), 0).astype(F32) * freqs
    low_cos, low_sin = jnp.cos(low), jnp.sin(low)
    high = lax.broadcasted_iota(jnp.int32, (PAGE // 8, HD), 0).astype(F32) * 8.0
    high = high * lane_freqs(PAGE // 8)
    high_cos, high_sin = jnp.cos(high), jnp.sin(high)
    first = lax.axis_index("seq") * local_pages
    base = by_row(local_pages, [meta[pages + first + p] for p in range(local_pages)])
    base = base * lane_freqs(local_pages)
    base_cos, base_sin = jnp.cos(base), jnp.sin(base)
    sign = sine_sign(8)
    for i in range(PAGE // 8):
        c, s = high_cos[i : i + 1], high_sin[i : i + 1]
        cosine, sine = low_cos * c - low_sin * s, low_sin * c + low_cos * s
        for p in range(local_pages):
            at = slice(p * PAGE + i * 8, p * PAGE + i * 8 + 8)
            c, s = base_cos[p : p + 1], base_sin[p : p + 1]
            cos_s[at] = cosine * c - sine * s
            sin_s[at] = sign * (sine * c + cosine * s)


def pair_columns(w_ref, pair, part):
    at = [(2 * head + part) * HD for head in (2 * pair, 2 * pair + 1)]
    return jnp.concatenate([w_ref[:, c : c + HD] for c in at], axis=1)


def pair_keys(x_ref, w_ref, cos_ref, sin_ref, pair, rows, k_ref, column):
    product = jnp.dot(x_ref[rows], pair_columns(w_ref, pair, 0), preferred_element_type=F32)
    cosine, sine = cos_ref[rows], sin_ref[rows]
    for h in range(2):
        k = product[:, h * HD : (h + 1) * HD]
        k = k * cosine + pltpu.roll(k, HD // 2, 1) * sine
        k_ref[rows, column + h * HD : column + (h + 1) * HD] = k.astype(BF16)


def load_kernel(pages, prompts, new_count, x_hbm, w_hbm, counts, tails, *refs):
    k_ref, x_ref, w_ref, cos_ref, sin_ref, cos_q, sin_q, meta, x_sems, w_sems = refs
    tokens = x_ref.shape[0]
    tall, wide = tokens // 2, 4 * HD

    def x_copy(i):
        at = pl.ds(i * tall, tall)
        return pltpu.make_async_copy(x_hbm.at[at], x_ref.at[at], x_sems.at[i])

    def w_copy(pair):
        at = pl.ds(pair * wide, wide)
        return pltpu.make_async_copy(w_hbm.at[:, at], w_ref.at[:, at], w_sems.at[pair])

    x_copy(0).start()
    w_copy(0).start()
    page_table(pages, prompts, counts, tails, meta)
    x_copy(1).start()
    rotation_tables(pages, tokens // PAGE, meta, cos_ref, sin_ref)
    spots = [meta[3 * pages + r] + n for r in range(prompts) for n in range(new_count)]
    angles = by_row(len(spots), spots) * lane_freqs(len(spots))
    cos_q[...] = jnp.cos(angles)
    sin_q[...] = jnp.sin(angles) * sine_sign(len(spots))
    w_copy(1).start()
    count = KVH // 2
    for pair in range(count // 2):
        w_copy(pair).wait()
        if pair + 2 < count:
            w_copy(pair + 2).start()
        for i in range(2):
            if pair == 0:
                x_copy(i).wait()
            rows = slice(i * tall, (i + 1) * tall)
            pair_keys(x_ref, w_ref, cos_ref, sin_ref, pair, rows, k_ref, 2 * pair * HD)
    for pair in range(count // 2, count):
        w_copy(pair).wait()


def load(x, kv_weight, counts, tails, pages, new_count):
    tokens, depth = x.shape
    columns = kv_weight.shape[1]
    prompts = counts.shape[0]
    hbm = pl.BlockSpec(memory_space=pltpu.HBM)
    return pl.pallas_call(
        functools.partial(load_kernel, pages, prompts, new_count),
        in_specs=[hbm, hbm, SMEM, SMEM],
        out_specs=[VMEM] * 7 + [SMEM],
        out_shape=[
            pltpu.VMEM((tokens, KVH // 2 * HD), BF16),
            pltpu.VMEM((tokens, depth), BF16),
            pltpu.VMEM((depth, columns), BF16),
            pltpu.VMEM((tokens, HD), F32),
            pltpu.VMEM((tokens, HD), F32),
            pltpu.VMEM((prompts * new_count, HD), F32),
            pltpu.VMEM((prompts * new_count, HD), F32),
            jax.ShapeDtypeStruct((3 * pages + prompts,), jnp.int32),
        ],
        scratch_shapes=[pltpu.SemaphoreType.DMA((2,)), pltpu.SemaphoreType.DMA((KVH // 2,))],
        compiler_params=pltpu.CompilerParams(vmem_limit_bytes=28 * MIB),
        cost_estimate=pl.CostEstimate(
            flops=tokens * depth * KVH * HD,
            bytes_accessed=2 * depth * (tokens + columns),
            transcendentals=0,
        ),
        name="load",
    )(*[in_hbm(a) for a in (x, kv_weight, counts, tails)])


def keys_kernel(x_ref, w_ref, cos_ref, sin_ref, after, k_ref):
    tokens = x_ref.shape[0]
    tall = tokens // 2
    for pair in range(KVH // 4, KVH // 2):
        for i in range(2):
            rows = slice(i * tall, (i + 1) * tall)
            column = (2 * pair - KVH // 2) * HD
            pair_keys(x_ref, w_ref, cos_ref, sin_ref, pair, rows, k_ref, column)


def rotated_keys(x, weight, cosine, sine, after):
    tokens, depth = x.shape
    return pl.pallas_call(
        keys_kernel,
        in_specs=[VMEM] * 4 + [ANY],
        out_specs=VMEM,
        out_shape=pltpu.VMEM((tokens, KVH // 2 * HD), BF16),
        compiler_params=pltpu.CompilerParams(vmem_limit_bytes=24 * MIB),
        cost_estimate=pl.CostEstimate(
            flops=tokens * depth * KVH * HD, bytes_accessed=8 * MIB, transcendentals=0
        ),
        name="keys",
    )(x, weight, cosine, sine, after)


def values_kernel(first, x_ref, w_ref, o_hbm, after, v_ref, o_ref, sem):
    depth = o_ref.shape[0]
    copy = pltpu.make_async_copy(o_hbm.at[pl.ds(first * depth, depth)], o_ref, sem)
    copy.start()
    tokens, columns = v_ref.shape
    tall = tokens // 2
    pairs_here = columns // (2 * HD)
    for pair in range(pairs_here):
        weight = pair_columns(w_ref, first * pairs_here + pair, 1)
        for i in range(2):
            at = slice(i * tall, (i + 1) * tall)
            product = jnp.dot(x_ref[at], weight, preferred_element_type=F32)
            v_ref[at, 2 * pair * HD : 2 * (pair + 1) * HD] = product.astype(BF16)
    copy.wait()


def project_values(x, weight, out_weight, first, after):
    tokens, depth = x.shape
    columns = KVH // 2 * HD
    rows = out_weight.shape[0] // 2
    return pl.pallas_call(
        functools.partial(values_kernel, first),
        in_specs=[VMEM] * 2 + [pl.BlockSpec(memory_space=pltpu.HBM), ANY],
        out_specs=[VMEM, VMEM],
        out_shape=[
            pltpu.VMEM((tokens, columns), BF16),
            pltpu.VMEM((rows, out_weight.shape[1]), BF16),
        ],
        scratch_shapes=[pltpu.SemaphoreType.DMA],
        compiler_params=pltpu.CompilerParams(vmem_limit_bytes=24 * MIB),
        cost_estimate=pl.CostEstimate(
            flops=2 * tokens * depth * columns, bytes_accessed=8 * MIB, transcendentals=0
        ),
        name="values",
    )(x, weight, in_hbm(out_weight), after)


def by_heads(row):
    return jnp.concatenate([row[:, c : c + HD] for c in range(0, row.shape[1], HD)], axis=0)


def prepare_kernel(q_ref, kv_ref, q_out, kv_out):
    for r in range(q_ref.shape[0]):
        q, kv = q_ref[r].astype(F32), kv_ref[r].astype(F32)
        for n in range(q_ref.shape[1]):
            q_out[r, n] = by_heads(q[n : n + 1]).astype(BF16)
            kv_out[r, n] = by_heads(kv[n : n + 1])


def prepare(new_query, new_keyval):
    own_rows, new_count, columns = new_query.shape
    shape = lambda a: (own_rows, new_count, a.shape[2] // HD, HD)
    return pl.pallas_call(
        prepare_kernel,
        in_specs=[VMEM, VMEM],
        out_specs=[VMEM, VMEM],
        out_shape=[
            jax.ShapeDtypeStruct(shape(new_query), BF16),
            jax.ShapeDtypeStruct(shape(new_keyval), F32),
        ],
        compiler_params=pltpu.CompilerParams(vmem_limit_bytes=8 * MIB),
        cost_estimate=pl.CostEstimate(flops=0, bytes_accessed=MIB, transcendentals=0),
        name="prepare",
    )(in_hbm(new_query), in_hbm(new_keyval))


def turned_kernel(n_tp, *refs):
    kv_ref, cos_q, sin_q, out_ref = refs[n_tp:]
    own_rows, new_count, heads, _ = refs[0].shape
    rows = new_count * GROUP
    kv_local = heads // GROUP
    me, seq = lax.axis_index("tp"), lax.axis_index("seq")
    for r in range(own_rows):
        spots = [pl.ds((seq * own_rows + r) * new_count + n, 1) for n in range(new_count)]
        turns = [(cos_q[spot], sin_q[spot]) for spot in spots]

        def turn(value, n):
            return value * turns[n][0] + pltpu.roll(value, HD // 2, 1) * turns[n][1]

        for d in range(n_tp):
            blocks = [refs[d][r, n].astype(F32) for n in range(new_count)]
            for g in range(kv_local):
                parts = [turn(q[g * GROUP : (g + 1) * GROUP], n) for n, q in enumerate(blocks)]
                at = ((me ^ d) * kv_local + g) * rows
                at = pl.ds(pl.multiple_of(at, rows), rows)
                out_ref[r, at] = jnp.concatenate(parts, axis=0).astype(BF16)
        fresh = []
        for n in range(new_count):
            row = lax.broadcasted_iota(jnp.int32, kv_ref.shape[2:], 0)
            fresh.append(jnp.where(row % 2 == 0, turn(kv_ref[r, n], n), kv_ref[r, n]))
        fresh.append(jnp.zeros((FRESH - new_count * 2 * kv_local, HD), F32))
        out_ref[r, KVH * rows :] = jnp.concatenate(fresh, axis=0).astype(BF16)


FRESH = 16


def turned(pieces, fresh, cos_q, sin_q):
    n_tp = len(pieces)
    own_rows, new_count, _, _ = pieces[0].shape
    rows = KVH * GROUP * new_count + FRESH
    return pl.pallas_call(
        functools.partial(turned_kernel, n_tp),
        in_specs=[VMEM] * (n_tp + 3),
        out_specs=VMEM,
        out_shape=jax.ShapeDtypeStruct((own_rows, rows, HD), BF16),
        compiler_params=pltpu.CompilerParams(vmem_limit_bytes=8 * MIB),
        name="turned",
    )(*pieces, fresh, cos_q, sin_q)


def scores_kernel(n_seq, n_tp, *refs):
    new = refs[:n_seq]
    ka_ref, kb_ref, meta = refs[n_seq : n_seq + 3]
    outs = refs[n_seq + 3 : n_seq + 3 + n_tp]
    all_q, ready = refs[n_seq + 3 + n_tp :]
    own_rows = new[0].shape[0]
    local_pages = ka_ref.shape[0] // PAGE
    half = ka_ref.shape[1] // HD
    rows = all_q.shape[1] // KVH
    count = all_q.shape[1] // n_tp
    scale = 1.0 / math.sqrt(HD)
    me = lax.axis_index("tp")
    seq = lax.axis_index("seq")
    first = seq * local_pages
    for ds in range(n_seq):
        for rr in range(own_rows):
            all_q[(seq ^ ds) * own_rows + rr] = new[ds][rr, : KVH * rows]
    for p in range(local_pages):
        request = meta[first + p]
        tokens = slice(p * PAGE, (p + 1) * PAGE)
        for head in range(KVH):
            k_ref = ka_ref if head < half else kb_ref
            k = k_ref[tokens, head % half * HD : (head % half + 1) * HD]
            q = all_q[request, head * rows : (head + 1) * rows]
            s = lax.dot_general(q, k, (((1,), (1,)), ((), ())), preferred_element_type=F32)
            ready[head * rows : (head + 1) * rows, tokens] = (s * scale).astype(BF16)
    for d in range(n_tp):
        outs[d][...] = ready[pl.ds(pl.multiple_of(partner(me, d, n_tp) * count, count), count)]


def partial_scores(new, ka, kb, meta, prompts, n_tp):
    n_seq = len(new)
    all_rows = new[0].shape[1] - FRESH
    tokens = ka.shape[0]
    rows = all_rows // n_tp
    return pl.pallas_call(
        functools.partial(scores_kernel, n_seq, n_tp),
        in_specs=[VMEM] * (n_seq + 2) + [SMEM],
        out_specs=[VMEM] * n_tp,
        out_shape=[jax.ShapeDtypeStruct((rows, tokens), BF16)] * n_tp,
        scratch_shapes=[
            pltpu.VMEM((prompts, all_rows, HD), BF16),
            pltpu.VMEM((all_rows, tokens), BF16),
        ],
        compiler_params=pltpu.CompilerParams(vmem_limit_bytes=24 * MIB),
        cost_estimate=pl.CostEstimate(
            flops=2 * tokens * all_rows * HD, bytes_accessed=6 * MIB, transcendentals=0
        ),
        name="scores",
    )(*new, ka, kb, meta)


def fresh_kernel(n_seq, *refs):
    new = refs[:n_seq]
    _, score_ref, value_ref = refs[n_seq:]
    new_count, rows_local, _ = score_ref.shape
    own_rows = new[0].shape[0]
    rows = new_count * GROUP
    kv_local = rows_local // rows
    scale = 1.0 / math.sqrt(HD)
    seq = lax.axis_index("seq")
    own = pl.ds(pl.multiple_of(lax.axis_index("tp") * rows_local, rows_local), rows_local)
    step = lax.broadcasted_iota(jnp.int32, (rows_local, HD), 0) % rows // GROUP
    lane = lax.broadcasted_iota(jnp.int32, (rows_local, HD), 1)
    found = [jnp.full((rows_local, HD), NEG, F32) for _ in range(new_count)]

    def spread(block, first):
        parts = [block[first + 2 * g : first + 2 * g + 1] for g in range(kv_local)]
        return jnp.concatenate([jnp.broadcast_to(a, (rows, HD)) for a in parts], axis=0)

    for ds in range(n_seq):
        for rr in range(own_rows):
            request = (seq ^ ds) * own_rows + rr
            q = new[ds][rr, own].astype(F32)
            both = new[ds][rr, KVH * rows :].astype(F32)
            for n in range(new_count):
                first = n * 2 * kv_local
                s = jnp.sum(q * spread(both, first), axis=1, keepdims=True) * scale
                found[n] = jnp.where((lane == request) & (step >= n), s, found[n])
                value_ref[request * new_count + n] = spread(both, first + 1)
    for n in range(new_count):
        score_ref[n] = found[n]


def fresh_scores(new, after, prompts, new_count, n_tp):
    n_seq = len(new)
    rows = (new[0].shape[1] - FRESH) // n_tp
    return pl.pallas_call(
        functools.partial(fresh_kernel, n_seq),
        in_specs=[VMEM] * n_seq + [ANY],
        out_specs=[VMEM, VMEM],
        out_shape=[
            jax.ShapeDtypeStruct((new_count, rows, HD), F32),
            jax.ShapeDtypeStruct((prompts * new_count, rows, HD), F32),
        ],
        compiler_params=pltpu.CompilerParams(vmem_limit_bytes=16 * MIB),
        cost_estimate=pl.CostEstimate(flops=0, bytes_accessed=2 * MIB, transcendentals=0),
        name="fresh",
    )(*new, after)


def weights_kernel(pages, prompts, n_tp, *refs):
    chunks = refs[:n_tp]
    meta, _, w_ref, stats_ref = refs[n_tp:]
    rows, tokens = w_ref.shape
    local_pages = tokens // PAGE
    first = lax.axis_index("seq") * local_pages
    lane = lax.broadcasted_iota(jnp.int32, (rows, PAGE), 1)
    scores, maxima, masks, owners = [], [], [], []
    for p in range(local_pages):
        at = slice(p * PAGE, (p + 1) * PAGE)
        total = chunks[0][:, at].astype(F32)
        for d in range(1, n_tp):
            total = total + chunks[d][:, at].astype(F32)
        mask = lane < meta[2 * pages + first + p]
        total = jnp.where(mask, total, NEG)
        masks.append(mask)
        scores.append(total)
        maxima.append(jnp.max(total, axis=1, keepdims=True))
        owners.append(meta[first + p])
    quarter = lane // prompts
    spot = lane % prompts
    stats = jnp.where(quarter == 0, NEG, 0.0)
    sums = []
    for p in range(local_pages):
        top = maxima[p]
        for other in range(local_pages):
            if other != p:
                top = jnp.where(owners[p] == owners[other], jnp.maximum(top, maxima[other]), top)
        high = top.astype(BF16).astype(F32)
        low = (top - high).astype(BF16).astype(F32)
        w = jnp.where(masks[p], jnp.exp(scores[p] - (high + low)), 0.0)
        w_ref[:, p * PAGE : (p + 1) * PAGE] = w.astype(BF16)
        here = spot == owners[p]
        stats = jnp.where(here & (quarter == 0), high, stats)
        stats = jnp.where(here & (quarter == 1), low, stats)
        part = jnp.sum(w, axis=1, keepdims=True)
        stats = stats + jnp.where(here & (quarter == 2), part, 0.0)
    high = stats.astype(BF16).astype(F32)
    low = pltpu.roll(stats - high, prompts, 1)
    stats_ref[...] = jnp.where(quarter == 3, low, stats).astype(BF16)


def softmax_weights(chunks, meta, after, pages, prompts):
    n_tp = len(chunks)
    rows, tokens = chunks[0].shape
    return pl.pallas_call(
        functools.partial(weights_kernel, pages, prompts, n_tp),
        in_specs=[VMEM] * n_tp + [SMEM, ANY],
        out_specs=[VMEM, VMEM],
        out_shape=[
            jax.ShapeDtypeStruct((rows, tokens), BF16),
            jax.ShapeDtypeStruct((rows, PAGE), BF16),
        ],
        compiler_params=pltpu.CompilerParams(vmem_limit_bytes=8 * MIB),
        name="weights",
    )(*chunks, meta, after)


def weighted_kernel(n_tp, *refs):
    pieces = refs[:n_tp]
    va_ref, vb_ref, meta = refs[n_tp : n_tp + 3]
    outs = refs[n_tp + 3 : n_tp + 3 + n_tp]
    ready, total = refs[n_tp + 3 + n_tp :]
    rows_local, tokens_here = pieces[0].shape
    kv_local = KVH // n_tp
    rows = rows_local // kv_local
    local_pages = tokens_here // PAGE
    first = lax.axis_index("seq") * local_pages
    me = lax.axis_index("tp")
    own = [pl.ds(pl.multiple_of(partner(me, d, n_tp) * rows_local, rows_local), rows_local) for d in range(n_tp)]
    for d in range(n_tp):
        at = pl.multiple_of((me ^ d) * rows_local, rows_local)
        ready[pl.ds(at, rows_local)] = pieces[d][...]
    total[...] = jnp.zeros_like(total)
    half = va_ref.shape[1] // HD
    for p in range(local_pages):
        request = meta[first + p]
        tokens = slice(p * PAGE, (p + 1) * PAGE)
        for head in range(KVH):
            v_ref = va_ref if head < half else vb_ref
            v = v_ref[tokens, head % half * HD : (head % half + 1) * HD]
            at = slice(head * rows, (head + 1) * rows)
            total[request, at] += jnp.dot(ready[at, tokens], v, preferred_element_type=F32)
    for d in range(n_tp):
        outs[d][...] = total[:, own[d]].astype(BF16)


def weighted_values(pieces, va, vb, meta, prompts):
    n_tp = len(pieces)
    rows, tokens = pieces[0].shape
    return pl.pallas_call(
        functools.partial(weighted_kernel, n_tp),
        in_specs=[VMEM] * (n_tp + 2) + [SMEM],
        out_specs=[VMEM] * n_tp,
        out_shape=[jax.ShapeDtypeStruct((prompts, rows, HD), BF16)] * n_tp,
        scratch_shapes=[
            pltpu.VMEM((rows * n_tp, tokens), BF16),
            pltpu.VMEM((prompts, rows * n_tp, HD), F32),
        ],
        compiler_params=pltpu.CompilerParams(vmem_limit_bytes=24 * MIB),
        cost_estimate=pl.CostEstimate(
            flops=2 * tokens * rows * n_tp * HD, bytes_accessed=8 * MIB, transcendentals=0
        ),
        name="weighted",
    )(*pieces, va, vb, meta)


def summed_kernel(n_tp, *refs):
    chunks = refs[:n_tp]
    stats_ref, out_ref = refs[n_tp:]
    prompts = chunks[0].shape[0]
    total = chunks[0][...].astype(F32)
    for d in range(1, n_tp):
        total = total + chunks[d][...].astype(F32)
    out_ref[:prompts] = total.astype(BF16)
    out_ref[prompts] = stats_ref[...]


def summed(chunks, stats):
    n_tp = len(chunks)
    prompts, rows, _ = chunks[0].shape
    return pl.pallas_call(
        functools.partial(summed_kernel, n_tp),
        in_specs=[VMEM] * (n_tp + 1),
        out_specs=VMEM,
        out_shape=jax.ShapeDtypeStruct((prompts + 1, rows, HD), BF16),
        compiler_params=pltpu.CompilerParams(vmem_limit_bytes=8 * MIB),
        cost_estimate=pl.CostEstimate(flops=0, bytes_accessed=4 * MIB, transcendentals=0),
        name="summed",
    )(*chunks, stats)


def output_kernel(n_seq, *refs):
    pieces = refs[:n_seq]
    fresh_ref, value_ref, wa_ref, wb_ref, out_ref, held = refs[n_seq:]
    more, rows_local, _ = pieces[0].shape
    prompts = more - 1
    new_count = fresh_ref.shape[0]
    rows = new_count * GROUP
    kv_local = rows_local // rows
    heads = kv_local * GROUP
    tops, parts = [], []
    for s in range(n_seq):
        stats = pieces[s][prompts].astype(F32)
        folded = stats + pltpu.roll(stats, HD - prompts, 1)
        tops.append(folded)
        parts.append(pltpu.roll(folded, HD - 2 * prompts, 1))
    fresh = [fresh_ref[n] for n in range(new_count)]
    top = fresh[0]
    for other in fresh[1:] + tops:
        top = jnp.maximum(top, other)
    weights = [jnp.exp(f - top) for f in fresh]
    factors = [jnp.exp(t - top) for t in tops]
    total = weights[0]
    for w in weights[1:]:
        total = total + w
    for f, part in zip(factors, parts):
        total = total + f * part
    weights = [w / total for w in weights]
    factors = [f / total for f in factors]
    for r in range(prompts):
        sums = jnp.zeros((rows_local, HD), F32)
        for s in range(n_seq):
            sums = sums + factors[s][:, r : r + 1] * pieces[s][r].astype(F32)
        for n in range(new_count):
            sums = sums + weights[n][:, r : r + 1] * value_ref[r * new_count + n]
        for g in range(kv_local):
            for n in range(new_count):
                at = g * rows + n * GROUP
                held[g * GROUP : (g + 1) * GROUP, r * new_count + n] = sums[at : at + GROUP]
    half = heads // 2
    product = jnp.zeros(out_ref.shape, F32)
    for w_ref, at in ((wa_ref, 0), (wb_ref, half)):
        left = [held[h].astype(BF16) for h in range(at, at + half)]
        left = jnp.concatenate(left, axis=1)
        product = product + jnp.dot(left, w_ref[...], preferred_element_type=F32)
    out_ref[...] = product.astype(BF16)


def output_partial(pieces, fresh, values, weights):
    n_seq = len(pieces)
    new_count = fresh.shape[0]
    prompts = pieces[0].shape[0] - 1
    depth, columns = weights[0].shape
    return pl.pallas_call(
        functools.partial(output_kernel, n_seq),
        in_specs=[VMEM] * (n_seq + 4),
        out_specs=VMEM,
        out_shape=jax.ShapeDtypeStruct((prompts * new_count, columns), BF16),
        scratch_shapes=[pltpu.VMEM((2 * depth // HD, prompts * new_count, HD), F32)],
        compiler_params=pltpu.CompilerParams(vmem_limit_bytes=24 * MIB),
        name="output",
    )(*pieces, fresh, values, *weights)


def final_kernel(n_tp, *refs):
    pieces = refs[:n_tp]
    res_ref, out_ref = refs[n_tp:]
    prompts, new_count, _ = out_ref.shape
    total = pieces[0][...].astype(F32)
    for d in range(1, n_tp):
        total = total + pieces[d][...].astype(F32)
    for r in range(prompts):
        out_ref[r] = res_ref[r].astype(F32) + total[r * new_count : (r + 1) * new_count]


def final_sum(pieces, residual):
    n_tp = len(pieces)
    return pl.pallas_call(
        functools.partial(final_kernel, n_tp),
        in_specs=[VMEM] * (n_tp + 1),
        out_specs=VMEM,
        out_shape=jax.ShapeDtypeStruct(residual.shape, F32),
        compiler_params=pltpu.CompilerParams(vmem_limit_bytes=8 * MIB),
        name="final",
    )(*pieces, residual)


def on_device(
    prefill_states, kv_weight, page_counts, tail_tokens, new_query, new_keyval, residual, out_weight
):
    n_seq, n_tp = lax.axis_size("seq"), lax.axis_size("tp")
    own_rows, new_count, _ = new_query.shape
    prompts = page_counts.shape[0]
    pages = prefill_states.shape[0] // PAGE * n_seq
    query, new_kv = prepare(new_query, new_keyval)
    query = gather(query, "tp")
    ka, x, w, cosine, sine, cos_q, sin_q, meta = load(
        prefill_states, kv_weight, page_counts, tail_tokens, pages, new_count
    )
    new = turned(query, new_kv, cos_q, sin_q)
    kb = rotated_keys(x, w, cosine, sine, new)
    new = gather(new, "seq")
    scores = partial_scores(new, ka, kb, meta, prompts, n_tp)
    va, oa = project_values(x, w, out_weight, 0, scores[0])
    weights, stats = softmax_weights(exchange(scores, "tp"), meta, va, pages, prompts)
    vb, ob = project_values(x, w, out_weight, 1, stats)
    fresh, values = fresh_scores(new, stats, prompts, new_count, n_tp)
    chunks = weighted_values(gather(weights, "tp"), va, vb, meta, prompts)
    pieces = gather(summed(exchange(chunks, "tp"), stats), "seq")
    partial = output_partial(pieces, fresh, values, (oa, ob))
    return final_sum(gather(partial, "tp"), residual)


def solution(mesh):
    placed = (
        P(("groups", "seq"), "tp"),
        P("tp", None),
        P("groups"),
        P("groups"),
        P(("groups", "seq"), None, "tp"),
        P(("groups", "seq"), None, "tp"),
        P("groups", None, "seq"),
        P("tp", "seq"),
    )
    return jax.shard_map(
        on_device, mesh=mesh, in_specs=placed, out_specs=P("groups", None, "seq"), check_vma=False
    )
```

```python
import functools
import math

import jax
import jax.numpy as jnp
from jax import lax
from jax.experimental import pallas as pl
from jax.experimental.pallas import tpu as pltpu
from jax.sharding import PartitionSpec as P

QH = 64
KVH = 8
HD = 128
PAGE = 128
GROUP = QH // KVH
NEG = -1e30
F32 = jnp.float32
BF16 = jnp.bfloat16
MIB = 1 << 20

VMEM = pl.BlockSpec(memory_space=pltpu.VMEM)
SMEM = pl.BlockSpec(memory_space=pltpu.SMEM)
ANY = pl.BlockSpec(memory_space=pl.ANY)


def partner(me, entry, size):
    return me ^ ((size - entry) % size)


def pairs(value, axis, entry):
    size = lax.axis_size(axis)
    return lax.ppermute(value, axis, [(i, partner(i, entry, size)) for i in range(size)])


def exchange(chunks, axis):
    return [chunks[0]] + [pairs(chunks[i], axis, i) for i in range(1, len(chunks))]


def gather(value, axis):
    size = lax.axis_size(axis)
    return [value] + [pairs(value, axis, size - d) for d in range(1, size)]


def lane_freqs(rows):
    lane = lax.broadcasted_iota(jnp.int32, (rows, HD), 1) % (HD // 2)
    return jnp.exp(-(lane.astype(F32) * (2.0 / HD)) * math.log(500000.0))


def sine_sign(rows):
    lane = lax.broadcasted_iota(jnp.int32, (rows, HD), 1)
    return jnp.where(lane < HD // 2, -1.0, 1.0)


def in_hbm(value):
    return pltpu.with_memory_space_constraint(value, pltpu.HBM)


def by_row(rows, numbers):
    row = lax.broadcasted_iota(jnp.int32, (rows, HD), 0)
    out = jnp.zeros((rows, HD), F32)
    for i, number in enumerate(numbers):
        out = jnp.where(row == i, number.astype(F32), out)
    return out


def page_table(pages, prompts, counts, tails, meta):
    def one_prompt(r, start):
        length = (counts[r] - 1) * PAGE + tails[r]
        meta[3 * pages + r] = length

        def one_page(i, carry):
            meta[start + i] = r
            meta[pages + start + i] = i * PAGE
            meta[2 * pages + start + i] = jnp.minimum(length - i * PAGE, PAGE)
            return carry

        lax.fori_loop(0, counts[r], one_page, 0)
        return start + counts[r]

    lax.fori_loop(0, prompts, one_prompt, 0)


def rotation_tables(pages, local_pages, meta, cos_s, sin_s):
    freqs = lane_freqs(8)
    low = lax.broadcasted_iota(jnp.int32, (8, HD), 0).astype(F32) * freqs
    low_cos, low_sin = jnp.cos(low), jnp.sin(low)
    high = lax.broadcasted_iota(jnp.int32, (PAGE // 8, HD), 0).astype(F32) * 8.0
    high = high * lane_freqs(PAGE // 8)
    high_cos, high_sin = jnp.cos(high), jnp.sin(high)
    first = lax.axis_index("seq") * local_pages
    base = by_row(local_pages, [meta[pages + first + p] for p in range(local_pages)])
    base = base * lane_freqs(local_pages)
    base_cos, base_sin = jnp.cos(base), jnp.sin(base)
    sign = sine_sign(8)
    for i in range(PAGE // 8):
        c, s = high_cos[i : i + 1], high_sin[i : i + 1]
        cosine, sine = low_cos * c - low_sin * s, low_sin * c + low_cos * s
        for p in range(local_pages):
            at = slice(p * PAGE + i * 8, p * PAGE + i * 8 + 8)
            c, s = base_cos[p : p + 1], base_sin[p : p + 1]
            cos_s[at] = cosine * c - sine * s
            sin_s[at] = sign * (sine * c + cosine * s)


def pair_columns(w_ref, rows, pair, part):
    at = [(2 * head + part) * HD for head in (2 * pair, 2 * pair + 1)]
    return jnp.concatenate([w_ref[rows, c : c + HD] for c in at], axis=1)


def copies_of(x_hbm, w_hbm, x_ref, w_ref, sems, first, size, count):
    pairs_of = []
    for i in range(count):
        source, to = pl.ds(first + i * size, size), pl.ds(i * size, size)
        x_copy = pltpu.make_async_copy(x_hbm.at[:, source], x_ref.at[:, to], sems.at[2 * i])
        w_copy = pltpu.make_async_copy(w_hbm.at[source], w_ref.at[to], sems.at[2 * i + 1])
        pairs_of.append((x_copy, w_copy))
    return pairs_of


def start(copies):
    for copy in copies:
        copy.start()


def wait(copies):
    for copy in copies:
        copy.wait()


def add_block(x_ref, w_ref, rows, acc, out, fresh):
    tokens = x_ref.shape[0]
    tall = tokens // 2
    for pair in range(KVH // 2):
        weight = pair_columns(w_ref, rows, pair, 0)
        columns = slice(2 * pair * HD, 2 * (pair + 1) * HD)
        for top in range(0, tokens, tall):
            at = slice(top, top + tall)
            product = jnp.dot(x_ref[at, rows], weight, preferred_element_type=F32)
            out[at, columns] = product if fresh else acc[at, columns] + product


def load_kernel(pages, prompts, new_count, x_hbm, w_hbm, counts, tails, *refs):
    acc, x_ref, w_ref, cos_ref, sin_ref, cos_q, sin_q, meta, sems = refs
    tokens = x_ref.shape[0]
    size = x_ref.shape[1] // 3
    copies = copies_of(x_hbm, w_hbm, x_ref, w_ref, sems, 0, size, 3)
    start(copies[0])
    page_table(pages, prompts, counts, tails, meta)
    rotation_tables(pages, tokens // PAGE, meta, cos_ref, sin_ref)
    spots = [meta[3 * pages + r] + n for r in range(prompts) for n in range(new_count)]
    angles = by_row(len(spots), spots) * lane_freqs(len(spots))
    cos_q[...] = jnp.cos(angles)
    sin_q[...] = jnp.sin(angles) * sine_sign(len(spots))
    start(copies[1])
    for i in range(2):
        wait(copies[i])
        if i == 0:
            start(copies[2])
        add_block(x_ref, w_ref, slice(i * size, (i + 1) * size), acc, acc, i == 0)
    wait(copies[2])


def load(x, kv_weight, counts, tails, pages, new_count):
    tokens, depth = x.shape
    columns = kv_weight.shape[1]
    prompts = counts.shape[0]
    part = depth // 4 * 3
    hbm = pl.BlockSpec(memory_space=pltpu.HBM)
    return pl.pallas_call(
        functools.partial(load_kernel, pages, prompts, new_count),
        in_specs=[hbm, hbm, SMEM, SMEM],
        out_specs=[VMEM] * 7 + [SMEM],
        out_shape=[
            pltpu.VMEM((tokens, KVH * HD), F32),
            pltpu.VMEM((tokens, part), BF16),
            pltpu.VMEM((part, columns), BF16),
            pltpu.VMEM((tokens, HD), F32),
            pltpu.VMEM((tokens, HD), F32),
            pltpu.VMEM((prompts * new_count, HD), F32),
            pltpu.VMEM((prompts * new_count, HD), F32),
            jax.ShapeDtypeStruct((3 * pages + prompts,), jnp.int32),
        ],
        scratch_shapes=[pltpu.SemaphoreType.DMA((6,))],
        compiler_params=pltpu.CompilerParams(vmem_limit_bytes=28 * MIB),
        cost_estimate=pl.CostEstimate(
            flops=tokens * depth * KVH * HD,
            bytes_accessed=2 * part * (tokens + columns),
            transcendentals=0,
        ),
        name="load",
    )(*[in_hbm(a) for a in (x, kv_weight, counts, tails)])


def keys_kernel(acc, xa_ref, wa_ref, x_hbm, w_hbm, cos_ref, sin_ref, after, k_ref, x_ref, w_ref, total, sems):
    tokens, size = x_ref.shape
    tall = tokens // 2
    (copies,) = copies_of(x_hbm, w_hbm, x_ref, w_ref, sems, 3 * size, size, 1)
    start(copies)
    add_block(xa_ref, wa_ref, slice(2 * size, 3 * size), acc, total, False)
    wait(copies)
    for pair in range(KVH // 2):
        weight = pair_columns(w_ref, slice(None), pair, 0)
        columns = slice(2 * pair * HD, 2 * (pair + 1) * HD)
        for top in range(0, tokens, tall):
            at = slice(top, top + tall)
            product = total[at, columns] + jnp.dot(x_ref[at], weight, preferred_element_type=F32)
            cosine, sine = cos_ref[at], sin_ref[at]
            for h in range(2):
                k = product[:, h * HD : (h + 1) * HD]
                k = k * cosine + pltpu.roll(k, HD // 2, 1) * sine
                k_ref[at, (2 * pair + h) * HD : (2 * pair + h + 1) * HD] = k.astype(BF16)


def rotated_keys(acc, xa, wa, x, kv_weight, cosine, sine, after):
    tokens, depth = x.shape
    columns = kv_weight.shape[1]
    hbm = pl.BlockSpec(memory_space=pltpu.HBM)
    return pl.pallas_call(
        keys_kernel,
        in_specs=[VMEM] * 3 + [hbm] * 2 + [VMEM] * 2 + [ANY],
        out_specs=[VMEM] * 3,
        out_shape=[
            pltpu.VMEM((tokens, KVH * HD), BF16),
            pltpu.VMEM((tokens, depth // 4), BF16),
            pltpu.VMEM((depth // 4, columns), BF16),
        ],
        scratch_shapes=[
            pltpu.VMEM((tokens, KVH * HD), F32),
            pltpu.SemaphoreType.DMA((2,)),
        ],
        compiler_params=pltpu.CompilerParams(vmem_limit_bytes=24 * MIB),
        cost_estimate=pl.CostEstimate(
            flops=tokens * depth * KVH * HD, bytes_accessed=8 * MIB, transcendentals=0
        ),
        name="keys",
    )(acc, xa, wa, in_hbm(x), in_hbm(kv_weight), cosine, sine, after)


def values_kernel(first, xa_ref, wa_ref, xb_ref, wb_ref, o_hbm, after, v_ref, o_ref, sem):
    depth = o_ref.shape[0]
    copy = pltpu.make_async_copy(o_hbm.at[pl.ds(first * depth, depth)], o_ref, sem)
    copy.start()
    tokens, columns = v_ref.shape
    tall = tokens // 2
    pairs_here = columns // (2 * HD)
    for pair in range(pairs_here):
        weights = [pair_columns(w, slice(None), first * pairs_here + pair, 1) for w in (wa_ref, wb_ref)]
        for i in range(2):
            at = slice(i * tall, (i + 1) * tall)
            product = jnp.dot(xa_ref[at], weights[0], preferred_element_type=F32)
            product = product + jnp.dot(xb_ref[at], weights[1], preferred_element_type=F32)
            v_ref[at, 2 * pair * HD : 2 * (pair + 1) * HD] = product.astype(BF16)
    copy.wait()


def project_values(blocks, out_weight, first, after):
    tokens, depth = blocks[0].shape
    columns = KVH // 2 * HD
    rows = out_weight.shape[0] // 2
    return pl.pallas_call(
        functools.partial(values_kernel, first),
        in_specs=[VMEM] * 4 + [pl.BlockSpec(memory_space=pltpu.HBM), ANY],
        out_specs=[VMEM, VMEM],
        out_shape=[
            pltpu.VMEM((tokens, columns), BF16),
            pltpu.VMEM((rows, out_weight.shape[1]), BF16),
        ],
        scratch_shapes=[pltpu.SemaphoreType.DMA],
        compiler_params=pltpu.CompilerParams(vmem_limit_bytes=24 * MIB),
        cost_estimate=pl.CostEstimate(
            flops=2 * tokens * depth * columns, bytes_accessed=8 * MIB, transcendentals=0
        ),
        name="values",
    )(*blocks, in_hbm(out_weight), after)


def by_heads(row):
    return jnp.concatenate([row[:, c : c + HD] for c in range(0, row.shape[1], HD)], axis=0)


def prepare_kernel(q_ref, kv_ref, q_out, kv_out):
    for r in range(q_ref.shape[0]):
        q, kv = q_ref[r].astype(F32), kv_ref[r].astype(F32)
        for n in range(q_ref.shape[1]):
            q_out[r, n] = by_heads(q[n : n + 1]).astype(BF16)
            kv_out[r, n] = by_heads(kv[n : n + 1])


def prepare(new_query, new_keyval):
    own_rows, new_count, columns = new_query.shape
    shape = lambda a: (own_rows, new_count, a.shape[2] // HD, HD)
    return pl.pallas_call(
        prepare_kernel,
        in_specs=[VMEM, VMEM],
        out_specs=[VMEM, VMEM],
        out_shape=[
            jax.ShapeDtypeStruct(shape(new_query), BF16),
            jax.ShapeDtypeStruct(shape(new_keyval), F32),
        ],
        compiler_params=pltpu.CompilerParams(vmem_limit_bytes=8 * MIB),
        cost_estimate=pl.CostEstimate(flops=0, bytes_accessed=MIB, transcendentals=0),
        name="prepare",
    )(in_hbm(new_query), in_hbm(new_keyval))


def turned_kernel(n_tp, *refs):
    kv_ref, cos_q, sin_q, out_ref = refs[n_tp:]
    own_rows, new_count, heads, _ = refs[0].shape
    rows = new_count * GROUP
    kv_local = heads // GROUP
    me, seq = lax.axis_index("tp"), lax.axis_index("seq")
    for r in range(own_rows):
        spots = [pl.ds((seq * own_rows + r) * new_count + n, 1) for n in range(new_count)]
        turns = [(cos_q[spot], sin_q[spot]) for spot in spots]

        def turn(value, n):
            return value * turns[n][0] + pltpu.roll(value, HD // 2, 1) * turns[n][1]

        for d in range(n_tp):
            blocks = [refs[d][r, n].astype(F32) for n in range(new_count)]
            for g in range(kv_local):
                parts = [turn(q[g * GROUP : (g + 1) * GROUP], n) for n, q in enumerate(blocks)]
                at = ((me ^ d) * kv_local + g) * rows
                at = pl.ds(pl.multiple_of(at, rows), rows)
                out_ref[r, at] = jnp.concatenate(parts, axis=0).astype(BF16)
        fresh = []
        for n in range(new_count):
            row = lax.broadcasted_iota(jnp.int32, kv_ref.shape[2:], 0)
            fresh.append(jnp.where(row % 2 == 0, turn(kv_ref[r, n], n), kv_ref[r, n]))
        fresh.append(jnp.zeros((FRESH - new_count * 2 * kv_local, HD), F32))
        out_ref[r, KVH * rows :] = jnp.concatenate(fresh, axis=0).astype(BF16)


FRESH = 16


def turned(pieces, fresh, cos_q, sin_q):
    n_tp = len(pieces)
    own_rows, new_count, _, _ = pieces[0].shape
    rows = KVH * GROUP * new_count + FRESH
    return pl.pallas_call(
        functools.partial(turned_kernel, n_tp),
        in_specs=[VMEM] * (n_tp + 3),
        out_specs=VMEM,
        out_shape=jax.ShapeDtypeStruct((own_rows, rows, HD), BF16),
        compiler_params=pltpu.CompilerParams(vmem_limit_bytes=8 * MIB),
        name="turned",
    )(*pieces, fresh, cos_q, sin_q)


def scores_kernel(n_seq, n_tp, *refs):
    new = refs[:n_seq]
    k_ref, meta = refs[n_seq : n_seq + 2]
    outs = refs[n_seq + 2 : n_seq + 2 + n_tp]
    all_q, ready = refs[n_seq + 2 + n_tp :]
    own_rows = new[0].shape[0]
    local_pages = k_ref.shape[0] // PAGE
    all_rows = all_q.shape[1]
    rows = all_rows // KVH
    count = all_rows // n_tp
    scale = 1.0 / math.sqrt(HD)
    me = lax.axis_index("tp")
    seq = lax.axis_index("seq")
    first = seq * local_pages
    even = lax.broadcasted_iota(jnp.int32, (all_rows, HD), 0) // rows % 2 == 0
    for ds in range(n_seq):
        for rr in range(own_rows):
            q = new[ds][rr, :all_rows].astype(F32)
            request = (seq ^ ds) * own_rows + rr
            all_q[request, :, :HD] = jnp.where(even, q, 0.0).astype(BF16)
            all_q[request, :, HD:] = jnp.where(even, 0.0, q).astype(BF16)
    for p in range(0, local_pages, 2):
        requests = [meta[first + p], meta[first + p + 1]]
        tokens = slice(p * PAGE, (p + 2) * PAGE)
        for pair in range(KVH // 2):
            k = k_ref[tokens, 2 * pair * HD : 2 * (pair + 1) * HD]
            at = slice(2 * pair * rows, 2 * (pair + 1) * rows)
            q = jnp.concatenate([all_q[request, at] for request in requests], axis=0)
            s = lax.dot_general(q, k, (((1,), (1,)), ((), ())), preferred_element_type=F32)
            for i in range(2):
                part = s[2 * i * rows : 2 * (i + 1) * rows, i * PAGE : (i + 1) * PAGE]
                here = slice((p + i) * PAGE, (p + i + 1) * PAGE)
                ready[at, here] = (part * scale).astype(BF16)
    for d in range(n_tp):
        outs[d][...] = ready[pl.ds(pl.multiple_of(partner(me, d, n_tp) * count, count), count)]


def partial_scores(new, k, meta, prompts, n_tp):
    n_seq = len(new)
    all_rows = new[0].shape[1] - FRESH
    tokens = k.shape[0]
    rows = all_rows // n_tp
    return pl.pallas_call(
        functools.partial(scores_kernel, n_seq, n_tp),
        in_specs=[VMEM] * (n_seq + 1) + [SMEM],
        out_specs=[VMEM] * n_tp,
        out_shape=[jax.ShapeDtypeStruct((rows, tokens), BF16)] * n_tp,
        scratch_shapes=[
            pltpu.VMEM((prompts, all_rows, 2 * HD), BF16),
            pltpu.VMEM((all_rows, tokens), BF16),
        ],
        compiler_params=pltpu.CompilerParams(vmem_limit_bytes=24 * MIB),
        cost_estimate=pl.CostEstimate(
            flops=2 * tokens * all_rows * HD, bytes_accessed=6 * MIB, transcendentals=0
        ),
        name="scores",
    )(*new, k, meta)


def fresh_kernel(n_seq, *refs):
    new = refs[:n_seq]
    _, score_ref, value_ref = refs[n_seq:]
    new_count, rows_local, _ = score_ref.shape
    own_rows = new[0].shape[0]
    rows = new_count * GROUP
    kv_local = rows_local // rows
    scale = 1.0 / math.sqrt(HD)
    seq = lax.axis_index("seq")
    own = pl.ds(pl.multiple_of(lax.axis_index("tp") * rows_local, rows_local), rows_local)
    step = lax.broadcasted_iota(jnp.int32, (rows_local, HD), 0) % rows // GROUP
    lane = lax.broadcasted_iota(jnp.int32, (rows_local, HD), 1)
    found = [jnp.full((rows_local, HD), NEG, F32) for _ in range(new_count)]

    def spread(block, first):
        parts = [block[first + 2 * g : first + 2 * g + 1] for g in range(kv_local)]
        return jnp.concatenate([jnp.broadcast_to(a, (rows, HD)) for a in parts], axis=0)

    for ds in range(n_seq):
        for rr in range(own_rows):
            request = (seq ^ ds) * own_rows + rr
            q = new[ds][rr, own].astype(F32)
            both = new[ds][rr, KVH * rows :].astype(F32)
            for n in range(new_count):
                first = n * 2 * kv_local
                s = jnp.sum(q * spread(both, first), axis=1, keepdims=True) * scale
                found[n] = jnp.where((lane == request) & (step >= n), s, found[n])
                value_ref[request * new_count + n] = spread(both, first + 1)
    for n in range(new_count):
        score_ref[n] = found[n]


def fresh_scores(new, after, prompts, new_count, n_tp):
    n_seq = len(new)
    rows = (new[0].shape[1] - FRESH) // n_tp
    return pl.pallas_call(
        functools.partial(fresh_kernel, n_seq),
        in_specs=[VMEM] * n_seq + [ANY],
        out_specs=[VMEM, VMEM],
        out_shape=[
            jax.ShapeDtypeStruct((new_count, rows, HD), F32),
            jax.ShapeDtypeStruct((prompts * new_count, rows, HD), F32),
        ],
        compiler_params=pltpu.CompilerParams(vmem_limit_bytes=16 * MIB),
        cost_estimate=pl.CostEstimate(flops=0, bytes_accessed=2 * MIB, transcendentals=0),
        name="fresh",
    )(*new, after)


def weights_kernel(pages, prompts, n_tp, *refs):
    chunks = refs[:n_tp]
    meta, _, w_ref, stats_ref = refs[n_tp:]
    rows, tokens = w_ref.shape
    local_pages = tokens // PAGE
    first = lax.axis_index("seq") * local_pages
    lane = lax.broadcasted_iota(jnp.int32, (rows, PAGE), 1)
    scores, maxima, masks, owners = [], [], [], []
    for p in range(local_pages):
        at = slice(p * PAGE, (p + 1) * PAGE)
        total = chunks[0][:, at].astype(F32)
        for d in range(1, n_tp):
            total = total + chunks[d][:, at].astype(F32)
        mask = lane < meta[2 * pages + first + p]
        total = jnp.where(mask, total, NEG)
        masks.append(mask)
        scores.append(total)
        maxima.append(jnp.max(total, axis=1, keepdims=True))
        owners.append(meta[first + p])
    quarter = lane // prompts
    spot = lane % prompts
    stats = jnp.where(quarter == 0, NEG, 0.0)
    sums = []
    for p in range(local_pages):
        top = maxima[p]
        for other in range(local_pages):
            if other != p:
                top = jnp.where(owners[p] == owners[other], jnp.maximum(top, maxima[other]), top)
        high = top.astype(BF16).astype(F32)
        low = (top - high).astype(BF16).astype(F32)
        w = jnp.where(masks[p], jnp.exp(scores[p] - (high + low)), 0.0)
        w_ref[:, p * PAGE : (p + 1) * PAGE] = w.astype(BF16)
        here = spot == owners[p]
        stats = jnp.where(here & (quarter == 0), high, stats)
        stats = jnp.where(here & (quarter == 1), low, stats)
        part = jnp.sum(w, axis=1, keepdims=True)
        stats = stats + jnp.where(here & (quarter == 2), part, 0.0)
    high = stats.astype(BF16).astype(F32)
    low = pltpu.roll(stats - high, prompts, 1)
    stats_ref[...] = jnp.where(quarter == 3, low, stats).astype(BF16)


def softmax_weights(chunks, meta, after, pages, prompts):
    n_tp = len(chunks)
    rows, tokens = chunks[0].shape
    return pl.pallas_call(
        functools.partial(weights_kernel, pages, prompts, n_tp),
        in_specs=[VMEM] * n_tp + [SMEM, ANY],
        out_specs=[VMEM, VMEM],
        out_shape=[
            jax.ShapeDtypeStruct((rows, tokens), BF16),
            jax.ShapeDtypeStruct((rows, PAGE), BF16),
        ],
        compiler_params=pltpu.CompilerParams(vmem_limit_bytes=8 * MIB),
        name="weights",
    )(*chunks, meta, after)


def weighted_kernel(n_tp, *refs):
    pieces = refs[:n_tp]
    va_ref, vb_ref, meta = refs[n_tp : n_tp + 3]
    outs = refs[n_tp + 3 : n_tp + 3 + n_tp]
    ready, total = refs[n_tp + 3 + n_tp :]
    rows_local, tokens_here = pieces[0].shape
    kv_local = KVH // n_tp
    rows = rows_local // kv_local
    local_pages = tokens_here // PAGE
    first = lax.axis_index("seq") * local_pages
    me = lax.axis_index("tp")
    own = [pl.ds(pl.multiple_of(partner(me, d, n_tp) * rows_local, rows_local), rows_local) for d in range(n_tp)]
    for d in range(n_tp):
        at = pl.multiple_of((me ^ d) * rows_local, rows_local)
        ready[pl.ds(at, rows_local)] = pieces[d][...]
    total[...] = jnp.zeros_like(total)
    half = va_ref.shape[1] // HD
    none = jnp.zeros((2 * rows, PAGE), BF16)
    for p in range(0, local_pages, 2):
        requests = [meta[first + p], meta[first + p + 1]]
        tokens = slice(p * PAGE, (p + 2) * PAGE)
        for pair in range(KVH // 2):
            head = 2 * pair
            v_ref = va_ref if head < half else vb_ref
            v = v_ref[tokens, head % half * HD : (head % half + 2) * HD]
            at = slice(head * rows, (head + 2) * rows)
            w = [ready[at, (p + i) * PAGE : (p + i + 1) * PAGE] for i in range(2)]
            w = [jnp.concatenate([w[0], none], axis=1), jnp.concatenate([none, w[1]], axis=1)]
            sums = jnp.dot(jnp.concatenate(w, axis=0), v, preferred_element_type=F32)
            for i, request in enumerate(requests):
                for h in range(2):
                    row = (2 * i + h) * rows
                    part = sums[row : row + rows, h * HD : (h + 1) * HD]
                    total[request, (head + h) * rows : (head + h + 1) * rows] += part
    for d in range(n_tp):
        outs[d][...] = total[:, own[d]].astype(BF16)


def weighted_values(pieces, va, vb, meta, prompts):
    n_tp = len(pieces)
    rows, tokens = pieces[0].shape
    return pl.pallas_call(
        functools.partial(weighted_kernel, n_tp),
        in_specs=[VMEM] * (n_tp + 2) + [SMEM],
        out_specs=[VMEM] * n_tp,
        out_shape=[jax.ShapeDtypeStruct((prompts, rows, HD), BF16)] * n_tp,
        scratch_shapes=[
            pltpu.VMEM((rows * n_tp, tokens), BF16),
            pltpu.VMEM((prompts, rows * n_tp, HD), F32),
        ],
        compiler_params=pltpu.CompilerParams(vmem_limit_bytes=24 * MIB),
        cost_estimate=pl.CostEstimate(
            flops=2 * tokens * rows * n_tp * HD, bytes_accessed=8 * MIB, transcendentals=0
        ),
        name="weighted",
    )(*pieces, va, vb, meta)


def summed_kernel(n_tp, *refs):
    chunks = refs[:n_tp]
    stats_ref, out_ref = refs[n_tp:]
    prompts = chunks[0].shape[0]
    total = chunks[0][...].astype(F32)
    for d in range(1, n_tp):
        total = total + chunks[d][...].astype(F32)
    out_ref[:prompts] = total.astype(BF16)
    out_ref[prompts] = stats_ref[...]


def summed(chunks, stats):
    n_tp = len(chunks)
    prompts, rows, _ = chunks[0].shape
    return pl.pallas_call(
        functools.partial(summed_kernel, n_tp),
        in_specs=[VMEM] * (n_tp + 1),
        out_specs=VMEM,
        out_shape=jax.ShapeDtypeStruct((prompts + 1, rows, HD), BF16),
        compiler_params=pltpu.CompilerParams(vmem_limit_bytes=8 * MIB),
        cost_estimate=pl.CostEstimate(flops=0, bytes_accessed=4 * MIB, transcendentals=0),
        name="summed",
    )(*chunks, stats)


def output_kernel(n_seq, *refs):
    pieces = refs[:n_seq]
    fresh_ref, value_ref, wa_ref, wb_ref, out_ref, held = refs[n_seq:]
    more, rows_local, _ = pieces[0].shape
    prompts = more - 1
    new_count = fresh_ref.shape[0]
    rows = new_count * GROUP
    kv_local = rows_local // rows
    heads = kv_local * GROUP
    tops, parts = [], []
    for s in range(n_seq):
        stats = pieces[s][prompts].astype(F32)
        folded = stats + pltpu.roll(stats, HD - prompts, 1)
        tops.append(folded)
        parts.append(pltpu.roll(folded, HD - 2 * prompts, 1))
    fresh = [fresh_ref[n] for n in range(new_count)]
    top = fresh[0]
    for other in fresh[1:] + tops:
        top = jnp.maximum(top, other)
    weights = [jnp.exp(f - top) for f in fresh]
    factors = [jnp.exp(t - top) for t in tops]
    total = weights[0]
    for w in weights[1:]:
        total = total + w
    for f, part in zip(factors, parts):
        total = total + f * part
    weights = [w / total for w in weights]
    factors = [f / total for f in factors]
    for r in range(prompts):
        sums = jnp.zeros((rows_local, HD), F32)
        for s in range(n_seq):
            sums = sums + factors[s][:, r : r + 1] * pieces[s][r].astype(F32)
        for n in range(new_count):
            sums = sums + weights[n][:, r : r + 1] * value_ref[r * new_count + n]
        for g in range(kv_local):
            for n in range(new_count):
                at = g * rows + n * GROUP
                held[g * GROUP : (g + 1) * GROUP, r * new_count + n] = sums[at : at + GROUP]
    half = heads // 2
    product = jnp.zeros(out_ref.shape, F32)
    for w_ref, at in ((wa_ref, 0), (wb_ref, half)):
        left = [held[h].astype(BF16) for h in range(at, at + half)]
        left = jnp.concatenate(left, axis=1)
        product = product + jnp.dot(left, w_ref[...], preferred_element_type=F32)
    out_ref[...] = product.astype(BF16)


def output_partial(pieces, fresh, values, weights):
    n_seq = len(pieces)
    new_count = fresh.shape[0]
    prompts = pieces[0].shape[0] - 1
    depth, columns = weights[0].shape
    return pl.pallas_call(
        functools.partial(output_kernel, n_seq),
        in_specs=[VMEM] * (n_seq + 4),
        out_specs=VMEM,
        out_shape=jax.ShapeDtypeStruct((prompts * new_count, columns), BF16),
        scratch_shapes=[pltpu.VMEM((2 * depth // HD, prompts * new_count, HD), F32)],
        compiler_params=pltpu.CompilerParams(vmem_limit_bytes=24 * MIB),
        name="output",
    )(*pieces, fresh, values, *weights)


def final_kernel(n_tp, *refs):
    pieces = refs[:n_tp]
    res_ref, out_ref = refs[n_tp:]
    prompts, new_count, _ = out_ref.shape
    total = pieces[0][...].astype(F32)
    for d in range(1, n_tp):
        total = total + pieces[d][...].astype(F32)
    for r in range(prompts):
        out_ref[r] = res_ref[r].astype(F32) + total[r * new_count : (r + 1) * new_count]


def final_sum(pieces, residual):
    n_tp = len(pieces)
    return pl.pallas_call(
        functools.partial(final_kernel, n_tp),
        in_specs=[VMEM] * (n_tp + 1),
        out_specs=VMEM,
        out_shape=jax.ShapeDtypeStruct(residual.shape, F32),
        compiler_params=pltpu.CompilerParams(vmem_limit_bytes=8 * MIB),
        name="final",
    )(*pieces, residual)


def on_device(
    prefill_states, kv_weight, page_counts, tail_tokens, new_query, new_keyval, residual, out_weight
):
    n_seq, n_tp = lax.axis_size("seq"), lax.axis_size("tp")
    own_rows, new_count, _ = new_query.shape
    prompts = page_counts.shape[0]
    pages = prefill_states.shape[0] // PAGE * n_seq
    query, new_kv = prepare(new_query, new_keyval)
    query = gather(query, "tp")
    acc, xa, wa, cosine, sine, cos_q, sin_q, meta = load(
        prefill_states, kv_weight, page_counts, tail_tokens, pages, new_count
    )
    new = turned(query, new_kv, cos_q, sin_q)
    k, xb, wb = rotated_keys(acc, xa, wa, prefill_states, kv_weight, cosine, sine, new)
    new = gather(new, "seq")
    scores = partial_scores(new, k, meta, prompts, n_tp)
    va, oa = project_values((xa, wa, xb, wb), out_weight, 0, scores[0])
    weights, stats = softmax_weights(exchange(scores, "tp"), meta, va, pages, prompts)
    vb, ob = project_values((xa, wa, xb, wb), out_weight, 1, stats)
    fresh, values = fresh_scores(new, stats, prompts, new_count, n_tp)
    chunks = weighted_values(gather(weights, "tp"), va, vb, meta, prompts)
    pieces = gather(summed(exchange(chunks, "tp"), stats), "seq")
    partial = output_partial(pieces, fresh, values, (oa, ob))
    return final_sum(gather(partial, "tp"), residual)


def solution(mesh):
    placed = (
        P(("groups", "seq"), "tp"),
        P("tp", None),
        P("groups"),
        P("groups"),
        P(("groups", "seq"), None, "tp"),
        P(("groups", "seq"), None, "tp"),
        P("groups", None, "seq"),
        P("tp", "seq"),
    )
    return jax.shard_map(
        on_device, mesh=mesh, in_specs=placed, out_specs=P("groups", None, "seq"), check_vma=False
    )
```

```python
import functools
import math

import jax
import jax.numpy as jnp
from jax import lax
from jax.experimental import pallas as pl
from jax.experimental.pallas import tpu as pltpu
from jax.sharding import PartitionSpec as P

QH = 64
KVH = 8
HD = 128
PAGE = 128
GROUP = QH // KVH
NEG = -1e30
F32 = jnp.float32
BF16 = jnp.bfloat16
MIB = 1 << 20

VMEM = pl.BlockSpec(memory_space=pltpu.VMEM)
SMEM = pl.BlockSpec(memory_space=pltpu.SMEM)
ANY = pl.BlockSpec(memory_space=pl.ANY)


def pairs(value, axis, d):
    return lax.ppermute(value, axis, [(i, i ^ d) for i in range(lax.axis_size(axis))])


def order(size):
    found, top = [0], size // 2
    while top:
        found += range(top, 2 * top)
        top //= 2
    return found


def reverse(size):
    return [0] + order(size)[:0:-1]


def exchange(chunks, axis):
    offsets = order(len(chunks))
    return [chunks[0]] + [pairs(c, axis, d) for c, d in zip(chunks[1:], offsets[1:])]


def gather(value, axis):
    return [value] + [pairs(value, axis, d) for d in reverse(lax.axis_size(axis))[1:]]


def lane_freqs(rows):
    lane = lax.broadcasted_iota(jnp.int32, (rows, HD), 1) % (HD // 2)
    return jnp.exp(-(lane.astype(F32) * (2.0 / HD)) * math.log(500000.0))


def sine_sign(rows):
    lane = lax.broadcasted_iota(jnp.int32, (rows, HD), 1)
    return jnp.where(lane < HD // 2, -1.0, 1.0)


def in_hbm(value):
    return pltpu.with_memory_space_constraint(value, pltpu.HBM)


def by_row(rows, numbers):
    row = lax.broadcasted_iota(jnp.int32, (rows, HD), 0)
    out = jnp.zeros((rows, HD), F32)
    for i, number in enumerate(numbers):
        out = jnp.where(row == i, number.astype(F32), out)
    return out


def page_table(pages, prompts, counts, tails, meta):
    def one_prompt(r, start):
        length = (counts[r] - 1) * PAGE + tails[r]
        meta[3 * pages + r] = length

        def one_page(i, carry):
            meta[start + i] = r
            meta[pages + start + i] = i * PAGE
            meta[2 * pages + start + i] = jnp.minimum(length - i * PAGE, PAGE)
            return carry

        lax.fori_loop(0, counts[r], one_page, 0)
        return start + counts[r]

    lax.fori_loop(0, prompts, one_prompt, 0)


def rotation_tables(pages, local_pages, meta, cos_s, sin_s):
    freqs = lane_freqs(8)
    low = lax.broadcasted_iota(jnp.int32, (8, HD), 0).astype(F32) * freqs
    low_cos, low_sin = jnp.cos(low), jnp.sin(low)
    high = lax.broadcasted_iota(jnp.int32, (PAGE // 8, HD), 0).astype(F32) * 8.0
    high = high * lane_freqs(PAGE // 8)
    high_cos, high_sin = jnp.cos(high), jnp.sin(high)
    first = lax.axis_index("seq") * local_pages
    base = by_row(local_pages, [meta[pages + first + p] for p in range(local_pages)])
    base = base * lane_freqs(local_pages)
    base_cos, base_sin = jnp.cos(base), jnp.sin(base)
    sign = sine_sign(8)
    for i in range(PAGE // 8):
        c, s = high_cos[i : i + 1], high_sin[i : i + 1]
        cosine, sine = low_cos * c - low_sin * s, low_sin * c + low_cos * s
        for p in range(local_pages):
            at = slice(p * PAGE + i * 8, p * PAGE + i * 8 + 8)
            c, s = base_cos[p : p + 1], base_sin[p : p + 1]
            cos_s[at] = cosine * c - sine * s
            sin_s[at] = sign * (sine * c + cosine * s)


def pair_columns(w_ref, rows, pair, part):
    at = [(2 * head + part) * HD for head in (2 * pair, 2 * pair + 1)]
    return jnp.concatenate([w_ref[rows, c : c + HD] for c in at], axis=1)


def copies_of(x_hbm, w_hbm, x_ref, w_ref, sems, first, size, count):
    pairs_of = []
    for i in range(count):
        source, to = pl.ds(first + i * size, size), pl.ds(i * size, size)
        x_copy = pltpu.make_async_copy(x_hbm.at[:, source], x_ref.at[:, to], sems.at[2 * i])
        w_copy = pltpu.make_async_copy(w_hbm.at[source], w_ref.at[to], sems.at[2 * i + 1])
        pairs_of.append((x_copy, w_copy))
    return pairs_of


def start(copies):
    for copy in copies:
        copy.start()


def wait(copies):
    for copy in copies:
        copy.wait()


def add_block(x_ref, w_ref, rows, acc, out, fresh):
    tokens = x_ref.shape[0]
    tall = tokens // 2
    for pair in range(KVH // 2):
        weight = pair_columns(w_ref, rows, pair, 0)
        columns = slice(2 * pair * HD, 2 * (pair + 1) * HD)
        for top in range(0, tokens, tall):
            at = slice(top, top + tall)
            product = jnp.dot(x_ref[at, rows], weight, preferred_element_type=F32)
            out[at, columns] = product if fresh else acc[at, columns] + product


def load_kernel(pages, prompts, new_count, x_hbm, w_hbm, counts, tails, *refs):
    acc, x_ref, w_ref, cos_ref, sin_ref, cos_q, sin_q, meta, sems = refs
    tokens = x_ref.shape[0]
    size = x_ref.shape[1] // 3
    copies = copies_of(x_hbm, w_hbm, x_ref, w_ref, sems, 0, size, 3)
    start(copies[0])
    page_table(pages, prompts, counts, tails, meta)
    rotation_tables(pages, tokens // PAGE, meta, cos_ref, sin_ref)
    spots = [meta[3 * pages + r] + n for r in range(prompts) for n in range(new_count)]
    angles = by_row(len(spots), spots) * lane_freqs(len(spots))
    cos_q[...] = jnp.cos(angles)
    sin_q[...] = jnp.sin(angles) * sine_sign(len(spots))
    start(copies[1])
    for i in range(2):
        wait(copies[i])
        if i == 0:
            start(copies[2])
        add_block(x_ref, w_ref, slice(i * size, (i + 1) * size), acc, acc, i == 0)
    wait(copies[2])


def load(x, kv_weight, counts, tails, pages, new_count):
    tokens, depth = x.shape
    columns = kv_weight.shape[1]
    prompts = counts.shape[0]
    part = depth // 4 * 3
    hbm = pl.BlockSpec(memory_space=pltpu.HBM)
    return pl.pallas_call(
        functools.partial(load_kernel, pages, prompts, new_count),
        in_specs=[hbm, hbm, SMEM, SMEM],
        out_specs=[VMEM] * 7 + [SMEM],
        out_shape=[
            pltpu.VMEM((tokens, KVH * HD), F32),
            pltpu.VMEM((tokens, part), BF16),
            pltpu.VMEM((part, columns), BF16),
            pltpu.VMEM((tokens, HD), F32),
            pltpu.VMEM((tokens, HD), F32),
            pltpu.VMEM((prompts * new_count, HD), F32),
            pltpu.VMEM((prompts * new_count, HD), F32),
            jax.ShapeDtypeStruct((3 * pages + prompts,), jnp.int32),
        ],
        scratch_shapes=[pltpu.SemaphoreType.DMA((6,))],
        compiler_params=pltpu.CompilerParams(vmem_limit_bytes=28 * MIB),
        cost_estimate=pl.CostEstimate(
            flops=tokens * depth * KVH * HD,
            bytes_accessed=2 * part * (tokens + columns),
            transcendentals=0,
        ),
        name="load",
    )(*[in_hbm(a) for a in (x, kv_weight, counts, tails)])


def keys_kernel(acc, xa_ref, wa_ref, x_hbm, w_hbm, cos_ref, sin_ref, after, k_ref, x_ref, w_ref, total, sems):
    tokens, size = x_ref.shape
    tall = tokens // 2
    (copies,) = copies_of(x_hbm, w_hbm, x_ref, w_ref, sems, 3 * size, size, 1)
    start(copies)
    add_block(xa_ref, wa_ref, slice(2 * size, 3 * size), acc, total, False)
    wait(copies)
    for pair in range(KVH // 2):
        weight = pair_columns(w_ref, slice(None), pair, 0)
        columns = slice(2 * pair * HD, 2 * (pair + 1) * HD)
        for top in range(0, tokens, tall):
            at = slice(top, top + tall)
            product = total[at, columns] + jnp.dot(x_ref[at], weight, preferred_element_type=F32)
            cosine, sine = cos_ref[at], sin_ref[at]
            for h in range(2):
                k = product[:, h * HD : (h + 1) * HD]
                k = k * cosine + pltpu.roll(k, HD // 2, 1) * sine
                k_ref[at, (2 * pair + h) * HD : (2 * pair + h + 1) * HD] = k.astype(BF16)


def rotated_keys(acc, xa, wa, x, kv_weight, cosine, sine, after):
    tokens, depth = x.shape
    columns = kv_weight.shape[1]
    hbm = pl.BlockSpec(memory_space=pltpu.HBM)
    return pl.pallas_call(
        keys_kernel,
        in_specs=[VMEM] * 3 + [hbm] * 2 + [VMEM] * 2 + [ANY],
        out_specs=[VMEM] * 3,
        out_shape=[
            pltpu.VMEM((tokens, KVH * HD), BF16),
            pltpu.VMEM((tokens, depth // 4), BF16),
            pltpu.VMEM((depth // 4, columns), BF16),
        ],
        scratch_shapes=[
            pltpu.VMEM((tokens, KVH * HD), F32),
            pltpu.SemaphoreType.DMA((2,)),
        ],
        compiler_params=pltpu.CompilerParams(vmem_limit_bytes=24 * MIB),
        cost_estimate=pl.CostEstimate(
            flops=tokens * depth * KVH * HD, bytes_accessed=8 * MIB, transcendentals=0
        ),
        name="keys",
    )(acc, xa, wa, in_hbm(x), in_hbm(kv_weight), cosine, sine, after)


def values_kernel(first, xa_ref, wa_ref, xb_ref, wb_ref, o_hbm, after, v_ref, o_ref, sem):
    depth = o_ref.shape[0]
    copy = pltpu.make_async_copy(o_hbm.at[pl.ds(first * depth, depth)], o_ref, sem)
    copy.start()
    tokens, columns = v_ref.shape
    tall = tokens // 2
    pairs_here = columns // (2 * HD)
    for pair in range(pairs_here):
        weights = [pair_columns(w, slice(None), first * pairs_here + pair, 1) for w in (wa_ref, wb_ref)]
        for i in range(2):
            at = slice(i * tall, (i + 1) * tall)
            product = jnp.dot(xa_ref[at], weights[0], preferred_element_type=F32)
            product = product + jnp.dot(xb_ref[at], weights[1], preferred_element_type=F32)
            v_ref[at, 2 * pair * HD : 2 * (pair + 1) * HD] = product.astype(BF16)
    copy.wait()


def project_values(blocks, out_weight, first, after):
    tokens, depth = blocks[0].shape
    columns = KVH // 2 * HD
    rows = out_weight.shape[0] // 2
    return pl.pallas_call(
        functools.partial(values_kernel, first),
        in_specs=[VMEM] * 4 + [pl.BlockSpec(memory_space=pltpu.HBM), ANY],
        out_specs=[VMEM, VMEM],
        out_shape=[
            pltpu.VMEM((tokens, columns), BF16),
            pltpu.VMEM((rows, out_weight.shape[1]), BF16),
        ],
        scratch_shapes=[pltpu.SemaphoreType.DMA],
        compiler_params=pltpu.CompilerParams(vmem_limit_bytes=24 * MIB),
        cost_estimate=pl.CostEstimate(
            flops=2 * tokens * depth * columns, bytes_accessed=8 * MIB, transcendentals=0
        ),
        name="values",
    )(*blocks, in_hbm(out_weight), after)


def by_heads(row):
    return jnp.concatenate([row[:, c : c + HD] for c in range(0, row.shape[1], HD)], axis=0)


def prepare_kernel(q_ref, kv_ref, q_out, kv_out):
    for r in range(q_ref.shape[0]):
        q, kv = q_ref[r].astype(F32), kv_ref[r].astype(F32)
        for n in range(q_ref.shape[1]):
            q_out[r, n] = by_heads(q[n : n + 1]).astype(BF16)
            kv_out[r, n] = by_heads(kv[n : n + 1])


def prepare(new_query, new_keyval):
    own_rows, new_count, columns = new_query.shape
    shape = lambda a: (own_rows, new_count, a.shape[2] // HD, HD)
    return pl.pallas_call(
        prepare_kernel,
        in_specs=[VMEM, VMEM],
        out_specs=[VMEM, VMEM],
        out_shape=[
            jax.ShapeDtypeStruct(shape(new_query), BF16),
            jax.ShapeDtypeStruct(shape(new_keyval), F32),
        ],
        compiler_params=pltpu.CompilerParams(vmem_limit_bytes=8 * MIB),
        cost_estimate=pl.CostEstimate(flops=0, bytes_accessed=MIB, transcendentals=0),
        name="prepare",
    )(in_hbm(new_query), in_hbm(new_keyval))


def turned_kernel(n_tp, *refs):
    kv_ref, cos_q, sin_q, out_ref = refs[n_tp:]
    own_rows, new_count, heads, _ = refs[0].shape
    rows = new_count * GROUP
    kv_local = heads // GROUP
    me, seq = lax.axis_index("tp"), lax.axis_index("seq")
    for r in range(own_rows):
        spots = [pl.ds((seq * own_rows + r) * new_count + n, 1) for n in range(new_count)]
        turns = [(cos_q[spot], sin_q[spot]) for spot in spots]

        def turn(value, n):
            return value * turns[n][0] + pltpu.roll(value, HD // 2, 1) * turns[n][1]

        for d in range(n_tp):
            blocks = [refs[d][r, n].astype(F32) for n in range(new_count)]
            for g in range(kv_local):
                parts = [turn(q[g * GROUP : (g + 1) * GROUP], n) for n, q in enumerate(blocks)]
                at = ((me ^ reverse(n_tp)[d]) * kv_local + g) * rows
                at = pl.ds(pl.multiple_of(at, rows), rows)
                out_ref[r, at] = jnp.concatenate(parts, axis=0).astype(BF16)
        fresh = []
        for n in range(new_count):
            row = lax.broadcasted_iota(jnp.int32, kv_ref.shape[2:], 0)
            fresh.append(jnp.where(row % 2 == 0, turn(kv_ref[r, n], n), kv_ref[r, n]))
        fresh.append(jnp.zeros((FRESH - new_count * 2 * kv_local, HD), F32))
        out_ref[r, KVH * rows :] = jnp.concatenate(fresh, axis=0).astype(BF16)


FRESH = 16


def turned(pieces, fresh, cos_q, sin_q):
    n_tp = len(pieces)
    own_rows, new_count, _, _ = pieces[0].shape
    rows = KVH * GROUP * new_count + FRESH
    return pl.pallas_call(
        functools.partial(turned_kernel, n_tp),
        in_specs=[VMEM] * (n_tp + 3),
        out_specs=VMEM,
        out_shape=jax.ShapeDtypeStruct((own_rows, rows, HD), BF16),
        compiler_params=pltpu.CompilerParams(vmem_limit_bytes=8 * MIB),
        name="turned",
    )(*pieces, fresh, cos_q, sin_q)


def scores_kernel(n_seq, n_tp, *refs):
    new = refs[:n_seq]
    k_ref, meta = refs[n_seq : n_seq + 2]
    outs = refs[n_seq + 2 : n_seq + 2 + n_tp]
    all_q, ready = refs[n_seq + 2 + n_tp :]
    own_rows = new[0].shape[0]
    local_pages = k_ref.shape[0] // PAGE
    all_rows = all_q.shape[1]
    rows = all_rows // KVH
    count = all_rows // n_tp
    scale = 1.0 / math.sqrt(HD)
    me = lax.axis_index("tp")
    seq = lax.axis_index("seq")
    first = seq * local_pages
    even = lax.broadcasted_iota(jnp.int32, (all_rows, HD), 0) // rows % 2 == 0
    for ds in range(n_seq):
        for rr in range(own_rows):
            q = new[ds][rr, :all_rows].astype(F32)
            request = (seq ^ reverse(n_seq)[ds]) * own_rows + rr
            all_q[request, :, :HD] = jnp.where(even, q, 0.0).astype(BF16)
            all_q[request, :, HD:] = jnp.where(even, 0.0, q).astype(BF16)
    for p in range(0, local_pages, 2):
        requests = [meta[first + p], meta[first + p + 1]]
        tokens = slice(p * PAGE, (p + 2) * PAGE)
        for pair in range(KVH // 2):
            k = k_ref[tokens, 2 * pair * HD : 2 * (pair + 1) * HD]
            at = slice(2 * pair * rows, 2 * (pair + 1) * rows)
            q = jnp.concatenate([all_q[request, at] for request in requests], axis=0)
            s = lax.dot_general(q, k, (((1,), (1,)), ((), ())), preferred_element_type=F32)
            for i in range(2):
                part = s[2 * i * rows : 2 * (i + 1) * rows, i * PAGE : (i + 1) * PAGE]
                here = slice((p + i) * PAGE, (p + i + 1) * PAGE)
                ready[at, here] = (part * scale).astype(BF16)
    for d in range(n_tp):
        outs[d][...] = ready[pl.ds(pl.multiple_of((me ^ order(n_tp)[d]) * count, count), count)]


def partial_scores(new, k, meta, prompts, n_tp):
    n_seq = len(new)
    all_rows = new[0].shape[1] - FRESH
    tokens = k.shape[0]
    rows = all_rows // n_tp
    return pl.pallas_call(
        functools.partial(scores_kernel, n_seq, n_tp),
        in_specs=[VMEM] * (n_seq + 1) + [SMEM],
        out_specs=[VMEM] * n_tp,
        out_shape=[jax.ShapeDtypeStruct((rows, tokens), BF16)] * n_tp,
        scratch_shapes=[
            pltpu.VMEM((prompts, all_rows, 2 * HD), BF16),
            pltpu.VMEM((all_rows, tokens), BF16),
        ],
        compiler_params=pltpu.CompilerParams(vmem_limit_bytes=24 * MIB),
        cost_estimate=pl.CostEstimate(
            flops=2 * tokens * all_rows * HD, bytes_accessed=6 * MIB, transcendentals=0
        ),
        name="scores",
    )(*new, k, meta)


def fresh_kernel(n_seq, *refs):
    new = refs[:n_seq]
    _, score_ref, value_ref = refs[n_seq:]
    new_count, rows_local, _ = score_ref.shape
    own_rows = new[0].shape[0]
    rows = new_count * GROUP
    kv_local = rows_local // rows
    scale = 1.0 / math.sqrt(HD)
    seq = lax.axis_index("seq")
    own = pl.ds(pl.multiple_of(lax.axis_index("tp") * rows_local, rows_local), rows_local)
    step = lax.broadcasted_iota(jnp.int32, (rows_local, HD), 0) % rows // GROUP
    lane = lax.broadcasted_iota(jnp.int32, (rows_local, HD), 1)
    found = [jnp.full((rows_local, HD), NEG, F32) for _ in range(new_count)]

    def spread(block, first):
        parts = [block[first + 2 * g : first + 2 * g + 1] for g in range(kv_local)]
        return jnp.concatenate([jnp.broadcast_to(a, (rows, HD)) for a in parts], axis=0)

    for ds in range(n_seq):
        for rr in range(own_rows):
            request = (seq ^ reverse(n_seq)[ds]) * own_rows + rr
            q = new[ds][rr, own].astype(F32)
            both = new[ds][rr, KVH * rows :].astype(F32)
            for n in range(new_count):
                first = n * 2 * kv_local
                s = jnp.sum(q * spread(both, first), axis=1, keepdims=True) * scale
                found[n] = jnp.where((lane == request) & (step >= n), s, found[n])
                value_ref[request * new_count + n] = spread(both, first + 1)
    for n in range(new_count):
        score_ref[n] = found[n]


def fresh_scores(new, after, prompts, new_count, n_tp):
    n_seq = len(new)
    rows = (new[0].shape[1] - FRESH) // n_tp
    return pl.pallas_call(
        functools.partial(fresh_kernel, n_seq),
        in_specs=[VMEM] * n_seq + [ANY],
        out_specs=[VMEM, VMEM],
        out_shape=[
            jax.ShapeDtypeStruct((new_count, rows, HD), F32),
            jax.ShapeDtypeStruct((prompts * new_count, rows, HD), F32),
        ],
        compiler_params=pltpu.CompilerParams(vmem_limit_bytes=16 * MIB),
        cost_estimate=pl.CostEstimate(flops=0, bytes_accessed=2 * MIB, transcendentals=0),
        name="fresh",
    )(*new, after)


def weights_kernel(pages, prompts, n_tp, *refs):
    chunks = refs[:n_tp]
    meta, _, w_ref, stats_ref = refs[n_tp:]
    rows, tokens = w_ref.shape
    local_pages = tokens // PAGE
    first = lax.axis_index("seq") * local_pages
    lane = lax.broadcasted_iota(jnp.int32, (rows, PAGE), 1)
    scores, maxima, masks, owners = [], [], [], []
    for p in range(local_pages):
        at = slice(p * PAGE, (p + 1) * PAGE)
        total = chunks[0][:, at].astype(F32)
        for d in range(1, n_tp):
            total = total + chunks[d][:, at].astype(F32)
        mask = lane < meta[2 * pages + first + p]
        total = jnp.where(mask, total, NEG)
        masks.append(mask)
        scores.append(total)
        maxima.append(jnp.max(total, axis=1, keepdims=True))
        owners.append(meta[first + p])
    quarter = lane // prompts
    spot = lane % prompts
    stats = jnp.where(quarter == 0, NEG, 0.0)
    same = [owners[p] == owners[p - 1] for p in range(1, local_pages)]
    for p in range(1, local_pages):
        maxima[p] = jnp.where(same[p - 1], jnp.maximum(maxima[p - 1], maxima[p]), maxima[p])
    for p in reversed(range(local_pages - 1)):
        maxima[p] = jnp.where(same[p], maxima[p + 1], maxima[p])
    for p in range(local_pages):
        top = maxima[p]
        high = top.astype(BF16).astype(F32)
        low = (top - high).astype(BF16).astype(F32)
        w = jnp.where(masks[p], jnp.exp(scores[p] - (high + low)), 0.0)
        w_ref[:, p * PAGE : (p + 1) * PAGE] = w.astype(BF16)
        here = spot == owners[p]
        stats = jnp.where(here & (quarter == 0), high, stats)
        stats = jnp.where(here & (quarter == 1), low, stats)
        part = jnp.sum(w, axis=1, keepdims=True)
        stats = stats + jnp.where(here & (quarter == 2), part, 0.0)
    high = stats.astype(BF16).astype(F32)
    low = pltpu.roll(stats - high, prompts, 1)
    stats_ref[...] = jnp.where(quarter == 3, low, stats).astype(BF16)


def softmax_weights(chunks, meta, after, pages, prompts):
    n_tp = len(chunks)
    rows, tokens = chunks[0].shape
    return pl.pallas_call(
        functools.partial(weights_kernel, pages, prompts, n_tp),
        in_specs=[VMEM] * n_tp + [SMEM, ANY],
        out_specs=[VMEM, VMEM],
        out_shape=[
            jax.ShapeDtypeStruct((rows, tokens), BF16),
            jax.ShapeDtypeStruct((rows, PAGE), BF16),
        ],
        compiler_params=pltpu.CompilerParams(vmem_limit_bytes=8 * MIB),
        name="weights",
    )(*chunks, meta, after)


def weighted_kernel(n_tp, *refs):
    pieces = refs[:n_tp]
    va_ref, vb_ref, meta = refs[n_tp : n_tp + 3]
    outs = refs[n_tp + 3 : n_tp + 3 + n_tp]
    ready, total = refs[n_tp + 3 + n_tp :]
    rows_local, tokens_here = pieces[0].shape
    kv_local = KVH // n_tp
    rows = rows_local // kv_local
    local_pages = tokens_here // PAGE
    first = lax.axis_index("seq") * local_pages
    me = lax.axis_index("tp")
    own = [pl.ds(pl.multiple_of((me ^ order(n_tp)[d]) * rows_local, rows_local), rows_local) for d in range(n_tp)]
    for d in range(n_tp):
        at = pl.multiple_of((me ^ reverse(n_tp)[d]) * rows_local, rows_local)
        ready[pl.ds(at, rows_local)] = pieces[d][...]
    total[...] = jnp.zeros_like(total)
    half = va_ref.shape[1] // HD
    none = jnp.zeros((2 * rows, PAGE), BF16)
    for p in range(0, local_pages, 2):
        requests = [meta[first + p], meta[first + p + 1]]
        tokens = slice(p * PAGE, (p + 2) * PAGE)
        for pair in range(KVH // 2):
            head = 2 * pair
            v_ref = va_ref if head < half else vb_ref
            v = v_ref[tokens, head % half * HD : (head % half + 2) * HD]
            at = slice(head * rows, (head + 2) * rows)
            w = [ready[at, (p + i) * PAGE : (p + i + 1) * PAGE] for i in range(2)]
            w = [jnp.concatenate([w[0], none], axis=1), jnp.concatenate([none, w[1]], axis=1)]
            sums = jnp.dot(jnp.concatenate(w, axis=0), v, preferred_element_type=F32)
            for i, request in enumerate(requests):
                for h in range(2):
                    row = (2 * i + h) * rows
                    part = sums[row : row + rows, h * HD : (h + 1) * HD]
                    total[request, (head + h) * rows : (head + h + 1) * rows] += part
    for d in range(n_tp):
        outs[d][...] = total[:, own[d]].astype(BF16)


def weighted_values(pieces, va, vb, meta, prompts):
    n_tp = len(pieces)
    rows, tokens = pieces[0].shape
    return pl.pallas_call(
        functools.partial(weighted_kernel, n_tp),
        in_specs=[VMEM] * (n_tp + 2) + [SMEM],
        out_specs=[VMEM] * n_tp,
        out_shape=[jax.ShapeDtypeStruct((prompts, rows, HD), BF16)] * n_tp,
        scratch_shapes=[
            pltpu.VMEM((rows * n_tp, tokens), BF16),
            pltpu.VMEM((prompts, rows * n_tp, HD), F32),
        ],
        compiler_params=pltpu.CompilerParams(vmem_limit_bytes=24 * MIB),
        cost_estimate=pl.CostEstimate(
            flops=2 * tokens * rows * n_tp * HD, bytes_accessed=8 * MIB, transcendentals=0
        ),
        name="weighted",
    )(*pieces, va, vb, meta)


def summed_kernel(n_tp, *refs):
    chunks = refs[:n_tp]
    stats_ref, out_ref = refs[n_tp:]
    prompts = chunks[0].shape[0]
    total = chunks[0][...].astype(F32)
    for d in range(1, n_tp):
        total = total + chunks[d][...].astype(F32)
    out_ref[:prompts] = total.astype(BF16)
    out_ref[prompts] = stats_ref[...]


def summed(chunks, stats):
    n_tp = len(chunks)
    prompts, rows, _ = chunks[0].shape
    return pl.pallas_call(
        functools.partial(summed_kernel, n_tp),
        in_specs=[VMEM] * (n_tp + 1),
        out_specs=VMEM,
        out_shape=jax.ShapeDtypeStruct((prompts + 1, rows, HD), BF16),
        compiler_params=pltpu.CompilerParams(vmem_limit_bytes=8 * MIB),
        cost_estimate=pl.CostEstimate(flops=0, bytes_accessed=4 * MIB, transcendentals=0),
        name="summed",
    )(*chunks, stats)


def output_kernel(n_seq, *refs):
    pieces = refs[:n_seq]
    fresh_ref, value_ref, wa_ref, wb_ref, out_ref, held = refs[n_seq:]
    more, rows_local, _ = pieces[0].shape
    prompts = more - 1
    new_count = fresh_ref.shape[0]
    rows = new_count * GROUP
    kv_local = rows_local // rows
    heads = kv_local * GROUP
    tops, parts = [], []
    for s in range(n_seq):
        stats = pieces[s][prompts].astype(F32)
        folded = stats + pltpu.roll(stats, HD - prompts, 1)
        tops.append(folded)
        parts.append(pltpu.roll(folded, HD - 2 * prompts, 1))
    fresh = [fresh_ref[n] for n in range(new_count)]
    top = fresh[0]
    for other in fresh[1:] + tops:
        top = jnp.maximum(top, other)
    weights = [jnp.exp(f - top) for f in fresh]
    factors = [jnp.exp(t - top) for t in tops]
    total = weights[0]
    for w in weights[1:]:
        total = total + w
    for f, part in zip(factors, parts):
        total = total + f * part
    weights = [w / total for w in weights]
    factors = [f / total for f in factors]
    for r in range(prompts):
        sums = jnp.zeros((rows_local, HD), F32)
        for s in range(n_seq):
            sums = sums + factors[s][:, r : r + 1] * pieces[s][r].astype(F32)
        for n in range(new_count):
            sums = sums + weights[n][:, r : r + 1] * value_ref[r * new_count + n]
        for g in range(kv_local):
            for n in range(new_count):
                at = g * rows + n * GROUP
                held[g * GROUP : (g + 1) * GROUP, r * new_count + n] = sums[at : at + GROUP]
    half = heads // 2
    product = jnp.zeros(out_ref.shape, F32)
    for w_ref, at in ((wa_ref, 0), (wb_ref, half)):
        left = [held[h].astype(BF16) for h in range(at, at + half)]
        left = jnp.concatenate(left, axis=1)
        product = product + jnp.dot(left, w_ref[...], preferred_element_type=F32)
    out_ref[...] = product.astype(BF16)


def output_partial(pieces, fresh, values, weights):
    n_seq = len(pieces)
    new_count = fresh.shape[0]
    prompts = pieces[0].shape[0] - 1
    depth, columns = weights[0].shape
    return pl.pallas_call(
        functools.partial(output_kernel, n_seq),
        in_specs=[VMEM] * (n_seq + 4),
        out_specs=VMEM,
        out_shape=jax.ShapeDtypeStruct((prompts * new_count, columns), BF16),
        scratch_shapes=[pltpu.VMEM((2 * depth // HD, prompts * new_count, HD), F32)],
        compiler_params=pltpu.CompilerParams(vmem_limit_bytes=24 * MIB),
        name="output",
    )(*pieces, fresh, values, *weights)


def final_kernel(n_tp, *refs):
    pieces = refs[:n_tp]
    res_ref, out_ref = refs[n_tp:]
    prompts, new_count, _ = out_ref.shape
    total = pieces[0][...].astype(F32)
    for d in range(1, n_tp):
        total = total + pieces[d][...].astype(F32)
    for r in range(prompts):
        out_ref[r] = res_ref[r].astype(F32) + total[r * new_count : (r + 1) * new_count]


def final_sum(pieces, residual):
    n_tp = len(pieces)
    return pl.pallas_call(
        functools.partial(final_kernel, n_tp),
        in_specs=[VMEM] * (n_tp + 1),
        out_specs=VMEM,
        out_shape=jax.ShapeDtypeStruct(residual.shape, F32),
        compiler_params=pltpu.CompilerParams(vmem_limit_bytes=8 * MIB),
        name="final",
    )(*pieces, residual)


def on_device(
    prefill_states, kv_weight, page_counts, tail_tokens, new_query, new_keyval, residual, out_weight
):
    n_seq, n_tp = lax.axis_size("seq"), lax.axis_size("tp")
    own_rows, new_count, _ = new_query.shape
    prompts = page_counts.shape[0]
    pages = prefill_states.shape[0] // PAGE * n_seq
    query, new_kv = prepare(new_query, new_keyval)
    query = gather(query, "tp")
    acc, xa, wa, cosine, sine, cos_q, sin_q, meta = load(
        prefill_states, kv_weight, page_counts, tail_tokens, pages, new_count
    )
    new = turned(query, new_kv, cos_q, sin_q)
    k, xb, wb = rotated_keys(acc, xa, wa, prefill_states, kv_weight, cosine, sine, new)
    new = gather(new, "seq")
    scores = partial_scores(new, k, meta, prompts, n_tp)
    va, oa = project_values((xa, wa, xb, wb), out_weight, 0, scores[0])
    weights, stats = softmax_weights(exchange(scores, "tp"), meta, va, pages, prompts)
    vb, ob = project_values((xa, wa, xb, wb), out_weight, 1, stats)
    fresh, values = fresh_scores(new, stats, prompts, new_count, n_tp)
    chunks = weighted_values(gather(weights, "tp"), va, vb, meta, prompts)
    pieces = gather(summed(exchange(chunks, "tp"), stats), "seq")
    partial = output_partial(pieces, fresh, values, (oa, ob))
    return final_sum(gather(partial, "tp"), residual)


def solution(mesh):
    placed = (
        P(("groups", "seq"), "tp"),
        P("tp", None),
        P("groups"),
        P("groups"),
        P(("groups", "seq"), None, "tp"),
        P(("groups", "seq"), None, "tp"),
        P("groups", None, "seq"),
        P("tp", "seq"),
    )
    return jax.shard_map(
        on_device, mesh=mesh, in_specs=placed, out_specs=P("groups", None, "seq"), check_vma=False
    )
```

```python
import functools
import math

import jax
import jax.numpy as jnp
from jax import lax
from jax.experimental import pallas as pl
from jax.experimental.pallas import tpu as pltpu
from jax.sharding import PartitionSpec as P

QH = 64
KVH = 8
HD = 128
PAGE = 128
GROUP = QH // KVH
NEG = -1e30
F32 = jnp.float32
BF16 = jnp.bfloat16
MIB = 1 << 20

VMEM = pl.BlockSpec(memory_space=pltpu.VMEM)
SMEM = pl.BlockSpec(memory_space=pltpu.SMEM)
ANY = pl.BlockSpec(memory_space=pl.ANY)


def pairs(value, axis, d):
    return lax.ppermute(value, axis, [(i, i ^ d) for i in range(lax.axis_size(axis))])


def order(size):
    found, top = [0], size // 2
    while top:
        found += range(top, 2 * top)
        top //= 2
    return found


def reverse(size):
    return [0] + order(size)[:0:-1]


def exchange(chunks, axis):
    offsets = order(len(chunks))
    return [chunks[0]] + [pairs(c, axis, d) for c, d in zip(chunks[1:], offsets[1:])]


def gather(value, axis, offsets=None):
    offsets = offsets or reverse(lax.axis_size(axis))
    return [value] + [pairs(value, axis, d) for d in offsets[1:]]


def falling(size):
    return [0] + list(range(size - 1, 0, -1))


def lane_freqs(rows):
    lane = lax.broadcasted_iota(jnp.int32, (rows, HD), 1) % (HD // 2)
    return jnp.exp(-(lane.astype(F32) * (2.0 / HD)) * math.log(500000.0))


def sine_sign(rows):
    lane = lax.broadcasted_iota(jnp.int32, (rows, HD), 1)
    return jnp.where(lane < HD // 2, -1.0, 1.0)


def in_hbm(value):
    return pltpu.with_memory_space_constraint(value, pltpu.HBM)


def by_row(rows, numbers):
    row = lax.broadcasted_iota(jnp.int32, (rows, HD), 0)
    out = jnp.zeros((rows, HD), F32)
    for i, number in enumerate(numbers):
        out = jnp.where(row == i, number.astype(F32), out)
    return out


def page_table(pages, prompts, counts, tails, meta):
    def one_prompt(r, start):
        length = (counts[r] - 1) * PAGE + tails[r]
        meta[3 * pages + r] = length

        def one_page(i, carry):
            meta[start + i] = r
            meta[pages + start + i] = i * PAGE
            meta[2 * pages + start + i] = jnp.minimum(length - i * PAGE, PAGE)
            return carry

        lax.fori_loop(0, counts[r], one_page, 0)
        return start + counts[r]

    lax.fori_loop(0, prompts, one_prompt, 0)


def rotation_tables(pages, local_pages, meta, cos_s, sin_s):
    freqs = lane_freqs(8)
    low = lax.broadcasted_iota(jnp.int32, (8, HD), 0).astype(F32) * freqs
    low_cos, low_sin = jnp.cos(low), jnp.sin(low)
    high = lax.broadcasted_iota(jnp.int32, (PAGE // 8, HD), 0).astype(F32) * 8.0
    high = high * lane_freqs(PAGE // 8)
    high_cos, high_sin = jnp.cos(high), jnp.sin(high)
    first = lax.axis_index("seq") * local_pages
    base = by_row(local_pages, [meta[pages + first + p] for p in range(local_pages)])
    base = base * lane_freqs(local_pages)
    base_cos, base_sin = jnp.cos(base), jnp.sin(base)
    sign = sine_sign(8)
    for i in range(PAGE // 8):
        c, s = high_cos[i : i + 1], high_sin[i : i + 1]
        cosine, sine = low_cos * c - low_sin * s, low_sin * c + low_cos * s
        for p in range(local_pages):
            at = slice(p * PAGE + i * 8, p * PAGE + i * 8 + 8)
            c, s = base_cos[p : p + 1], base_sin[p : p + 1]
            cos_s[at] = cosine * c - sine * s
            sin_s[at] = sign * (sine * c + cosine * s)


def pair_columns(w_ref, rows, pair, part):
    at = [(2 * head + part) * HD for head in (2 * pair, 2 * pair + 1)]
    return jnp.concatenate([w_ref[rows, c : c + HD] for c in at], axis=1)


def copies_of(x_hbm, w_hbm, x_ref, w_ref, sems, first, size, count):
    pairs_of = []
    for i in range(count):
        source, to = pl.ds(first + i * size, size), pl.ds(i * size, size)
        x_copy = pltpu.make_async_copy(x_hbm.at[:, source], x_ref.at[:, to], sems.at[2 * i])
        w_copy = pltpu.make_async_copy(w_hbm.at[source], w_ref.at[to], sems.at[2 * i + 1])
        pairs_of.append((x_copy, w_copy))
    return pairs_of


def start(copies):
    for copy in copies:
        copy.start()


def wait(copies):
    for copy in copies:
        copy.wait()


def add_block(x_ref, w_ref, rows, acc, out, fresh):
    tokens = x_ref.shape[0]
    tall = tokens
    for pair in range(KVH // 2):
        weight = pair_columns(w_ref, rows, pair, 0)
        columns = slice(2 * pair * HD, 2 * (pair + 1) * HD)
        for top in range(0, tokens, tall):
            at = slice(top, top + tall)
            product = jnp.dot(x_ref[at, rows], weight, preferred_element_type=F32)
            out[at, columns] = product if fresh else acc[at, columns] + product


def load_kernel(pages, prompts, new_count, x_hbm, w_hbm, counts, tails, *refs):
    acc, x_ref, w_ref, cos_ref, sin_ref, cos_q, sin_q, meta, sems = refs
    tokens = x_ref.shape[0]
    size = x_ref.shape[1] // 3
    copies = copies_of(x_hbm, w_hbm, x_ref, w_ref, sems, 0, size, 3)
    start(copies[0])
    page_table(pages, prompts, counts, tails, meta)
    rotation_tables(pages, tokens // PAGE, meta, cos_ref, sin_ref)
    spots = [meta[3 * pages + r] + n for r in range(prompts) for n in range(new_count)]
    angles = by_row(len(spots), spots) * lane_freqs(len(spots))
    cos_q[...] = jnp.cos(angles)
    sin_q[...] = jnp.sin(angles) * sine_sign(len(spots))
    start(copies[1])
    for i in range(2):
        wait(copies[i])
        if i == 0:
            start(copies[2])
        add_block(x_ref, w_ref, slice(i * size, (i + 1) * size), acc, acc, i == 0)
    wait(copies[2])


def load(x, kv_weight, counts, tails, pages, new_count):
    tokens, depth = x.shape
    columns = kv_weight.shape[1]
    prompts = counts.shape[0]
    part = depth // 4 * 3
    hbm = pl.BlockSpec(memory_space=pltpu.HBM)
    return pl.pallas_call(
        functools.partial(load_kernel, pages, prompts, new_count),
        in_specs=[hbm, hbm, SMEM, SMEM],
        out_specs=[VMEM] * 7 + [SMEM],
        out_shape=[
            pltpu.VMEM((tokens, KVH * HD), F32),
            pltpu.VMEM((tokens, part), BF16),
            pltpu.VMEM((part, columns), BF16),
            pltpu.VMEM((tokens, HD), F32),
            pltpu.VMEM((tokens, HD), F32),
            pltpu.VMEM((prompts * new_count, HD), F32),
            pltpu.VMEM((prompts * new_count, HD), F32),
            jax.ShapeDtypeStruct((3 * pages + prompts,), jnp.int32),
        ],
        scratch_shapes=[pltpu.SemaphoreType.DMA((6,))],
        compiler_params=pltpu.CompilerParams(vmem_limit_bytes=28 * MIB),
        cost_estimate=pl.CostEstimate(
            flops=tokens * depth * KVH * HD,
            bytes_accessed=2 * part * (tokens + columns),
            transcendentals=0,
        ),
        name="load",
    )(*[in_hbm(a) for a in (x, kv_weight, counts, tails)])


def keys_kernel(acc, xa_ref, wa_ref, x_hbm, w_hbm, cos_ref, sin_ref, after, k_ref, x_ref, w_ref, total, sems):
    tokens, size = x_ref.shape
    tall = tokens
    (copies,) = copies_of(x_hbm, w_hbm, x_ref, w_ref, sems, 3 * size, size, 1)
    start(copies)
    add_block(xa_ref, wa_ref, slice(2 * size, 3 * size), acc, total, False)
    wait(copies)
    for pair in range(KVH // 2):
        weight = pair_columns(w_ref, slice(None), pair, 0)
        columns = slice(2 * pair * HD, 2 * (pair + 1) * HD)
        for top in range(0, tokens, tall):
            at = slice(top, top + tall)
            product = total[at, columns] + jnp.dot(x_ref[at], weight, preferred_element_type=F32)
            cosine, sine = cos_ref[at], sin_ref[at]
            for h in range(2):
                k = product[:, h * HD : (h + 1) * HD]
                k = k * cosine + pltpu.roll(k, HD // 2, 1) * sine
                k_ref[at, (2 * pair + h) * HD : (2 * pair + h + 1) * HD] = k.astype(BF16)


def rotated_keys(acc, xa, wa, x, kv_weight, cosine, sine, after):
    tokens, depth = x.shape
    columns = kv_weight.shape[1]
    hbm = pl.BlockSpec(memory_space=pltpu.HBM)
    return pl.pallas_call(
        keys_kernel,
        in_specs=[VMEM] * 3 + [hbm] * 2 + [VMEM] * 2 + [ANY],
        out_specs=[VMEM] * 3,
        out_shape=[
            pltpu.VMEM((tokens, KVH * HD), BF16),
            pltpu.VMEM((tokens, depth // 4), BF16),
            pltpu.VMEM((depth // 4, columns), BF16),
        ],
        scratch_shapes=[
            pltpu.VMEM((tokens, KVH * HD), F32),
            pltpu.SemaphoreType.DMA((2,)),
        ],
        compiler_params=pltpu.CompilerParams(vmem_limit_bytes=24 * MIB),
        cost_estimate=pl.CostEstimate(
            flops=tokens * depth * KVH * HD, bytes_accessed=8 * MIB, transcendentals=0
        ),
        name="keys",
    )(acc, xa, wa, in_hbm(x), in_hbm(kv_weight), cosine, sine, after)


def values_kernel(first, xa_ref, wa_ref, xb_ref, wb_ref, o_hbm, after, v_ref, o_ref, sem):
    depth = o_ref.shape[0]
    copy = pltpu.make_async_copy(o_hbm.at[pl.ds(first * depth, depth)], o_ref, sem)
    copy.start()
    tokens, columns = v_ref.shape
    tall = tokens // 2
    pairs_here = columns // (2 * HD)
    for pair in range(pairs_here):
        weights = [pair_columns(w, slice(None), first * pairs_here + pair, 1) for w in (wa_ref, wb_ref)]
        for i in range(2):
            at = slice(i * tall, (i + 1) * tall)
            product = jnp.dot(xa_ref[at], weights[0], preferred_element_type=F32)
            product = product + jnp.dot(xb_ref[at], weights[1], preferred_element_type=F32)
            v_ref[at, 2 * pair * HD : 2 * (pair + 1) * HD] = product.astype(BF16)
    copy.wait()


def project_values(blocks, out_weight, first, after):
    tokens, depth = blocks[0].shape
    columns = KVH // 2 * HD
    rows = out_weight.shape[0] // 2
    return pl.pallas_call(
        functools.partial(values_kernel, first),
        in_specs=[VMEM] * 4 + [pl.BlockSpec(memory_space=pltpu.HBM), ANY],
        out_specs=[VMEM, VMEM],
        out_shape=[
            pltpu.VMEM((tokens, columns), BF16),
            pltpu.VMEM((rows, out_weight.shape[1]), BF16),
        ],
        scratch_shapes=[pltpu.SemaphoreType.DMA],
        compiler_params=pltpu.CompilerParams(vmem_limit_bytes=24 * MIB),
        cost_estimate=pl.CostEstimate(
            flops=2 * tokens * depth * columns, bytes_accessed=8 * MIB, transcendentals=0
        ),
        name="values",
    )(*blocks, in_hbm(out_weight), after)


def by_heads(row):
    return jnp.concatenate([row[:, c : c + HD] for c in range(0, row.shape[1], HD)], axis=0)


def turned_kernel(n_tp, *refs):
    kv_ref, cos_q, sin_q, out_ref = refs[n_tp:]
    own_rows, new_count, columns = refs[0].shape
    rows = new_count * GROUP
    kv_local = columns // HD // GROUP
    me, seq = lax.axis_index("tp"), lax.axis_index("seq")
    for r in range(own_rows):
        spots = [pl.ds((seq * own_rows + r) * new_count + n, 1) for n in range(new_count)]
        turns = [(cos_q[spot], sin_q[spot]) for spot in spots]

        def turn(value, n):
            return value * turns[n][0] + pltpu.roll(value, HD // 2, 1) * turns[n][1]

        for d in range(n_tp):
            raw = refs[d][r].astype(F32)
            blocks = [by_heads(raw[n : n + 1]) for n in range(new_count)]
            for g in range(kv_local):
                parts = [turn(q[g * GROUP : (g + 1) * GROUP], n) for n, q in enumerate(blocks)]
                at = ((me ^ falling(n_tp)[d]) * kv_local + g) * rows
                at = pl.ds(pl.multiple_of(at, rows), rows)
                out_ref[r, at] = jnp.concatenate(parts, axis=0).astype(BF16)
        raw = kv_ref[r].astype(F32)
        fresh = []
        for n in range(new_count):
            kv = by_heads(raw[n : n + 1])
            row = lax.broadcasted_iota(jnp.int32, kv.shape, 0)
            fresh.append(jnp.where(row % 2 == 0, turn(kv, n), kv))
        fresh.append(jnp.zeros((FRESH - new_count * 2 * kv_local, HD), F32))
        out_ref[r, KVH * rows :] = jnp.concatenate(fresh, axis=0).astype(BF16)


FRESH = 16


def turned(pieces, fresh, cos_q, sin_q):
    n_tp = len(pieces)
    own_rows, new_count, _ = pieces[0].shape
    rows = KVH * GROUP * new_count + FRESH
    return pl.pallas_call(
        functools.partial(turned_kernel, n_tp),
        in_specs=[VMEM] * (n_tp + 3),
        out_specs=VMEM,
        out_shape=jax.ShapeDtypeStruct((own_rows, rows, HD), BF16),
        compiler_params=pltpu.CompilerParams(vmem_limit_bytes=8 * MIB),
        name="turned",
    )(*pieces, fresh, cos_q, sin_q)


def scores_kernel(n_seq, n_tp, *refs):
    new = refs[:n_seq]
    k_ref, meta = refs[n_seq : n_seq + 2]
    outs = refs[n_seq + 2 : n_seq + 2 + n_tp]
    all_q, ready = refs[n_seq + 2 + n_tp :]
    own_rows = new[0].shape[0]
    local_pages = k_ref.shape[0] // PAGE
    all_rows = all_q.shape[1]
    rows = all_rows // KVH
    count = all_rows // n_tp
    scale = 1.0 / math.sqrt(HD)
    me = lax.axis_index("tp")
    seq = lax.axis_index("seq")
    first = seq * local_pages
    even = lax.broadcasted_iota(jnp.int32, (all_rows, HD), 0) // rows % 2 == 0
    for ds in range(n_seq):
        for rr in range(own_rows):
            q = new[ds][rr, :all_rows].astype(F32)
            request = (seq ^ reverse(n_seq)[ds]) * own_rows + rr
            all_q[request, :, :HD] = jnp.where(even, q, 0.0).astype(BF16)
            all_q[request, :, HD:] = jnp.where(even, 0.0, q).astype(BF16)
    for p in range(0, local_pages, 2):
        requests = [meta[first + p], meta[first + p + 1]]
        tokens = slice(p * PAGE, (p + 2) * PAGE)
        for pair in range(KVH // 2):
            k = k_ref[tokens, 2 * pair * HD : 2 * (pair + 1) * HD]
            at = slice(2 * pair * rows, 2 * (pair + 1) * rows)
            q = jnp.concatenate([all_q[request, at] for request in requests], axis=0)
            s = lax.dot_general(q, k, (((1,), (1,)), ((), ())), preferred_element_type=F32)
            for i in range(2):
                part = s[2 * i * rows : 2 * (i + 1) * rows, i * PAGE : (i + 1) * PAGE]
                here = slice((p + i) * PAGE, (p + i + 1) * PAGE)
                ready[at, here] = (part * scale).astype(BF16)
    for d in range(n_tp):
        outs[d][...] = ready[pl.ds(pl.multiple_of((me ^ order(n_tp)[d]) * count, count), count)]


def partial_scores(new, k, meta, prompts, n_tp):
    n_seq = len(new)
    all_rows = new[0].shape[1] - FRESH
    tokens = k.shape[0]
    rows = all_rows // n_tp
    return pl.pallas_call(
        functools.partial(scores_kernel, n_seq, n_tp),
        in_specs=[VMEM] * (n_seq + 1) + [SMEM],
        out_specs=[VMEM] * n_tp,
        out_shape=[jax.ShapeDtypeStruct((rows, tokens), BF16)] * n_tp,
        scratch_shapes=[
            pltpu.VMEM((prompts, all_rows, 2 * HD), BF16),
            pltpu.VMEM((all_rows, tokens), BF16),
        ],
        compiler_params=pltpu.CompilerParams(vmem_limit_bytes=24 * MIB),
        cost_estimate=pl.CostEstimate(
            flops=2 * tokens * all_rows * HD, bytes_accessed=6 * MIB, transcendentals=0
        ),
        name="scores",
    )(*new, k, meta)


def fresh_kernel(n_seq, *refs):
    new = refs[:n_seq]
    _, score_ref, value_ref = refs[n_seq:]
    new_count, rows_local, _ = score_ref.shape
    own_rows = new[0].shape[0]
    rows = new_count * GROUP
    kv_local = rows_local // rows
    scale = 1.0 / math.sqrt(HD)
    seq = lax.axis_index("seq")
    own = pl.ds(pl.multiple_of(lax.axis_index("tp") * rows_local, rows_local), rows_local)
    step = lax.broadcasted_iota(jnp.int32, (rows_local, HD), 0) % rows // GROUP
    lane = lax.broadcasted_iota(jnp.int32, (rows_local, HD), 1)
    found = [jnp.full((rows_local, HD), NEG, F32) for _ in range(new_count)]

    def spread(block, first):
        parts = [block[first + 2 * g : first + 2 * g + 1] for g in range(kv_local)]
        return jnp.concatenate([jnp.broadcast_to(a, (rows, HD)) for a in parts], axis=0)

    for ds in range(n_seq):
        for rr in range(own_rows):
            request = (seq ^ reverse(n_seq)[ds]) * own_rows + rr
            q = new[ds][rr, own].astype(F32)
            both = new[ds][rr, KVH * rows :].astype(F32)
            for n in range(new_count):
                first = n * 2 * kv_local
                s = jnp.sum(q * spread(both, first), axis=1, keepdims=True) * scale
                found[n] = jnp.where((lane == request) & (step >= n), s, found[n])
                value_ref[request * new_count + n] = spread(both, first + 1)
    for n in range(new_count):
        score_ref[n] = found[n]


def fresh_scores(new, after, prompts, new_count, n_tp):
    n_seq = len(new)
    rows = (new[0].shape[1] - FRESH) // n_tp
    return pl.pallas_call(
        functools.partial(fresh_kernel, n_seq),
        in_specs=[VMEM] * n_seq + [ANY],
        out_specs=[VMEM, VMEM],
        out_shape=[
            jax.ShapeDtypeStruct((new_count, rows, HD), F32),
            jax.ShapeDtypeStruct((prompts * new_count, rows, HD), F32),
        ],
        compiler_params=pltpu.CompilerParams(vmem_limit_bytes=16 * MIB),
        cost_estimate=pl.CostEstimate(flops=0, bytes_accessed=2 * MIB, transcendentals=0),
        name="fresh",
    )(*new, after)


def weights_kernel(pages, prompts, n_tp, *refs):
    chunks = refs[:n_tp]
    meta, _, w_ref, stats_ref = refs[n_tp:]
    rows, tokens = w_ref.shape
    local_pages = tokens // PAGE
    first = lax.axis_index("seq") * local_pages
    lane = lax.broadcasted_iota(jnp.int32, (rows, PAGE), 1)
    scores, maxima, masks, owners = [], [], [], []
    for p in range(local_pages):
        at = slice(p * PAGE, (p + 1) * PAGE)
        total = chunks[0][:, at].astype(F32)
        for d in range(1, n_tp):
            total = total + chunks[d][:, at].astype(F32)
        mask = lane < meta[2 * pages + first + p]
        total = jnp.where(mask, total, NEG)
        masks.append(mask)
        scores.append(total)
        maxima.append(jnp.max(total, axis=1, keepdims=True))
        owners.append(meta[first + p])
    quarter = lane // prompts
    spot = lane % prompts
    stats = jnp.where(quarter == 0, NEG, 0.0)
    same = [owners[p] == owners[p - 1] for p in range(1, local_pages)]
    for p in range(1, local_pages):
        maxima[p] = jnp.where(same[p - 1], jnp.maximum(maxima[p - 1], maxima[p]), maxima[p])
    for p in reversed(range(local_pages - 1)):
        maxima[p] = jnp.where(same[p], maxima[p + 1], maxima[p])
    for p in range(local_pages):
        top = maxima[p]
        high = top.astype(BF16).astype(F32)
        low = (top - high).astype(BF16).astype(F32)
        w = jnp.where(masks[p], jnp.exp(scores[p] - (high + low)), 0.0)
        w_ref[:, p * PAGE : (p + 1) * PAGE] = w.astype(BF16)
        here = spot == owners[p]
        stats = jnp.where(here & (quarter == 0), high, stats)
        stats = jnp.where(here & (quarter == 1), low, stats)
        part = jnp.sum(w, axis=1, keepdims=True)
        stats = stats + jnp.where(here & (quarter == 2), part, 0.0)
    high = stats.astype(BF16).astype(F32)
    low = pltpu.roll(stats - high, prompts, 1)
    stats_ref[...] = jnp.where(quarter == 3, low, stats).astype(BF16)


def softmax_weights(chunks, meta, after, pages, prompts):
    n_tp = len(chunks)
    rows, tokens = chunks[0].shape
    return pl.pallas_call(
        functools.partial(weights_kernel, pages, prompts, n_tp),
        in_specs=[VMEM] * n_tp + [SMEM, ANY],
        out_specs=[VMEM, VMEM],
        out_shape=[
            jax.ShapeDtypeStruct((rows, tokens), BF16),
            jax.ShapeDtypeStruct((rows, PAGE), BF16),
        ],
        compiler_params=pltpu.CompilerParams(vmem_limit_bytes=8 * MIB),
        name="weights",
    )(*chunks, meta, after)


def weighted_kernel(n_tp, *refs):
    pieces = refs[:n_tp]
    va_ref, vb_ref, meta = refs[n_tp : n_tp + 3]
    outs = refs[n_tp + 3 : n_tp + 3 + n_tp]
    ready, total = refs[n_tp + 3 + n_tp :]
    rows_local, tokens_here = pieces[0].shape
    kv_local = KVH // n_tp
    rows = rows_local // kv_local
    local_pages = tokens_here // PAGE
    first = lax.axis_index("seq") * local_pages
    me = lax.axis_index("tp")
    own = [pl.ds(pl.multiple_of((me ^ order(n_tp)[d]) * rows_local, rows_local), rows_local) for d in range(n_tp)]
    for d in range(n_tp):
        at = pl.multiple_of((me ^ reverse(n_tp)[d]) * rows_local, rows_local)
        ready[pl.ds(at, rows_local)] = pieces[d][...]
    total[...] = jnp.zeros_like(total)
    half = va_ref.shape[1] // HD
    none = jnp.zeros((2 * rows, PAGE), BF16)
    for p in range(0, local_pages, 2):
        requests = [meta[first + p], meta[first + p + 1]]
        tokens = slice(p * PAGE, (p + 2) * PAGE)
        for pair in range(KVH // 2):
            head = 2 * pair
            v_ref = va_ref if head < half else vb_ref
            v = v_ref[tokens, head % half * HD : (head % half + 2) * HD]
            at = slice(head * rows, (head + 2) * rows)
            w = [ready[at, (p + i) * PAGE : (p + i + 1) * PAGE] for i in range(2)]
            w = [jnp.concatenate([w[0], none], axis=1), jnp.concatenate([none, w[1]], axis=1)]
            sums = jnp.dot(jnp.concatenate(w, axis=0), v, preferred_element_type=F32)
            for i, request in enumerate(requests):
                for h in range(2):
                    row = (2 * i + h) * rows
                    part = sums[row : row + rows, h * HD : (h + 1) * HD]
                    total[request, (head + h) * rows : (head + h + 1) * rows] += part
    for d in range(n_tp):
        outs[d][...] = total[:, own[d]].astype(BF16)


def weighted_values(pieces, va, vb, meta, prompts):
    n_tp = len(pieces)
    rows, tokens = pieces[0].shape
    return pl.pallas_call(
        functools.partial(weighted_kernel, n_tp),
        in_specs=[VMEM] * (n_tp + 2) + [SMEM],
        out_specs=[VMEM] * n_tp,
        out_shape=[jax.ShapeDtypeStruct((prompts, rows, HD), BF16)] * n_tp,
        scratch_shapes=[
            pltpu.VMEM((rows * n_tp, tokens), BF16),
            pltpu.VMEM((prompts, rows * n_tp, HD), F32),
        ],
        compiler_params=pltpu.CompilerParams(vmem_limit_bytes=24 * MIB),
        cost_estimate=pl.CostEstimate(
            flops=2 * tokens * rows * n_tp * HD, bytes_accessed=8 * MIB, transcendentals=0
        ),
        name="weighted",
    )(*pieces, va, vb, meta)


def summed_kernel(n_tp, *refs):
    chunks = refs[:n_tp]
    stats_ref, out_ref = refs[n_tp:]
    prompts = chunks[0].shape[0]
    total = chunks[0][...].astype(F32)
    for d in range(1, n_tp):
        total = total + chunks[d][...].astype(F32)
    out_ref[:prompts] = total.astype(BF16)
    out_ref[prompts] = stats_ref[...]


def summed(chunks, stats):
    n_tp = len(chunks)
    prompts, rows, _ = chunks[0].shape
    return pl.pallas_call(
        functools.partial(summed_kernel, n_tp),
        in_specs=[VMEM] * (n_tp + 1),
        out_specs=VMEM,
        out_shape=jax.ShapeDtypeStruct((prompts + 1, rows, HD), BF16),
        compiler_params=pltpu.CompilerParams(vmem_limit_bytes=8 * MIB),
        cost_estimate=pl.CostEstimate(flops=0, bytes_accessed=4 * MIB, transcendentals=0),
        name="summed",
    )(*chunks, stats)


def output_kernel(n_seq, *refs):
    pieces = refs[:n_seq]
    fresh_ref, value_ref, wa_ref, wb_ref, out_ref, held = refs[n_seq:]
    more, rows_local, _ = pieces[0].shape
    prompts = more - 1
    new_count = fresh_ref.shape[0]
    rows = new_count * GROUP
    kv_local = rows_local // rows
    heads = kv_local * GROUP
    tops, parts = [], []
    for s in range(n_seq):
        stats = pieces[s][prompts].astype(F32)
        folded = stats + pltpu.roll(stats, HD - prompts, 1)
        tops.append(folded)
        parts.append(pltpu.roll(folded, HD - 2 * prompts, 1))
    fresh = [fresh_ref[n] for n in range(new_count)]
    top = fresh[0]
    for other in fresh[1:] + tops:
        top = jnp.maximum(top, other)
    weights = [jnp.exp(f - top) for f in fresh]
    factors = [jnp.exp(t - top) for t in tops]
    total = weights[0]
    for w in weights[1:]:
        total = total + w
    for f, part in zip(factors, parts):
        total = total + f * part
    weights = [w / total for w in weights]
    factors = [f / total for f in factors]
    for r in range(prompts):
        sums = jnp.zeros((rows_local, HD), F32)
        for s in range(n_seq):
            sums = sums + factors[s][:, r : r + 1] * pieces[s][r].astype(F32)
        for n in range(new_count):
            sums = sums + weights[n][:, r : r + 1] * value_ref[r * new_count + n]
        for g in range(kv_local):
            for n in range(new_count):
                at = g * rows + n * GROUP
                held[g * GROUP : (g + 1) * GROUP, r * new_count + n] = sums[at : at + GROUP]
    half = heads // 2
    product = jnp.zeros(out_ref.shape, F32)
    for w_ref, at in ((wa_ref, 0), (wb_ref, half)):
        left = [held[h].astype(BF16) for h in range(at, at + half)]
        left = jnp.concatenate(left, axis=1)
        product = product + jnp.dot(left, w_ref[...], preferred_element_type=F32)
    out_ref[...] = product.astype(BF16)


def output_partial(pieces, fresh, values, weights):
    n_seq = len(pieces)
    new_count = fresh.shape[0]
    prompts = pieces[0].shape[0] - 1
    depth, columns = weights[0].shape
    return pl.pallas_call(
        functools.partial(output_kernel, n_seq),
        in_specs=[VMEM] * (n_seq + 4),
        out_specs=VMEM,
        out_shape=jax.ShapeDtypeStruct((prompts * new_count, columns), BF16),
        scratch_shapes=[pltpu.VMEM((2 * depth // HD, prompts * new_count, HD), F32)],
        compiler_params=pltpu.CompilerParams(vmem_limit_bytes=24 * MIB),
        name="output",
    )(*pieces, fresh, values, *weights)


def final_kernel(n_tp, *refs):
    pieces = refs[:n_tp]
    res_ref, out_ref = refs[n_tp:]
    prompts, new_count, _ = out_ref.shape
    total = pieces[0][...].astype(F32)
    for d in range(1, n_tp):
        total = total + pieces[d][...].astype(F32)
    for r in range(prompts):
        out_ref[r] = res_ref[r].astype(F32) + total[r * new_count : (r + 1) * new_count]


def final_sum(pieces, residual):
    n_tp = len(pieces)
    return pl.pallas_call(
        functools.partial(final_kernel, n_tp),
        in_specs=[VMEM] * (n_tp + 1),
        out_specs=VMEM,
        out_shape=jax.ShapeDtypeStruct(residual.shape, F32),
        compiler_params=pltpu.CompilerParams(vmem_limit_bytes=8 * MIB),
        name="final",
    )(*pieces, residual)


def on_device(
    prefill_states, kv_weight, page_counts, tail_tokens, new_query, new_keyval, residual, out_weight
):
    n_seq, n_tp = lax.axis_size("seq"), lax.axis_size("tp")
    own_rows, new_count, _ = new_query.shape
    prompts = page_counts.shape[0]
    pages = prefill_states.shape[0] // PAGE * n_seq
    query = gather(new_query, "tp", falling(n_tp))
    acc, xa, wa, cosine, sine, cos_q, sin_q, meta = load(
        prefill_states, kv_weight, page_counts, tail_tokens, pages, new_count
    )
    new = turned(query, new_keyval, cos_q, sin_q)
    k, xb, wb = rotated_keys(acc, xa, wa, prefill_states, kv_weight, cosine, sine, new)
    new = gather(new, "seq")
    scores = partial_scores(new, k, meta, prompts, n_tp)
    va, oa = project_values((xa, wa, xb, wb), out_weight, 0, scores[0])
    weights, stats = softmax_weights(exchange(scores, "tp"), meta, va, pages, prompts)
    vb, ob = project_values((xa, wa, xb, wb), out_weight, 1, stats)
    fresh, values = fresh_scores(new, stats, prompts, new_count, n_tp)
    chunks = weighted_values(gather(weights, "tp"), va, vb, meta, prompts)
    pieces = gather(summed(exchange(chunks, "tp"), stats), "seq")
    partial = output_partial(pieces, fresh, values, (oa, ob))
    return final_sum(gather(partial, "tp"), residual)


def solution(mesh):
    placed = (
        P(("groups", "seq"), "tp"),
        P("tp", None),
        P("groups"),
        P("groups"),
        P(("groups", "seq"), None, "tp"),
        P(("groups", "seq"), None, "tp"),
        P("groups", None, "seq"),
        P("tp", "seq"),
    )
    return jax.shard_map(
        on_device, mesh=mesh, in_specs=placed, out_specs=P("groups", None, "seq"), check_vma=False
    )
```

```python
import functools
import math

import jax
import jax.numpy as jnp
from jax import lax
from jax.experimental import pallas as pl
from jax.experimental.pallas import tpu as pltpu
from jax.sharding import PartitionSpec as P

QH = 64
KVH = 8
HD = 128
PAGE = 128
GROUP = QH // KVH
NEG = -1e30
F32 = jnp.float32
BF16 = jnp.bfloat16
MIB = 1 << 20

VMEM = pl.BlockSpec(memory_space=pltpu.VMEM)
SMEM = pl.BlockSpec(memory_space=pltpu.SMEM)
ANY = pl.BlockSpec(memory_space=pl.ANY)


def pairs(value, axis, d):
    return lax.ppermute(value, axis, [(i, i ^ d) for i in range(lax.axis_size(axis))])


def order(size):
    found, top = [0], size // 2
    while top:
        found += range(top, 2 * top)
        top //= 2
    return found


def reverse(size):
    return [0] + order(size)[:0:-1]


def exchange(chunks, axis):
    offsets = order(len(chunks))
    return [chunks[0]] + [pairs(c, axis, d) for c, d in zip(chunks[1:], offsets[1:])]


def gather(value, axis, offsets=None):
    offsets = offsets or reverse(lax.axis_size(axis))
    return [value] + [pairs(value, axis, d) for d in offsets[1:]]


def falling(size):
    return [0] + list(range(size - 1, 0, -1))


def lane_freqs(rows):
    lane = lax.broadcasted_iota(jnp.int32, (rows, HD), 1) % (HD // 2)
    return jnp.exp(-(lane.astype(F32) * (2.0 / HD)) * math.log(500000.0))


def sine_sign(rows):
    lane = lax.broadcasted_iota(jnp.int32, (rows, HD), 1)
    return jnp.where(lane < HD // 2, -1.0, 1.0)


def in_hbm(value):
    return pltpu.with_memory_space_constraint(value, pltpu.HBM)


def by_row(rows, numbers):
    row = lax.broadcasted_iota(jnp.int32, (rows, HD), 0)
    out = jnp.zeros((rows, HD), F32)
    for i, number in enumerate(numbers):
        out = jnp.where(row == i, number.astype(F32), out)
    return out


def page_table(pages, prompts, counts, tails, meta):
    def one_prompt(r, start):
        length = (counts[r] - 1) * PAGE + tails[r]
        meta[3 * pages + r] = length

        def one_page(i, carry):
            meta[start + i] = r
            meta[pages + start + i] = i * PAGE
            meta[2 * pages + start + i] = jnp.minimum(length - i * PAGE, PAGE)
            return carry

        lax.fori_loop(0, counts[r], one_page, 0)
        return start + counts[r]

    lax.fori_loop(0, prompts, one_prompt, 0)


def rotation_tables(pages, local_pages, meta, cos_s, sin_s):
    freqs = lane_freqs(8)
    low = lax.broadcasted_iota(jnp.int32, (8, HD), 0).astype(F32) * freqs
    low_cos, low_sin = jnp.cos(low), jnp.sin(low)
    high = lax.broadcasted_iota(jnp.int32, (PAGE // 8, HD), 0).astype(F32) * 8.0
    high = high * lane_freqs(PAGE // 8)
    high_cos, high_sin = jnp.cos(high), jnp.sin(high)
    first = lax.axis_index("seq") * local_pages
    base = by_row(local_pages, [meta[pages + first + p] for p in range(local_pages)])
    base = base * lane_freqs(local_pages)
    base_cos, base_sin = jnp.cos(base), jnp.sin(base)
    sign = sine_sign(8)
    for i in range(PAGE // 8):
        c, s = high_cos[i : i + 1], high_sin[i : i + 1]
        cosine, sine = low_cos * c - low_sin * s, low_sin * c + low_cos * s
        for p in range(local_pages):
            at = slice(p * PAGE + i * 8, p * PAGE + i * 8 + 8)
            c, s = base_cos[p : p + 1], base_sin[p : p + 1]
            cos_s[at] = cosine * c - sine * s
            sin_s[at] = sign * (sine * c + cosine * s)


def pair_columns(w_ref, rows, pair, part):
    at = [(2 * head + part) * HD for head in (2 * pair, 2 * pair + 1)]
    return jnp.concatenate([w_ref[rows, c : c + HD] for c in at], axis=1)


def copies_of(x_hbm, w_hbm, x_ref, w_ref, sems, first, size, count):
    pairs_of = []
    for i in range(count):
        source, to = pl.ds(first + i * size, size), pl.ds(i * size, size)
        x_copy = pltpu.make_async_copy(x_hbm.at[:, source], x_ref.at[:, to], sems.at[2 * i])
        w_copy = pltpu.make_async_copy(w_hbm.at[source], w_ref.at[to], sems.at[2 * i + 1])
        pairs_of.append((x_copy, w_copy))
    return pairs_of


def start(copies):
    for copy in copies:
        copy.start()


def wait(copies):
    for copy in copies:
        copy.wait()


def add_block(x_ref, w_ref, rows, acc, out, fresh):
    tokens = x_ref.shape[0]
    tall = tokens // 2
    for pair in range(KVH // 2):
        weight = pair_columns(w_ref, rows, pair, 0)
        columns = slice(2 * pair * HD, 2 * (pair + 1) * HD)
        for top in range(0, tokens, tall):
            at = slice(top, top + tall)
            product = jnp.dot(x_ref[at, rows], weight, preferred_element_type=F32)
            out[at, columns] = product if fresh else acc[at, columns] + product


def load_kernel(pages, prompts, new_count, x_hbm, w_hbm, counts, tails, *refs):
    acc, x_ref, w_ref, cos_ref, sin_ref, cos_q, sin_q, meta, sems = refs
    tokens = x_ref.shape[0]
    size = x_ref.shape[1] // 3
    copies = copies_of(x_hbm, w_hbm, x_ref, w_ref, sems, 0, size, 3)
    start(copies[0])
    page_table(pages, prompts, counts, tails, meta)
    rotation_tables(pages, tokens // PAGE, meta, cos_ref, sin_ref)
    spots = [meta[3 * pages + r] + n for r in range(prompts) for n in range(new_count)]
    angles = by_row(len(spots), spots) * lane_freqs(len(spots))
    cos_q[...] = jnp.cos(angles)
    sin_q[...] = jnp.sin(angles) * sine_sign(len(spots))
    start(copies[1])
    for i in range(2):
        wait(copies[i])
        if i == 0:
            start(copies[2])
        add_block(x_ref, w_ref, slice(i * size, (i + 1) * size), acc, acc, i == 0)
    wait(copies[2])


def load(x, kv_weight, counts, tails, pages, new_count):
    tokens, depth = x.shape
    columns = kv_weight.shape[1]
    prompts = counts.shape[0]
    part = depth // 4 * 3
    hbm = pl.BlockSpec(memory_space=pltpu.HBM)
    return pl.pallas_call(
        functools.partial(load_kernel, pages, prompts, new_count),
        in_specs=[hbm, hbm, SMEM, SMEM],
        out_specs=[VMEM] * 7 + [SMEM],
        out_shape=[
            pltpu.VMEM((tokens, KVH * HD), F32),
            pltpu.VMEM((tokens, part), BF16),
            pltpu.VMEM((part, columns), BF16),
            pltpu.VMEM((tokens, HD), F32),
            pltpu.VMEM((tokens, HD), F32),
            pltpu.VMEM((prompts * new_count, HD), F32),
            pltpu.VMEM((prompts * new_count, HD), F32),
            jax.ShapeDtypeStruct((3 * pages + prompts,), jnp.int32),
        ],
        scratch_shapes=[pltpu.SemaphoreType.DMA((6,))],
        compiler_params=pltpu.CompilerParams(vmem_limit_bytes=28 * MIB),
        cost_estimate=pl.CostEstimate(
            flops=tokens * depth * KVH * HD,
            bytes_accessed=2 * part * (tokens + columns),
            transcendentals=0,
        ),
        name="load",
    )(*[in_hbm(a) for a in (x, kv_weight, counts, tails)])


def keys_kernel(acc, xa_ref, wa_ref, x_hbm, w_hbm, cos_ref, sin_ref, after, k_ref, x_ref, w_ref, total, sems):
    tokens, size = x_ref.shape
    tall = tokens // 2
    (copies,) = copies_of(x_hbm, w_hbm, x_ref, w_ref, sems, 3 * size, size, 1)
    start(copies)
    add_block(xa_ref, wa_ref, slice(2 * size, 3 * size), acc, total, False)
    wait(copies)
    for pair in range(KVH // 2):
        weight = pair_columns(w_ref, slice(None), pair, 0)
        columns = slice(2 * pair * HD, 2 * (pair + 1) * HD)
        for top in range(0, tokens, tall):
            at = slice(top, top + tall)
            product = total[at, columns] + jnp.dot(x_ref[at], weight, preferred_element_type=F32)
            cosine, sine = cos_ref[at], sin_ref[at]
            for h in range(2):
                k = product[:, h * HD : (h + 1) * HD]
                k = k * cosine + pltpu.roll(k, HD // 2, 1) * sine
                k_ref[at, (2 * pair + h) * HD : (2 * pair + h + 1) * HD] = k.astype(BF16)


def rotated_keys(acc, xa, wa, x, kv_weight, cosine, sine, after):
    tokens, depth = x.shape
    columns = kv_weight.shape[1]
    hbm = pl.BlockSpec(memory_space=pltpu.HBM)
    return pl.pallas_call(
        keys_kernel,
        in_specs=[VMEM] * 3 + [hbm] * 2 + [VMEM] * 2 + [ANY],
        out_specs=[VMEM] * 3,
        out_shape=[
            pltpu.VMEM((tokens, KVH * HD), BF16),
            pltpu.VMEM((tokens, depth // 4), BF16),
            pltpu.VMEM((depth // 4, columns), BF16),
        ],
        scratch_shapes=[
            pltpu.VMEM((tokens, KVH * HD), F32),
            pltpu.SemaphoreType.DMA((2,)),
        ],
        compiler_params=pltpu.CompilerParams(vmem_limit_bytes=24 * MIB),
        cost_estimate=pl.CostEstimate(
            flops=tokens * depth * KVH * HD, bytes_accessed=8 * MIB, transcendentals=0
        ),
        name="keys",
    )(acc, xa, wa, in_hbm(x), in_hbm(kv_weight), cosine, sine, after)


def values_kernel(first, xa_ref, wa_ref, xb_ref, wb_ref, o_hbm, after, v_ref, o_ref, sem):
    depth = o_ref.shape[0]
    copy = pltpu.make_async_copy(o_hbm.at[pl.ds(first * depth, depth)], o_ref, sem)
    copy.start()
    tokens, columns = v_ref.shape
    tall = tokens // 2
    pairs_here = columns // (2 * HD)
    for pair in range(pairs_here):
        weights = [pair_columns(w, slice(None), first * pairs_here + pair, 1) for w in (wa_ref, wb_ref)]
        for i in range(2):
            at = slice(i * tall, (i + 1) * tall)
            product = jnp.dot(xa_ref[at], weights[0], preferred_element_type=F32)
            product = product + jnp.dot(xb_ref[at], weights[1], preferred_element_type=F32)
            v_ref[at, 2 * pair * HD : 2 * (pair + 1) * HD] = product.astype(BF16)
    copy.wait()


def project_values(blocks, out_weight, first, after):
    tokens, depth = blocks[0].shape
    columns = KVH // 2 * HD
    rows = out_weight.shape[0] // 2
    return pl.pallas_call(
        functools.partial(values_kernel, first),
        in_specs=[VMEM] * 4 + [pl.BlockSpec(memory_space=pltpu.HBM), ANY],
        out_specs=[VMEM, VMEM],
        out_shape=[
            pltpu.VMEM((tokens, columns), BF16),
            pltpu.VMEM((rows, out_weight.shape[1]), BF16),
        ],
        scratch_shapes=[pltpu.SemaphoreType.DMA],
        compiler_params=pltpu.CompilerParams(vmem_limit_bytes=24 * MIB),
        cost_estimate=pl.CostEstimate(
            flops=2 * tokens * depth * columns, bytes_accessed=8 * MIB, transcendentals=0
        ),
        name="values",
    )(*blocks, in_hbm(out_weight), after)


def by_heads(row):
    return jnp.concatenate([row[:, c : c + HD] for c in range(0, row.shape[1], HD)], axis=0)


def turned_kernel(n_tp, *refs):
    kv_ref, cos_q, sin_q, out_ref = refs[n_tp:]
    own_rows, new_count, columns = refs[0].shape
    rows = new_count * GROUP
    kv_local = columns // HD // GROUP
    me, seq = lax.axis_index("tp"), lax.axis_index("seq")
    for r in range(own_rows):
        spots = [pl.ds((seq * own_rows + r) * new_count + n, 1) for n in range(new_count)]
        turns = [(cos_q[spot], sin_q[spot]) for spot in spots]

        def turn(value, n):
            return value * turns[n][0] + pltpu.roll(value, HD // 2, 1) * turns[n][1]

        for d in range(n_tp):
            raw = refs[d][r].astype(F32)
            blocks = [by_heads(raw[n : n + 1]) for n in range(new_count)]
            for g in range(kv_local):
                parts = [turn(q[g * GROUP : (g + 1) * GROUP], n) for n, q in enumerate(blocks)]
                at = ((me ^ falling(n_tp)[d]) * kv_local + g) * rows
                at = pl.ds(pl.multiple_of(at, rows), rows)
                out_ref[r, at] = jnp.concatenate(parts, axis=0).astype(BF16)
        raw = kv_ref[r].astype(F32)
        fresh = []
        for n in range(new_count):
            kv = by_heads(raw[n : n + 1])
            row = lax.broadcasted_iota(jnp.int32, kv.shape, 0)
            fresh.append(jnp.where(row % 2 == 0, turn(kv, n), kv))
        fresh.append(jnp.zeros((FRESH - new_count * 2 * kv_local, HD), F32))
        out_ref[r, KVH * rows :] = jnp.concatenate(fresh, axis=0).astype(BF16)


FRESH = 16


def turned(pieces, fresh, cos_q, sin_q):
    n_tp = len(pieces)
    own_rows, new_count, _ = pieces[0].shape
    rows = KVH * GROUP * new_count + FRESH
    return pl.pallas_call(
        functools.partial(turned_kernel, n_tp),
        in_specs=[VMEM] * (n_tp + 3),
        out_specs=VMEM,
        out_shape=jax.ShapeDtypeStruct((own_rows, rows, HD), BF16),
        compiler_params=pltpu.CompilerParams(vmem_limit_bytes=8 * MIB),
        name="turned",
    )(*pieces, fresh, cos_q, sin_q)


def scores_kernel(n_seq, n_tp, *refs):
    new = refs[:n_seq]
    k_ref, meta = refs[n_seq : n_seq + 2]
    outs = refs[n_seq + 2 : n_seq + 2 + n_tp]
    all_q, ready = refs[n_seq + 2 + n_tp :]
    own_rows = new[0].shape[0]
    local_pages = k_ref.shape[0] // PAGE
    all_rows = all_q.shape[1]
    rows = all_rows // KVH
    count = all_rows // n_tp
    scale = 1.0 / math.sqrt(HD)
    me = lax.axis_index("tp")
    seq = lax.axis_index("seq")
    first = seq * local_pages
    even = lax.broadcasted_iota(jnp.int32, (all_rows, HD), 0) // rows % 2 == 0
    for ds in range(n_seq):
        for rr in range(own_rows):
            q = new[ds][rr, :all_rows].astype(F32)
            request = (seq ^ reverse(n_seq)[ds]) * own_rows + rr
            all_q[request, :, :HD] = jnp.where(even, q, 0.0).astype(BF16)
            all_q[request, :, HD:] = jnp.where(even, 0.0, q).astype(BF16)
    for p in range(0, local_pages, 2):
        requests = [meta[first + p], meta[first + p + 1]]
        tokens = slice(p * PAGE, (p + 2) * PAGE)
        for pair in range(KVH // 2):
            k = k_ref[tokens, 2 * pair * HD : 2 * (pair + 1) * HD]
            at = slice(2 * pair * rows, 2 * (pair + 1) * rows)
            q = jnp.concatenate([all_q[request, at] for request in requests], axis=0)
            s = lax.dot_general(q, k, (((1,), (1,)), ((), ())), preferred_element_type=F32)
            for i in range(2):
                part = s[2 * i * rows : 2 * (i + 1) * rows, i * PAGE : (i + 1) * PAGE]
                here = slice((p + i) * PAGE, (p + i + 1) * PAGE)
                ready[at, here] = (part * scale).astype(BF16)
    for d in range(n_tp):
        outs[d][...] = ready[pl.ds(pl.multiple_of((me ^ order(n_tp)[d]) * count, count), count)]


def partial_scores(new, k, meta, prompts, n_tp):
    n_seq = len(new)
    all_rows = new[0].shape[1] - FRESH
    tokens = k.shape[0]
    rows = all_rows // n_tp
    return pl.pallas_call(
        functools.partial(scores_kernel, n_seq, n_tp),
        in_specs=[VMEM] * (n_seq + 1) + [SMEM],
        out_specs=[VMEM] * n_tp,
        out_shape=[jax.ShapeDtypeStruct((rows, tokens), BF16)] * n_tp,
        scratch_shapes=[
            pltpu.VMEM((prompts, all_rows, 2 * HD), BF16),
            pltpu.VMEM((all_rows, tokens), BF16),
        ],
        compiler_params=pltpu.CompilerParams(vmem_limit_bytes=24 * MIB),
        cost_estimate=pl.CostEstimate(
            flops=2 * tokens * all_rows * HD, bytes_accessed=6 * MIB, transcendentals=0
        ),
        name="scores",
    )(*new, k, meta)


def fresh_kernel(n_seq, *refs):
    new = refs[:n_seq]
    _, score_ref, value_ref = refs[n_seq:]
    new_count, rows_local, _ = score_ref.shape
    own_rows = new[0].shape[0]
    rows = new_count * GROUP
    kv_local = rows_local // rows
    scale = 1.0 / math.sqrt(HD)
    seq = lax.axis_index("seq")
    own = pl.ds(pl.multiple_of(lax.axis_index("tp") * rows_local, rows_local), rows_local)
    step = lax.broadcasted_iota(jnp.int32, (rows_local, HD), 0) % rows // GROUP
    lane = lax.broadcasted_iota(jnp.int32, (rows_local, HD), 1)
    found = [jnp.full((rows_local, HD), NEG, F32) for _ in range(new_count)]

    def spread(block, first):
        parts = [block[first + 2 * g : first + 2 * g + 1] for g in range(kv_local)]
        return jnp.concatenate([jnp.broadcast_to(a, (rows, HD)) for a in parts], axis=0)

    for ds in range(n_seq):
        for rr in range(own_rows):
            request = (seq ^ reverse(n_seq)[ds]) * own_rows + rr
            q = new[ds][rr, own].astype(F32)
            both = new[ds][rr, KVH * rows :].astype(F32)
            for n in range(new_count):
                first = n * 2 * kv_local
                s = jnp.sum(q * spread(both, first), axis=1, keepdims=True) * scale
                found[n] = jnp.where((lane == request) & (step >= n), s, found[n])
                value_ref[request * new_count + n] = spread(both, first + 1)
    for n in range(new_count):
        score_ref[n] = found[n]


def fresh_scores(new, after, prompts, new_count, n_tp):
    n_seq = len(new)
    rows = (new[0].shape[1] - FRESH) // n_tp
    return pl.pallas_call(
        functools.partial(fresh_kernel, n_seq),
        in_specs=[VMEM] * n_seq + [ANY],
        out_specs=[VMEM, VMEM],
        out_shape=[
            jax.ShapeDtypeStruct((new_count, rows, HD), F32),
            jax.ShapeDtypeStruct((prompts * new_count, rows, HD), F32),
        ],
        compiler_params=pltpu.CompilerParams(vmem_limit_bytes=16 * MIB),
        cost_estimate=pl.CostEstimate(flops=0, bytes_accessed=2 * MIB, transcendentals=0),
        name="fresh",
    )(*new, after)


def weights_kernel(pages, prompts, n_tp, *refs):
    chunks = refs[:n_tp]
    meta, _, w_ref, stats_ref = refs[n_tp:]
    rows, tokens = w_ref.shape
    local_pages = tokens // PAGE
    first = lax.axis_index("seq") * local_pages
    lane = lax.broadcasted_iota(jnp.int32, (rows, PAGE), 1)
    scores, maxima, masks, owners = [], [], [], []
    for p in range(local_pages):
        at = slice(p * PAGE, (p + 1) * PAGE)
        total = chunks[0][:, at].astype(F32)
        for d in range(1, n_tp):
            total = total + chunks[d][:, at].astype(F32)
        mask = lane < meta[2 * pages + first + p]
        total = jnp.where(mask, total, NEG)
        masks.append(mask)
        scores.append(total)
        maxima.append(jnp.max(total, axis=1, keepdims=True))
        owners.append(meta[first + p])
    quarter = lane // prompts
    spot = lane % prompts
    stats = jnp.where(quarter == 0, NEG, 0.0)
    same = [owners[p] == owners[p - 1] for p in range(1, local_pages)]
    for p in range(1, local_pages):
        maxima[p] = jnp.where(same[p - 1], jnp.maximum(maxima[p - 1], maxima[p]), maxima[p])
    for p in reversed(range(local_pages - 1)):
        maxima[p] = jnp.where(same[p], maxima[p + 1], maxima[p])
    for p in range(local_pages):
        top = maxima[p]
        high = top.astype(BF16).astype(F32)
        low = (top - high).astype(BF16).astype(F32)
        w = jnp.where(masks[p], jnp.exp(scores[p] - (high + low)), 0.0)
        w_ref[:, p * PAGE : (p + 1) * PAGE] = w.astype(BF16)
        here = spot == owners[p]
        stats = jnp.where(here & (quarter == 0), high, stats)
        stats = jnp.where(here & (quarter == 1), low, stats)
        part = jnp.sum(w, axis=1, keepdims=True)
        stats = stats + jnp.where(here & (quarter == 2), part, 0.0)
    high = stats.astype(BF16).astype(F32)
    low = pltpu.roll(stats - high, prompts, 1)
    stats_ref[...] = jnp.where(quarter == 3, low, stats).astype(BF16)


def softmax_weights(chunks, meta, after, pages, prompts):
    n_tp = len(chunks)
    rows, tokens = chunks[0].shape
    return pl.pallas_call(
        functools.partial(weights_kernel, pages, prompts, n_tp),
        in_specs=[VMEM] * n_tp + [SMEM, ANY],
        out_specs=[VMEM, VMEM],
        out_shape=[
            jax.ShapeDtypeStruct((rows, tokens), BF16),
            jax.ShapeDtypeStruct((rows, PAGE), BF16),
        ],
        compiler_params=pltpu.CompilerParams(vmem_limit_bytes=8 * MIB),
        name="weights",
    )(*chunks, meta, after)


def weighted_kernel(n_tp, *refs):
    pieces = refs[:n_tp]
    va_ref, vb_ref, meta, stats_ref = refs[n_tp : n_tp + 4]
    outs = refs[n_tp + 4 : n_tp + 4 + n_tp]
    late_ref, ready, total = refs[n_tp + 4 + n_tp :]
    late_ref[...] = stats_ref[...]
    rows_local, tokens_here = pieces[0].shape
    kv_local = KVH // n_tp
    rows = rows_local // kv_local
    local_pages = tokens_here // PAGE
    first = lax.axis_index("seq") * local_pages
    me = lax.axis_index("tp")
    own = [pl.ds(pl.multiple_of((me ^ order(n_tp)[d]) * rows_local, rows_local), rows_local) for d in range(n_tp)]
    for d in range(n_tp):
        at = pl.multiple_of((me ^ reverse(n_tp)[d]) * rows_local, rows_local)
        ready[pl.ds(at, rows_local)] = pieces[d][...]
    total[...] = jnp.zeros_like(total)
    half = va_ref.shape[1] // HD
    none = jnp.zeros((2 * rows, PAGE), BF16)
    for p in range(0, local_pages, 2):
        requests = [meta[first + p], meta[first + p + 1]]
        tokens = slice(p * PAGE, (p + 2) * PAGE)
        for pair in range(KVH // 2):
            head = 2 * pair
            v_ref = va_ref if head < half else vb_ref
            v = v_ref[tokens, head % half * HD : (head % half + 2) * HD]
            at = slice(head * rows, (head + 2) * rows)
            w = [ready[at, (p + i) * PAGE : (p + i + 1) * PAGE] for i in range(2)]
            w = [jnp.concatenate([w[0], none], axis=1), jnp.concatenate([none, w[1]], axis=1)]
            sums = jnp.dot(jnp.concatenate(w, axis=0), v, preferred_element_type=F32)
            for i, request in enumerate(requests):
                for h in range(2):
                    row = (2 * i + h) * rows
                    part = sums[row : row + rows, h * HD : (h + 1) * HD]
                    total[request, (head + h) * rows : (head + h + 1) * rows] += part
    for d in range(n_tp):
        outs[d][...] = total[:, own[d]].astype(BF16)


def weighted_values(pieces, va, vb, meta, stats, prompts):
    n_tp = len(pieces)
    rows, tokens = pieces[0].shape
    return pl.pallas_call(
        functools.partial(weighted_kernel, n_tp),
        in_specs=[VMEM] * (n_tp + 2) + [SMEM, VMEM],
        out_specs=[VMEM] * (n_tp + 1),
        out_shape=[jax.ShapeDtypeStruct((prompts, rows, HD), BF16)] * n_tp
        + [jax.ShapeDtypeStruct(stats.shape, stats.dtype)],
        scratch_shapes=[
            pltpu.VMEM((rows * n_tp, tokens), BF16),
            pltpu.VMEM((prompts, rows * n_tp, HD), F32),
        ],
        compiler_params=pltpu.CompilerParams(vmem_limit_bytes=24 * MIB),
        cost_estimate=pl.CostEstimate(
            flops=2 * tokens * rows * n_tp * HD, bytes_accessed=8 * MIB, transcendentals=0
        ),
        name="weighted",
    )(*pieces, va, vb, meta, stats)


def merge_kernel(n_seq, prompts, *refs):
    stats = refs[:n_seq]
    fresh_ref, factor_ref, weight_ref = refs[n_seq:]
    tops, parts = [], []
    for piece in stats:
        value = piece[...].astype(F32)
        folded = value + pltpu.roll(value, HD - prompts, 1)
        tops.append(folded)
        parts.append(pltpu.roll(folded, HD - 2 * prompts, 1))
    fresh = [fresh_ref[n] for n in range(fresh_ref.shape[0])]
    top = fresh[0]
    for other in fresh[1:] + tops:
        top = jnp.maximum(top, other)
    weights = [jnp.exp(f - top) for f in fresh]
    factors = [jnp.exp(t - top) for t in tops]
    total = weights[0]
    for w in weights[1:]:
        total = total + w
    for f, part in zip(factors, parts):
        total = total + f * part
    for n, w in enumerate(weights):
        weight_ref[n] = w / total
    for i, f in enumerate(factors):
        factor_ref[i] = f / total


def merge(stats, fresh, prompts):
    n_seq = len(stats)
    return pl.pallas_call(
        functools.partial(merge_kernel, n_seq, prompts),
        in_specs=[VMEM] * (n_seq + 1),
        out_specs=[VMEM, VMEM],
        out_shape=[
            jax.ShapeDtypeStruct((n_seq,) + fresh.shape[1:], F32),
            jax.ShapeDtypeStruct(fresh.shape, F32),
        ],
        compiler_params=pltpu.CompilerParams(vmem_limit_bytes=8 * MIB),
        name="merge",
    )(*stats, fresh)


def summed_kernel(*refs):
    total = refs[0][...].astype(F32)
    for chunk in refs[1:-2]:
        total = total + chunk[...].astype(F32)
    refs[-1][...] = total.astype(BF16)


def summed(chunks, after):
    return pl.pallas_call(
        summed_kernel,
        in_specs=[VMEM] * len(chunks) + [ANY],
        out_specs=VMEM,
        out_shape=jax.ShapeDtypeStruct(chunks[0].shape, BF16),
        compiler_params=pltpu.CompilerParams(vmem_limit_bytes=8 * MIB),
        cost_estimate=pl.CostEstimate(flops=0, bytes_accessed=16 * MIB, transcendentals=0),
        name="summed",
    )(*chunks, after)


def output_kernel(n_seq, *refs):
    pieces = refs[:n_seq]
    factor_ref, weight_ref, value_ref, wa_ref, wb_ref, out_ref, held = refs[n_seq:]
    prompts, rows_local, _ = pieces[0].shape
    new_count = weight_ref.shape[0]
    rows = new_count * GROUP
    kv_local = rows_local // rows
    heads = kv_local * GROUP
    factors = [factor_ref[s] for s in range(n_seq)]
    weights = [weight_ref[n] for n in range(new_count)]
    for r in range(prompts):
        sums = jnp.zeros((rows_local, HD), F32)
        for s in range(n_seq):
            sums = sums + factors[s][:, r : r + 1] * pieces[s][r].astype(F32)
        for n in range(new_count):
            sums = sums + weights[n][:, r : r + 1] * value_ref[r * new_count + n]
        for g in range(kv_local):
            for n in range(new_count):
                at = g * rows + n * GROUP
                held[g * GROUP : (g + 1) * GROUP, r * new_count + n] = sums[at : at + GROUP]
    half = heads // 2
    product = jnp.zeros(out_ref.shape, F32)
    for w_ref, at in ((wa_ref, 0), (wb_ref, half)):
        left = [held[h].astype(BF16) for h in range(at, at + half)]
        left = jnp.concatenate(left, axis=1)
        product = product + jnp.dot(left, w_ref[...], preferred_element_type=F32)
    out_ref[...] = product.astype(BF16)


def output_partial(pieces, factors, fresh, values, weights):
    n_seq = len(pieces)
    new_count = fresh.shape[0]
    prompts = pieces[0].shape[0]
    depth, columns = weights[0].shape
    return pl.pallas_call(
        functools.partial(output_kernel, n_seq),
        in_specs=[VMEM] * (n_seq + 5),
        out_specs=VMEM,
        out_shape=jax.ShapeDtypeStruct((prompts * new_count, columns), BF16),
        scratch_shapes=[pltpu.VMEM((2 * depth // HD, prompts * new_count, HD), F32)],
        compiler_params=pltpu.CompilerParams(vmem_limit_bytes=24 * MIB),
        name="output",
    )(*pieces, factors, fresh, values, *weights)


def final_kernel(n_tp, *refs):
    pieces = refs[:n_tp]
    res_ref, out_ref = refs[n_tp:]
    prompts, new_count, _ = out_ref.shape
    total = pieces[0][...].astype(F32)
    for d in range(1, n_tp):
        total = total + pieces[d][...].astype(F32)
    for r in range(prompts):
        out_ref[r] = res_ref[r].astype(F32) + total[r * new_count : (r + 1) * new_count]


def final_sum(pieces, residual):
    n_tp = len(pieces)
    return pl.pallas_call(
        functools.partial(final_kernel, n_tp),
        in_specs=[VMEM] * (n_tp + 1),
        out_specs=VMEM,
        out_shape=jax.ShapeDtypeStruct(residual.shape, F32),
        compiler_params=pltpu.CompilerParams(vmem_limit_bytes=8 * MIB),
        name="final",
    )(*pieces, residual)


def on_device(
    prefill_states, kv_weight, page_counts, tail_tokens, new_query, new_keyval, residual, out_weight
):
    n_seq, n_tp = lax.axis_size("seq"), lax.axis_size("tp")
    own_rows, new_count, _ = new_query.shape
    prompts = page_counts.shape[0]
    pages = prefill_states.shape[0] // PAGE * n_seq
    query = gather(new_query, "tp", falling(n_tp))
    acc, xa, wa, cosine, sine, cos_q, sin_q, meta = load(
        prefill_states, kv_weight, page_counts, tail_tokens, pages, new_count
    )
    new = turned(query, new_keyval, cos_q, sin_q)
    k, xb, wb = rotated_keys(acc, xa, wa, prefill_states, kv_weight, cosine, sine, new)
    new = gather(new, "seq")
    scores = partial_scores(new, k, meta, prompts, n_tp)
    va, oa = project_values((xa, wa, xb, wb), out_weight, 0, scores[0])
    weights, stats = softmax_weights(exchange(scores, "tp"), meta, va, pages, prompts)
    vb, ob = project_values((xa, wa, xb, wb), out_weight, 1, stats)
    fresh, values = fresh_scores(new, stats, prompts, new_count, n_tp)
    *chunks, stats = weighted_values(gather(weights, "tp"), va, vb, meta, stats, prompts)
    chunks = exchange(chunks, "tp")
    factors, fresh = merge(gather(stats, "seq"), fresh, prompts)
    pieces = gather(summed(chunks, factors), "seq")
    partial = output_partial(pieces, factors, fresh, values, (oa, ob))
    return final_sum(gather(partial, "tp"), residual)


def solution(mesh):
    placed = (
        P(("groups", "seq"), "tp"),
        P("tp", None),
        P("groups"),
        P("groups"),
        P(("groups", "seq"), None, "tp"),
        P(("groups", "seq"), None, "tp"),
        P("groups", None, "seq"),
        P("tp", "seq"),
    )
    return jax.shard_map(
        on_device, mesh=mesh, in_specs=placed, out_specs=P("groups", None, "seq"), check_vma=False
    )
```

```python
import functools
import math

import jax
import jax.numpy as jnp
from jax import lax
from jax.experimental import pallas as pl
from jax.experimental.pallas import tpu as pltpu
from jax.sharding import PartitionSpec as P

QH = 64
KVH = 8
HD = 128
PAGE = 128
GROUP = QH // KVH
NEG = -1e30
F32 = jnp.float32
BF16 = jnp.bfloat16
MIB = 1 << 20

VMEM = pl.BlockSpec(memory_space=pltpu.VMEM)
SMEM = pl.BlockSpec(memory_space=pltpu.SMEM)
ANY = pl.BlockSpec(memory_space=pl.ANY)


def pairs(value, axis, d):
    return lax.ppermute(value, axis, [(i, i ^ d) for i in range(lax.axis_size(axis))])


def order(size):
    found, top = [0], size // 2
    while top:
        found += range(top, 2 * top)
        top //= 2
    return found


def reverse(size):
    return [0] + order(size)[:0:-1]


def exchange(chunks, axis):
    offsets = order(len(chunks))
    return [chunks[0]] + [pairs(c, axis, d) for c, d in zip(chunks[1:], offsets[1:])]


def gather(value, axis, offsets=None):
    offsets = offsets or reverse(lax.axis_size(axis))
    return [value] + [pairs(value, axis, d) for d in offsets[1:]]


def falling(size):
    return [0] + list(range(size - 1, 0, -1))


def lane_freqs(rows):
    lane = lax.broadcasted_iota(jnp.int32, (rows, HD), 1) % (HD // 2)
    return jnp.exp(-(lane.astype(F32) * (2.0 / HD)) * math.log(500000.0))


def sine_sign(rows):
    lane = lax.broadcasted_iota(jnp.int32, (rows, HD), 1)
    return jnp.where(lane < HD // 2, -1.0, 1.0)


def in_hbm(value):
    return pltpu.with_memory_space_constraint(value, pltpu.HBM)


def by_row(rows, numbers):
    row = lax.broadcasted_iota(jnp.int32, (rows, HD), 0)
    out = jnp.zeros((rows, HD), F32)
    for i, number in enumerate(numbers):
        out = jnp.where(row == i, number.astype(F32), out)
    return out


def page_table(pages, prompts, counts, tails, meta):
    def one_prompt(r, start):
        length = (counts[r] - 1) * PAGE + tails[r]
        meta[3 * pages + r] = length

        def one_page(i, carry):
            meta[start + i] = r
            meta[pages + start + i] = i * PAGE
            meta[2 * pages + start + i] = jnp.minimum(length - i * PAGE, PAGE)
            return carry

        lax.fori_loop(0, counts[r], one_page, 0)
        return start + counts[r]

    lax.fori_loop(0, prompts, one_prompt, 0)


def rotation_tables(pages, local_pages, meta, cos_s, sin_s):
    freqs = lane_freqs(8)
    low = lax.broadcasted_iota(jnp.int32, (8, HD), 0).astype(F32) * freqs
    low_cos, low_sin = jnp.cos(low), jnp.sin(low)
    high = lax.broadcasted_iota(jnp.int32, (PAGE // 8, HD), 0).astype(F32) * 8.0
    high = high * lane_freqs(PAGE // 8)
    high_cos, high_sin = jnp.cos(high), jnp.sin(high)
    first = lax.axis_index("seq") * local_pages
    base = by_row(local_pages, [meta[pages + first + p] for p in range(local_pages)])
    base = base * lane_freqs(local_pages)
    base_cos, base_sin = jnp.cos(base), jnp.sin(base)
    sign = sine_sign(8)
    for i in range(PAGE // 8):
        c, s = high_cos[i : i + 1], high_sin[i : i + 1]
        cosine, sine = low_cos * c - low_sin * s, low_sin * c + low_cos * s
        for p in range(local_pages):
            at = slice(p * PAGE + i * 8, p * PAGE + i * 8 + 8)
            c, s = base_cos[p : p + 1], base_sin[p : p + 1]
            cos_s[at] = cosine * c - sine * s
            sin_s[at] = sign * (sine * c + cosine * s)


def pair_columns(w_ref, rows, pair, part):
    at = [(2 * head + part) * HD for head in (2 * pair, 2 * pair + 1)]
    return jnp.concatenate([w_ref[rows, c : c + HD] for c in at], axis=1)


def copies_of(x_hbm, w_hbm, x_ref, w_ref, sems, first, size, count):
    pairs_of = []
    for i in range(count):
        source, to = pl.ds(first + i * size, size), pl.ds(i * size, size)
        x_copy = pltpu.make_async_copy(x_hbm.at[:, source], x_ref.at[:, to], sems.at[2 * i])
        w_copy = pltpu.make_async_copy(w_hbm.at[source], w_ref.at[to], sems.at[2 * i + 1])
        pairs_of.append((x_copy, w_copy))
    return pairs_of


def start(copies):
    for copy in copies:
        copy.start()


def wait(copies):
    for copy in copies:
        copy.wait()


def add_block(x_ref, w_ref, rows, acc, out, fresh):
    tokens = x_ref.shape[0]
    tall = tokens // 2
    for pair in range(KVH // 2):
        weight = pair_columns(w_ref, rows, pair, 0)
        columns = slice(2 * pair * HD, 2 * (pair + 1) * HD)
        for top in range(0, tokens, tall):
            at = slice(top, top + tall)
            product = jnp.dot(x_ref[at, rows], weight, preferred_element_type=F32)
            out[at, columns] = product if fresh else acc[at, columns] + product


def load_kernel(pages, prompts, new_count, x_hbm, w_hbm, counts, tails, *refs):
    acc, x_ref, w_ref, cos_ref, sin_ref, cos_q, sin_q, meta, sems = refs
    tokens = x_ref.shape[0]
    size = x_ref.shape[1] // 3
    copies = copies_of(x_hbm, w_hbm, x_ref, w_ref, sems, 0, size, 3)
    start(copies[0])
    page_table(pages, prompts, counts, tails, meta)
    rotation_tables(pages, tokens // PAGE, meta, cos_ref, sin_ref)
    spots = [meta[3 * pages + r] + n for r in range(prompts) for n in range(new_count)]
    angles = by_row(len(spots), spots) * lane_freqs(len(spots))
    cos_q[...] = jnp.cos(angles)
    sin_q[...] = jnp.sin(angles) * sine_sign(len(spots))
    start(copies[1])
    for i in range(2):
        wait(copies[i])
        if i == 0:
            start(copies[2])
        add_block(x_ref, w_ref, slice(i * size, (i + 1) * size), acc, acc, i == 0)
    wait(copies[2])


def load(x, kv_weight, counts, tails, pages, new_count):
    tokens, depth = x.shape
    columns = kv_weight.shape[1]
    prompts = counts.shape[0]
    part = depth // 4 * 3
    hbm = pl.BlockSpec(memory_space=pltpu.HBM)
    return pl.pallas_call(
        functools.partial(load_kernel, pages, prompts, new_count),
        in_specs=[hbm, hbm, SMEM, SMEM],
        out_specs=[VMEM] * 7 + [SMEM],
        out_shape=[
            pltpu.VMEM((tokens, KVH * HD), F32),
            pltpu.VMEM((tokens, part), BF16),
            pltpu.VMEM((part, columns), BF16),
            pltpu.VMEM((tokens, HD), F32),
            pltpu.VMEM((tokens, HD), F32),
            pltpu.VMEM((prompts * new_count, HD), F32),
            pltpu.VMEM((prompts * new_count, HD), F32),
            jax.ShapeDtypeStruct((3 * pages + prompts,), jnp.int32),
        ],
        scratch_shapes=[pltpu.SemaphoreType.DMA((6,))],
        compiler_params=pltpu.CompilerParams(vmem_limit_bytes=28 * MIB),
        cost_estimate=pl.CostEstimate(
            flops=tokens * depth * KVH * HD,
            bytes_accessed=2 * part * (tokens + columns),
            transcendentals=0,
        ),
        name="load",
    )(*[in_hbm(a) for a in (x, kv_weight, counts, tails)])


def keys_kernel(acc, xa_ref, wa_ref, x_hbm, w_hbm, cos_ref, sin_ref, after, k_ref, x_ref, w_ref, total, sems):
    tokens, size = x_ref.shape
    tall = tokens // 2
    (copies,) = copies_of(x_hbm, w_hbm, x_ref, w_ref, sems, 3 * size, size, 1)
    start(copies)
    add_block(xa_ref, wa_ref, slice(2 * size, 3 * size), acc, total, False)
    wait(copies)
    for pair in range(KVH // 2):
        weight = pair_columns(w_ref, slice(None), pair, 0)
        columns = slice(2 * pair * HD, 2 * (pair + 1) * HD)
        for top in range(0, tokens, tall):
            at = slice(top, top + tall)
            product = total[at, columns] + jnp.dot(x_ref[at], weight, preferred_element_type=F32)
            cosine, sine = cos_ref[at], sin_ref[at]
            for h in range(2):
                k = product[:, h * HD : (h + 1) * HD]
                k = k * cosine + pltpu.roll(k, HD // 2, 1) * sine
                k_ref[at, (2 * pair + h) * HD : (2 * pair + h + 1) * HD] = k.astype(BF16)


def rotated_keys(acc, xa, wa, x, kv_weight, cosine, sine, after):
    tokens, depth = x.shape
    columns = kv_weight.shape[1]
    hbm = pl.BlockSpec(memory_space=pltpu.HBM)
    return pl.pallas_call(
        keys_kernel,
        in_specs=[VMEM] * 3 + [hbm] * 2 + [VMEM] * 2 + [ANY],
        out_specs=[VMEM] * 3,
        out_shape=[
            pltpu.VMEM((tokens, KVH * HD), BF16),
            pltpu.VMEM((tokens, depth // 4), BF16),
            pltpu.VMEM((depth // 4, columns), BF16),
        ],
        scratch_shapes=[
            pltpu.VMEM((tokens, KVH * HD), F32),
            pltpu.SemaphoreType.DMA((2,)),
        ],
        compiler_params=pltpu.CompilerParams(vmem_limit_bytes=24 * MIB),
        cost_estimate=pl.CostEstimate(
            flops=tokens * depth * KVH * HD, bytes_accessed=8 * MIB, transcendentals=0
        ),
        name="keys",
    )(acc, xa, wa, in_hbm(x), in_hbm(kv_weight), cosine, sine, after)


def values_kernel(first, xa_ref, wa_ref, xb_ref, wb_ref, o_hbm, after, v_ref, o_ref, sem):
    depth = o_ref.shape[0]
    copy = pltpu.make_async_copy(o_hbm.at[pl.ds(first * depth, depth)], o_ref, sem)
    copy.start()
    tokens, columns = v_ref.shape
    tall = tokens // 2
    pairs_here = columns // (2 * HD)
    for pair in range(pairs_here):
        weights = [pair_columns(w, slice(None), first * pairs_here + pair, 1) for w in (wa_ref, wb_ref)]
        for i in range(2):
            at = slice(i * tall, (i + 1) * tall)
            product = jnp.dot(xa_ref[at], weights[0], preferred_element_type=F32)
            product = product + jnp.dot(xb_ref[at], weights[1], preferred_element_type=F32)
            v_ref[at, 2 * pair * HD : 2 * (pair + 1) * HD] = product.astype(BF16)
    copy.wait()


def project_values(blocks, out_weight, first, after):
    tokens, depth = blocks[0].shape
    columns = KVH // 2 * HD
    rows = out_weight.shape[0] // 2
    return pl.pallas_call(
        functools.partial(values_kernel, first),
        in_specs=[VMEM] * 4 + [pl.BlockSpec(memory_space=pltpu.HBM), ANY],
        out_specs=[VMEM, VMEM],
        out_shape=[
            pltpu.VMEM((tokens, columns), BF16),
            pltpu.VMEM((rows, out_weight.shape[1]), BF16),
        ],
        scratch_shapes=[pltpu.SemaphoreType.DMA],
        compiler_params=pltpu.CompilerParams(vmem_limit_bytes=24 * MIB),
        cost_estimate=pl.CostEstimate(
            flops=2 * tokens * depth * columns, bytes_accessed=8 * MIB, transcendentals=0
        ),
        name="values",
    )(*blocks, in_hbm(out_weight), after)


def by_heads(row):
    return jnp.concatenate([row[:, c : c + HD] for c in range(0, row.shape[1], HD)], axis=0)


def turned_kernel(n_tp, *refs):
    kv_ref, cos_q, sin_q, out_ref = refs[n_tp:]
    own_rows, new_count, columns = refs[0].shape
    rows = new_count * GROUP
    kv_local = columns // HD // GROUP
    me, seq = lax.axis_index("tp"), lax.axis_index("seq")
    for r in range(own_rows):
        spots = [pl.ds((seq * own_rows + r) * new_count + n, 1) for n in range(new_count)]
        turns = [(cos_q[spot], sin_q[spot]) for spot in spots]

        def turn(value, n):
            return value * turns[n][0] + pltpu.roll(value, HD // 2, 1) * turns[n][1]

        for d in range(n_tp):
            raw = refs[d][r].astype(F32)
            blocks = [by_heads(raw[n : n + 1]) for n in range(new_count)]
            for g in range(kv_local):
                parts = [turn(q[g * GROUP : (g + 1) * GROUP], n) for n, q in enumerate(blocks)]
                at = ((me ^ falling(n_tp)[d]) * kv_local + g) * rows
                at = pl.ds(pl.multiple_of(at, rows), rows)
                out_ref[r, at] = jnp.concatenate(parts, axis=0).astype(BF16)
        raw = kv_ref[r].astype(F32)
        fresh = []
        for n in range(new_count):
            kv = by_heads(raw[n : n + 1])
            row = lax.broadcasted_iota(jnp.int32, kv.shape, 0)
            fresh.append(jnp.where(row % 2 == 0, turn(kv, n), kv))
        fresh.append(jnp.zeros((FRESH - new_count * 2 * kv_local, HD), F32))
        out_ref[r, KVH * rows :] = jnp.concatenate(fresh, axis=0).astype(BF16)


FRESH = 16


def turned(pieces, fresh, cos_q, sin_q):
    n_tp = len(pieces)
    own_rows, new_count, _ = pieces[0].shape
    rows = KVH * GROUP * new_count + FRESH
    return pl.pallas_call(
        functools.partial(turned_kernel, n_tp),
        in_specs=[VMEM] * (n_tp + 3),
        out_specs=VMEM,
        out_shape=jax.ShapeDtypeStruct((own_rows, rows, HD), BF16),
        compiler_params=pltpu.CompilerParams(vmem_limit_bytes=8 * MIB),
        name="turned",
    )(*pieces, fresh, cos_q, sin_q)


def scores_kernel(n_seq, n_tp, *refs):
    new = refs[:n_seq]
    k_ref, meta = refs[n_seq : n_seq + 2]
    outs = refs[n_seq + 2 : n_seq + 2 + n_tp]
    all_q, ready = refs[n_seq + 2 + n_tp :]
    own_rows = new[0].shape[0]
    local_pages = k_ref.shape[0] // PAGE
    all_rows = all_q.shape[1]
    rows = all_rows // KVH
    count = all_rows // n_tp
    scale = 1.0 / math.sqrt(HD)
    me = lax.axis_index("tp")
    seq = lax.axis_index("seq")
    first = seq * local_pages
    even = lax.broadcasted_iota(jnp.int32, (all_rows, HD), 0) // rows % 2 == 0
    for ds in range(n_seq):
        for rr in range(own_rows):
            q = new[ds][rr, :all_rows].astype(F32)
            request = (seq ^ reverse(n_seq)[ds]) * own_rows + rr
            all_q[request, :, :HD] = jnp.where(even, q, 0.0).astype(BF16)
            all_q[request, :, HD:] = jnp.where(even, 0.0, q).astype(BF16)
    for p in range(0, local_pages, 2):
        requests = [meta[first + p], meta[first + p + 1]]
        tokens = slice(p * PAGE, (p + 2) * PAGE)
        for pair in range(KVH // 2):
            k = k_ref[tokens, 2 * pair * HD : 2 * (pair + 1) * HD]
            at = slice(2 * pair * rows, 2 * (pair + 1) * rows)
            q = jnp.concatenate([all_q[request, at] for request in requests], axis=0)
            s = lax.dot_general(q, k, (((1,), (1,)), ((), ())), preferred_element_type=F32)
            for i in range(2):
                part = s[2 * i * rows : 2 * (i + 1) * rows, i * PAGE : (i + 1) * PAGE]
                here = slice((p + i) * PAGE, (p + i + 1) * PAGE)
                ready[at, here] = (part * scale).astype(BF16)
    for d in range(n_tp):
        outs[d][...] = ready[pl.ds(pl.multiple_of((me ^ order(n_tp)[d]) * count, count), count)]


def partial_scores(new, k, meta, prompts, n_tp):
    n_seq = len(new)
    all_rows = new[0].shape[1] - FRESH
    tokens = k.shape[0]
    rows = all_rows // n_tp
    return pl.pallas_call(
        functools.partial(scores_kernel, n_seq, n_tp),
        in_specs=[VMEM] * (n_seq + 1) + [SMEM],
        out_specs=[VMEM] * n_tp,
        out_shape=[jax.ShapeDtypeStruct((rows, tokens), BF16)] * n_tp,
        scratch_shapes=[
            pltpu.VMEM((prompts, all_rows, 2 * HD), BF16),
            pltpu.VMEM((all_rows, tokens), BF16),
        ],
        compiler_params=pltpu.CompilerParams(vmem_limit_bytes=24 * MIB),
        cost_estimate=pl.CostEstimate(
            flops=2 * tokens * all_rows * HD, bytes_accessed=6 * MIB, transcendentals=0
        ),
        name="scores",
    )(*new, k, meta)


def fresh_kernel(n_seq, *refs):
    new = refs[:n_seq]
    _, score_ref, value_ref = refs[n_seq:]
    new_count, rows_local, _ = score_ref.shape
    own_rows = new[0].shape[0]
    rows = new_count * GROUP
    kv_local = rows_local // rows
    scale = 1.0 / math.sqrt(HD)
    seq = lax.axis_index("seq")
    own = pl.ds(pl.multiple_of(lax.axis_index("tp") * rows_local, rows_local), rows_local)
    step = lax.broadcasted_iota(jnp.int32, (rows_local, HD), 0) % rows // GROUP
    lane = lax.broadcasted_iota(jnp.int32, (rows_local, HD), 1)
    found = [jnp.full((rows_local, HD), NEG, F32) for _ in range(new_count)]

    def spread(block, first):
        parts = [block[first + 2 * g : first + 2 * g + 1] for g in range(kv_local)]
        return jnp.concatenate([jnp.broadcast_to(a, (rows, HD)) for a in parts], axis=0)

    for ds in range(n_seq):
        for rr in range(own_rows):
            request = (seq ^ reverse(n_seq)[ds]) * own_rows + rr
            q = new[ds][rr, own].astype(F32)
            both = new[ds][rr, KVH * rows :].astype(F32)
            for n in range(new_count):
                first = n * 2 * kv_local
                s = jnp.sum(q * spread(both, first), axis=1, keepdims=True) * scale
                found[n] = jnp.where((lane == request) & (step >= n), s, found[n])
                value_ref[request * new_count + n] = spread(both, first + 1)
    for n in range(new_count):
        score_ref[n] = found[n]


def fresh_scores(new, after, prompts, new_count, n_tp):
    n_seq = len(new)
    rows = (new[0].shape[1] - FRESH) // n_tp
    return pl.pallas_call(
        functools.partial(fresh_kernel, n_seq),
        in_specs=[VMEM] * n_seq + [ANY],
        out_specs=[VMEM, VMEM],
        out_shape=[
            jax.ShapeDtypeStruct((new_count, rows, HD), F32),
            jax.ShapeDtypeStruct((prompts * new_count, rows, HD), F32),
        ],
        compiler_params=pltpu.CompilerParams(vmem_limit_bytes=16 * MIB),
        cost_estimate=pl.CostEstimate(flops=0, bytes_accessed=2 * MIB, transcendentals=0),
        name="fresh",
    )(*new, after)


def weights_kernel(pages, prompts, n_tp, *refs):
    chunks = refs[:n_tp]
    meta, _, w_ref, stats_ref = refs[n_tp:]
    rows, tokens = w_ref.shape
    local_pages = tokens // PAGE
    first = lax.axis_index("seq") * local_pages
    lane = lax.broadcasted_iota(jnp.int32, (rows, PAGE), 1)
    scores, maxima, masks, owners = [], [], [], []
    for p in range(local_pages):
        at = slice(p * PAGE, (p + 1) * PAGE)
        total = chunks[0][:, at].astype(F32)
        for d in range(1, n_tp):
            total = total + chunks[d][:, at].astype(F32)
        mask = lane < meta[2 * pages + first + p]
        total = jnp.where(mask, total, NEG)
        masks.append(mask)
        scores.append(total)
        maxima.append(jnp.max(total, axis=1, keepdims=True))
        owners.append(meta[first + p])
    quarter = lane // prompts
    spot = lane % prompts
    stats = jnp.where(quarter == 0, NEG, 0.0)
    same = [owners[p] == owners[p - 1] for p in range(1, local_pages)]
    for p in range(1, local_pages):
        maxima[p] = jnp.where(same[p - 1], jnp.maximum(maxima[p - 1], maxima[p]), maxima[p])
    for p in reversed(range(local_pages - 1)):
        maxima[p] = jnp.where(same[p], maxima[p + 1], maxima[p])
    for p in range(local_pages):
        top = maxima[p]
        high = top.astype(BF16).astype(F32)
        low = (top - high).astype(BF16).astype(F32)
        w = jnp.where(masks[p], jnp.exp(scores[p] - (high + low)), 0.0)
        w_ref[:, p * PAGE : (p + 1) * PAGE] = w.astype(BF16)
        here = spot == owners[p]
        stats = jnp.where(here & (quarter == 0), high, stats)
        stats = jnp.where(here & (quarter == 1), low, stats)
        part = jnp.sum(w, axis=1, keepdims=True)
        stats = stats + jnp.where(here & (quarter == 2), part, 0.0)
    high = stats.astype(BF16).astype(F32)
    low = pltpu.roll(stats - high, prompts, 1)
    stats_ref[...] = jnp.where(quarter == 3, low, stats).astype(BF16)


def softmax_weights(chunks, meta, after, pages, prompts):
    n_tp = len(chunks)
    rows, tokens = chunks[0].shape
    return pl.pallas_call(
        functools.partial(weights_kernel, pages, prompts, n_tp),
        in_specs=[VMEM] * n_tp + [SMEM, ANY],
        out_specs=[VMEM, VMEM],
        out_shape=[
            jax.ShapeDtypeStruct((rows, tokens), BF16),
            jax.ShapeDtypeStruct((rows, PAGE), BF16),
        ],
        compiler_params=pltpu.CompilerParams(vmem_limit_bytes=8 * MIB),
        name="weights",
    )(*chunks, meta, after)


def weighted_kernel(n_tp, *refs):
    pieces = refs[:n_tp]
    va_ref, vb_ref, meta = refs[n_tp : n_tp + 3]
    outs = refs[n_tp + 3 : n_tp + 3 + n_tp]
    ready, total = refs[n_tp + 3 + n_tp :]
    rows_local, tokens_here = pieces[0].shape
    kv_local = KVH // n_tp
    rows = rows_local // kv_local
    local_pages = tokens_here // PAGE
    first = lax.axis_index("seq") * local_pages
    me = lax.axis_index("tp")
    own = [pl.ds(pl.multiple_of((me ^ order(n_tp)[d]) * rows_local, rows_local), rows_local) for d in range(n_tp)]
    for d in range(n_tp):
        at = pl.multiple_of((me ^ reverse(n_tp)[d]) * rows_local, rows_local)
        ready[pl.ds(at, rows_local)] = pieces[d][...]
    total[...] = jnp.zeros_like(total)
    half = va_ref.shape[1] // HD
    none = jnp.zeros((2 * rows, PAGE), BF16)
    for p in range(0, local_pages, 2):
        requests = [meta[first + p], meta[first + p + 1]]
        tokens = slice(p * PAGE, (p + 2) * PAGE)
        for pair in range(KVH // 2):
            head = 2 * pair
            v_ref = va_ref if head < half else vb_ref
            v = v_ref[tokens, head % half * HD : (head % half + 2) * HD]
            at = slice(head * rows, (head + 2) * rows)
            w = [ready[at, (p + i) * PAGE : (p + i + 1) * PAGE] for i in range(2)]
            w = [jnp.concatenate([w[0], none], axis=1), jnp.concatenate([none, w[1]], axis=1)]
            sums = jnp.dot(jnp.concatenate(w, axis=0), v, preferred_element_type=F32)
            for i, request in enumerate(requests):
                for h in range(2):
                    row = (2 * i + h) * rows
                    part = sums[row : row + rows, h * HD : (h + 1) * HD]
                    total[request, (head + h) * rows : (head + h + 1) * rows] += part
    for d in range(n_tp):
        outs[d][...] = total[:, own[d]].astype(BF16)


def weighted_values(pieces, va, vb, meta, prompts):
    n_tp = len(pieces)
    rows, tokens = pieces[0].shape
    return pl.pallas_call(
        functools.partial(weighted_kernel, n_tp),
        in_specs=[VMEM] * (n_tp + 2) + [SMEM],
        out_specs=[VMEM] * n_tp,
        out_shape=[jax.ShapeDtypeStruct((prompts, rows, HD), BF16)] * n_tp,
        scratch_shapes=[
            pltpu.VMEM((rows * n_tp, tokens), BF16),
            pltpu.VMEM((prompts, rows * n_tp, HD), F32),
        ],
        compiler_params=pltpu.CompilerParams(vmem_limit_bytes=24 * MIB),
        cost_estimate=pl.CostEstimate(
            flops=2 * tokens * rows * n_tp * HD, bytes_accessed=8 * MIB, transcendentals=0
        ),
        name="weighted",
    )(*pieces, va, vb, meta)


def summed_kernel(n_tp, *refs):
    chunks = refs[:n_tp]
    stats_ref, out_ref = refs[n_tp:]
    prompts = chunks[0].shape[0]
    total = chunks[0][...].astype(F32)
    for d in range(1, n_tp):
        total = total + chunks[d][...].astype(F32)
    out_ref[:prompts] = total.astype(BF16)
    out_ref[prompts] = stats_ref[...]


def summed(chunks, stats):
    n_tp = len(chunks)
    prompts, rows, _ = chunks[0].shape
    return pl.pallas_call(
        functools.partial(summed_kernel, n_tp),
        in_specs=[VMEM] * (n_tp + 1),
        out_specs=VMEM,
        out_shape=jax.ShapeDtypeStruct((prompts + 1, rows, HD), BF16),
        compiler_params=pltpu.CompilerParams(vmem_limit_bytes=8 * MIB),
        cost_estimate=pl.CostEstimate(flops=0, bytes_accessed=4 * MIB, transcendentals=0),
        name="summed",
    )(*chunks, stats)


def output_kernel(n_seq, *refs):
    pieces = refs[:n_seq]
    fresh_ref, value_ref, wa_ref, wb_ref, out_ref, held = refs[n_seq:]
    more, rows_local, _ = pieces[0].shape
    prompts = more - 1
    new_count = fresh_ref.shape[0]
    rows = new_count * GROUP
    kv_local = rows_local // rows
    heads = kv_local * GROUP
    tops, parts = [], []
    for s in range(n_seq):
        stats = pieces[s][prompts].astype(F32)
        folded = stats + pltpu.roll(stats, HD - prompts, 1)
        tops.append(folded)
        parts.append(pltpu.roll(folded, HD - 2 * prompts, 1))
    fresh = [fresh_ref[n] for n in range(new_count)]
    top = fresh[0]
    for other in fresh[1:] + tops:
        top = jnp.maximum(top, other)
    weights = [jnp.exp(f - top) for f in fresh]
    factors = [jnp.exp(t - top) for t in tops]
    total = weights[0]
    for w in weights[1:]:
        total = total + w
    for f, part in zip(factors, parts):
        total = total + f * part
    weights = [w / total for w in weights]
    factors = [f / total for f in factors]
    for r in range(prompts):
        sums = jnp.zeros((rows_local, HD), F32)
        for s in range(n_seq):
            sums = sums + factors[s][:, r : r + 1] * pieces[s][r].astype(F32)
        for n in range(new_count):
            sums = sums + weights[n][:, r : r + 1] * value_ref[r * new_count + n]
        for g in range(kv_local):
            for n in range(new_count):
                at = g * rows + n * GROUP
                held[g * GROUP : (g + 1) * GROUP, r * new_count + n] = sums[at : at + GROUP]
    half = heads // 2
    product = jnp.zeros(out_ref.shape, F32)
    for w_ref, at in ((wa_ref, 0), (wb_ref, half)):
        left = [held[h].astype(BF16) for h in range(at, at + half)]
        left = jnp.concatenate(left, axis=1)
        product = product + jnp.dot(left, w_ref[...], preferred_element_type=F32)
    out_ref[...] = product.astype(BF16)


def output_partial(pieces, fresh, values, weights):
    n_seq = len(pieces)
    new_count = fresh.shape[0]
    prompts = pieces[0].shape[0] - 1
    depth, columns = weights[0].shape
    return pl.pallas_call(
        functools.partial(output_kernel, n_seq),
        in_specs=[VMEM] * (n_seq + 4),
        out_specs=VMEM,
        out_shape=jax.ShapeDtypeStruct((prompts * new_count, columns), BF16),
        scratch_shapes=[pltpu.VMEM((2 * depth // HD, prompts * new_count, HD), F32)],
        compiler_params=pltpu.CompilerParams(vmem_limit_bytes=24 * MIB),
        name="output",
    )(*pieces, fresh, values, *weights)


def final_kernel(n_tp, *refs):
    pieces = refs[:n_tp]
    res_ref, out_ref = refs[n_tp:]
    prompts, new_count, _ = out_ref.shape
    total = pieces[0][...].astype(F32)
    for d in range(1, n_tp):
        total = total + pieces[d][...].astype(F32)
    for r in range(prompts):
        out_ref[r] = res_ref[r].astype(F32) + total[r * new_count : (r + 1) * new_count]


def final_sum(pieces, residual):
    n_tp = len(pieces)
    return pl.pallas_call(
        functools.partial(final_kernel, n_tp),
        in_specs=[VMEM] * (n_tp + 1),
        out_specs=VMEM,
        out_shape=jax.ShapeDtypeStruct(residual.shape, F32),
        compiler_params=pltpu.CompilerParams(vmem_limit_bytes=8 * MIB),
        name="final",
    )(*pieces, residual)


def on_device(
    prefill_states, kv_weight, page_counts, tail_tokens, new_query, new_keyval, residual, out_weight
):
    n_seq, n_tp = lax.axis_size("seq"), lax.axis_size("tp")
    own_rows, new_count, _ = new_query.shape
    prompts = page_counts.shape[0]
    pages = prefill_states.shape[0] // PAGE * n_seq
    query = gather(new_query, "tp", falling(n_tp))
    acc, xa, wa, cosine, sine, cos_q, sin_q, meta = load(
        prefill_states, kv_weight, page_counts, tail_tokens, pages, new_count
    )
    new = turned(query, new_keyval, cos_q, sin_q)
    k, xb, wb = rotated_keys(acc, xa, wa, prefill_states, kv_weight, cosine, sine, new)
    new = gather(new, "seq")
    scores = partial_scores(new, k, meta, prompts, n_tp)
    va, oa = project_values((xa, wa, xb, wb), out_weight, 0, scores[0])
    weights, stats = softmax_weights(exchange(scores, "tp"), meta, va, pages, prompts)
    vb, ob = project_values((xa, wa, xb, wb), out_weight, 1, stats)
    fresh, values = fresh_scores(new, stats, prompts, new_count, n_tp)
    chunks = weighted_values(gather(weights, "tp"), va, vb, meta, prompts)
    pieces = gather(summed(exchange(chunks, "tp"), stats), "seq")
    partial = output_partial(pieces, fresh, values, (oa, ob))
    return final_sum(gather(partial, "tp"), residual)


def solution(mesh):
    placed = (
        P(("groups", "seq"), "tp"),
        P("tp", None),
        P("groups"),
        P("groups"),
        P(("groups", "seq"), None, "tp"),
        P(("groups", "seq"), None, "tp"),
        P("groups", None, "seq"),
        P("tp", "seq"),
    )
    return jax.shard_map(
        on_device, mesh=mesh, in_specs=placed, out_specs=P("groups", None, "seq"), check_vma=False
    )
```

```python
import functools
import math

import jax
import jax.numpy as jnp
from jax import lax
from jax.experimental import pallas as pl
from jax.experimental.pallas import tpu as pltpu
from jax.sharding import PartitionSpec as P

QH = 64
KVH = 8
HD = 128
PAGE = 128
GROUP = QH // KVH
NEG = -1e30
F32 = jnp.float32
BF16 = jnp.bfloat16
MIB = 1 << 20

VMEM = pl.BlockSpec(memory_space=pltpu.VMEM)
SMEM = pl.BlockSpec(memory_space=pltpu.SMEM)
ANY = pl.BlockSpec(memory_space=pl.ANY)


def pairs(value, axis, d):
    return lax.ppermute(value, axis, [(i, i ^ d) for i in range(lax.axis_size(axis))])


def order(size):
    found, top = [0], size // 2
    while top:
        found += range(top, 2 * top)
        top //= 2
    return found


def reverse(size):
    return [0] + order(size)[:0:-1]


def exchange(chunks, axis):
    offsets = order(len(chunks))
    return [chunks[0]] + [pairs(c, axis, d) for c, d in zip(chunks[1:], offsets[1:])]


def gather(value, axis, offsets=None):
    offsets = offsets or reverse(lax.axis_size(axis))
    return [value] + [pairs(value, axis, d) for d in offsets[1:]]


def falling(size):
    return [0] + list(range(size - 1, 0, -1))


def lane_freqs(rows):
    lane = lax.broadcasted_iota(jnp.int32, (rows, HD), 1) % (HD // 2)
    return jnp.exp(-(lane.astype(F32) * (2.0 / HD)) * math.log(500000.0))


def sine_sign(rows):
    lane = lax.broadcasted_iota(jnp.int32, (rows, HD), 1)
    return jnp.where(lane < HD // 2, -1.0, 1.0)


def in_hbm(value):
    return pltpu.with_memory_space_constraint(value, pltpu.HBM)


def by_row(rows, numbers):
    row = lax.broadcasted_iota(jnp.int32, (rows, HD), 0)
    out = jnp.zeros((rows, HD), F32)
    for i, number in enumerate(numbers):
        out = jnp.where(row == i, number.astype(F32), out)
    return out


def page_table(pages, prompts, counts, tails, meta):
    def one_prompt(r, start):
        length = (counts[r] - 1) * PAGE + tails[r]
        meta[3 * pages + r] = length

        def one_page(i, carry):
            meta[start + i] = r
            meta[pages + start + i] = i * PAGE
            meta[2 * pages + start + i] = jnp.minimum(length - i * PAGE, PAGE)
            return carry

        lax.fori_loop(0, counts[r], one_page, 0)
        return start + counts[r]

    lax.fori_loop(0, prompts, one_prompt, 0)


def rotation_tables(pages, local_pages, meta, cos_s, sin_s):
    freqs = lane_freqs(8)
    low = lax.broadcasted_iota(jnp.int32, (8, HD), 0).astype(F32) * freqs
    low_cos, low_sin = jnp.cos(low), jnp.sin(low)
    high = lax.broadcasted_iota(jnp.int32, (PAGE // 8, HD), 0).astype(F32) * 8.0
    high = high * lane_freqs(PAGE // 8)
    high_cos, high_sin = jnp.cos(high), jnp.sin(high)
    first = lax.axis_index("seq") * local_pages
    base = by_row(local_pages, [meta[pages + first + p] for p in range(local_pages)])
    base = base * lane_freqs(local_pages)
    base_cos, base_sin = jnp.cos(base), jnp.sin(base)
    sign = sine_sign(8)
    for i in range(PAGE // 8):
        c, s = high_cos[i : i + 1], high_sin[i : i + 1]
        cosine, sine = low_cos * c - low_sin * s, low_sin * c + low_cos * s
        for p in range(local_pages):
            at = slice(p * PAGE + i * 8, p * PAGE + i * 8 + 8)
            c, s = base_cos[p : p + 1], base_sin[p : p + 1]
            cos_s[at] = cosine * c - sine * s
            sin_s[at] = sign * (sine * c + cosine * s)


def pair_columns(w_ref, rows, pair, part):
    at = [(2 * head + part) * HD for head in (2 * pair, 2 * pair + 1)]
    return jnp.concatenate([w_ref[rows, c : c + HD] for c in at], axis=1)


def copies_of(x_hbm, w_hbm, x_ref, w_ref, sems, first, size, count):
    pairs_of = []
    for i in range(count):
        source, to = pl.ds(first + i * size, size), pl.ds(i * size, size)
        x_copy = pltpu.make_async_copy(x_hbm.at[:, source], x_ref.at[:, to], sems.at[2 * i])
        w_copy = pltpu.make_async_copy(w_hbm.at[source], w_ref.at[to], sems.at[2 * i + 1])
        pairs_of.append((x_copy, w_copy))
    return pairs_of


def start(copies):
    for copy in copies:
        copy.start()


def wait(copies):
    for copy in copies:
        copy.wait()


def add_block(x_ref, w_ref, rows, acc, out, fresh):
    tokens = x_ref.shape[0]
    tall = tokens // 2
    for pair in range(KVH // 2):
        weight = pair_columns(w_ref, rows, pair, 0)
        columns = slice(2 * pair * HD, 2 * (pair + 1) * HD)
        for top in range(0, tokens, tall):
            at = slice(top, top + tall)
            product = jnp.dot(x_ref[at, rows], weight, preferred_element_type=F32)
            out[at, columns] = product if fresh else acc[at, columns] + product


def load_kernel(pages, prompts, new_count, x_hbm, w_hbm, counts, tails, *refs):
    acc, x_ref, w_ref, cos_ref, sin_ref, cos_q, sin_q, meta, sems = refs[:9]
    counts_s, tails_s, small_sems = refs[9:]
    tokens = x_ref.shape[0]
    size = x_ref.shape[1] // 3
    copies = copies_of(x_hbm, w_hbm, x_ref, w_ref, sems, 0, size, 3)
    start(copies[0])
    small = [
        pltpu.make_async_copy(counts, counts_s, small_sems.at[0]),
        pltpu.make_async_copy(tails, tails_s, small_sems.at[1]),
    ]
    start(small)
    wait(small)
    page_table(pages, prompts, counts_s, tails_s, meta)
    rotation_tables(pages, tokens // PAGE, meta, cos_ref, sin_ref)
    spots = [meta[3 * pages + r] + n for r in range(prompts) for n in range(new_count)]
    angles = by_row(len(spots), spots) * lane_freqs(len(spots))
    cos_q[...] = jnp.cos(angles)
    sin_q[...] = jnp.sin(angles) * sine_sign(len(spots))
    start(copies[1])
    for i in range(2):
        wait(copies[i])
        if i == 0:
            start(copies[2])
        add_block(x_ref, w_ref, slice(i * size, (i + 1) * size), acc, acc, i == 0)
    wait(copies[2])


def load(x, kv_weight, counts, tails, pages, new_count):
    tokens, depth = x.shape
    columns = kv_weight.shape[1]
    prompts = counts.shape[0]
    part = depth // 4 * 3
    hbm = pl.BlockSpec(memory_space=pltpu.HBM)
    return pl.pallas_call(
        functools.partial(load_kernel, pages, prompts, new_count),
        in_specs=[hbm] * 4,
        out_specs=[VMEM] * 7 + [SMEM],
        out_shape=[
            pltpu.VMEM((tokens, KVH * HD), F32),
            pltpu.VMEM((tokens, part), BF16),
            pltpu.VMEM((part, columns), BF16),
            pltpu.VMEM((tokens, HD), F32),
            pltpu.VMEM((tokens, HD), F32),
            pltpu.VMEM((prompts * new_count, HD), F32),
            pltpu.VMEM((prompts * new_count, HD), F32),
            jax.ShapeDtypeStruct((3 * pages + prompts,), jnp.int32),
        ],
        scratch_shapes=[
            pltpu.SemaphoreType.DMA((6,)),
            pltpu.SMEM((prompts,), jnp.int32),
            pltpu.SMEM((prompts,), jnp.int32),
            pltpu.SemaphoreType.DMA((2,)),
        ],
        compiler_params=pltpu.CompilerParams(vmem_limit_bytes=28 * MIB),
        cost_estimate=pl.CostEstimate(
            flops=tokens * depth * KVH * HD,
            bytes_accessed=2 * part * (tokens + columns),
            transcendentals=0,
        ),
        name="load",
    )(*[in_hbm(a) for a in (x, kv_weight, counts, tails)])


def keys_kernel(acc, xa_ref, wa_ref, x_hbm, w_hbm, cos_ref, sin_ref, after, k_ref, x_ref, w_ref, total, sems):
    tokens, size = x_ref.shape
    tall = tokens // 2
    (copies,) = copies_of(x_hbm, w_hbm, x_ref, w_ref, sems, 3 * size, size, 1)
    start(copies)
    add_block(xa_ref, wa_ref, slice(2 * size, 3 * size), acc, total, False)
    wait(copies)
    for pair in range(KVH // 2):
        weight = pair_columns(w_ref, slice(None), pair, 0)
        columns = slice(2 * pair * HD, 2 * (pair + 1) * HD)
        for top in range(0, tokens, tall):
            at = slice(top, top + tall)
            product = total[at, columns] + jnp.dot(x_ref[at], weight, preferred_element_type=F32)
            cosine, sine = cos_ref[at], sin_ref[at]
            for h in range(2):
                k = product[:, h * HD : (h + 1) * HD]
                k = k * cosine + pltpu.roll(k, HD // 2, 1) * sine
                k_ref[at, (2 * pair + h) * HD : (2 * pair + h + 1) * HD] = k.astype(BF16)


def rotated_keys(acc, xa, wa, x, kv_weight, cosine, sine, after):
    tokens, depth = x.shape
    columns = kv_weight.shape[1]
    hbm = pl.BlockSpec(memory_space=pltpu.HBM)
    return pl.pallas_call(
        keys_kernel,
        in_specs=[VMEM] * 3 + [hbm] * 2 + [VMEM] * 2 + [ANY],
        out_specs=[VMEM] * 3,
        out_shape=[
            pltpu.VMEM((tokens, KVH * HD), BF16),
            pltpu.VMEM((tokens, depth // 4), BF16),
            pltpu.VMEM((depth // 4, columns), BF16),
        ],
        scratch_shapes=[
            pltpu.VMEM((tokens, KVH * HD), F32),
            pltpu.SemaphoreType.DMA((2,)),
        ],
        compiler_params=pltpu.CompilerParams(vmem_limit_bytes=24 * MIB),
        cost_estimate=pl.CostEstimate(
            flops=tokens * depth * KVH * HD, bytes_accessed=8 * MIB, transcendentals=0
        ),
        name="keys",
    )(acc, xa, wa, in_hbm(x), in_hbm(kv_weight), cosine, sine, after)


def values_kernel(first, xa_ref, wa_ref, xb_ref, wb_ref, o_hbm, after, v_ref, o_ref, sem):
    depth = o_ref.shape[0]
    copy = pltpu.make_async_copy(o_hbm.at[pl.ds(first * depth, depth)], o_ref, sem)
    copy.start()
    tokens, columns = v_ref.shape
    tall = tokens // 2
    pairs_here = columns // (2 * HD)
    for pair in range(pairs_here):
        weights = [pair_columns(w, slice(None), first * pairs_here + pair, 1) for w in (wa_ref, wb_ref)]
        for i in range(2):
            at = slice(i * tall, (i + 1) * tall)
            product = jnp.dot(xa_ref[at], weights[0], preferred_element_type=F32)
            product = product + jnp.dot(xb_ref[at], weights[1], preferred_element_type=F32)
            v_ref[at, 2 * pair * HD : 2 * (pair + 1) * HD] = product.astype(BF16)
    copy.wait()


def project_values(blocks, out_weight, first, after):
    tokens, depth = blocks[0].shape
    columns = KVH // 2 * HD
    rows = out_weight.shape[0] // 2
    return pl.pallas_call(
        functools.partial(values_kernel, first),
        in_specs=[VMEM] * 4 + [pl.BlockSpec(memory_space=pltpu.HBM), ANY],
        out_specs=[VMEM, VMEM],
        out_shape=[
            pltpu.VMEM((tokens, columns), BF16),
            pltpu.VMEM((rows, out_weight.shape[1]), BF16),
        ],
        scratch_shapes=[pltpu.SemaphoreType.DMA],
        compiler_params=pltpu.CompilerParams(vmem_limit_bytes=24 * MIB),
        cost_estimate=pl.CostEstimate(
            flops=2 * tokens * depth * columns, bytes_accessed=8 * MIB, transcendentals=0
        ),
        name="values",
    )(*blocks, in_hbm(out_weight), after)


def by_heads(row):
    return jnp.concatenate([row[:, c : c + HD] for c in range(0, row.shape[1], HD)], axis=0)


def turned_kernel(n_tp, *refs):
    kv_ref, cos_q, sin_q, out_ref = refs[n_tp:]
    own_rows, new_count, columns = refs[0].shape
    rows = new_count * GROUP
    kv_local = columns // HD // GROUP
    me, seq = lax.axis_index("tp"), lax.axis_index("seq")
    for r in range(own_rows):
        spots = [pl.ds((seq * own_rows + r) * new_count + n, 1) for n in range(new_count)]
        turns = [(cos_q[spot], sin_q[spot]) for spot in spots]

        def turn(value, n):
            return value * turns[n][0] + pltpu.roll(value, HD // 2, 1) * turns[n][1]

        for d in range(n_tp):
            raw = refs[d][r].astype(F32)
            blocks = [by_heads(raw[n : n + 1]) for n in range(new_count)]
            for g in range(kv_local):
                parts = [turn(q[g * GROUP : (g + 1) * GROUP], n) for n, q in enumerate(blocks)]
                at = ((me ^ falling(n_tp)[d]) * kv_local + g) * rows
                at = pl.ds(pl.multiple_of(at, rows), rows)
                out_ref[r, at] = jnp.concatenate(parts, axis=0).astype(BF16)
        raw = kv_ref[r].astype(F32)
        fresh = []
        for n in range(new_count):
            kv = by_heads(raw[n : n + 1])
            row = lax.broadcasted_iota(jnp.int32, kv.shape, 0)
            fresh.append(jnp.where(row % 2 == 0, turn(kv, n), kv))
        fresh.append(jnp.zeros((FRESH - new_count * 2 * kv_local, HD), F32))
        out_ref[r, KVH * rows :] = jnp.concatenate(fresh, axis=0).astype(BF16)


FRESH = 16


def turned(pieces, fresh, cos_q, sin_q):
    n_tp = len(pieces)
    own_rows, new_count, _ = pieces[0].shape
    rows = KVH * GROUP * new_count + FRESH
    return pl.pallas_call(
        functools.partial(turned_kernel, n_tp),
        in_specs=[VMEM] * (n_tp + 3),
        out_specs=VMEM,
        out_shape=jax.ShapeDtypeStruct((own_rows, rows, HD), BF16),
        compiler_params=pltpu.CompilerParams(vmem_limit_bytes=8 * MIB),
        name="turned",
    )(*pieces, fresh, cos_q, sin_q)


def scores_kernel(n_seq, n_tp, *refs):
    new = refs[:n_seq]
    k_ref, meta = refs[n_seq : n_seq + 2]
    outs = refs[n_seq + 2 : n_seq + 2 + n_tp]
    all_q, ready = refs[n_seq + 2 + n_tp :]
    own_rows = new[0].shape[0]
    local_pages = k_ref.shape[0] // PAGE
    all_rows = all_q.shape[1]
    rows = all_rows // KVH
    count = all_rows // n_tp
    scale = 1.0 / math.sqrt(HD)
    me = lax.axis_index("tp")
    seq = lax.axis_index("seq")
    first = seq * local_pages
    even = lax.broadcasted_iota(jnp.int32, (all_rows, HD), 0) // rows % 2 == 0
    for ds in range(n_seq):
        for rr in range(own_rows):
            q = new[ds][rr, :all_rows].astype(F32)
            request = (seq ^ reverse(n_seq)[ds]) * own_rows + rr
            all_q[request, :, :HD] = jnp.where(even, q, 0.0).astype(BF16)
            all_q[request, :, HD:] = jnp.where(even, 0.0, q).astype(BF16)
    for p in range(0, local_pages, 2):
        requests = [meta[first + p], meta[first + p + 1]]
        tokens = slice(p * PAGE, (p + 2) * PAGE)
        for pair in range(KVH // 2):
            k = k_ref[tokens, 2 * pair * HD : 2 * (pair + 1) * HD]
            at = slice(2 * pair * rows, 2 * (pair + 1) * rows)
            q = jnp.concatenate([all_q[request, at] for request in requests], axis=0)
            s = lax.dot_general(q, k, (((1,), (1,)), ((), ())), preferred_element_type=F32)
            for i in range(2):
                part = s[2 * i * rows : 2 * (i + 1) * rows, i * PAGE : (i + 1) * PAGE]
                here = slice((p + i) * PAGE, (p + i + 1) * PAGE)
                ready[at, here] = (part * scale).astype(BF16)
    for d in range(n_tp):
        outs[d][...] = ready[pl.ds(pl.multiple_of((me ^ order(n_tp)[d]) * count, count), count)]


def partial_scores(new, k, meta, prompts, n_tp):
    n_seq = len(new)
    all_rows = new[0].shape[1] - FRESH
    tokens = k.shape[0]
    rows = all_rows // n_tp
    return pl.pallas_call(
        functools.partial(scores_kernel, n_seq, n_tp),
        in_specs=[VMEM] * (n_seq + 1) + [SMEM],
        out_specs=[VMEM] * n_tp,
        out_shape=[jax.ShapeDtypeStruct((rows, tokens), BF16)] * n_tp,
        scratch_shapes=[
            pltpu.VMEM((prompts, all_rows, 2 * HD), BF16),
            pltpu.VMEM((all_rows, tokens), BF16),
        ],
        compiler_params=pltpu.CompilerParams(vmem_limit_bytes=24 * MIB),
        cost_estimate=pl.CostEstimate(
            flops=2 * tokens * all_rows * HD, bytes_accessed=6 * MIB, transcendentals=0
        ),
        name="scores",
    )(*new, k, meta)


def fresh_kernel(n_seq, *refs):
    new = refs[:n_seq]
    _, score_ref, value_ref = refs[n_seq:]
    new_count, rows_local, _ = score_ref.shape
    own_rows = new[0].shape[0]
    rows = new_count * GROUP
    kv_local = rows_local // rows
    scale = 1.0 / math.sqrt(HD)
    seq = lax.axis_index("seq")
    own = pl.ds(pl.multiple_of(lax.axis_index("tp") * rows_local, rows_local), rows_local)
    step = lax.broadcasted_iota(jnp.int32, (rows_local, HD), 0) % rows // GROUP
    lane = lax.broadcasted_iota(jnp.int32, (rows_local, HD), 1)
    found = [jnp.full((rows_local, HD), NEG, F32) for _ in range(new_count)]

    def spread(block, first):
        parts = [block[first + 2 * g : first + 2 * g + 1] for g in range(kv_local)]
        return jnp.concatenate([jnp.broadcast_to(a, (rows, HD)) for a in parts], axis=0)

    for ds in range(n_seq):
        for rr in range(own_rows):
            request = (seq ^ reverse(n_seq)[ds]) * own_rows + rr
            q = new[ds][rr, own].astype(F32)
            both = new[ds][rr, KVH * rows :].astype(F32)
            for n in range(new_count):
                first = n * 2 * kv_local
                s = jnp.sum(q * spread(both, first), axis=1, keepdims=True) * scale
                found[n] = jnp.where((lane == request) & (step >= n), s, found[n])
                value_ref[request * new_count + n] = spread(both, first + 1)
    for n in range(new_count):
        score_ref[n] = found[n]


def fresh_scores(new, after, prompts, new_count, n_tp):
    n_seq = len(new)
    rows = (new[0].shape[1] - FRESH) // n_tp
    return pl.pallas_call(
        functools.partial(fresh_kernel, n_seq),
        in_specs=[VMEM] * n_seq + [ANY],
        out_specs=[VMEM, VMEM],
        out_shape=[
            jax.ShapeDtypeStruct((new_count, rows, HD), F32),
            jax.ShapeDtypeStruct((prompts * new_count, rows, HD), F32),
        ],
        compiler_params=pltpu.CompilerParams(vmem_limit_bytes=16 * MIB),
        cost_estimate=pl.CostEstimate(flops=0, bytes_accessed=2 * MIB, transcendentals=0),
        name="fresh",
    )(*new, after)


def weights_kernel(pages, prompts, n_tp, *refs):
    chunks = refs[:n_tp]
    meta, _, w_ref, stats_ref = refs[n_tp:]
    rows, tokens = w_ref.shape
    local_pages = tokens // PAGE
    first = lax.axis_index("seq") * local_pages
    lane = lax.broadcasted_iota(jnp.int32, (rows, PAGE), 1)
    scores, maxima, masks, owners = [], [], [], []
    for p in range(local_pages):
        at = slice(p * PAGE, (p + 1) * PAGE)
        total = chunks[0][:, at].astype(F32)
        for d in range(1, n_tp):
            total = total + chunks[d][:, at].astype(F32)
        mask = lane < meta[2 * pages + first + p]
        total = jnp.where(mask, total, NEG)
        masks.append(mask)
        scores.append(total)
        maxima.append(jnp.max(total, axis=1, keepdims=True))
        owners.append(meta[first + p])
    quarter = lane // prompts
    spot = lane % prompts
    stats = jnp.where(quarter == 0, NEG, 0.0)
    same = [owners[p] == owners[p - 1] for p in range(1, local_pages)]
    for p in range(1, local_pages):
        maxima[p] = jnp.where(same[p - 1], jnp.maximum(maxima[p - 1], maxima[p]), maxima[p])
    for p in reversed(range(local_pages - 1)):
        maxima[p] = jnp.where(same[p], maxima[p + 1], maxima[p])
    for p in range(local_pages):
        top = maxima[p]
        high = top.astype(BF16).astype(F32)
        low = (top - high).astype(BF16).astype(F32)
        w = jnp.where(masks[p], jnp.exp(scores[p] - (high + low)), 0.0)
        w_ref[:, p * PAGE : (p + 1) * PAGE] = w.astype(BF16)
        here = spot == owners[p]
        stats = jnp.where(here & (quarter == 0), high, stats)
        stats = jnp.where(here & (quarter == 1), low, stats)
        part = jnp.sum(w, axis=1, keepdims=True)
        stats = stats + jnp.where(here & (quarter == 2), part, 0.0)
    high = stats.astype(BF16).astype(F32)
    low = pltpu.roll(stats - high, prompts, 1)
    stats_ref[...] = jnp.where(quarter == 3, low, stats).astype(BF16)


def softmax_weights(chunks, meta, after, pages, prompts):
    n_tp = len(chunks)
    rows, tokens = chunks[0].shape
    return pl.pallas_call(
        functools.partial(weights_kernel, pages, prompts, n_tp),
        in_specs=[VMEM] * n_tp + [SMEM, ANY],
        out_specs=[VMEM, VMEM],
        out_shape=[
            jax.ShapeDtypeStruct((rows, tokens), BF16),
            jax.ShapeDtypeStruct((rows, PAGE), BF16),
        ],
        compiler_params=pltpu.CompilerParams(vmem_limit_bytes=8 * MIB),
        name="weights",
    )(*chunks, meta, after)


def weighted_kernel(n_tp, *refs):
    pieces = refs[:n_tp]
    va_ref, vb_ref, meta = refs[n_tp : n_tp + 3]
    outs = refs[n_tp + 3 : n_tp + 3 + n_tp]
    ready, total = refs[n_tp + 3 + n_tp :]
    rows_local, tokens_here = pieces[0].shape
    kv_local = KVH // n_tp
    rows = rows_local // kv_local
    local_pages = tokens_here // PAGE
    first = lax.axis_index("seq") * local_pages
    me = lax.axis_index("tp")
    own = [pl.ds(pl.multiple_of((me ^ order(n_tp)[d]) * rows_local, rows_local), rows_local) for d in range(n_tp)]
    for d in range(n_tp):
        at = pl.multiple_of((me ^ reverse(n_tp)[d]) * rows_local, rows_local)
        ready[pl.ds(at, rows_local)] = pieces[d][...]
    total[...] = jnp.zeros_like(total)
    half = va_ref.shape[1] // HD
    none = jnp.zeros((2 * rows, PAGE), BF16)
    for p in range(0, local_pages, 2):
        requests = [meta[first + p], meta[first + p + 1]]
        tokens = slice(p * PAGE, (p + 2) * PAGE)
        for pair in range(KVH // 2):
            head = 2 * pair
            v_ref = va_ref if head < half else vb_ref
            v = v_ref[tokens, head % half * HD : (head % half + 2) * HD]
            at = slice(head * rows, (head + 2) * rows)
            w = [ready[at, (p + i) * PAGE : (p + i + 1) * PAGE] for i in range(2)]
            w = [jnp.concatenate([w[0], none], axis=1), jnp.concatenate([none, w[1]], axis=1)]
            sums = jnp.dot(jnp.concatenate(w, axis=0), v, preferred_element_type=F32)
            for i, request in enumerate(requests):
                for h in range(2):
                    row = (2 * i + h) * rows
                    part = sums[row : row + rows, h * HD : (h + 1) * HD]
                    total[request, (head + h) * rows : (head + h + 1) * rows] += part
    for d in range(n_tp):
        outs[d][...] = total[:, own[d]].astype(BF16)


def weighted_values(pieces, va, vb, meta, prompts):
    n_tp = len(pieces)
    rows, tokens = pieces[0].shape
    return pl.pallas_call(
        functools.partial(weighted_kernel, n_tp),
        in_specs=[VMEM] * (n_tp + 2) + [SMEM],
        out_specs=[VMEM] * n_tp,
        out_shape=[jax.ShapeDtypeStruct((prompts, rows, HD), BF16)] * n_tp,
        scratch_shapes=[
            pltpu.VMEM((rows * n_tp, tokens), BF16),
            pltpu.VMEM((prompts, rows * n_tp, HD), F32),
        ],
        compiler_params=pltpu.CompilerParams(vmem_limit_bytes=24 * MIB),
        cost_estimate=pl.CostEstimate(
            flops=2 * tokens * rows * n_tp * HD, bytes_accessed=8 * MIB, transcendentals=0
        ),
        name="weighted",
    )(*pieces, va, vb, meta)


def summed_kernel(n_tp, *refs):
    chunks = refs[:n_tp]
    stats_ref, out_ref = refs[n_tp:]
    prompts = chunks[0].shape[0]
    total = chunks[0][...].astype(F32)
    for d in range(1, n_tp):
        total = total + chunks[d][...].astype(F32)
    out_ref[:prompts] = total.astype(BF16)
    out_ref[prompts] = stats_ref[...]


def summed(chunks, stats):
    n_tp = len(chunks)
    prompts, rows, _ = chunks[0].shape
    return pl.pallas_call(
        functools.partial(summed_kernel, n_tp),
        in_specs=[VMEM] * (n_tp + 1),
        out_specs=VMEM,
        out_shape=jax.ShapeDtypeStruct((prompts + 1, rows, HD), BF16),
        compiler_params=pltpu.CompilerParams(vmem_limit_bytes=8 * MIB),
        cost_estimate=pl.CostEstimate(flops=0, bytes_accessed=4 * MIB, transcendentals=0),
        name="summed",
    )(*chunks, stats)


def output_kernel(n_seq, *refs):
    pieces = refs[:n_seq]
    fresh_ref, value_ref, wa_ref, wb_ref, out_ref, held = refs[n_seq:]
    more, rows_local, _ = pieces[0].shape
    prompts = more - 1
    new_count = fresh_ref.shape[0]
    rows = new_count * GROUP
    kv_local = rows_local // rows
    heads = kv_local * GROUP
    tops, parts = [], []
    for s in range(n_seq):
        stats = pieces[s][prompts].astype(F32)
        folded = stats + pltpu.roll(stats, HD - prompts, 1)
        tops.append(folded)
        parts.append(pltpu.roll(folded, HD - 2 * prompts, 1))
    fresh = [fresh_ref[n] for n in range(new_count)]
    top = fresh[0]
    for other in fresh[1:] + tops:
        top = jnp.maximum(top, other)
    weights = [jnp.exp(f - top) for f in fresh]
    factors = [jnp.exp(t - top) for t in tops]
    total = weights[0]
    for w in weights[1:]:
        total = total + w
    for f, part in zip(factors, parts):
        total = total + f * part
    weights = [w / total for w in weights]
    factors = [f / total for f in factors]
    for r in range(prompts):
        sums = jnp.zeros((rows_local, HD), F32)
        for s in range(n_seq):
            sums = sums + factors[s][:, r : r + 1] * pieces[s][r].astype(F32)
        for n in range(new_count):
            sums = sums + weights[n][:, r : r + 1] * value_ref[r * new_count + n]
        for g in range(kv_local):
            for n in range(new_count):
                at = g * rows + n * GROUP
                held[g * GROUP : (g + 1) * GROUP, r * new_count + n] = sums[at : at + GROUP]
    half = heads // 2
    product = jnp.zeros(out_ref.shape, F32)
    for w_ref, at in ((wa_ref, 0), (wb_ref, half)):
        left = [held[h].astype(BF16) for h in range(at, at + half)]
        left = jnp.concatenate(left, axis=1)
        product = product + jnp.dot(left, w_ref[...], preferred_element_type=F32)
    out_ref[...] = product.astype(BF16)


def output_partial(pieces, fresh, values, weights):
    n_seq = len(pieces)
    new_count = fresh.shape[0]
    prompts = pieces[0].shape[0] - 1
    depth, columns = weights[0].shape
    return pl.pallas_call(
        functools.partial(output_kernel, n_seq),
        in_specs=[VMEM] * (n_seq + 4),
        out_specs=VMEM,
        out_shape=jax.ShapeDtypeStruct((prompts * new_count, columns), BF16),
        scratch_shapes=[pltpu.VMEM((2 * depth // HD, prompts * new_count, HD), F32)],
        compiler_params=pltpu.CompilerParams(vmem_limit_bytes=24 * MIB),
        name="output",
    )(*pieces, fresh, values, *weights)


def final_kernel(n_tp, *refs):
    pieces = refs[:n_tp]
    res_ref, out_ref = refs[n_tp:]
    prompts, new_count, _ = out_ref.shape
    total = pieces[0][...].astype(F32)
    for d in range(1, n_tp):
        total = total + pieces[d][...].astype(F32)
    for r in range(prompts):
        out_ref[r] = res_ref[r].astype(F32) + total[r * new_count : (r + 1) * new_count]


def final_sum(pieces, residual):
    n_tp = len(pieces)
    return pl.pallas_call(
        functools.partial(final_kernel, n_tp),
        in_specs=[VMEM] * (n_tp + 1),
        out_specs=VMEM,
        out_shape=jax.ShapeDtypeStruct(residual.shape, F32),
        compiler_params=pltpu.CompilerParams(vmem_limit_bytes=8 * MIB),
        name="final",
    )(*pieces, residual)


def on_device(
    prefill_states, kv_weight, page_counts, tail_tokens, new_query, new_keyval, residual, out_weight
):
    n_seq, n_tp = lax.axis_size("seq"), lax.axis_size("tp")
    own_rows, new_count, _ = new_query.shape
    prompts = page_counts.shape[0]
    pages = prefill_states.shape[0] // PAGE * n_seq
    query = gather(new_query, "tp", falling(n_tp))
    acc, xa, wa, cosine, sine, cos_q, sin_q, meta = load(
        prefill_states, kv_weight, page_counts, tail_tokens, pages, new_count
    )
    new = turned(query, new_keyval, cos_q, sin_q)
    k, xb, wb = rotated_keys(acc, xa, wa, prefill_states, kv_weight, cosine, sine, new)
    new = gather(new, "seq")
    scores = partial_scores(new, k, meta, prompts, n_tp)
    va, oa = project_values((xa, wa, xb, wb), out_weight, 0, scores[0])
    weights, stats = softmax_weights(exchange(scores, "tp"), meta, va, pages, prompts)
    vb, ob = project_values((xa, wa, xb, wb), out_weight, 1, stats)
    fresh, values = fresh_scores(new, stats, prompts, new_count, n_tp)
    chunks = weighted_values(gather(weights, "tp"), va, vb, meta, prompts)
    pieces = gather(summed(exchange(chunks, "tp"), stats), "seq")
    partial = output_partial(pieces, fresh, values, (oa, ob))
    return final_sum(gather(partial, "tp"), residual)


def solution(mesh):
    placed = (
        P(("groups", "seq"), "tp"),
        P("tp", None),
        P("groups"),
        P("groups"),
        P(("groups", "seq"), None, "tp"),
        P(("groups", "seq"), None, "tp"),
        P("groups", None, "seq"),
        P("tp", "seq"),
    )
    return jax.shard_map(
        on_device, mesh=mesh, in_specs=placed, out_specs=P("groups", None, "seq"), check_vma=False
    )
```

```python
import functools
import math

import jax
import jax.numpy as jnp
from jax import lax
from jax.experimental import pallas as pl
from jax.experimental.pallas import tpu as pltpu
from jax.sharding import PartitionSpec as P

QH = 64
KVH = 8
HD = 128
PAGE = 128
GROUP = QH // KVH
NEG = -1e30
F32 = jnp.float32
BF16 = jnp.bfloat16
MIB = 1 << 20

VMEM = pl.BlockSpec(memory_space=pltpu.VMEM)
SMEM = pl.BlockSpec(memory_space=pltpu.SMEM)
ANY = pl.BlockSpec(memory_space=pl.ANY)


def pairs(value, axis, d):
    return lax.ppermute(value, axis, [(i, i ^ d) for i in range(lax.axis_size(axis))])


def order(size):
    found, top = [0], size // 2
    while top:
        found += range(top, 2 * top)
        top //= 2
    return found


def reverse(size):
    return [0] + order(size)[:0:-1]


def exchange(chunks, axis):
    offsets = order(len(chunks))
    return [chunks[0]] + [pairs(c, axis, d) for c, d in zip(chunks[1:], offsets[1:])]


def gather(value, axis, offsets=None):
    offsets = offsets or reverse(lax.axis_size(axis))
    return [value] + [pairs(value, axis, d) for d in offsets[1:]]


def falling(size):
    return [0] + list(range(size - 1, 0, -1))


def lane_freqs(rows):
    lane = lax.broadcasted_iota(jnp.int32, (rows, HD), 1) % (HD // 2)
    return jnp.exp(-(lane.astype(F32) * (2.0 / HD)) * math.log(500000.0))


def sine_sign(rows):
    lane = lax.broadcasted_iota(jnp.int32, (rows, HD), 1)
    return jnp.where(lane < HD // 2, -1.0, 1.0)


def in_hbm(value):
    return pltpu.with_memory_space_constraint(value, pltpu.HBM)


def by_row(rows, numbers):
    row = lax.broadcasted_iota(jnp.int32, (rows, HD), 0)
    out = jnp.zeros((rows, HD), F32)
    for i, number in enumerate(numbers):
        out = jnp.where(row == i, number.astype(F32), out)
    return out


def page_table(pages, prompts, counts, tails, meta):
    def one_prompt(r, start):
        length = (counts[r] - 1) * PAGE + tails[r]
        meta[3 * pages + r] = length

        def one_page(i, carry):
            meta[start + i] = r
            meta[pages + start + i] = i * PAGE
            meta[2 * pages + start + i] = jnp.minimum(length - i * PAGE, PAGE)
            return carry

        lax.fori_loop(0, counts[r], one_page, 0)
        return start + counts[r]

    lax.fori_loop(0, prompts, one_prompt, 0)


def rotation_tables(pages, local_pages, meta, cos_s, sin_s):
    freqs = lane_freqs(8)
    low = lax.broadcasted_iota(jnp.int32, (8, HD), 0).astype(F32) * freqs
    low_cos, low_sin = jnp.cos(low), jnp.sin(low)
    high = lax.broadcasted_iota(jnp.int32, (PAGE // 8, HD), 0).astype(F32) * 8.0
    high = high * lane_freqs(PAGE // 8)
    high_cos, high_sin = jnp.cos(high), jnp.sin(high)
    first = lax.axis_index("seq") * local_pages
    base = by_row(local_pages, [meta[pages + first + p] for p in range(local_pages)])
    base = base * lane_freqs(local_pages)
    base_cos, base_sin = jnp.cos(base), jnp.sin(base)
    sign = sine_sign(8)
    for i in range(PAGE // 8):
        c, s = high_cos[i : i + 1], high_sin[i : i + 1]
        cosine, sine = low_cos * c - low_sin * s, low_sin * c + low_cos * s
        for p in range(local_pages):
            at = slice(p * PAGE + i * 8, p * PAGE + i * 8 + 8)
            c, s = base_cos[p : p + 1], base_sin[p : p + 1]
            cos_s[at] = cosine * c - sine * s
            sin_s[at] = sign * (sine * c + cosine * s)


def pair_columns(w_ref, rows, pair, part):
    at = [(2 * head + part) * HD for head in (2 * pair, 2 * pair + 1)]
    return jnp.concatenate([w_ref[rows, c : c + HD] for c in at], axis=1)


def copies_of(x_hbm, w_hbm, x_ref, w_ref, sems, first, size, count):
    pairs_of = []
    for i in range(count):
        source, to = pl.ds(first + i * size, size), pl.ds(i * size, size)
        x_copy = pltpu.make_async_copy(x_hbm.at[:, source], x_ref.at[:, to], sems.at[2 * i])
        w_copy = pltpu.make_async_copy(w_hbm.at[source], w_ref.at[to], sems.at[2 * i + 1])
        pairs_of.append((x_copy, w_copy))
    return pairs_of


def start(copies):
    for copy in copies:
        copy.start()


def wait(copies):
    for copy in copies:
        copy.wait()


def add_block(x_ref, w_ref, rows, acc, out, fresh):
    tokens = x_ref.shape[0]
    tall = tokens // 2
    for pair in range(KVH // 2):
        weight = pair_columns(w_ref, rows, pair, 0)
        columns = slice(2 * pair * HD, 2 * (pair + 1) * HD)
        for top in range(0, tokens, tall):
            at = slice(top, top + tall)
            product = jnp.dot(x_ref[at, rows], weight, preferred_element_type=F32)
            out[at, columns] = product if fresh else acc[at, columns] + product


def load_kernel(pages, prompts, new_count, x_hbm, w_hbm, counts, tails, *refs):
    acc, x_ref, w_ref, cos_ref, sin_ref, cos_q, sin_q, meta, sems = refs[:9]
    counts_s, tails_s, small_sems = refs[9:]
    tokens = x_ref.shape[0]
    size = x_ref.shape[1] // 3
    copies = copies_of(x_hbm, w_hbm, x_ref, w_ref, sems, 0, size, 3)
    start(copies[0])
    small = [
        pltpu.make_async_copy(counts, counts_s, small_sems.at[0]),
        pltpu.make_async_copy(tails, tails_s, small_sems.at[1]),
    ]
    start(small)
    wait(small)
    page_table(pages, prompts, counts_s, tails_s, meta)
    rotation_tables(pages, tokens // PAGE, meta, cos_ref, sin_ref)
    spots = [meta[3 * pages + r] + n for r in range(prompts) for n in range(new_count)]
    angles = by_row(len(spots), spots) * lane_freqs(len(spots))
    cos_q[...] = jnp.cos(angles)
    sin_q[...] = jnp.sin(angles) * sine_sign(len(spots))
    start(copies[1])
    for i in range(2):
        wait(copies[i])
        if i == 0:
            start(copies[2])
        add_block(x_ref, w_ref, slice(i * size, (i + 1) * size), acc, acc, i == 0)
    wait(copies[2])


def load(x, kv_weight, counts, tails, pages, new_count):
    tokens, depth = x.shape
    columns = kv_weight.shape[1]
    prompts = counts.shape[0]
    part = depth // 4 * 3
    hbm = pl.BlockSpec(memory_space=pltpu.HBM)
    return pl.pallas_call(
        functools.partial(load_kernel, pages, prompts, new_count),
        in_specs=[hbm] * 4,
        out_specs=[VMEM] * 7 + [SMEM],
        out_shape=[
            pltpu.VMEM((tokens, KVH * HD), F32),
            pltpu.VMEM((tokens, part), BF16),
            pltpu.VMEM((part, columns), BF16),
            pltpu.VMEM((tokens, HD), F32),
            pltpu.VMEM((tokens, HD), F32),
            pltpu.VMEM((prompts * new_count, HD), F32),
            pltpu.VMEM((prompts * new_count, HD), F32),
            jax.ShapeDtypeStruct((3 * pages + prompts,), jnp.int32),
        ],
        scratch_shapes=[
            pltpu.SemaphoreType.DMA((6,)),
            pltpu.SMEM((prompts,), jnp.int32),
            pltpu.SMEM((prompts,), jnp.int32),
            pltpu.SemaphoreType.DMA((2,)),
        ],
        compiler_params=pltpu.CompilerParams(vmem_limit_bytes=28 * MIB),
        cost_estimate=pl.CostEstimate(
            flops=tokens * depth * KVH * HD,
            bytes_accessed=2 * part * (tokens + columns),
            transcendentals=0,
        ),
        name="load",
    )(*[in_hbm(a) for a in (x, kv_weight, counts, tails)])


def keys_kernel(acc, xa_ref, wa_ref, x_hbm, w_hbm, cos_ref, sin_ref, after, k_ref, x_ref, w_ref, total, sems):
    tokens, size = x_ref.shape
    tall = tokens // 2
    (copies,) = copies_of(x_hbm, w_hbm, x_ref, w_ref, sems, 3 * size, size, 1)
    start(copies)
    add_block(xa_ref, wa_ref, slice(2 * size, 3 * size), acc, total, False)
    wait(copies)
    for pair in range(KVH // 2):
        weight = pair_columns(w_ref, slice(None), pair, 0)
        columns = slice(2 * pair * HD, 2 * (pair + 1) * HD)
        for top in range(0, tokens, tall):
            at = slice(top, top + tall)
            product = total[at, columns] + jnp.dot(x_ref[at], weight, preferred_element_type=F32)
            cosine, sine = cos_ref[at], sin_ref[at]
            for h in range(2):
                k = product[:, h * HD : (h + 1) * HD]
                k = k * cosine + pltpu.roll(k, HD // 2, 1) * sine
                k_ref[at, (2 * pair + h) * HD : (2 * pair + h + 1) * HD] = k.astype(BF16)


def rotated_keys(acc, xa, wa, x, kv_weight, cosine, sine, after):
    tokens, depth = x.shape
    columns = kv_weight.shape[1]
    hbm = pl.BlockSpec(memory_space=pltpu.HBM)
    return pl.pallas_call(
        keys_kernel,
        in_specs=[VMEM] * 3 + [hbm] * 2 + [VMEM] * 2 + [ANY],
        out_specs=[VMEM] * 3,
        out_shape=[
            pltpu.VMEM((tokens, KVH * HD), BF16),
            pltpu.VMEM((tokens, depth // 4), BF16),
            pltpu.VMEM((depth // 4, columns), BF16),
        ],
        scratch_shapes=[
            pltpu.VMEM((tokens, KVH * HD), F32),
            pltpu.SemaphoreType.DMA((2,)),
        ],
        compiler_params=pltpu.CompilerParams(vmem_limit_bytes=24 * MIB),
        cost_estimate=pl.CostEstimate(
            flops=tokens * depth * KVH * HD, bytes_accessed=8 * MIB, transcendentals=0
        ),
        name="keys",
    )(acc, xa, wa, in_hbm(x), in_hbm(kv_weight), cosine, sine, after)


def values_kernel(first, xa_ref, wa_ref, xb_ref, wb_ref, o_hbm, after, v_ref, o_ref, sem):
    depth = o_ref.shape[0]
    copy = pltpu.make_async_copy(o_hbm.at[pl.ds(first * depth, depth)], o_ref, sem)
    copy.start()
    tokens, columns = v_ref.shape
    tall = tokens // 2
    pairs_here = columns // (2 * HD)
    for pair in range(pairs_here):
        weights = [pair_columns(w, slice(None), first * pairs_here + pair, 1) for w in (wa_ref, wb_ref)]
        for i in range(2):
            at = slice(i * tall, (i + 1) * tall)
            product = jnp.dot(xa_ref[at], weights[0], preferred_element_type=F32)
            product = product + jnp.dot(xb_ref[at], weights[1], preferred_element_type=F32)
            v_ref[at, 2 * pair * HD : 2 * (pair + 1) * HD] = product.astype(BF16)
    copy.wait()


def project_values(blocks, out_weight, first, after):
    tokens, depth = blocks[0].shape
    columns = KVH // 2 * HD
    rows = out_weight.shape[0] // 2
    return pl.pallas_call(
        functools.partial(values_kernel, first),
        in_specs=[VMEM] * 4 + [pl.BlockSpec(memory_space=pltpu.HBM), ANY],
        out_specs=[VMEM, VMEM],
        out_shape=[
            pltpu.VMEM((tokens, columns), BF16),
            pltpu.VMEM((rows, out_weight.shape[1]), BF16),
        ],
        scratch_shapes=[pltpu.SemaphoreType.DMA],
        compiler_params=pltpu.CompilerParams(vmem_limit_bytes=24 * MIB),
        cost_estimate=pl.CostEstimate(
            flops=2 * tokens * depth * columns, bytes_accessed=8 * MIB, transcendentals=0
        ),
        name="values",
    )(*blocks, in_hbm(out_weight), after)


def by_heads(row):
    return jnp.concatenate([row[:, c : c + HD] for c in range(0, row.shape[1], HD)], axis=0)


def turned_kernel(n_tp, *refs):
    kv_ref, cos_q, sin_q, out_ref = refs[n_tp:]
    own_rows, new_count, columns = refs[0].shape
    rows = new_count * GROUP
    kv_local = columns // HD // GROUP
    me, seq = lax.axis_index("tp"), lax.axis_index("seq")
    for r in range(own_rows):
        spots = [pl.ds((seq * own_rows + r) * new_count + n, 1) for n in range(new_count)]
        turns = [(cos_q[spot], sin_q[spot]) for spot in spots]

        def turn(value, n):
            return value * turns[n][0] + pltpu.roll(value, HD // 2, 1) * turns[n][1]

        for d in range(n_tp):
            raw = refs[d][r].astype(F32)
            blocks = [by_heads(raw[n : n + 1]) for n in range(new_count)]
            for g in range(kv_local):
                parts = [turn(q[g * GROUP : (g + 1) * GROUP], n) for n, q in enumerate(blocks)]
                at = ((me ^ falling(n_tp)[d]) * kv_local + g) * rows
                at = pl.ds(pl.multiple_of(at, rows), rows)
                out_ref[r, at] = jnp.concatenate(parts, axis=0).astype(BF16)
        raw = kv_ref[r].astype(F32)
        fresh = []
        for n in range(new_count):
            kv = by_heads(raw[n : n + 1])
            row = lax.broadcasted_iota(jnp.int32, kv.shape, 0)
            fresh.append(jnp.where(row % 2 == 0, turn(kv, n), kv))
        fresh.append(jnp.zeros((FRESH - new_count * 2 * kv_local, HD), F32))
        out_ref[r, KVH * rows :] = jnp.concatenate(fresh, axis=0).astype(BF16)


FRESH = 16


def turned(pieces, fresh, cos_q, sin_q):
    n_tp = len(pieces)
    own_rows, new_count, _ = pieces[0].shape
    rows = KVH * GROUP * new_count + FRESH
    return pl.pallas_call(
        functools.partial(turned_kernel, n_tp),
        in_specs=[VMEM] * (n_tp + 3),
        out_specs=VMEM,
        out_shape=jax.ShapeDtypeStruct((own_rows, rows, HD), BF16),
        compiler_params=pltpu.CompilerParams(vmem_limit_bytes=8 * MIB),
        name="turned",
    )(*pieces, fresh, cos_q, sin_q)


def scores_kernel(n_seq, n_tp, *refs):
    new = refs[:n_seq]
    k_ref, meta = refs[n_seq : n_seq + 2]
    outs = refs[n_seq + 2 : n_seq + 2 + n_tp]
    all_q, ready, table, sem = refs[n_seq + 2 + n_tp :]
    copy = pltpu.make_async_copy(meta, table, sem)
    copy.start()
    own_rows = new[0].shape[0]
    local_pages = k_ref.shape[0] // PAGE
    all_rows = all_q.shape[1]
    rows = all_rows // KVH
    count = all_rows // n_tp
    scale = 1.0 / math.sqrt(HD)
    me = lax.axis_index("tp")
    seq = lax.axis_index("seq")
    first = seq * local_pages
    even = lax.broadcasted_iota(jnp.int32, (all_rows, HD), 0) // rows % 2 == 0
    for ds in range(n_seq):
        for rr in range(own_rows):
            q = new[ds][rr, :all_rows].astype(F32)
            request = (seq ^ reverse(n_seq)[ds]) * own_rows + rr
            all_q[request, :, :HD] = jnp.where(even, q, 0.0).astype(BF16)
            all_q[request, :, HD:] = jnp.where(even, 0.0, q).astype(BF16)
    copy.wait()
    for p in range(0, local_pages, 2):
        requests = [table[first + p], table[first + p + 1]]
        tokens = slice(p * PAGE, (p + 2) * PAGE)
        for pair in range(KVH // 2):
            k = k_ref[tokens, 2 * pair * HD : 2 * (pair + 1) * HD]
            at = slice(2 * pair * rows, 2 * (pair + 1) * rows)
            q = jnp.concatenate([all_q[request, at] for request in requests], axis=0)
            s = lax.dot_general(q, k, (((1,), (1,)), ((), ())), preferred_element_type=F32)
            for i in range(2):
                part = s[2 * i * rows : 2 * (i + 1) * rows, i * PAGE : (i + 1) * PAGE]
                here = slice((p + i) * PAGE, (p + i + 1) * PAGE)
                ready[at, here] = (part * scale).astype(BF16)
    for d in range(n_tp):
        outs[d][...] = ready[pl.ds(pl.multiple_of((me ^ order(n_tp)[d]) * count, count), count)]


def partial_scores(new, k, meta, prompts, n_tp):
    n_seq = len(new)
    all_rows = new[0].shape[1] - FRESH
    tokens = k.shape[0]
    rows = all_rows // n_tp
    return pl.pallas_call(
        functools.partial(scores_kernel, n_seq, n_tp),
        in_specs=[VMEM] * (n_seq + 1) + [pl.BlockSpec(memory_space=pltpu.HBM)],
        out_specs=[VMEM] * n_tp,
        out_shape=[jax.ShapeDtypeStruct((rows, tokens), BF16)] * n_tp,
        scratch_shapes=[
            pltpu.VMEM((prompts, all_rows, 2 * HD), BF16),
            pltpu.VMEM((all_rows, tokens), BF16),
            pltpu.SMEM(meta.shape, jnp.int32),
            pltpu.SemaphoreType.DMA,
        ],
        compiler_params=pltpu.CompilerParams(vmem_limit_bytes=24 * MIB),
        cost_estimate=pl.CostEstimate(
            flops=2 * tokens * all_rows * HD, bytes_accessed=6 * MIB, transcendentals=0
        ),
        name="scores",
    )(*new, k, in_hbm(meta))


def fresh_kernel(n_seq, *refs):
    new = refs[:n_seq]
    _, score_ref, value_ref = refs[n_seq:]
    new_count, rows_local, _ = score_ref.shape
    own_rows = new[0].shape[0]
    rows = new_count * GROUP
    kv_local = rows_local // rows
    scale = 1.0 / math.sqrt(HD)
    seq = lax.axis_index("seq")
    own = pl.ds(pl.multiple_of(lax.axis_index("tp") * rows_local, rows_local), rows_local)
    step = lax.broadcasted_iota(jnp.int32, (rows_local, HD), 0) % rows // GROUP
    lane = lax.broadcasted_iota(jnp.int32, (rows_local, HD), 1)
    found = [jnp.full((rows_local, HD), NEG, F32) for _ in range(new_count)]

    def spread(block, first):
        parts = [block[first + 2 * g : first + 2 * g + 1] for g in range(kv_local)]
        return jnp.concatenate([jnp.broadcast_to(a, (rows, HD)) for a in parts], axis=0)

    for ds in range(n_seq):
        for rr in range(own_rows):
            request = (seq ^ reverse(n_seq)[ds]) * own_rows + rr
            q = new[ds][rr, own].astype(F32)
            both = new[ds][rr, KVH * rows :].astype(F32)
            for n in range(new_count):
                first = n * 2 * kv_local
                s = jnp.sum(q * spread(both, first), axis=1, keepdims=True) * scale
                found[n] = jnp.where((lane == request) & (step >= n), s, found[n])
                value_ref[request * new_count + n] = spread(both, first + 1)
    for n in range(new_count):
        score_ref[n] = found[n]


def fresh_scores(new, after, prompts, new_count, n_tp):
    n_seq = len(new)
    rows = (new[0].shape[1] - FRESH) // n_tp
    return pl.pallas_call(
        functools.partial(fresh_kernel, n_seq),
        in_specs=[VMEM] * n_seq + [ANY],
        out_specs=[VMEM, VMEM],
        out_shape=[
            jax.ShapeDtypeStruct((new_count, rows, HD), F32),
            jax.ShapeDtypeStruct((prompts * new_count, rows, HD), F32),
        ],
        compiler_params=pltpu.CompilerParams(vmem_limit_bytes=16 * MIB),
        cost_estimate=pl.CostEstimate(flops=0, bytes_accessed=2 * MIB, transcendentals=0),
        name="fresh",
    )(*new, after)


def weights_kernel(pages, prompts, n_tp, *refs):
    chunks = refs[:n_tp]
    meta, _, w_ref, stats_ref = refs[n_tp:]
    rows, tokens = w_ref.shape
    local_pages = tokens // PAGE
    first = lax.axis_index("seq") * local_pages
    lane = lax.broadcasted_iota(jnp.int32, (rows, PAGE), 1)
    scores, maxima, masks, owners = [], [], [], []
    for p in range(local_pages):
        at = slice(p * PAGE, (p + 1) * PAGE)
        total = chunks[0][:, at].astype(F32)
        for d in range(1, n_tp):
            total = total + chunks[d][:, at].astype(F32)
        mask = lane < meta[2 * pages + first + p]
        total = jnp.where(mask, total, NEG)
        masks.append(mask)
        scores.append(total)
        maxima.append(jnp.max(total, axis=1, keepdims=True))
        owners.append(meta[first + p])
    quarter = lane // prompts
    spot = lane % prompts
    stats = jnp.where(quarter == 0, NEG, 0.0)
    same = [owners[p] == owners[p - 1] for p in range(1, local_pages)]
    for p in range(1, local_pages):
        maxima[p] = jnp.where(same[p - 1], jnp.maximum(maxima[p - 1], maxima[p]), maxima[p])
    for p in reversed(range(local_pages - 1)):
        maxima[p] = jnp.where(same[p], maxima[p + 1], maxima[p])
    for p in range(local_pages):
        top = maxima[p]
        high = top.astype(BF16).astype(F32)
        low = (top - high).astype(BF16).astype(F32)
        w = jnp.where(masks[p], jnp.exp(scores[p] - (high + low)), 0.0)
        w_ref[:, p * PAGE : (p + 1) * PAGE] = w.astype(BF16)
        here = spot == owners[p]
        stats = jnp.where(here & (quarter == 0), high, stats)
        stats = jnp.where(here & (quarter == 1), low, stats)
        part = jnp.sum(w, axis=1, keepdims=True)
        stats = stats + jnp.where(here & (quarter == 2), part, 0.0)
    high = stats.astype(BF16).astype(F32)
    low = pltpu.roll(stats - high, prompts, 1)
    stats_ref[...] = jnp.where(quarter == 3, low, stats).astype(BF16)


def softmax_weights(chunks, meta, after, pages, prompts):
    n_tp = len(chunks)
    rows, tokens = chunks[0].shape
    return pl.pallas_call(
        functools.partial(weights_kernel, pages, prompts, n_tp),
        in_specs=[VMEM] * n_tp + [SMEM, ANY],
        out_specs=[VMEM, VMEM],
        out_shape=[
            jax.ShapeDtypeStruct((rows, tokens), BF16),
            jax.ShapeDtypeStruct((rows, PAGE), BF16),
        ],
        compiler_params=pltpu.CompilerParams(vmem_limit_bytes=8 * MIB),
        name="weights",
    )(*chunks, meta, after)


def weighted_kernel(n_tp, *refs):
    pieces = refs[:n_tp]
    va_ref, vb_ref, meta = refs[n_tp : n_tp + 3]
    outs = refs[n_tp + 3 : n_tp + 3 + n_tp]
    ready, total, table, sem = refs[n_tp + 3 + n_tp :]
    copy = pltpu.make_async_copy(meta, table, sem)
    copy.start()
    rows_local, tokens_here = pieces[0].shape
    kv_local = KVH // n_tp
    rows = rows_local // kv_local
    local_pages = tokens_here // PAGE
    first = lax.axis_index("seq") * local_pages
    me = lax.axis_index("tp")
    own = [pl.ds(pl.multiple_of((me ^ order(n_tp)[d]) * rows_local, rows_local), rows_local) for d in range(n_tp)]
    for d in range(n_tp):
        at = pl.multiple_of((me ^ reverse(n_tp)[d]) * rows_local, rows_local)
        ready[pl.ds(at, rows_local)] = pieces[d][...]
    total[...] = jnp.zeros_like(total)
    half = va_ref.shape[1] // HD
    none = jnp.zeros((2 * rows, PAGE), BF16)
    copy.wait()
    for p in range(0, local_pages, 2):
        requests = [table[first + p], table[first + p + 1]]
        tokens = slice(p * PAGE, (p + 2) * PAGE)
        for pair in range(KVH // 2):
            head = 2 * pair
            v_ref = va_ref if head < half else vb_ref
            v = v_ref[tokens, head % half * HD : (head % half + 2) * HD]
            at = slice(head * rows, (head + 2) * rows)
            w = [ready[at, (p + i) * PAGE : (p + i + 1) * PAGE] for i in range(2)]
            w = [jnp.concatenate([w[0], none], axis=1), jnp.concatenate([none, w[1]], axis=1)]
            sums = jnp.dot(jnp.concatenate(w, axis=0), v, preferred_element_type=F32)
            for i, request in enumerate(requests):
                for h in range(2):
                    row = (2 * i + h) * rows
                    part = sums[row : row + rows, h * HD : (h + 1) * HD]
                    total[request, (head + h) * rows : (head + h + 1) * rows] += part
    for d in range(n_tp):
        outs[d][...] = total[:, own[d]].astype(BF16)


def weighted_values(pieces, va, vb, meta, prompts):
    n_tp = len(pieces)
    rows, tokens = pieces[0].shape
    return pl.pallas_call(
        functools.partial(weighted_kernel, n_tp),
        in_specs=[VMEM] * (n_tp + 2) + [pl.BlockSpec(memory_space=pltpu.HBM)],
        out_specs=[VMEM] * n_tp,
        out_shape=[jax.ShapeDtypeStruct((prompts, rows, HD), BF16)] * n_tp,
        scratch_shapes=[
            pltpu.VMEM((rows * n_tp, tokens), BF16),
            pltpu.VMEM((prompts, rows * n_tp, HD), F32),
            pltpu.SMEM(meta.shape, jnp.int32),
            pltpu.SemaphoreType.DMA,
        ],
        compiler_params=pltpu.CompilerParams(vmem_limit_bytes=24 * MIB),
        cost_estimate=pl.CostEstimate(
            flops=2 * tokens * rows * n_tp * HD, bytes_accessed=8 * MIB, transcendentals=0
        ),
        name="weighted",
    )(*pieces, va, vb, in_hbm(meta))


def summed_kernel(n_tp, *refs):
    chunks = refs[:n_tp]
    stats_ref, out_ref = refs[n_tp:]
    prompts = chunks[0].shape[0]
    total = chunks[0][...].astype(F32)
    for d in range(1, n_tp):
        total = total + chunks[d][...].astype(F32)
    out_ref[:prompts] = total.astype(BF16)
    out_ref[prompts] = stats_ref[...]


def summed(chunks, stats):
    n_tp = len(chunks)
    prompts, rows, _ = chunks[0].shape
    return pl.pallas_call(
        functools.partial(summed_kernel, n_tp),
        in_specs=[VMEM] * (n_tp + 1),
        out_specs=VMEM,
        out_shape=jax.ShapeDtypeStruct((prompts + 1, rows, HD), BF16),
        compiler_params=pltpu.CompilerParams(vmem_limit_bytes=8 * MIB),
        cost_estimate=pl.CostEstimate(flops=0, bytes_accessed=4 * MIB, transcendentals=0),
        name="summed",
    )(*chunks, stats)


def output_kernel(n_seq, *refs):
    pieces = refs[:n_seq]
    fresh_ref, value_ref, wa_ref, wb_ref, out_ref, held = refs[n_seq:]
    more, rows_local, _ = pieces[0].shape
    prompts = more - 1
    new_count = fresh_ref.shape[0]
    rows = new_count * GROUP
    kv_local = rows_local // rows
    heads = kv_local * GROUP
    tops, parts = [], []
    for s in range(n_seq):
        stats = pieces[s][prompts].astype(F32)
        folded = stats + pltpu.roll(stats, HD - prompts, 1)
        tops.append(folded)
        parts.append(pltpu.roll(folded, HD - 2 * prompts, 1))
    fresh = [fresh_ref[n] for n in range(new_count)]
    top = fresh[0]
    for other in fresh[1:] + tops:
        top = jnp.maximum(top, other)
    weights = [jnp.exp(f - top) for f in fresh]
    factors = [jnp.exp(t - top) for t in tops]
    total = weights[0]
    for w in weights[1:]:
        total = total + w
    for f, part in zip(factors, parts):
        total = total + f * part
    weights = [w / total for w in weights]
    factors = [f / total for f in factors]
    for r in range(prompts):
        sums = jnp.zeros((rows_local, HD), F32)
        for s in range(n_seq):
            sums = sums + factors[s][:, r : r + 1] * pieces[s][r].astype(F32)
        for n in range(new_count):
            sums = sums + weights[n][:, r : r + 1] * value_ref[r * new_count + n]
        for g in range(kv_local):
            for n in range(new_count):
                at = g * rows + n * GROUP
                held[g * GROUP : (g + 1) * GROUP, r * new_count + n] = sums[at : at + GROUP]
    half = heads // 2
    product = jnp.zeros(out_ref.shape, F32)
    for w_ref, at in ((wa_ref, 0), (wb_ref, half)):
        left = [held[h].astype(BF16) for h in range(at, at + half)]
        left = jnp.concatenate(left, axis=1)
        product = product + jnp.dot(left, w_ref[...], preferred_element_type=F32)
    out_ref[...] = product.astype(BF16)


def output_partial(pieces, fresh, values, weights):
    n_seq = len(pieces)
    new_count = fresh.shape[0]
    prompts = pieces[0].shape[0] - 1
    depth, columns = weights[0].shape
    return pl.pallas_call(
        functools.partial(output_kernel, n_seq),
        in_specs=[VMEM] * (n_seq + 4),
        out_specs=VMEM,
        out_shape=jax.ShapeDtypeStruct((prompts * new_count, columns), BF16),
        scratch_shapes=[pltpu.VMEM((2 * depth // HD, prompts * new_count, HD), F32)],
        compiler_params=pltpu.CompilerParams(vmem_limit_bytes=24 * MIB),
        name="output",
    )(*pieces, fresh, values, *weights)


def final_kernel(n_tp, *refs):
    pieces = refs[:n_tp]
    res_ref, out_ref = refs[n_tp:]
    prompts, new_count, _ = out_ref.shape
    total = pieces[0][...].astype(F32)
    for d in range(1, n_tp):
        total = total + pieces[d][...].astype(F32)
    for r in range(prompts):
        out_ref[r] = res_ref[r].astype(F32) + total[r * new_count : (r + 1) * new_count]


def final_sum(pieces, residual):
    n_tp = len(pieces)
    return pl.pallas_call(
        functools.partial(final_kernel, n_tp),
        in_specs=[VMEM] * (n_tp + 1),
        out_specs=VMEM,
        out_shape=jax.ShapeDtypeStruct(residual.shape, F32),
        compiler_params=pltpu.CompilerParams(vmem_limit_bytes=8 * MIB),
        name="final",
    )(*pieces, residual)


def on_device(
    prefill_states, kv_weight, page_counts, tail_tokens, new_query, new_keyval, residual, out_weight
):
    n_seq, n_tp = lax.axis_size("seq"), lax.axis_size("tp")
    own_rows, new_count, _ = new_query.shape
    prompts = page_counts.shape[0]
    pages = prefill_states.shape[0] // PAGE * n_seq
    query = gather(new_query, "tp", falling(n_tp))
    acc, xa, wa, cosine, sine, cos_q, sin_q, meta = load(
        prefill_states, kv_weight, page_counts, tail_tokens, pages, new_count
    )
    new = turned(query, new_keyval, cos_q, sin_q)
    k, xb, wb = rotated_keys(acc, xa, wa, prefill_states, kv_weight, cosine, sine, new)
    new = gather(new, "seq")
    scores = partial_scores(new, k, meta, prompts, n_tp)
    va, oa = project_values((xa, wa, xb, wb), out_weight, 0, scores[0])
    weights, stats = softmax_weights(exchange(scores, "tp"), meta, va, pages, prompts)
    vb, ob = project_values((xa, wa, xb, wb), out_weight, 1, stats)
    fresh, values = fresh_scores(new, stats, prompts, new_count, n_tp)
    chunks = weighted_values(gather(weights, "tp"), va, vb, meta, prompts)
    pieces = gather(summed(exchange(chunks, "tp"), stats), "seq")
    partial = output_partial(pieces, fresh, values, (oa, ob))
    return final_sum(gather(partial, "tp"), residual)


def solution(mesh):
    placed = (
        P(("groups", "seq"), "tp"),
        P("tp", None),
        P("groups"),
        P("groups"),
        P(("groups", "seq"), None, "tp"),
        P(("groups", "seq"), None, "tp"),
        P("groups", None, "seq"),
        P("tp", "seq"),
    )
    return jax.shard_map(
        on_device, mesh=mesh, in_specs=placed, out_specs=P("groups", None, "seq"), check_vma=False
    )
```
